32 devices in a mesh: wide: 16 (over z, y, core), narrow: 2 (over x).
Axes of the slice: x: 2, y: 2, z: 4, core: 2. Of those that a mesh axis runs over, the one named last changes fastest.
Arguments:
- adjoint_rhs: bfloat16 [16, 2, 768, 256], P('wide', 'narrow'), may hold values from -6 to 6
- inverse_rows: bfloat16 [16, 2, 768, 1024], P('wide', 'narrow'), may hold values from -0.2 to 1.2
- blocks: bfloat16 [16, 2, 6, 3, 128, 128], P('wide', 'narrow'), may hold values from -0.3 to 1.3
- block_cols: int32 [16, 2, 6, 3], P('wide', 'narrow'), may hold values from 0 to 7, as said below
- send_rows: int32 [16, 2, 4, 64], P('wide', 'narrow'), may hold values from 0 to 767, as said below
- cov_plane: bfloat16 [192, 192], replicated, may hold values from -0.4375 to 0.4375
- cov_vert: bfloat16 [128, 128], replicated, may hold values from -0.5 to 0.5
Outputs:
- adjoint: bfloat16 [16, 2, 768, 256], P('wide', 'narrow')
- smoothed: bfloat16 [16, 2, 768, 256], P('wide', 'narrow')
The draws below stay inside these ranges and needn't reach their ends.
Inputs may be any that keep to these rules, and one draw needn't show every extreme that they name: `block_cols`: entry 0 of every block row's list is that block row itself; subdomain blocks are numbered with the own blocks first, then the margin. `send_rows`: the 256 entries of one device are distinct and include rows 0 and 767.
All inputs are finite; a program needn't handle non-finite values.
Results may differ from the reference program's by a relative error of at most 0.0085.
Values may be sent and summed in bfloat16 or wider, within the bound.
No kernel may reach another device: no remote copies, remote signals or barrier semaphores. Data moves between devices by JAX's collectives and lax.ppermute only.
A program may use at most 64 MiB of HBM per device.

```python
import math
import jax
import jax.numpy as jnp

SUB = 1024
OV = 64
BS = 128
LINKS = 3
ZL = 64
SWEEPS = 4
NRHS = 256
OWN = 768
TILE = 12
TILES = 16
SLABS = 2
PLANE = 192
NZ = 128


def draw_inverse_rows(key, part):
    noise = jax.random.normal(key, (TILES, SLABS, OWN, SUB), jnp.float32)
    noise = jnp.clip(noise, -6.0, 6.0) * (0.3 / math.sqrt(SUB))
    identity = (jnp.arange(OWN)[:, None] == jnp.arange(SUB)[None, :]).astype(jnp.float32)
    return (identity + noise).astype(jnp.bfloat16)


def draw_blocks(key, part):
    noise = jax.random.normal(key, (TILES, SLABS, OWN // BS, LINKS, BS, BS), jnp.float32)
    noise = jnp.clip(noise, -6.0, 6.0) * (0.25 / math.sqrt(BS))
    identity = (jnp.arange(BS)[:, None] == jnp.arange(BS)[None, :]).astype(jnp.float32)
    first_link = (jnp.arange(LINKS) == 0).astype(jnp.float32)
    diagonal = first_link[:, None, None] * identity[None, :, :]
    return (noise + diagonal[None, None, None]).astype(jnp.bfloat16)


def draw_block_cols(key, part):
    array_dims = (TILES, SLABS, OWN // BS, LINKS)
    choices_drawn = jax.random.randint(key, array_dims, 0, SUB // BS)
    own_block = jnp.arange(OWN // BS, dtype=jnp.int32)[None, None, :, None]
    first_link = (jnp.arange(LINKS) == 0)[None, None, None, :]
    return jnp.where(first_link, own_block, choices_drawn).astype(jnp.int32)


def draw_send_rows(key, part):
    scores = jax.random.randint(key, (TILES, SLABS, OWN), 0, 1 << 20)
    position = jnp.arange(OWN, dtype=jnp.int32)
    scores = scores * OWN + position[None, None, :]
    scores = jnp.where(position == 0, -2, jnp.where(position == OWN - 1, -1, scores))
    ordering = jnp.argsort(scores, axis=-1, stable=True)
    return ordering[:, :, :4 * OV].reshape(TILES, SLABS, 4, OV).astype(jnp.int32)


def levels(rng, dims, cuts, smallest, top_value):
    def one(dim, shards_of):
        steps = jax.random.uniform(jax.random.fold_in(jax.random.fold_in(rng, 6), dim), (shards_of,), jnp.float32, smallest / len(cuts), top_value / len(cuts))
        return jnp.repeat(jnp.exp(steps), dims[dim] // shards_of).reshape((-1,) + (1,) * (len(dims) - dim - 1))

    gain = one(*cuts[0])
    for cut in cuts[1:]:
        gain = gain * one(*cut)
    return gain


def scatter_about(stream_key, dims, width, bound, cuts=(), kind=jnp.bfloat16):
    result = width * jax.random.normal(stream_key, dims, jnp.float32)
    if cuts:
        result = result * levels(stream_key, dims, cuts, -0.22, 0.18)
    return jnp.clip(result, -bound, bound).astype(kind)


def setup_inputs(seed: int = 0) -> dict:
    keys = jax.random.split(jax.random.key(seed), 8)
    return {
        "adjoint_rhs": scatter_about(keys[0], (TILES, SLABS, OWN, NRHS), 1.0, 6.0, ((0, 16), (1, 2))),
        "inverse_rows": draw_inverse_rows(jax.random.fold_in(keys[7], 71), 0),
        "blocks": draw_blocks(jax.random.fold_in(keys[7], 71), 0),
        "block_cols": draw_block_cols(jax.random.fold_in(keys[7], 71), 0),
        "send_rows": draw_send_rows(jax.random.fold_in(keys[7], 71), 0),
        "cov_plane": scatter_about(keys[5], (PLANE, PLANE), PLANE ** -0.5, 0.4375),
        "cov_vert": scatter_about(keys[6], (NZ, NZ), NZ ** -0.5, 0.5),
    }


def pick_rows(values, rows_index):
    return jax.vmap(jax.vmap(lambda matrix, index_list: matrix[index_list]))(values, rows_index)


def neighbour_rows(picked):
    zeros_wide = jnp.zeros_like(picked[:1, :, 0])
    lower_wide = jnp.concatenate([zeros_wide, picked[:-1, :, 1]], axis=0)
    upper_wide = jnp.concatenate([picked[1:, :, 0], zeros_wide], axis=0)
    zeros_narrow = jnp.zeros_like(picked[:, :1, 2])
    lower_narrow = jnp.concatenate([zeros_narrow, picked[:, :-1, 3]], axis=1)
    upper_narrow = jnp.concatenate([picked[:, 1:, 2], zeros_narrow], axis=1)
    return jnp.concatenate([lower_wide, upper_wide, lower_narrow, upper_narrow], axis=2)


def apply_local(subdomain, block_values, block_index):
    block_size = block_values.shape[-1]
    tiled = subdomain.reshape(-1, block_size, subdomain.shape[-1])[block_index]
    product = jnp.einsum("jkab,jkbr->jar", block_values.astype(jnp.float32), tiled.astype(jnp.float32))
    return product.reshape(-1, subdomain.shape[-1])


def solve_part(left, right):
    return jnp.dot(left, right, preferred_element_type=jnp.float32)


def reference(adjoint_rhs, inverse_rows, blocks, block_cols, send_rows, cov_plane, cov_vert):
    local_apply = jax.vmap(jax.vmap(apply_local))
    solve_apply = jax.vmap(jax.vmap(solve_part))
    adjoint_f = jnp.zeros(adjoint_rhs.shape, jnp.float32)
    for sweep_index in range(SWEEPS):
        rounded = adjoint_f.astype(jnp.bfloat16)
        halo_x = neighbour_rows(pick_rows(rounded, send_rows))
        sub_x = jnp.concatenate([rounded, halo_x], axis=2)
        residual = (adjoint_rhs.astype(jnp.float32) - local_apply(sub_x, blocks, block_cols)).astype(jnp.bfloat16)
        halo_r = neighbour_rows(pick_rows(residual, send_rows))
        adjoint_f = adjoint_f + solve_apply(inverse_rows, jnp.concatenate([residual, halo_r], axis=2))
    adjoint = adjoint_f.astype(jnp.bfloat16)
    layered = adjoint.reshape(TILES, SLABS, ZL, TILE, NRHS).transpose(1, 2, 0, 3, 4)
    layered = layered.reshape(SLABS, ZL, TILES * TILE, NRHS)
    planar = jnp.einsum("pq,nlqr->nlpr", cov_plane.astype(jnp.float32), layered.astype(jnp.float32)).astype(jnp.bfloat16)
    columns = planar.reshape(SLABS * ZL, TILES * TILE * NRHS)
    vertical_mix = jnp.dot(cov_vert, columns, preferred_element_type=jnp.float32).astype(jnp.bfloat16)
    smoothed = vertical_mix.reshape(SLABS, ZL, TILES, TILE, NRHS).transpose(2, 0, 1, 3, 4)
    smoothed = smoothed.reshape(TILES, SLABS, OWN, NRHS)
    return adjoint, smoothed
```

```python
import functools

import jax
import jax.numpy as jnp
from jax import lax
from jax.experimental import pallas as pl
from jax.experimental.pallas import tpu as pltpu
from jax.sharding import PartitionSpec as P

ZL = 64
SWEEPS = 4
LANES = 128
BF = jnp.bfloat16
F32 = jnp.float32
VM = pl.BlockSpec(memory_space=pltpu.VMEM)
SM = pl.BlockSpec(memory_space=pltpu.SMEM)


def matchings():
    found = []
    for place, axis in enumerate(("wide", "narrow")):
        count = lax.axis_size(axis)
        for parity in range(2):
            pairs = []
            for i in range(parity, count - 1, 2):
                pairs += [(i, i + 1), (i + 1, i)]
            if pairs:
                found.append((place, axis, parity, tuple(pairs)))
    return found


def swap(messages, found):
    return [lax.ppermute(m, axis, list(pairs)) for m, (_, axis, _, pairs) in zip(messages, found)]


def mm(a, b):
    return jnp.dot(a, b, preferred_element_type=F32)


def mm_t(a, b):
    return lax.dot_general(a, b, (((1,), (1,)), ((), ())), preferred_element_type=F32)


def iota(shape, dim):
    return lax.broadcasted_iota(jnp.int32, shape, dim)


def call(body, outs, args, scratch=(), specs=None, flops=0):
    size = sum(a.size * a.dtype.itemsize for a in args)
    return pl.pallas_call(
        body,
        out_shape=outs,
        in_specs=specs or [VM] * len(args),
        out_specs=[VM] * len(outs),
        scratch_shapes=list(scratch),
        compiler_params=pltpu.CompilerParams(vmem_limit_bytes=16 * 1024 * 1024),
        cost_estimate=pl.CostEstimate(flops=flops, bytes_accessed=size, transcendentals=0),
    )(*args)


def fill_halo(halo_ref, base, flags_ref, found, got):
    width = got[0].shape[0]
    kinds = {}
    for m, (place, _, _, _) in enumerate(found):
        kinds.setdefault(place, []).append(m)
    for place in range(2):
        members = kinds.get(place, [])
        if len(members) < 2:
            zeros = jnp.zeros((2 * width, halo_ref.shape[1]), halo_ref.dtype)
            halo_ref[base + 2 * place * width:base + (2 * place + 2) * width, :] = zeros
        for m in members:
            start = pl.multiple_of(base + (2 * place + flags_ref[m]) * width, width)
            halo_ref[pl.ds(start, width), :] = got[m][...]


def pick_body(found, flags_ref, send_ref, rhs_ref, *outs):
    width = send_ref.shape[1]
    own = rhs_ref.shape[0]
    select_ref = outs[0]
    diagonal = iota((width, width), 0) == iota((width, width), 1)
    for m, (place, _, _, _) in enumerate(found):
        rows = jnp.where(
            flags_ref[m] == 1,
            send_ref[2 * place + 1:2 * place + 2, :],
            send_ref[2 * place:2 * place + 1, :],
        ).astype(F32)
        column = jnp.sum(jnp.where(diagonal, rows, 0.0), axis=1, keepdims=True).astype(jnp.int32)
        chosen = (iota((width, own), 1) == column).astype(F32).astype(BF)
        select_ref[m * width:(m + 1) * width, :] = chosen
    send_picked(select_ref, rhs_ref, outs[1:])


def send_picked(select_ref, values_ref, messages):
    picked = mm(select_ref[...], values_ref[...]).astype(BF)
    width = messages[0].shape[0]
    for m, message in enumerate(messages):
        message[...] = picked[m * width:(m + 1) * width, :]


def update_body(found, first, last, flags_ref, inverse_ref, resid_ref, select_ref, *rest):
    count = len(found)
    got, rest = rest[:count], list(rest[count:])
    old_ref = None if first else rest.pop(0)
    halo_ref = rest.pop()
    own, columns = resid_ref.shape
    fill_halo(halo_ref, 0, flags_ref, found, got)
    step = 256
    round_ref = rest.pop(0)
    new_ref = None if last else rest.pop(0)
    for i in range(0, own, step):
        part = mm(inverse_ref[i:i + step, :own], resid_ref[...])
        part = part + mm(inverse_ref[i:i + step, own:], halo_ref[...])
        if not first:
            part = old_ref[i:i + step, :] + part
        if not last:
            new_ref[i:i + step, :] = part
        round_ref[i:i + step, :] = part.astype(BF)
    if not last:
        send_picked(select_ref, round_ref, rest)


def residual_body(found, flags_ref, cols_ref, blocks_ref, rhs_ref, round_ref, select_ref, *rest):
    count = len(found)
    got, rest = rest[:count], list(rest[count:])
    sub_ref = rest.pop()
    resid_ref = rest.pop(0)
    own, columns = rhs_ref.shape
    sub_ref[:own, :] = round_ref[...]
    fill_halo(sub_ref, own, flags_ref, found, got)
    rows, links, size, _ = blocks_ref.shape
    for j in range(rows):
        total = None
        for k in range(links):
            start = pl.multiple_of(cols_ref[j * links + k] * size, size)
            part = mm(blocks_ref[j, k], sub_ref[pl.ds(start, size), :])
            total = part if total is None else total + part
        here = slice(j * size, (j + 1) * size)
        resid_ref[here, :] = (rhs_ref[here, :].astype(F32) - total).astype(BF)
    send_picked(select_ref, resid_ref, rest)


def one_hot(rows_of, shape):
    return (iota(shape, 0) == rows_of(iota((1, shape[1]), 1))).astype(F32).astype(BF)


def tables_body(wide, narrow, cov_plane_ref, cov_vert_ref, order_ref, plane_ref, spread_ref, vert_ref):
    own = order_ref.shape[0]
    tile = own // ZL
    order_ref[...] = one_hot(lambda k: lax.rem(k, ZL) * tile + lax.div(k, ZL), (own, own))
    plane = wide * tile
    turn = one_hot(lambda k: lax.rem(k, wide) * tile + lax.div(k, wide), (plane, plane))
    half = mm(cov_plane_ref[...], turn).astype(BF)
    plane_ref[...] = mm(half.T, turn).astype(BF).T
    share = LANES // ZL
    depth = narrow * ZL
    width = narrow * LANES

    def source(k):
        e, n, l = lax.div(k, depth), lax.rem(lax.div(k, ZL), narrow), lax.rem(k, ZL)
        return n * LANES + e * ZL + l

    spread = one_hot(source, (width, width))
    spread_ref[...] = spread
    turned = cov_vert_ref[...].astype(F32).T
    zero = jnp.zeros_like(turned)
    blocks = jnp.concatenate(
        [jnp.concatenate([turned if i == e else zero for i in range(share)], axis=1) for e in range(share)],
        axis=0,
    ).astype(BF)
    vert_ref[...] = mm_t(blocks, spread).astype(BF)


def wire_body(round_ref, order_ref, wire_ref):
    step = 256
    own = order_ref.shape[1]
    for i in range(0, own, step):
        turned = lax.dot_general(
            round_ref[...], order_ref[:, i:i + step], (((0,), (0,)), ((), ())), preferred_element_type=F32
        )
        wire_ref[:, i:i + step] = turned.astype(BF)


def mix_body(wide, narrow, group, in_ref, plane_ref, spread_ref, vert_ref, out_ref, cells_ref, flat_ref, wire_ref):
    own = in_ref.shape[1]
    tile = own // ZL
    share = LANES // ZL
    depth = narrow * ZL
    block = narrow * group
    taken = in_ref[...].astype(F32).reshape(wide, narrow, group, own)
    slabs = [taken[:, n].reshape(wide * group, own).astype(BF) for n in range(narrow)]
    for g in range(tile // share):
        lanes = slice(g * LANES, (g + 1) * LANES)
        joined = jnp.concatenate([s[:, lanes] for s in slabs], axis=1)
        spread = mm(joined, spread_ref[...])
        for e in range(share):
            cells_ref[g * share + e] = spread[:, e * depth:(e + 1) * depth]
    for r in range(group):
        for c in range(tile):
            flat_ref[c * wide:(c + 1) * wide, r * depth:(r + 1) * depth] = cells_ref[
                c, pl.ds(r, wide, stride=group), :
            ].astype(BF)
    planar = mm(plane_ref[...], flat_ref[...]).astype(BF)
    for g in range(tile // share):
        stacked = jnp.concatenate(
            [
                jnp.concatenate(
                    [
                        planar[c * wide:(c + 1) * wide, r * depth:(r + 1) * depth]
                        for c in range(g * share, (g + 1) * share)
                    ],
                    axis=1,
                )
                for r in range(group)
            ],
            axis=0,
        )
        mixed = mm(stacked, vert_ref[...])
        for r in range(group):
            for n in range(narrow):
                wire_ref[g, pl.ds(n * group + r, wide, stride=block), :] = mixed[
                    r * wide:(r + 1) * wide, n * LANES:(n + 1) * LANES
                ]
        out_ref[:, g * LANES:(g + 1) * LANES] = wire_ref[g].astype(BF)


def unwire_body(in_ref, order_ref, out_ref):
    step = 256
    for i in range(0, out_ref.shape[0], step):
        out_ref[i:i + step, :] = mm_t(order_ref[i:i + step, :], in_ref[...]).astype(BF)


def smooth_by_columns(adjoint, cov_plane, cov_vert):
    wide, narrow = lax.axis_size("wide"), lax.axis_size("narrow")
    own, columns = adjoint.shape
    devices = wide * narrow
    group = columns // devices
    width = narrow * LANES
    plane = cov_plane.shape[0]
    depth = narrow * ZL
    tile = own // ZL
    shape = jax.ShapeDtypeStruct
    order, plane_mix, spread, vert_mix = call(
        functools.partial(tables_body, wide, narrow),
        [shape((own, own), BF), shape((plane, plane), BF), shape((width, width), BF), shape((width, width), BF)],
        [cov_plane, cov_vert],
    )
    (wire,) = call(wire_body, [shape((columns, own), BF)], [adjoint, order])
    there = lax.all_to_all(
        wire.reshape(devices, group, own), ("wide", "narrow"), split_axis=0, concat_axis=0, tiled=True
    )
    (mixed,) = call(
        functools.partial(mix_body, wide, narrow, group),
        [shape((columns, own), BF)],
        [there.reshape(columns, own), plane_mix, spread, vert_mix],
        [
            pltpu.VMEM((tile, wide * group, depth), F32),
            pltpu.VMEM((plane, group * depth), BF),
            pltpu.VMEM((tile * ZL // LANES, columns, LANES), F32),
        ],
    )
    back = lax.all_to_all(
        mixed.reshape(devices, group, own), ("wide", "narrow"), split_axis=0, concat_axis=0, tiled=True
    )
    (smoothed,) = call(unwire_body, [shape((own, columns), BF)], [back.reshape(columns, own), order])
    return smoothed


def smooth_by_layers(adjoint, cov_plane, cov_vert):
    own, columns = adjoint.shape
    layered = adjoint.reshape(ZL, own // ZL, -1)
    planar = jnp.einsum(
        "pq,lqr->lpr",
        cov_plane,
        lax.all_to_all(layered, "wide", split_axis=0, concat_axis=1, tiled=True),
        preferred_element_type=F32,
    ).astype(BF)
    restored = lax.all_to_all(planar, "wide", split_axis=1, concat_axis=0, tiled=True)
    slab_weights = lax.dynamic_slice_in_dim(cov_vert, lax.axis_index("narrow") * ZL, ZL, 0)
    summed = jnp.dot(
        slab_weights,
        lax.all_gather(restored.reshape(ZL, -1), "narrow", axis=0, tiled=True),
        preferred_element_type=F32,
    )
    return summed.astype(BF).reshape(own, -1)


def shards(adjoint_rhs, inverse_rows, blocks, block_cols, send_rows, cov_plane, cov_vert):
    rhs = adjoint_rhs[0, 0]
    inverse = inverse_rows[0, 0]
    block_values = blocks[0, 0]
    cols = block_cols[0, 0].reshape(-1)
    send = send_rows[0, 0]
    own, columns = rhs.shape
    width = send.shape[1]
    wide, narrow = lax.axis_size("wide"), lax.axis_size("narrow")
    found = matchings()
    count = len(found)
    flags = jnp.stack([(lax.axis_index(axis) % 2 == parity).astype(jnp.int32) for _, axis, parity, _ in found])
    shape = jax.ShapeDtypeStruct
    note = shape((width, columns), BF)
    cells = shape((own, columns), BF)
    select, *messages = call(
        functools.partial(pick_body, found),
        [shape((count * width, own), BF)] + [note] * count,
        [flags, send, rhs],
        specs=[SM, VM, VM],
    )
    halo = pltpu.VMEM((4 * width, columns), BF)
    resid = rhs
    iterate = None
    for sweep in range(SWEEPS):
        first, last = sweep == 0, sweep == SWEEPS - 1
        if not first:
            got = swap(messages, found)
            resid, *messages = call(
                functools.partial(residual_body, found),
                [cells] + [note] * count,
                [flags, cols, block_values, rhs, rounded, select, *got],
                [pltpu.VMEM((own + 4 * width, columns), BF)],
                [SM, SM] + [VM] * (4 + count),
            )
        got = swap(messages, found)
        outs = [cells] if last else [cells, shape((own, columns), F32)] + [note] * count
        rounded, *rest = call(
            functools.partial(update_body, found, first, last),
            outs,
            [flags, inverse, resid, select, *got] + ([] if first else [iterate]),
            [halo],
            [SM] + [VM] * (3 + count + (0 if first else 1)),
        )
        if not last:
            iterate, *messages = rest
    group = columns // (wide * narrow)
    by_columns = columns % (wide * narrow) == 0 and group % 8 == 0 and narrow * ZL == LANES and wide % 16 == 0
    smooth = smooth_by_columns if by_columns else smooth_by_layers
    smoothed = smooth(rounded, cov_plane, cov_vert)
    return (rounded[None, None], smoothed[None, None])


def solution(mesh):
    in_specs = (
        P("wide", "narrow", None, None),
        P("wide", "narrow", None, None),
        P("wide", "narrow", None, None, None, None),
        P("wide", "narrow", None, None),
        P("wide", "narrow", None, None),
        P(),
        P(),
    )
    out_specs = (P("wide", "narrow", None, None), P("wide", "narrow", None, None))
    return jax.shard_map(shards, mesh=mesh, in_specs=in_specs, out_specs=out_specs, check_vma=False)
```

```python
import functools

import jax
import jax.numpy as jnp
from jax import lax
from jax.experimental import pallas as pl
from jax.experimental.pallas import tpu as pltpu
from jax.sharding import PartitionSpec as P

ZL = 64
SWEEPS = 4
LANES = 128
BF = jnp.bfloat16
F32 = jnp.float32
VM = pl.BlockSpec(memory_space=pltpu.VMEM)
SM = pl.BlockSpec(memory_space=pltpu.SMEM)


def matchings():
    found = []
    for place, axis in enumerate(("wide", "narrow")):
        count = lax.axis_size(axis)
        for parity in range(2):
            pairs = []
            for i in range(parity, count - 1, 2):
                pairs += [(i, i + 1), (i + 1, i)]
            if pairs:
                found.append((place, axis, parity, tuple(pairs)))
    return sorted(found, key=lambda f: (f[0] == 0 and f[2] == 0, f[0], -f[2]))


def swap(messages, found):
    return [lax.ppermute(m, axis, list(pairs)) for m, (_, axis, _, pairs) in zip(messages, found)]


def mm(a, b):
    return jnp.dot(a, b, preferred_element_type=F32)


def mm_t(a, b):
    return lax.dot_general(a, b, (((1,), (1,)), ((), ())), preferred_element_type=F32)


def iota(shape, dim):
    return lax.broadcasted_iota(jnp.int32, shape, dim)


def call(body, outs, args, scratch=(), specs=None, flops=0):
    size = sum(a.size * a.dtype.itemsize for a in args)
    return pl.pallas_call(
        body,
        out_shape=outs,
        in_specs=specs or [VM] * len(args),
        out_specs=[VM] * len(outs),
        scratch_shapes=list(scratch),
        compiler_params=pltpu.CompilerParams(vmem_limit_bytes=6 * 1024 * 1024),
        cost_estimate=pl.CostEstimate(flops=flops, bytes_accessed=size, transcendentals=0),
    )(*args)


def fill_halo(halo_ref, base, flags_ref, found, got):
    width = got[0].shape[0]
    kinds = {}
    for m, (place, _, _, _) in enumerate(found):
        kinds.setdefault(place, []).append(m)
    for place in range(2):
        members = kinds.get(place, [])
        if len(members) < 2:
            zeros = jnp.zeros((2 * width, halo_ref.shape[1]), halo_ref.dtype)
            halo_ref[base + 2 * place * width:base + (2 * place + 2) * width, :] = zeros
        for m in members:
            start = pl.multiple_of(base + (2 * place + flags_ref[m]) * width, width)
            halo_ref[pl.ds(start, width), :] = got[m][...]


def pick_body(found, flags_ref, send_ref, rhs_ref, *outs):
    width = send_ref.shape[1]
    own = rhs_ref.shape[0]
    select_ref = outs[0]
    diagonal = iota((width, width), 0) == iota((width, width), 1)
    for m, (place, _, _, _) in enumerate(found):
        rows = jnp.where(
            flags_ref[m] == 1,
            send_ref[2 * place + 1:2 * place + 2, :],
            send_ref[2 * place:2 * place + 1, :],
        ).astype(F32)
        column = jnp.sum(jnp.where(diagonal, rows, 0.0), axis=1, keepdims=True).astype(jnp.int32)
        chosen = (iota((width, own), 1) == column).astype(F32).astype(BF)
        select_ref[m * width:(m + 1) * width, :] = chosen
    send_picked(select_ref, rhs_ref, outs[1:])


def send_picked(select_ref, values_ref, messages):
    picked = mm(select_ref[...], values_ref[...]).astype(BF)
    width = messages[0].shape[0]
    for m, message in enumerate(messages):
        message[...] = picked[m * width:(m + 1) * width, :]


def update_body(found, first, last, flags_ref, inverse_ref, resid_ref, select_ref, *rest):
    count = len(found)
    got, rest = rest[:count], list(rest[count:])
    old_ref = None if first else rest.pop(0)
    halo_ref = rest.pop()
    own, columns = resid_ref.shape
    fill_halo(halo_ref, 0, flags_ref, found, got)
    step = 256
    round_ref = rest.pop(0)
    new_ref = None if last else rest.pop(0)
    for i in range(0, own, step):
        part = mm(inverse_ref[i:i + step, :own], resid_ref[...])
        part = part + mm(inverse_ref[i:i + step, own:], halo_ref[...])
        if not first:
            part = old_ref[i:i + step, :] + part
        if not last:
            new_ref[i:i + step, :] = part
        round_ref[i:i + step, :] = part.astype(BF)
    if not last:
        send_picked(select_ref, round_ref, rest)


def residual_body(found, flags_ref, cols_ref, blocks_ref, rhs_ref, round_ref, select_ref, *rest):
    count = len(found)
    got, rest = rest[:count], list(rest[count:])
    sub_ref = rest.pop()
    resid_ref = rest.pop(0)
    own, columns = rhs_ref.shape
    sub_ref[:own, :] = round_ref[...]
    fill_halo(sub_ref, own, flags_ref, found, got)
    rows, links, size, _ = blocks_ref.shape
    for j in range(rows):
        total = None
        for k in range(links):
            start = pl.multiple_of(cols_ref[j * links + k] * size, size)
            part = mm(blocks_ref[j, k], sub_ref[pl.ds(start, size), :])
            total = part if total is None else total + part
        here = slice(j * size, (j + 1) * size)
        resid_ref[here, :] = (rhs_ref[here, :].astype(F32) - total).astype(BF)
    send_picked(select_ref, resid_ref, rest)


def one_hot(rows_of, shape):
    return (iota(shape, 0) == rows_of(iota((1, shape[1]), 1))).astype(F32).astype(BF)


def tables_body(wide, narrow, cov_plane_ref, cov_vert_ref, order_ref, plane_ref, spread_ref, vert_ref):
    own = order_ref.shape[0]
    tile = own // ZL
    order_ref[...] = one_hot(lambda k: lax.rem(k, ZL) * tile + lax.div(k, ZL), (own, own))
    plane = wide * tile
    turn = one_hot(lambda k: lax.rem(k, wide) * tile + lax.div(k, wide), (plane, plane))
    half = mm(cov_plane_ref[...], turn).astype(BF)
    plane_ref[...] = mm(half.T, turn).astype(BF).T
    share = LANES // ZL
    depth = narrow * ZL
    width = narrow * LANES

    def source(k):
        e, n, l = lax.div(k, depth), lax.rem(lax.div(k, ZL), narrow), lax.rem(k, ZL)
        return n * LANES + e * ZL + l

    spread = one_hot(source, (width, width))
    spread_ref[...] = spread
    turned = cov_vert_ref[...].astype(F32).T
    zero = jnp.zeros_like(turned)
    blocks = jnp.concatenate(
        [jnp.concatenate([turned if i == e else zero for i in range(share)], axis=1) for e in range(share)],
        axis=0,
    ).astype(BF)
    vert_ref[...] = mm_t(blocks, spread).astype(BF)


def wire_body(round_ref, order_ref, wire_ref):
    step = 256
    own = order_ref.shape[1]
    for i in range(0, own, step):
        turned = lax.dot_general(
            round_ref[...], order_ref[:, i:i + step], (((0,), (0,)), ((), ())), preferred_element_type=F32
        )
        wire_ref[:, i:i + step] = turned.astype(BF)


def mix_body(wide, narrow, group, in_ref, plane_ref, spread_ref, vert_ref, out_ref, cells_ref, flat_ref, wire_ref):
    own = in_ref.shape[1]
    tile = own // ZL
    share = LANES // ZL
    depth = narrow * ZL
    block = narrow * group
    taken = in_ref[...].astype(F32).reshape(wide, narrow, group, own)
    slabs = [taken[:, n].reshape(wide * group, own).astype(BF) for n in range(narrow)]
    for g in range(tile // share):
        lanes = slice(g * LANES, (g + 1) * LANES)
        joined = jnp.concatenate([s[:, lanes] for s in slabs], axis=1)
        spread = mm(joined, spread_ref[...])
        for e in range(share):
            cells_ref[g * share + e] = spread[:, e * depth:(e + 1) * depth]
    for r in range(group):
        for c in range(tile):
            flat_ref[c * wide:(c + 1) * wide, r * depth:(r + 1) * depth] = cells_ref[
                c, pl.ds(r, wide, stride=group), :
            ].astype(BF)
    planar = mm(plane_ref[...], flat_ref[...]).astype(BF)
    for g in range(tile // share):
        stacked = jnp.concatenate(
            [
                jnp.concatenate(
                    [
                        planar[c * wide:(c + 1) * wide, r * depth:(r + 1) * depth]
                        for c in range(g * share, (g + 1) * share)
                    ],
                    axis=1,
                )
                for r in range(group)
            ],
            axis=0,
        )
        mixed = mm(stacked, vert_ref[...])
        for r in range(group):
            for n in range(narrow):
                wire_ref[g, pl.ds(n * group + r, wide, stride=block), :] = mixed[
                    r * wide:(r + 1) * wide, n * LANES:(n + 1) * LANES
                ]
        out_ref[:, g * LANES:(g + 1) * LANES] = wire_ref[g].astype(BF)


def unwire_body(in_ref, order_ref, out_ref):
    step = 256
    for i in range(0, out_ref.shape[0], step):
        out_ref[i:i + step, :] = mm_t(order_ref[i:i + step, :], in_ref[...]).astype(BF)


def smooth_by_columns(adjoint, cov_plane, cov_vert):
    wide, narrow = lax.axis_size("wide"), lax.axis_size("narrow")
    own, columns = adjoint.shape
    devices = wide * narrow
    group = columns // devices
    width = narrow * LANES
    plane = cov_plane.shape[0]
    depth = narrow * ZL
    tile = own // ZL
    shape = jax.ShapeDtypeStruct
    order, plane_mix, spread, vert_mix = call(
        functools.partial(tables_body, wide, narrow),
        [shape((own, own), BF), shape((plane, plane), BF), shape((width, width), BF), shape((width, width), BF)],
        [cov_plane, cov_vert],
    )
    (wire,) = call(wire_body, [shape((columns, own), BF)], [adjoint, order])
    there = lax.all_to_all(
        wire.reshape(devices, group, own), ("wide", "narrow"), split_axis=0, concat_axis=0, tiled=True
    )
    (mixed,) = call(
        functools.partial(mix_body, wide, narrow, group),
        [shape((columns, own), BF)],
        [there.reshape(columns, own), plane_mix, spread, vert_mix],
        [
            pltpu.VMEM((tile, wide * group, depth), F32),
            pltpu.VMEM((plane, group * depth), BF),
            pltpu.VMEM((tile * ZL // LANES, columns, LANES), F32),
        ],
    )
    back = lax.all_to_all(
        mixed.reshape(devices, group, own), ("wide", "narrow"), split_axis=0, concat_axis=0, tiled=True
    )
    (smoothed,) = call(unwire_body, [shape((own, columns), BF)], [back.reshape(columns, own), order])
    return smoothed


def smooth_by_layers(adjoint, cov_plane, cov_vert):
    own, columns = adjoint.shape
    layered = adjoint.reshape(ZL, own // ZL, -1)
    planar = jnp.einsum(
        "pq,lqr->lpr",
        cov_plane,
        lax.all_to_all(layered, "wide", split_axis=0, concat_axis=1, tiled=True),
        preferred_element_type=F32,
    ).astype(BF)
    restored = lax.all_to_all(planar, "wide", split_axis=1, concat_axis=0, tiled=True)
    slab_weights = lax.dynamic_slice_in_dim(cov_vert, lax.axis_index("narrow") * ZL, ZL, 0)
    summed = jnp.dot(
        slab_weights,
        lax.all_gather(restored.reshape(ZL, -1), "narrow", axis=0, tiled=True),
        preferred_element_type=F32,
    )
    return summed.astype(BF).reshape(own, -1)


def shards(adjoint_rhs, inverse_rows, blocks, block_cols, send_rows, cov_plane, cov_vert):
    rhs = adjoint_rhs[0, 0]
    inverse = inverse_rows[0, 0]
    block_values = blocks[0, 0]
    cols = block_cols[0, 0].reshape(-1)
    send = send_rows[0, 0]
    own, columns = rhs.shape
    width = send.shape[1]
    wide, narrow = lax.axis_size("wide"), lax.axis_size("narrow")
    found = matchings()
    count = len(found)
    flags = jnp.stack([(lax.axis_index(axis) % 2 == parity).astype(jnp.int32) for _, axis, parity, _ in found])
    shape = jax.ShapeDtypeStruct
    note = shape((width, columns), BF)
    cells = shape((own, columns), BF)
    select, *messages = call(
        functools.partial(pick_body, found),
        [shape((count * width, own), BF)] + [note] * count,
        [flags, send, rhs],
        specs=[SM, VM, VM],
    )
    halo = pltpu.VMEM((4 * width, columns), BF)
    resid = rhs
    iterate = None
    for sweep in range(SWEEPS):
        first, last = sweep == 0, sweep == SWEEPS - 1
        if not first:
            got = swap(messages, found)
            resid, *messages = call(
                functools.partial(residual_body, found),
                [cells] + [note] * count,
                [flags, cols, block_values, rhs, rounded, select, *got],
                [pltpu.VMEM((own + 4 * width, columns), BF)],
                [SM, SM] + [VM] * (4 + count),
            )
        got = swap(messages, found)
        outs = [cells] if last else [cells, shape((own, columns), F32)] + [note] * count
        rounded, *rest = call(
            functools.partial(update_body, found, first, last),
            outs,
            [flags, inverse, resid, select, *got] + ([] if first else [iterate]),
            [halo],
            [SM] + [VM] * (3 + count + (0 if first else 1)),
        )
        if not last:
            iterate, *messages = rest
    group = columns // (wide * narrow)
    by_columns = columns % (wide * narrow) == 0 and group % 8 == 0 and narrow * ZL == LANES and wide % 16 == 0
    smooth = smooth_by_columns if by_columns else smooth_by_layers
    smoothed = smooth(rounded, cov_plane, cov_vert)
    return (rounded[None, None], smoothed[None, None])


def solution(mesh):
    in_specs = (
        P("wide", "narrow", None, None),
        P("wide", "narrow", None, None),
        P("wide", "narrow", None, None, None, None),
        P("wide", "narrow", None, None),
        P("wide", "narrow", None, None),
        P(),
        P(),
    )
    out_specs = (P("wide", "narrow", None, None), P("wide", "narrow", None, None))
    return jax.shard_map(shards, mesh=mesh, in_specs=in_specs, out_specs=out_specs, check_vma=False)
```

```python
import functools

import jax
import jax.numpy as jnp
from jax import lax
from jax.experimental import pallas as pl
from jax.experimental.pallas import tpu as pltpu
from jax.sharding import PartitionSpec as P

ZL = 64
SWEEPS = 4
LANES = 128
SELECT_FLOPS = 2 * 10 ** 9
BF = jnp.bfloat16
F32 = jnp.float32
VM = pl.BlockSpec(memory_space=pltpu.VMEM)
SM = pl.BlockSpec(memory_space=pltpu.SMEM)
ANY = pl.BlockSpec(memory_space=pl.ANY)


def matchings():
    found = []
    for place, axis in enumerate(("wide", "narrow")):
        count = lax.axis_size(axis)
        for parity in range(2):
            pairs = []
            for i in range(parity, count - 1, 2):
                pairs += [(i, i + 1), (i + 1, i)]
            if pairs:
                found.append((place, axis, parity, tuple(pairs)))
    return sorted(found, key=lambda f: (-f[0], -f[2]))


def swap(messages, found):
    return [lax.ppermute(m, axis, list(pairs)) for m, (_, axis, _, pairs) in zip(messages, found)]


def mm(a, b):
    return jnp.dot(a, b, preferred_element_type=F32)


def mm_t(a, b):
    return lax.dot_general(a, b, (((1,), (1,)), ((), ())), preferred_element_type=F32)


def iota(shape, dim):
    return lax.broadcasted_iota(jnp.int32, shape, dim)


def call(body, outs, args, scratch=(), specs=None, flops=0, limit=8, out_specs=None):
    size = sum(a.size * a.dtype.itemsize for a in args)
    return pl.pallas_call(
        body,
        out_shape=outs,
        in_specs=specs or [VM] * len(args),
        out_specs=out_specs or [VM] * len(outs),
        scratch_shapes=list(scratch),
        compiler_params=pltpu.CompilerParams(vmem_limit_bytes=limit * 1024 * 1024),
        cost_estimate=pl.CostEstimate(flops=flops, bytes_accessed=size, transcendentals=0),
    )(*args)


def fill_halo(halo_ref, got):
    width = got[0].shape[0]
    for m, piece in enumerate(got):
        halo_ref[m * width:(m + 1) * width, :] = piece[...]
    filled = len(got) * width
    if filled < halo_ref.shape[0]:
        halo_ref[filled:, :] = jnp.zeros((halo_ref.shape[0] - filled, halo_ref.shape[1]), halo_ref.dtype)


def send(messages, values):
    width = messages[0].shape[0]
    for m, message in enumerate(messages):
        message[...] = values[m * width:(m + 1) * width, :].astype(BF)


def keep_split(high_ref, low_ref, rows, value):
    high = value.astype(BF)
    high_ref[rows, :] = high
    low_ref[rows, :] = (value - high.astype(F32)).astype(BF)


def select_body(found, own, flags_ref, send_ref, select_ref):
    width = send_ref.shape[1]
    diagonal = iota((width, width), 0) == iota((width, width), 1)
    for m, (place, _, _, _) in enumerate(found):
        rows = jnp.where(
            flags_ref[m] == 1,
            send_ref[2 * place + 1:2 * place + 2, :],
            send_ref[2 * place:2 * place + 1, :],
        ).astype(F32)
        column = jnp.sum(jnp.where(diagonal, rows, 0.0), axis=1, keepdims=True).astype(jnp.int32)
        chosen = (iota((width, own), 1) == column).astype(F32).astype(BF)
        select_ref[m * width:(m + 1) * width, :] = chosen


def pick_body(select_ref, rhs_ref, *messages):
    send(messages, mm(select_ref[...], rhs_ref[...]))


def setup_body(found, width, flags_ref, cols_ref, inverse_ref, blocks_ref, rhs_ref, select_ref, *rest):
    inverse_halo_ref, blocks_halo_ref, inverse_sent_ref, blocks_sent_ref, state_ref, base_ref = rest[:6]
    sum_ref, high_ref, low_ref = rest[6:]
    own = rhs_ref.shape[0]
    halo = 4 * width
    places = iota((1, halo), 1)
    starts = jnp.full((1, halo), -halo, jnp.int32)
    for m, (place, _, _, _) in enumerate(found):
        here = lax.div(places, width) == m
        starts = jnp.where(here, (2 * place + flags_ref[m]) * width + lax.rem(places, width), starts)
    arrange = (iota((halo, halo), 0) == starts).astype(F32).astype(BF)
    rows, links, size, _ = blocks_ref.shape
    sum_ref[...] = jnp.zeros(sum_ref.shape, F32)
    for j in range(rows):
        for k in range(links):
            column = cols_ref[j * links + k]

            @pl.when(column * size >= own)
            def _():
                lanes = pl.ds(pl.multiple_of(column * size - own, size), size)
                here = slice(j * size, (j + 1) * size)
                sum_ref[here, lanes] = sum_ref[here, lanes] + blocks_ref[j, k].astype(F32)

    step = 256
    for i in range(0, own, step):
        here = slice(i, i + step)
        inverse_halo_ref[here, :] = mm(inverse_ref[here, own:], arrange).astype(BF)
        total = sum_ref[here, :]
        high = total.astype(BF)
        low = (total - high.astype(F32)).astype(BF)
        blocks_halo_ref[0, here, :] = mm(high, arrange).astype(BF)
        blocks_halo_ref[1, here, :] = mm(low, arrange).astype(BF)
        value = mm(inverse_ref[here, :own], rhs_ref[...])
        state_ref[here, :] = value
        keep_split(high_ref, low_ref, here, value)
    inverse_sent_ref[...] = mm(select_ref[...], inverse_halo_ref[...]).astype(BF)
    for part in range(2):
        blocks_sent_ref[part] = mm(select_ref[...], blocks_halo_ref[part]).astype(BF)
    base_ref[...] = mm(select_ref[...], high_ref[...]) + mm(select_ref[...], low_ref[...])


def sent_update_body(count, base_ref, sent_ref, *rest):
    got, messages, halo_ref = rest[:count], rest[count:-1], rest[-1]
    fill_halo(halo_ref, got)
    send(messages, base_ref[...] + mm(sent_ref[...], halo_ref[...]))


def sent_residual_body(count, base_ref, sent_ref, *rest):
    got, messages, halo_ref = rest[:count], rest[count:-1], rest[-1]
    fill_halo(halo_ref, got)
    part = mm(sent_ref[0], halo_ref[...]) + mm(sent_ref[1], halo_ref[...])
    send(messages, base_ref[...] - part)


def update_body(count, cols_ref, state_ref, inverse_halo_ref, blocks_ref, rhs_ref, select_ref, *rest):
    got, (iterate_ref, part_ref, base_ref, halo_ref, sub_ref, high_ref, low_ref) = rest[:count], rest[count:]
    own = state_ref.shape[0]
    fill_halo(halo_ref, got)
    step = 256
    for i in range(0, own, step):
        here = slice(i, i + step)
        value = state_ref[here, :] + mm(inverse_halo_ref[here, :], halo_ref[...])
        iterate_ref[here, :] = value
        sub_ref[here, :] = value.astype(BF)
    sub_ref[own:, :] = jnp.zeros((sub_ref.shape[0] - own, sub_ref.shape[1]), BF)
    rows, links, size, _ = blocks_ref.shape
    for j in range(rows):
        total = None
        for k in range(links):
            start = pl.multiple_of(cols_ref[j * links + k] * size, size)
            part = mm(blocks_ref[j, k], sub_ref[pl.ds(start, size), :])
            total = part if total is None else total + part
        here = slice(j * size, (j + 1) * size)
        value = rhs_ref[here, :].astype(F32) - total
        part_ref[here, :] = value
        keep_split(high_ref, low_ref, here, value)
    base_ref[...] = mm(select_ref[...], high_ref[...]) + mm(select_ref[...], low_ref[...])


def residual_body(count, part_ref, blocks_halo_ref, iterate_ref, inverse_ref, select_ref, *rest):
    got, (state_ref, base_ref, halo_ref, resid_ref, high_ref, low_ref) = rest[:count], rest[count:]
    own = part_ref.shape[0]
    fill_halo(halo_ref, got)
    step = 256
    for i in range(0, own, step):
        here = slice(i, i + step)
        outer = mm(blocks_halo_ref[0, here, :], halo_ref[...]) + mm(blocks_halo_ref[1, here, :], halo_ref[...])
        resid_ref[here, :] = (part_ref[here, :] - outer).astype(BF)
    for i in range(0, own, step):
        here = slice(i, i + step)
        value = iterate_ref[here, :] + mm(inverse_ref[here, :own], resid_ref[...])
        state_ref[here, :] = value
        keep_split(high_ref, low_ref, here, value)
    base_ref[...] = mm(select_ref[...], high_ref[...]) + mm(select_ref[...], low_ref[...])


def last_update_body(count, state_ref, inverse_halo_ref, *rest):
    got, rest = rest[:count], rest[count:]
    halo_ref = rest[-1]
    fill_halo(halo_ref, got)
    outs = rest[:-1]
    order_ref = outs[0] if len(outs) == 3 else None
    round_ref = outs[-2] if order_ref is not None else outs[0]
    step = 256
    own = state_ref.shape[0]
    for i in range(0, own, step):
        here = slice(i, i + step)
        value = state_ref[here, :] + mm(inverse_halo_ref[here, :], halo_ref[...])
        round_ref[here, :] = value.astype(BF)
    if order_ref is not None:
        wire_ref = outs[-1]
        for i in range(0, own, step):
            turned = lax.dot_general(
                round_ref[...], order_ref[:, i:i + step], (((0,), (0,)), ((), ())), preferred_element_type=F32
            )
            wire_ref[:, i:i + step] = turned.astype(BF)


def one_hot(rows_of, shape):
    return (iota(shape, 0) == rows_of(iota((1, shape[1]), 1))).astype(F32).astype(BF)


def tables_body(wide, narrow, cov_plane_ref, cov_vert_ref, order_ref, plane_ref, spread_ref, vert_ref):
    own = order_ref.shape[0]
    tile = own // ZL
    order_ref[...] = one_hot(lambda k: lax.rem(k, ZL) * tile + lax.div(k, ZL), (own, own))
    plane = wide * tile
    turn = one_hot(lambda k: lax.rem(k, wide) * tile + lax.div(k, wide), (plane, plane))
    half = mm(cov_plane_ref[...], turn).astype(BF)
    plane_ref[...] = mm(half.T, turn).astype(BF).T
    share = LANES // ZL
    depth = narrow * ZL
    width = narrow * LANES

    def source(k):
        e, n, l = lax.div(k, depth), lax.rem(lax.div(k, ZL), narrow), lax.rem(k, ZL)
        return n * LANES + e * ZL + l

    spread = one_hot(source, (width, width))
    spread_ref[...] = spread
    turned = cov_vert_ref[...].astype(F32).T
    zero = jnp.zeros_like(turned)
    blocks = jnp.concatenate(
        [jnp.concatenate([turned if i == e else zero for i in range(share)], axis=1) for e in range(share)],
        axis=0,
    ).astype(BF)
    vert_ref[...] = mm_t(blocks, spread).astype(BF)


def mix_body(wide, narrow, group, in_ref, plane_ref, spread_ref, vert_ref, round_ref, *rest):
    out_ref, adjoint_hbm, cells_ref, flat_ref, wire_ref, sem = rest
    keep = pltpu.make_async_copy(round_ref, adjoint_hbm, sem)
    keep.start()
    own = in_ref.shape[1]
    tile = own // ZL
    share = LANES // ZL
    depth = narrow * ZL
    block = narrow * group
    taken = in_ref[...].astype(F32).reshape(wide, narrow, group, own)
    slabs = [taken[:, n].reshape(wide * group, own).astype(BF) for n in range(narrow)]
    for g in range(tile // share):
        lanes = slice(g * LANES, (g + 1) * LANES)
        joined = jnp.concatenate([s[:, lanes] for s in slabs], axis=1)
        spread = mm(joined, spread_ref[...])
        for e in range(share):
            cells_ref[g * share + e] = spread[:, e * depth:(e + 1) * depth]
    for r in range(group):
        for c in range(tile):
            flat_ref[c * wide:(c + 1) * wide, r * depth:(r + 1) * depth] = cells_ref[
                c, pl.ds(r, wide, stride=group), :
            ].astype(BF)
    planar = mm(plane_ref[...], flat_ref[...]).astype(BF)
    for g in range(tile // share):
        stacked = jnp.concatenate(
            [
                jnp.concatenate(
                    [
                        planar[c * wide:(c + 1) * wide, r * depth:(r + 1) * depth]
                        for c in range(g * share, (g + 1) * share)
                    ],
                    axis=1,
                )
                for r in range(group)
            ],
            axis=0,
        )
        mixed = mm(stacked, vert_ref[...])
        for r in range(group):
            for n in range(narrow):
                wire_ref[g, pl.ds(n * group + r, wide, stride=block), :] = mixed[
                    r * wide:(r + 1) * wide, n * LANES:(n + 1) * LANES
                ]
        out_ref[:, g * LANES:(g + 1) * LANES] = wire_ref[g].astype(BF)
    keep.wait()


def unwire_body(in_ref, order_ref, out_hbm, out_ref, sems):
    step = 256
    copies = []
    for n, i in enumerate(range(0, out_ref.shape[0], step)):
        here = pl.ds(i, step)
        out_ref[here, :] = mm_t(order_ref[here, :], in_ref[...]).astype(BF)
        copy = pltpu.make_async_copy(out_ref.at[here], out_hbm.at[here], sems.at[n])
        copy.start()
        copies.append(copy)
    for copy in copies:
        copy.wait()


def column_tables(own, cov_plane, cov_vert):
    wide, narrow = lax.axis_size("wide"), lax.axis_size("narrow")
    width = narrow * LANES
    plane = cov_plane.shape[0]
    shape = jax.ShapeDtypeStruct
    return call(
        functools.partial(tables_body, wide, narrow),
        [shape((own, own), BF), shape((plane, plane), BF), shape((width, width), BF), shape((width, width), BF)],
        [cov_plane, cov_vert],
    )


def smooth_by_columns(rounded, wire, tables):
    wide, narrow = lax.axis_size("wide"), lax.axis_size("narrow")
    own, columns = rounded.shape
    devices = wide * narrow
    group = columns // devices
    depth = narrow * ZL
    tile = own // ZL
    shape = jax.ShapeDtypeStruct
    order, plane_mix, spread, vert_mix = tables
    there = lax.all_to_all(
        wire.reshape(devices, group, own), ("wide", "narrow"), split_axis=0, concat_axis=0, tiled=True
    )
    mixed, adjoint = call(
        functools.partial(mix_body, wide, narrow, group),
        [shape((columns, own), BF), shape((own, columns), BF)],
        [there.reshape(columns, own), plane_mix, spread, vert_mix, rounded],
        [
            pltpu.VMEM((tile, wide * group, depth), F32),
            pltpu.VMEM((plane_mix.shape[0], group * depth), BF),
            pltpu.VMEM((own // LANES, columns, LANES), F32),
            pltpu.SemaphoreType.DMA,
        ],
        out_specs=[VM, ANY],
    )
    back = lax.all_to_all(
        mixed.reshape(devices, group, own), ("wide", "narrow"), split_axis=0, concat_axis=0, tiled=True
    )
    (smoothed,) = call(
        unwire_body,
        [shape((own, columns), BF)],
        [back.reshape(columns, own), order],
        [pltpu.VMEM((own, columns), BF), pltpu.SemaphoreType.DMA((own // 256,))],
        out_specs=[ANY],
    )
    return adjoint, smoothed


def smooth_by_layers(adjoint, cov_plane, cov_vert):
    own, columns = adjoint.shape
    layered = adjoint.reshape(ZL, own // ZL, -1)
    planar = jnp.einsum(
        "pq,lqr->lpr",
        cov_plane,
        lax.all_to_all(layered, "wide", split_axis=0, concat_axis=1, tiled=True),
        preferred_element_type=F32,
    ).astype(BF)
    restored = lax.all_to_all(planar, "wide", split_axis=1, concat_axis=0, tiled=True)
    slab_weights = lax.dynamic_slice_in_dim(cov_vert, lax.axis_index("narrow") * ZL, ZL, 0)
    summed = jnp.dot(
        slab_weights,
        lax.all_gather(restored.reshape(ZL, -1), "narrow", axis=0, tiled=True),
        preferred_element_type=F32,
    )
    return summed.astype(BF).reshape(own, -1)


def shards(adjoint_rhs, inverse_rows, blocks, block_cols, send_rows, cov_plane, cov_vert):
    rhs = adjoint_rhs[0, 0]
    inverse = inverse_rows[0, 0]
    block_values = blocks[0, 0]
    cols = block_cols[0, 0].reshape(-1)
    send_index = send_rows[0, 0]
    own, columns = rhs.shape
    width = send_index.shape[1]
    halo = 4 * width
    wide, narrow = lax.axis_size("wide"), lax.axis_size("narrow")
    group = columns // (wide * narrow)
    by_columns = columns % (wide * narrow) == 0 and group % 8 == 0 and narrow * ZL == LANES and wide % 16 == 0
    found = matchings()
    count = len(found)
    sent = count * width
    flags = jnp.stack([(lax.axis_index(axis) % 2 == parity).astype(jnp.int32) for _, axis, parity, _ in found])
    shape = jax.ShapeDtypeStruct
    notes = [shape((width, columns), BF)] * count
    full = shape((own, columns), F32)
    base_shape = shape((sent, columns), F32)
    halo_space = pltpu.VMEM((halo, columns), BF)
    cell_space = pltpu.VMEM((own, columns), BF)
    (select,) = call(
        functools.partial(select_body, found, own),
        [shape((sent, own), BF)],
        [flags, send_index],
        specs=[SM, VM],
        flops=SELECT_FLOPS,
    )
    messages = call(pick_body, notes, [select, rhs], flops=SELECT_FLOPS)
    got = swap(messages, found)
    inverse_halo, blocks_halo, inverse_sent, blocks_sent, state, base = call(
        functools.partial(setup_body, found, width),
        [
            shape((own, halo), BF),
            shape((2, own, halo), BF),
            shape((sent, halo), BF),
            shape((2, sent, halo), BF),
            full,
            base_shape,
        ],
        [flags, cols, inverse, block_values, rhs, select],
        [
            pltpu.VMEM((own, halo), F32),
            cell_space,
            cell_space,
        ],
        [SM, SM, VM, VM, VM, VM],
        limit=12,
    )
    tables = column_tables(own, cov_plane, cov_vert) if by_columns else ()
    for sweep in range(SWEEPS - 1):
        messages = call(
            functools.partial(sent_update_body, count), notes, [base, inverse_sent, *got], [halo_space], limit=4
        )
        arrived, got = got, swap(messages, found)
        iterate, part, base = call(
            functools.partial(update_body, count),
            [full, full, base_shape],
            [cols, state, inverse_halo, block_values, rhs, select, *arrived],
            [halo_space, pltpu.VMEM((own + halo, columns), BF), cell_space, cell_space],
            [SM] + [VM] * (5 + count),
        )
        messages = call(
            functools.partial(sent_residual_body, count), notes, [base, blocks_sent, *got], [halo_space], limit=4
        )
        arrived, got = got, swap(messages, found)
        if sweep == 1:
            tables, part = lax.optimization_barrier((tables, part))
        state, base = call(
            functools.partial(residual_body, count),
            [full, base_shape],
            [part, blocks_halo, iterate, inverse, select, *arrived],
            [halo_space, cell_space, cell_space, cell_space],
        )
    cells = shape((own, columns), BF)
    last = functools.partial(last_update_body, count)
    if by_columns:
        rounded, wire = call(
            last, [cells, shape((columns, own), BF)], [state, inverse_halo, *got, tables[0]], [halo_space]
        )
        adjoint, smoothed = smooth_by_columns(rounded, wire, tables)
    else:
        (adjoint,) = call(last, [cells], [state, inverse_halo, *got], [halo_space])
        smoothed = smooth_by_layers(adjoint, cov_plane, cov_vert)
    return (adjoint[None, None], smoothed[None, None])


def solution(mesh):
    in_specs = (
        P("wide", "narrow", None, None),
        P("wide", "narrow", None, None),
        P("wide", "narrow", None, None, None, None),
        P("wide", "narrow", None, None),
        P("wide", "narrow", None, None),
        P(),
        P(),
    )
    out_specs = (P("wide", "narrow", None, None), P("wide", "narrow", None, None))
    return jax.shard_map(shards, mesh=mesh, in_specs=in_specs, out_specs=out_specs, check_vma=False)
```

```python
import functools

import jax
import jax.numpy as jnp
from jax import lax
from jax.experimental import pallas as pl
from jax.experimental.pallas import tpu as pltpu
from jax.sharding import PartitionSpec as P

ZL = 64
SWEEPS = 4
LANES = 128
SELECT_FLOPS = 2 * 10 ** 9
BF = jnp.bfloat16
F32 = jnp.float32
VM = pl.BlockSpec(memory_space=pltpu.VMEM)
SM = pl.BlockSpec(memory_space=pltpu.SMEM)
ANY = pl.BlockSpec(memory_space=pl.ANY)


def host(w):
    return w ^ ((w >> 1) & 1)


def matchings(traded):
    found = []
    for place, axis in enumerate(("wide", "narrow")):
        count = lax.axis_size(axis)
        at = host if traded and axis == "wide" else (lambda w: w)
        for parity in range(2):
            pairs = []
            for i in range(parity, count - 1, 2):
                pairs += [(at(i), at(i + 1)), (at(i + 1), at(i))]
            if pairs:
                found.append((place, axis, parity, tuple(pairs)))
    return sorted(found, key=lambda f: (-f[0], -f[2]))


def trade(values):
    count = lax.axis_size("wide")
    return lax.ppermute(values, "wide", [(w, host(w)) for w in range(count)])


def swap(messages, found):
    return [lax.ppermute(m, axis, list(pairs)) for m, (_, axis, _, pairs) in zip(messages, found)]


def mm(a, b):
    return jnp.dot(a, b, preferred_element_type=F32)


def mm_t(a, b):
    return lax.dot_general(a, b, (((1,), (1,)), ((), ())), preferred_element_type=F32)


def iota(shape, dim):
    return lax.broadcasted_iota(jnp.int32, shape, dim)


def call(body, outs, args, scratch=(), specs=None, flops=0, limit=8, out_specs=None):
    size = sum(a.size * a.dtype.itemsize for a in args)
    return pl.pallas_call(
        body,
        out_shape=outs,
        in_specs=specs or [VM] * len(args),
        out_specs=out_specs or [VM] * len(outs),
        scratch_shapes=list(scratch),
        compiler_params=pltpu.CompilerParams(vmem_limit_bytes=limit * 1024 * 1024),
        cost_estimate=pl.CostEstimate(flops=flops, bytes_accessed=size, transcendentals=0),
    )(*args)


def fill_halo(halo_ref, got):
    width = got[0].shape[0]
    for m, piece in enumerate(got):
        halo_ref[m * width:(m + 1) * width, :] = piece[...]
    filled = len(got) * width
    if filled < halo_ref.shape[0]:
        halo_ref[filled:, :] = jnp.zeros((halo_ref.shape[0] - filled, halo_ref.shape[1]), halo_ref.dtype)


def send(messages, values):
    width = messages[0].shape[0]
    for m, message in enumerate(messages):
        message[...] = values[m * width:(m + 1) * width, :].astype(BF)


def keep_split(high_ref, low_ref, rows, value):
    high = value.astype(BF)
    high_ref[rows, :] = high
    low_ref[rows, :] = (value - high.astype(F32)).astype(BF)


def select_body(found, own, flags_ref, send_ref, select_ref):
    width = send_ref.shape[1]
    diagonal = iota((width, width), 0) == iota((width, width), 1)
    for m, (place, _, _, _) in enumerate(found):
        rows = jnp.where(
            flags_ref[m] == 1,
            send_ref[2 * place + 1:2 * place + 2, :],
            send_ref[2 * place:2 * place + 1, :],
        ).astype(F32)
        column = jnp.sum(jnp.where(diagonal, rows, 0.0), axis=1, keepdims=True).astype(jnp.int32)
        chosen = (iota((width, own), 1) == column).astype(F32).astype(BF)
        select_ref[m * width:(m + 1) * width, :] = chosen


def pick_body(select_ref, rhs_ref, *messages):
    send(messages, mm(select_ref[...], rhs_ref[...]))


def setup_body(found, width, flags_ref, cols_ref, inverse_ref, blocks_ref, rhs_ref, select_ref, *rest):
    inverse_halo_ref, blocks_halo_ref, inverse_sent_ref, blocks_sent_ref, state_ref, base_ref = rest[:6]
    sum_ref, high_ref, low_ref = rest[6:]
    own = rhs_ref.shape[0]
    halo = 4 * width
    places = iota((1, halo), 1)
    starts = jnp.full((1, halo), -halo, jnp.int32)
    for m, (place, _, _, _) in enumerate(found):
        here = lax.div(places, width) == m
        starts = jnp.where(here, (2 * place + flags_ref[m]) * width + lax.rem(places, width), starts)
    arrange = (iota((halo, halo), 0) == starts).astype(F32).astype(BF)
    rows, links, size, _ = blocks_ref.shape
    sum_ref[...] = jnp.zeros(sum_ref.shape, F32)
    for j in range(rows):
        for k in range(links):
            column = cols_ref[j * links + k]

            @pl.when(column * size >= own)
            def _():
                lanes = pl.ds(pl.multiple_of(column * size - own, size), size)
                here = slice(j * size, (j + 1) * size)
                sum_ref[here, lanes] = sum_ref[here, lanes] + blocks_ref[j, k].astype(F32)

    step = 256
    for i in range(0, own, step):
        here = slice(i, i + step)
        inverse_halo_ref[here, :] = mm(inverse_ref[here, own:], arrange).astype(BF)
        total = sum_ref[here, :]
        high = total.astype(BF)
        low = (total - high.astype(F32)).astype(BF)
        blocks_halo_ref[0, here, :] = mm(high, arrange).astype(BF)
        blocks_halo_ref[1, here, :] = mm(low, arrange).astype(BF)
        value = mm(inverse_ref[here, :own], rhs_ref[...])
        state_ref[here, :] = value
        keep_split(high_ref, low_ref, here, value)
    inverse_sent_ref[...] = mm(select_ref[...], inverse_halo_ref[...]).astype(BF)
    for part in range(2):
        blocks_sent_ref[part] = mm(select_ref[...], blocks_halo_ref[part]).astype(BF)
    base_ref[...] = mm(select_ref[...], high_ref[...]) + mm(select_ref[...], low_ref[...])


def sent_update_body(count, base_ref, sent_ref, *rest):
    got, messages, halo_ref = rest[:count], rest[count:-1], rest[-1]
    fill_halo(halo_ref, got)
    send(messages, base_ref[...] + mm(sent_ref[...], halo_ref[...]))


def sent_residual_body(count, base_ref, sent_ref, *rest):
    got, messages, halo_ref = rest[:count], rest[count:-1], rest[-1]
    fill_halo(halo_ref, got)
    part = mm(sent_ref[0], halo_ref[...]) + mm(sent_ref[1], halo_ref[...])
    send(messages, base_ref[...] - part)


def update_body(count, cols_ref, state_ref, inverse_halo_ref, blocks_ref, rhs_ref, select_ref, *rest):
    got, (iterate_ref, part_ref, base_ref, halo_ref, sub_ref, high_ref, low_ref) = rest[:count], rest[count:]
    own = state_ref.shape[0]
    fill_halo(halo_ref, got)
    step = 256
    for i in range(0, own, step):
        here = slice(i, i + step)
        value = state_ref[here, :] + mm(inverse_halo_ref[here, :], halo_ref[...])
        iterate_ref[here, :] = value
        sub_ref[here, :] = value.astype(BF)
    sub_ref[own:, :] = jnp.zeros((sub_ref.shape[0] - own, sub_ref.shape[1]), BF)
    rows, links, size, _ = blocks_ref.shape
    for j in range(rows):
        total = None
        for k in range(links):
            start = pl.multiple_of(cols_ref[j * links + k] * size, size)
            part = mm(blocks_ref[j, k], sub_ref[pl.ds(start, size), :])
            total = part if total is None else total + part
        here = slice(j * size, (j + 1) * size)
        value = rhs_ref[here, :].astype(F32) - total
        part_ref[here, :] = value
        keep_split(high_ref, low_ref, here, value)
    base_ref[...] = mm(select_ref[...], high_ref[...]) + mm(select_ref[...], low_ref[...])


def residual_body(count, part_ref, blocks_halo_ref, iterate_ref, inverse_ref, select_ref, *rest):
    got, (state_ref, base_ref, halo_ref, resid_ref, high_ref, low_ref) = rest[:count], rest[count:]
    own = part_ref.shape[0]
    fill_halo(halo_ref, got)
    step = 256
    for i in range(0, own, step):
        here = slice(i, i + step)
        outer = mm(blocks_halo_ref[0, here, :], halo_ref[...]) + mm(blocks_halo_ref[1, here, :], halo_ref[...])
        resid_ref[here, :] = (part_ref[here, :] - outer).astype(BF)
    for i in range(0, own, step):
        here = slice(i, i + step)
        value = iterate_ref[here, :] + mm(inverse_ref[here, :own], resid_ref[...])
        state_ref[here, :] = value
        keep_split(high_ref, low_ref, here, value)
    base_ref[...] = mm(select_ref[...], high_ref[...]) + mm(select_ref[...], low_ref[...])


def last_update_body(count, state_ref, inverse_halo_ref, *rest):
    got, rest = rest[:count], rest[count:]
    halo_ref = rest[-1]
    fill_halo(halo_ref, got)
    outs = rest[:-1]
    order_ref = outs[0] if len(outs) == 3 else None
    round_ref = outs[-2] if order_ref is not None else outs[0]
    step = 256
    own = state_ref.shape[0]
    for i in range(0, own, step):
        here = slice(i, i + step)
        value = state_ref[here, :] + mm(inverse_halo_ref[here, :], halo_ref[...])
        round_ref[here, :] = value.astype(BF)
    if order_ref is not None:
        wire_ref = outs[-1]
        for i in range(0, own, step):
            turned = lax.dot_general(
                round_ref[...], order_ref[:, i:i + step], (((0,), (0,)), ((), ())), preferred_element_type=F32
            )
            wire_ref[:, i:i + step] = turned.astype(BF)


def one_hot(rows_of, shape):
    return (iota(shape, 0) == rows_of(iota((1, shape[1]), 1))).astype(F32).astype(BF)


def tables_body(wide, narrow, cov_plane_ref, cov_vert_ref, order_ref, plane_ref, spread_ref, vert_ref):
    own = order_ref.shape[0]
    tile = own // ZL
    order_ref[...] = one_hot(lambda k: lax.rem(k, ZL) * tile + lax.div(k, ZL), (own, own))
    plane = wide * tile
    turn = one_hot(lambda k: lax.rem(k, wide) * tile + lax.div(k, wide), (plane, plane))
    turn_in = one_hot(lambda k: host(lax.rem(k, wide)) * tile + lax.div(k, wide), (plane, plane))
    half = mm(cov_plane_ref[...], turn_in).astype(BF)
    plane_ref[...] = mm(half.T, turn).astype(BF).T
    share = LANES // ZL
    depth = narrow * ZL
    width = narrow * LANES

    def source(k):
        e, n, l = lax.div(k, depth), lax.rem(lax.div(k, ZL), narrow), lax.rem(k, ZL)
        return n * LANES + e * ZL + l

    spread = one_hot(source, (width, width))
    spread_ref[...] = spread
    turned = cov_vert_ref[...].astype(F32).T
    zero = jnp.zeros_like(turned)
    blocks = jnp.concatenate(
        [jnp.concatenate([turned if i == e else zero for i in range(share)], axis=1) for e in range(share)],
        axis=0,
    ).astype(BF)
    vert_ref[...] = mm_t(blocks, spread).astype(BF)


def mix_body(wide, narrow, group, in_ref, plane_ref, spread_ref, vert_ref, *rest):
    out_ref, cells_ref, flat_ref, wire_ref = rest
    own = in_ref.shape[1]
    tile = own // ZL
    share = LANES // ZL
    depth = narrow * ZL
    block = narrow * group
    taken = in_ref[...].astype(F32).reshape(wide, narrow, group, own)
    slabs = [taken[:, n].reshape(wide * group, own).astype(BF) for n in range(narrow)]
    for g in range(tile // share):
        lanes = slice(g * LANES, (g + 1) * LANES)
        joined = jnp.concatenate([s[:, lanes] for s in slabs], axis=1)
        spread = mm(joined, spread_ref[...])
        for e in range(share):
            cells_ref[g * share + e] = spread[:, e * depth:(e + 1) * depth]
    for r in range(group):
        for c in range(tile):
            flat_ref[c * wide:(c + 1) * wide, r * depth:(r + 1) * depth] = cells_ref[
                c, pl.ds(r, wide, stride=group), :
            ].astype(BF)
    planar = mm(plane_ref[...], flat_ref[...]).astype(BF)
    for g in range(tile // share):
        stacked = jnp.concatenate(
            [
                jnp.concatenate(
                    [
                        planar[c * wide:(c + 1) * wide, r * depth:(r + 1) * depth]
                        for c in range(g * share, (g + 1) * share)
                    ],
                    axis=1,
                )
                for r in range(group)
            ],
            axis=0,
        )
        mixed = mm(stacked, vert_ref[...])
        for r in range(group):
            for n in range(narrow):
                wire_ref[g, pl.ds(n * group + r, wide, stride=block), :] = mixed[
                    r * wide:(r + 1) * wide, n * LANES:(n + 1) * LANES
                ]
        out_ref[:, g * LANES:(g + 1) * LANES] = wire_ref[g].astype(BF)


def unwire_body(in_ref, order_ref, adjoint_ref, out_hbm, adjoint_hbm, out_ref, sems):
    step = 256
    keep = pltpu.make_async_copy(adjoint_ref, adjoint_hbm, sems.at[sems.shape[0] - 1])
    keep.start()
    copies = [keep]
    for n, i in enumerate(range(0, out_ref.shape[0], step)):
        here = pl.ds(i, step)
        out_ref[here, :] = mm_t(order_ref[here, :], in_ref[...]).astype(BF)
        copy = pltpu.make_async_copy(out_ref.at[here], out_hbm.at[here], sems.at[n])
        copy.start()
        copies.append(copy)
    for copy in copies:
        copy.wait()


def column_tables(own, cov_plane, cov_vert):
    wide, narrow = lax.axis_size("wide"), lax.axis_size("narrow")
    width = narrow * LANES
    plane = cov_plane.shape[0]
    shape = jax.ShapeDtypeStruct
    return call(
        functools.partial(tables_body, wide, narrow),
        [shape((own, own), BF), shape((plane, plane), BF), shape((width, width), BF), shape((width, width), BF)],
        [cov_plane, cov_vert],
    )


def smooth_by_columns(adjoint, wire, tables):
    wide, narrow = lax.axis_size("wide"), lax.axis_size("narrow")
    own, columns = adjoint.shape
    devices = wide * narrow
    group = columns // devices
    depth = narrow * ZL
    tile = own // ZL
    shape = jax.ShapeDtypeStruct
    order, plane_mix, spread, vert_mix = tables
    there = lax.all_to_all(
        wire.reshape(devices, group, own), ("wide", "narrow"), split_axis=0, concat_axis=0, tiled=True
    )
    (mixed,) = call(
        functools.partial(mix_body, wide, narrow, group),
        [shape((columns, own), BF)],
        [there.reshape(columns, own), plane_mix, spread, vert_mix],
        [
            pltpu.VMEM((tile, wide * group, depth), F32),
            pltpu.VMEM((plane_mix.shape[0], group * depth), BF),
            pltpu.VMEM((own // LANES, columns, LANES), F32),
        ],
    )
    back = lax.all_to_all(
        mixed.reshape(devices, group, own), ("wide", "narrow"), split_axis=0, concat_axis=0, tiled=True
    )
    smoothed, adjoint = call(
        unwire_body,
        [shape((own, columns), BF)] * 2,
        [back.reshape(columns, own), order, adjoint],
        [pltpu.VMEM((own, columns), BF), pltpu.SemaphoreType.DMA((own // 256 + 1,))],
        out_specs=[ANY, ANY],
    )
    return adjoint, smoothed


def smooth_by_layers(adjoint, cov_plane, cov_vert):
    own, columns = adjoint.shape
    layered = adjoint.reshape(ZL, own // ZL, -1)
    planar = jnp.einsum(
        "pq,lqr->lpr",
        cov_plane,
        lax.all_to_all(layered, "wide", split_axis=0, concat_axis=1, tiled=True),
        preferred_element_type=F32,
    ).astype(BF)
    restored = lax.all_to_all(planar, "wide", split_axis=1, concat_axis=0, tiled=True)
    slab_weights = lax.dynamic_slice_in_dim(cov_vert, lax.axis_index("narrow") * ZL, ZL, 0)
    summed = jnp.dot(
        slab_weights,
        lax.all_gather(restored.reshape(ZL, -1), "narrow", axis=0, tiled=True),
        preferred_element_type=F32,
    )
    return summed.astype(BF).reshape(own, -1)


def shards(adjoint_rhs, inverse_rows, blocks, block_cols, send_rows, cov_plane, cov_vert):
    rhs = adjoint_rhs[0, 0]
    inverse = inverse_rows[0, 0]
    block_values = blocks[0, 0]
    cols = block_cols[0, 0].reshape(-1)
    send_index = send_rows[0, 0]
    own, columns = rhs.shape
    width = send_index.shape[1]
    halo = 4 * width
    wide, narrow = lax.axis_size("wide"), lax.axis_size("narrow")
    group = columns // (wide * narrow)
    by_columns = columns % (wide * narrow) == 0 and group % 8 == 0 and narrow * ZL == LANES and wide % 16 == 0
    if by_columns:
        send_index, rhs, inverse, block_values, cols = [
            trade(a) for a in (send_index, rhs, inverse, block_values, cols)
        ]
    found = matchings(by_columns)
    count = len(found)
    sent = count * width
    index = {axis: lax.axis_index(axis) for axis in ("wide", "narrow")}
    if by_columns:
        index["wide"] = host(index["wide"])
    flags = jnp.stack([(index[axis] % 2 == parity).astype(jnp.int32) for _, axis, parity, _ in found])
    shape = jax.ShapeDtypeStruct
    notes = [shape((width, columns), BF)] * count
    full = shape((own, columns), F32)
    base_shape = shape((sent, columns), F32)
    halo_space = pltpu.VMEM((halo, columns), BF)
    cell_space = pltpu.VMEM((own, columns), BF)
    (select,) = call(
        functools.partial(select_body, found, own),
        [shape((sent, own), BF)],
        [flags, send_index],
        specs=[SM, VM],
        flops=SELECT_FLOPS,
    )
    messages = call(pick_body, notes, [select, rhs], flops=SELECT_FLOPS)
    got = swap(messages, found)
    inverse_halo, blocks_halo, inverse_sent, blocks_sent, state, base = call(
        functools.partial(setup_body, found, width),
        [
            shape((own, halo), BF),
            shape((2, own, halo), BF),
            shape((sent, halo), BF),
            shape((2, sent, halo), BF),
            full,
            base_shape,
        ],
        [flags, cols, inverse, block_values, rhs, select],
        [
            pltpu.VMEM((own, halo), F32),
            cell_space,
            cell_space,
        ],
        [SM, SM, VM, VM, VM, VM],
        limit=12,
    )
    tables = column_tables(own, cov_plane, cov_vert) if by_columns else ()
    for sweep in range(SWEEPS - 1):
        messages = call(
            functools.partial(sent_update_body, count), notes, [base, inverse_sent, *got], [halo_space], limit=4
        )
        arrived, got = got, swap(messages, found)
        iterate, part, base = call(
            functools.partial(update_body, count),
            [full, full, base_shape],
            [cols, state, inverse_halo, block_values, rhs, select, *arrived],
            [halo_space, pltpu.VMEM((own + halo, columns), BF), cell_space, cell_space],
            [SM] + [VM] * (5 + count),
        )
        messages = call(
            functools.partial(sent_residual_body, count), notes, [base, blocks_sent, *got], [halo_space], limit=4
        )
        arrived, got = got, swap(messages, found)
        if sweep == 1:
            tables, part = lax.optimization_barrier((tables, part))
        state, base = call(
            functools.partial(residual_body, count),
            [full, base_shape],
            [part, blocks_halo, iterate, inverse, select, *arrived],
            [halo_space, cell_space, cell_space, cell_space],
        )
    cells = shape((own, columns), BF)
    last = functools.partial(last_update_body, count)
    if by_columns:
        rounded, wire = call(
            last, [cells, shape((columns, own), BF)], [state, inverse_halo, *got, tables[0]], [halo_space]
        )
        adjoint, smoothed = smooth_by_columns(trade(rounded), wire, tables)
    else:
        (adjoint,) = call(last, [cells], [state, inverse_halo, *got], [halo_space])
        smoothed = smooth_by_layers(adjoint, cov_plane, cov_vert)
    return (adjoint[None, None], smoothed[None, None])


def solution(mesh):
    in_specs = (
        P("wide", "narrow", None, None),
        P("wide", "narrow", None, None),
        P("wide", "narrow", None, None, None, None),
        P("wide", "narrow", None, None),
        P("wide", "narrow", None, None),
        P(),
        P(),
    )
    out_specs = (P("wide", "narrow", None, None), P("wide", "narrow", None, None))
    return jax.shard_map(shards, mesh=mesh, in_specs=in_specs, out_specs=out_specs, check_vma=False)
```

```python
import functools

import jax
import jax.numpy as jnp
from jax import lax
from jax.experimental import pallas as pl
from jax.experimental.pallas import tpu as pltpu
from jax.sharding import PartitionSpec as P

ZL = 64
SWEEPS = 4
LANES = 128
SELECT_FLOPS = 2 * 10 ** 9
BF = jnp.bfloat16
F32 = jnp.float32
VM = pl.BlockSpec(memory_space=pltpu.VMEM)
SM = pl.BlockSpec(memory_space=pltpu.SMEM)
ANY = pl.BlockSpec(memory_space=pl.ANY)


def matchings():
    axes = ("wide", "narrow")
    counts = [lax.axis_size(axis) for axis in axes]
    found = []
    for place in range(2):
        count, other = counts[place], counts[1 - place]
        for parity in range(2):
            if count <= parity + 1:
                continue
            pairs = []
            for i in range(count):
                partner = i + 1 if i % 2 == parity else i - 1
                for j in range(other):
                    source, target = (i, j), (partner, j)
                    if not 0 <= partner < count:
                        target = (i, j ^ 1 if j ^ 1 < other else j)
                    if place == 1:
                        source, target = source[::-1], target[::-1]
                    pairs.append((source[0] * counts[1] + source[1], target[0] * counts[1] + target[1]))
            found.append((place, parity, tuple(pairs)))
    return sorted(found, key=lambda f: (-f[0], -f[1]))


def swap(messages, found):
    return [lax.ppermute(m, ("wide", "narrow"), list(f[-1])) for m, f in zip(messages, found)]


def mm(a, b):
    return jnp.dot(a, b, preferred_element_type=F32)


def mm_t(a, b):
    return lax.dot_general(a, b, (((1,), (1,)), ((), ())), preferred_element_type=F32)


def iota(shape, dim):
    return lax.broadcasted_iota(jnp.int32, shape, dim)


def call(body, outs, args, scratch=(), specs=None, flops=0, limit=8, out_specs=None):
    size = sum(a.size * a.dtype.itemsize for a in args)
    return pl.pallas_call(
        body,
        out_shape=outs,
        in_specs=specs or [VM] * len(args),
        out_specs=out_specs or [VM] * len(outs),
        scratch_shapes=list(scratch),
        compiler_params=pltpu.CompilerParams(vmem_limit_bytes=limit * 1024 * 1024),
        cost_estimate=pl.CostEstimate(flops=flops, bytes_accessed=size, transcendentals=0),
    )(*args)


def fill_halo(halo_ref, got):
    width = got[0].shape[0]
    for m, piece in enumerate(got):
        halo_ref[m * width:(m + 1) * width, :] = piece[...]
    filled = len(got) * width
    if filled < halo_ref.shape[0]:
        halo_ref[filled:, :] = jnp.zeros((halo_ref.shape[0] - filled, halo_ref.shape[1]), halo_ref.dtype)


def send(messages, values):
    width = messages[0].shape[0]
    for m, message in enumerate(messages):
        message[...] = values[m * width:(m + 1) * width, :].astype(BF)


def keep_split(high_ref, low_ref, rows, value):
    high = value.astype(BF)
    high_ref[rows, :] = high
    low_ref[rows, :] = (value - high.astype(F32)).astype(BF)


def select_body(found, own, flags_ref, send_ref, select_ref):
    width = send_ref.shape[1]
    diagonal = iota((width, width), 0) == iota((width, width), 1)
    for m, (place, _, _) in enumerate(found):
        rows = jnp.where(
            flags_ref[m] == 1,
            send_ref[2 * place + 1:2 * place + 2, :],
            send_ref[2 * place:2 * place + 1, :],
        ).astype(F32)
        column = jnp.sum(jnp.where(diagonal, rows, 0.0), axis=1, keepdims=True).astype(jnp.int32)
        column = jnp.where(flags_ref[len(found) + m] == 1, column, -1)
        chosen = (iota((width, own), 1) == column).astype(F32).astype(BF)
        select_ref[m * width:(m + 1) * width, :] = chosen


def pick_body(select_ref, rhs_ref, *messages):
    send(messages, mm(select_ref[...], rhs_ref[...]))


def setup_body(found, width, flags_ref, cols_ref, inverse_ref, blocks_ref, rhs_ref, select_ref, *rest):
    inverse_halo_ref, blocks_halo_ref, inverse_sent_ref, blocks_sent_ref, state_ref, base_ref = rest[:6]
    sum_ref, high_ref, low_ref = rest[6:]
    own = rhs_ref.shape[0]
    halo = 4 * width
    places = iota((1, halo), 1)
    starts = jnp.full((1, halo), -halo, jnp.int32)
    for m, (place, _, _) in enumerate(found):
        here = lax.div(places, width) == m
        starts = jnp.where(here, (2 * place + flags_ref[m]) * width + lax.rem(places, width), starts)
    arrange = (iota((halo, halo), 0) == starts).astype(F32).astype(BF)
    rows, links, size, _ = blocks_ref.shape
    sum_ref[...] = jnp.zeros(sum_ref.shape, F32)
    for j in range(rows):
        for k in range(links):
            column = cols_ref[j * links + k]

            @pl.when(column * size >= own)
            def _():
                lanes = pl.ds(pl.multiple_of(column * size - own, size), size)
                here = slice(j * size, (j + 1) * size)
                sum_ref[here, lanes] = sum_ref[here, lanes] + blocks_ref[j, k].astype(F32)

    step = 256
    for i in range(0, own, step):
        here = slice(i, i + step)
        inverse_halo_ref[here, :] = mm(inverse_ref[here, own:], arrange).astype(BF)
        total = sum_ref[here, :]
        high = total.astype(BF)
        low = (total - high.astype(F32)).astype(BF)
        blocks_halo_ref[0, here, :] = mm(high, arrange).astype(BF)
        blocks_halo_ref[1, here, :] = mm(low, arrange).astype(BF)
        value = mm(inverse_ref[here, :own], rhs_ref[...])
        state_ref[here, :] = value
        keep_split(high_ref, low_ref, here, value)
    inverse_sent_ref[...] = mm(select_ref[...], inverse_halo_ref[...]).astype(BF)
    for part in range(2):
        blocks_sent_ref[part] = mm(select_ref[...], blocks_halo_ref[part]).astype(BF)
    base_ref[...] = mm(select_ref[...], high_ref[...]) + mm(select_ref[...], low_ref[...])


def sent_update_body(count, base_ref, sent_ref, *rest):
    got, messages, halo_ref = rest[:count], rest[count:-1], rest[-1]
    fill_halo(halo_ref, got)
    send(messages, base_ref[...] + mm(sent_ref[...], halo_ref[...]))


def sent_residual_body(count, base_ref, sent_ref, *rest):
    got, messages, halo_ref = rest[:count], rest[count:-1], rest[-1]
    fill_halo(halo_ref, got)
    part = mm(sent_ref[0], halo_ref[...]) + mm(sent_ref[1], halo_ref[...])
    send(messages, base_ref[...] - part)


def update_body(count, cols_ref, state_ref, inverse_halo_ref, blocks_ref, rhs_ref, select_ref, *rest):
    got, (iterate_ref, part_ref, base_ref, halo_ref, sub_ref, high_ref, low_ref) = rest[:count], rest[count:]
    own = state_ref.shape[0]
    fill_halo(halo_ref, got)
    step = 256
    for i in range(0, own, step):
        here = slice(i, i + step)
        value = state_ref[here, :] + mm(inverse_halo_ref[here, :], halo_ref[...])
        iterate_ref[here, :] = value
        sub_ref[here, :] = value.astype(BF)
    sub_ref[own:, :] = jnp.zeros((sub_ref.shape[0] - own, sub_ref.shape[1]), BF)
    rows, links, size, _ = blocks_ref.shape
    for j in range(rows):
        total = None
        for k in range(links):
            start = pl.multiple_of(cols_ref[j * links + k] * size, size)
            part = mm(blocks_ref[j, k], sub_ref[pl.ds(start, size), :])
            total = part if total is None else total + part
        here = slice(j * size, (j + 1) * size)
        value = rhs_ref[here, :].astype(F32) - total
        part_ref[here, :] = value
        keep_split(high_ref, low_ref, here, value)
    base_ref[...] = mm(select_ref[...], high_ref[...]) + mm(select_ref[...], low_ref[...])


def residual_body(count, part_ref, blocks_halo_ref, iterate_ref, inverse_ref, select_ref, *rest):
    got, (state_ref, base_ref, halo_ref, resid_ref, high_ref, low_ref) = rest[:count], rest[count:]
    own = part_ref.shape[0]
    fill_halo(halo_ref, got)
    step = 256
    for i in range(0, own, step):
        here = slice(i, i + step)
        outer = mm(blocks_halo_ref[0, here, :], halo_ref[...]) + mm(blocks_halo_ref[1, here, :], halo_ref[...])
        resid_ref[here, :] = (part_ref[here, :] - outer).astype(BF)
    for i in range(0, own, step):
        here = slice(i, i + step)
        value = iterate_ref[here, :] + mm(inverse_ref[here, :own], resid_ref[...])
        state_ref[here, :] = value
        keep_split(high_ref, low_ref, here, value)
    base_ref[...] = mm(select_ref[...], high_ref[...]) + mm(select_ref[...], low_ref[...])


def last_update_body(count, state_ref, inverse_halo_ref, *rest):
    got, rest = rest[:count], rest[count:]
    halo_ref = rest[-1]
    fill_halo(halo_ref, got)
    outs = rest[:-1]
    order_ref = outs[0] if len(outs) == 3 else None
    round_ref = outs[-2] if order_ref is not None else outs[0]
    step = 256
    own = state_ref.shape[0]
    for i in range(0, own, step):
        here = slice(i, i + step)
        value = state_ref[here, :] + mm(inverse_halo_ref[here, :], halo_ref[...])
        round_ref[here, :] = value.astype(BF)
    if order_ref is not None:
        wire_ref = outs[-1]
        for i in range(0, own, step):
            turned = lax.dot_general(
                round_ref[...], order_ref[:, i:i + step], (((0,), (0,)), ((), ())), preferred_element_type=F32
            )
            wire_ref[:, i:i + step] = turned.astype(BF)


def one_hot(rows_of, shape):
    return (iota(shape, 0) == rows_of(iota((1, shape[1]), 1))).astype(F32).astype(BF)


def tables_body(wide, narrow, cov_plane_ref, cov_vert_ref, order_ref, plane_ref, spread_ref, vert_ref):
    own = order_ref.shape[0]
    tile = own // ZL
    order_ref[...] = one_hot(lambda k: lax.rem(k, ZL) * tile + lax.div(k, ZL), (own, own))
    plane = wide * tile
    turn = one_hot(lambda k: lax.rem(k, wide) * tile + lax.div(k, wide), (plane, plane))
    half = mm(cov_plane_ref[...], turn).astype(BF)
    plane_ref[...] = mm(half.T, turn).astype(BF).T
    share = LANES // ZL
    depth = narrow * ZL
    width = narrow * LANES

    def source(k):
        e, n, l = lax.div(k, depth), lax.rem(lax.div(k, ZL), narrow), lax.rem(k, ZL)
        return n * LANES + e * ZL + l

    spread = one_hot(source, (width, width))
    spread_ref[...] = spread
    turned = cov_vert_ref[...].astype(F32).T
    zero = jnp.zeros_like(turned)
    blocks = jnp.concatenate(
        [jnp.concatenate([turned if i == e else zero for i in range(share)], axis=1) for e in range(share)],
        axis=0,
    ).astype(BF)
    vert_ref[...] = mm_t(blocks, spread).astype(BF)


def mix_body(wide, narrow, group, in_ref, plane_ref, spread_ref, vert_ref, round_ref, *rest):
    out_ref, adjoint_hbm, cells_ref, flat_ref, wire_ref, sem = rest
    keep = pltpu.make_async_copy(round_ref, adjoint_hbm, sem)
    keep.start()
    own = in_ref.shape[1]
    tile = own // ZL
    share = LANES // ZL
    depth = narrow * ZL
    block = narrow * group
    taken = in_ref[...].astype(F32).reshape(wide, narrow, group, own)
    slabs = [taken[:, n].reshape(wide * group, own).astype(BF) for n in range(narrow)]
    for g in range(tile // share):
        lanes = slice(g * LANES, (g + 1) * LANES)
        joined = jnp.concatenate([s[:, lanes] for s in slabs], axis=1)
        spread = mm(joined, spread_ref[...])
        for e in range(share):
            cells_ref[g * share + e] = spread[:, e * depth:(e + 1) * depth]
    for r in range(group):
        for c in range(tile):
            flat_ref[c * wide:(c + 1) * wide, r * depth:(r + 1) * depth] = cells_ref[
                c, pl.ds(r, wide, stride=group), :
            ].astype(BF)
    planar = mm(plane_ref[...], flat_ref[...]).astype(BF)
    for g in range(tile // share):
        stacked = jnp.concatenate(
            [
                jnp.concatenate(
                    [
                        planar[c * wide:(c + 1) * wide, r * depth:(r + 1) * depth]
                        for c in range(g * share, (g + 1) * share)
                    ],
                    axis=1,
                )
                for r in range(group)
            ],
            axis=0,
        )
        mixed = mm(stacked, vert_ref[...])
        for r in range(group):
            for n in range(narrow):
                wire_ref[g, pl.ds(n * group + r, wide, stride=block), :] = mixed[
                    r * wide:(r + 1) * wide, n * LANES:(n + 1) * LANES
                ]
        out_ref[:, g * LANES:(g + 1) * LANES] = wire_ref[g].astype(BF)
    keep.wait()


def unwire_body(in_ref, order_ref, out_hbm, out_ref, sems):
    step = 256
    copies = []
    for n, i in enumerate(range(0, out_ref.shape[0], step)):
        here = pl.ds(i, step)
        out_ref[here, :] = mm_t(order_ref[here, :], in_ref[...]).astype(BF)
        copy = pltpu.make_async_copy(out_ref.at[here], out_hbm.at[here], sems.at[n])
        copy.start()
        copies.append(copy)
    for copy in copies:
        copy.wait()


def column_tables(own, cov_plane, cov_vert):
    wide, narrow = lax.axis_size("wide"), lax.axis_size("narrow")
    width = narrow * LANES
    plane = cov_plane.shape[0]
    shape = jax.ShapeDtypeStruct
    return call(
        functools.partial(tables_body, wide, narrow),
        [shape((own, own), BF), shape((plane, plane), BF), shape((width, width), BF), shape((width, width), BF)],
        [cov_plane, cov_vert],
    )


def smooth_by_columns(rounded, wire, tables):
    wide, narrow = lax.axis_size("wide"), lax.axis_size("narrow")
    own, columns = rounded.shape
    devices = wide * narrow
    group = columns // devices
    depth = narrow * ZL
    tile = own // ZL
    shape = jax.ShapeDtypeStruct
    order, plane_mix, spread, vert_mix = tables
    there = lax.all_to_all(
        wire.reshape(devices, group, own), ("wide", "narrow"), split_axis=0, concat_axis=0, tiled=True
    )
    mixed, adjoint = call(
        functools.partial(mix_body, wide, narrow, group),
        [shape((columns, own), BF), shape((own, columns), BF)],
        [there.reshape(columns, own), plane_mix, spread, vert_mix, rounded],
        [
            pltpu.VMEM((tile, wide * group, depth), F32),
            pltpu.VMEM((plane_mix.shape[0], group * depth), BF),
            pltpu.VMEM((own // LANES, columns, LANES), F32),
            pltpu.SemaphoreType.DMA,
        ],
        out_specs=[VM, ANY],
    )
    back = lax.all_to_all(
        mixed.reshape(devices, group, own), ("wide", "narrow"), split_axis=0, concat_axis=0, tiled=True
    )
    (smoothed,) = call(
        unwire_body,
        [shape((own, columns), BF)],
        [back.reshape(columns, own), order],
        [pltpu.VMEM((own, columns), BF), pltpu.SemaphoreType.DMA((own // 256,))],
        out_specs=[ANY],
    )
    return adjoint, smoothed


def smooth_by_layers(adjoint, cov_plane, cov_vert):
    own, columns = adjoint.shape
    layered = adjoint.reshape(ZL, own // ZL, -1)
    planar = jnp.einsum(
        "pq,lqr->lpr",
        cov_plane,
        lax.all_to_all(layered, "wide", split_axis=0, concat_axis=1, tiled=True),
        preferred_element_type=F32,
    ).astype(BF)
    restored = lax.all_to_all(planar, "wide", split_axis=1, concat_axis=0, tiled=True)
    slab_weights = lax.dynamic_slice_in_dim(cov_vert, lax.axis_index("narrow") * ZL, ZL, 0)
    summed = jnp.dot(
        slab_weights,
        lax.all_gather(restored.reshape(ZL, -1), "narrow", axis=0, tiled=True),
        preferred_element_type=F32,
    )
    return summed.astype(BF).reshape(own, -1)


def shards(adjoint_rhs, inverse_rows, blocks, block_cols, send_rows, cov_plane, cov_vert):
    rhs = adjoint_rhs[0, 0]
    inverse = inverse_rows[0, 0]
    block_values = blocks[0, 0]
    cols = block_cols[0, 0].reshape(-1)
    send_index = send_rows[0, 0]
    own, columns = rhs.shape
    width = send_index.shape[1]
    halo = 4 * width
    wide, narrow = lax.axis_size("wide"), lax.axis_size("narrow")
    group = columns // (wide * narrow)
    by_columns = columns % (wide * narrow) == 0 and group % 8 == 0 and narrow * ZL == LANES and wide % 16 == 0
    found = matchings()
    count = len(found)
    sent = count * width
    index, counts = [lax.axis_index("wide"), lax.axis_index("narrow")], [wide, narrow]
    above = [index[place] % 2 == parity for place, parity, _ in found]
    paired = [
        jnp.where(up, index[place] + 1 < counts[place], index[place] > 0) for up, (place, _, _) in zip(above, found)
    ]
    flags = jnp.stack(above + paired).astype(jnp.int32)
    shape = jax.ShapeDtypeStruct
    notes = [shape((width, columns), BF)] * count
    full = shape((own, columns), F32)
    base_shape = shape((sent, columns), F32)
    halo_space = pltpu.VMEM((halo, columns), BF)
    cell_space = pltpu.VMEM((own, columns), BF)
    (select,) = call(
        functools.partial(select_body, found, own),
        [shape((sent, own), BF)],
        [flags, send_index],
        specs=[SM, VM],
        flops=SELECT_FLOPS,
    )
    messages = call(pick_body, notes, [select, rhs], flops=SELECT_FLOPS)
    got = swap(messages, found)
    inverse_halo, blocks_halo, inverse_sent, blocks_sent, state, base = call(
        functools.partial(setup_body, found, width),
        [
            shape((own, halo), BF),
            shape((2, own, halo), BF),
            shape((sent, halo), BF),
            shape((2, sent, halo), BF),
            full,
            base_shape,
        ],
        [flags, cols, inverse, block_values, rhs, select],
        [
            pltpu.VMEM((own, halo), F32),
            cell_space,
            cell_space,
        ],
        [SM, SM, VM, VM, VM, VM],
        limit=12,
    )
    tables = column_tables(own, cov_plane, cov_vert) if by_columns else ()
    for sweep in range(SWEEPS - 1):
        messages = call(
            functools.partial(sent_update_body, count), notes, [base, inverse_sent, *got], [halo_space], limit=4
        )
        arrived, got = got, swap(messages, found)
        iterate, part, base = call(
            functools.partial(update_body, count),
            [full, full, base_shape],
            [cols, state, inverse_halo, block_values, rhs, select, *arrived],
            [halo_space, pltpu.VMEM((own + halo, columns), BF), cell_space, cell_space],
            [SM] + [VM] * (5 + count),
        )
        messages = call(
            functools.partial(sent_residual_body, count), notes, [base, blocks_sent, *got], [halo_space], limit=4
        )
        arrived, got = got, swap(messages, found)
        if sweep == 1:
            tables, part = lax.optimization_barrier((tables, part))
        state, base = call(
            functools.partial(residual_body, count),
            [full, base_shape],
            [part, blocks_halo, iterate, inverse, select, *arrived],
            [halo_space, cell_space, cell_space, cell_space],
        )
    cells = shape((own, columns), BF)
    last = functools.partial(last_update_body, count)
    if by_columns:
        rounded, wire = call(
            last, [cells, shape((columns, own), BF)], [state, inverse_halo, *got, tables[0]], [halo_space]
        )
        adjoint, smoothed = smooth_by_columns(rounded, wire, tables)
    else:
        (adjoint,) = call(last, [cells], [state, inverse_halo, *got], [halo_space])
        smoothed = smooth_by_layers(adjoint, cov_plane, cov_vert)
    return (adjoint[None, None], smoothed[None, None])


def solution(mesh):
    in_specs = (
        P("wide", "narrow", None, None),
        P("wide", "narrow", None, None),
        P("wide", "narrow", None, None, None, None),
        P("wide", "narrow", None, None),
        P("wide", "narrow", None, None),
        P(),
        P(),
    )
    out_specs = (P("wide", "narrow", None, None), P("wide", "narrow", None, None))
    return jax.shard_map(shards, mesh=mesh, in_specs=in_specs, out_specs=out_specs, check_vma=False)
```

```python
import functools

import jax
import jax.numpy as jnp
from jax import lax
from jax.experimental import pallas as pl
from jax.experimental.pallas import tpu as pltpu
from jax.sharding import PartitionSpec as P

ZL = 64
SWEEPS = 4
LANES = 128
PARTS = 2
SELECT_FLOPS = 2 * 10 ** 9
BF = jnp.bfloat16
F32 = jnp.float32
VM = pl.BlockSpec(memory_space=pltpu.VMEM)
SM = pl.BlockSpec(memory_space=pltpu.SMEM)
ANY = pl.BlockSpec(memory_space=pl.ANY)


def matchings():
    axes = ("wide", "narrow")
    counts = [lax.axis_size(axis) for axis in axes]
    found = []
    for place in range(2):
        count, other = counts[place], counts[1 - place]
        for parity in range(2):
            if count <= parity + 1:
                continue
            pairs = []
            for i in range(count):
                partner = i + 1 if i % 2 == parity else i - 1
                for j in range(other):
                    source, target = (i, j), (partner, j)
                    if not 0 <= partner < count:
                        target = (i, j ^ 1 if j ^ 1 < other else j)
                    if place == 1:
                        source, target = source[::-1], target[::-1]
                    pairs.append((source[0] * counts[1] + source[1], target[0] * counts[1] + target[1]))
            found.append((place, parity, tuple(pairs)))
    return sorted(found, key=lambda f: (-f[0], -f[1]))


def swap(messages, found):
    return [lax.ppermute(m, ("wide", "narrow"), list(f[-1])) for m, f in zip(messages, found)]


def mm(a, b):
    return jnp.dot(a, b, preferred_element_type=F32)


def mm_t(a, b):
    return lax.dot_general(a, b, (((1,), (1,)), ((), ())), preferred_element_type=F32)


def iota(shape, dim):
    return lax.broadcasted_iota(jnp.int32, shape, dim)


def call(body, outs, args, scratch=(), specs=None, flops=0, limit=8, out_specs=None):
    size = sum(a.size * a.dtype.itemsize for a in args)
    return pl.pallas_call(
        body,
        out_shape=outs,
        in_specs=specs or [VM] * len(args),
        out_specs=out_specs or [VM] * len(outs),
        scratch_shapes=list(scratch),
        compiler_params=pltpu.CompilerParams(vmem_limit_bytes=limit * 1024 * 1024),
        cost_estimate=pl.CostEstimate(flops=flops, bytes_accessed=size, transcendentals=0),
    )(*args)


def fill_halo(halo_ref, got):
    width = got[0].shape[0]
    for m, piece in enumerate(got):
        halo_ref[m * width:(m + 1) * width, :] = piece[...]
    filled = len(got) * width
    if filled < halo_ref.shape[0]:
        halo_ref[filled:, :] = jnp.zeros((halo_ref.shape[0] - filled, halo_ref.shape[1]), halo_ref.dtype)


def send(messages, values):
    width = messages[0].shape[0]
    for m, message in enumerate(messages):
        message[...] = values[m * width:(m + 1) * width, :].astype(BF)


def keep_split(high_ref, low_ref, rows, value):
    high = value.astype(BF)
    high_ref[rows, :] = high
    low_ref[rows, :] = (value - high.astype(F32)).astype(BF)


def select_body(found, own, flags_ref, send_ref, select_ref):
    width = send_ref.shape[1]
    diagonal = iota((width, width), 0) == iota((width, width), 1)
    for m, (place, _, _) in enumerate(found):
        rows = jnp.where(
            flags_ref[m] == 1,
            send_ref[2 * place + 1:2 * place + 2, :],
            send_ref[2 * place:2 * place + 1, :],
        ).astype(F32)
        column = jnp.sum(jnp.where(diagonal, rows, 0.0), axis=1, keepdims=True).astype(jnp.int32)
        column = jnp.where(flags_ref[len(found) + m] == 1, column, -1)
        chosen = (iota((width, own), 1) == column).astype(F32).astype(BF)
        select_ref[m * width:(m + 1) * width, :] = chosen


def pick_body(select_ref, rhs_ref, *messages):
    send(messages, mm(select_ref[...], rhs_ref[...]))


def setup_body(found, width, flags_ref, cols_ref, inverse_ref, blocks_ref, rhs_ref, select_ref, *rest):
    inverse_halo_ref, blocks_halo_ref, inverse_sent_ref, blocks_sent_ref, state_ref, base_ref = rest[:6]
    sum_ref, high_ref, low_ref = rest[6:]
    own = rhs_ref.shape[0]
    halo = 4 * width
    places = iota((1, halo), 1)
    starts = jnp.full((1, halo), -halo, jnp.int32)
    for m, (place, _, _) in enumerate(found):
        here = lax.div(places, width) == m
        starts = jnp.where(here, (2 * place + flags_ref[m]) * width + lax.rem(places, width), starts)
    arrange = (iota((halo, halo), 0) == starts).astype(F32).astype(BF)
    rows, links, size, _ = blocks_ref.shape
    sum_ref[...] = jnp.zeros(sum_ref.shape, F32)
    for j in range(rows):
        for k in range(links):
            column = cols_ref[j * links + k]

            @pl.when(column * size >= own)
            def _():
                lanes = pl.ds(pl.multiple_of(column * size - own, size), size)
                here = slice(j * size, (j + 1) * size)
                sum_ref[here, lanes] = sum_ref[here, lanes] + blocks_ref[j, k].astype(F32)

    step = 256
    for i in range(0, own, step):
        here = slice(i, i + step)
        inverse_halo_ref[here, :] = mm(inverse_ref[here, own:], arrange).astype(BF)
        total = sum_ref[here, :]
        high = total.astype(BF)
        low = (total - high.astype(F32)).astype(BF)
        blocks_halo_ref[0, here, :] = mm(high, arrange).astype(BF)
        blocks_halo_ref[1, here, :] = mm(low, arrange).astype(BF)
        value = mm(inverse_ref[here, :own], rhs_ref[...])
        state_ref[here, :] = value
        keep_split(high_ref, low_ref, here, value)
    inverse_sent_ref[...] = mm(select_ref[...], inverse_halo_ref[...]).astype(BF)
    for part in range(2):
        blocks_sent_ref[part] = mm(select_ref[...], blocks_halo_ref[part]).astype(BF)
    base_ref[...] = mm(select_ref[...], high_ref[...]) + mm(select_ref[...], low_ref[...])


def sent_update_body(count, base_ref, sent_ref, *rest):
    got, messages, halo_ref = rest[:count], rest[count:-1], rest[-1]
    fill_halo(halo_ref, got)
    send(messages, base_ref[...] + mm(sent_ref[...], halo_ref[...]))


def sent_residual_body(count, base_ref, sent_ref, *rest):
    got, messages, halo_ref = rest[:count], rest[count:-1], rest[-1]
    fill_halo(halo_ref, got)
    part = mm(sent_ref[0], halo_ref[...]) + mm(sent_ref[1], halo_ref[...])
    send(messages, base_ref[...] - part)


def update_body(count, cols_ref, state_ref, inverse_halo_ref, blocks_ref, rhs_ref, select_ref, *rest):
    got, (iterate_ref, part_ref, base_ref, halo_ref, sub_ref, high_ref, low_ref) = rest[:count], rest[count:]
    own = state_ref.shape[0]
    fill_halo(halo_ref, got)
    step = 256
    for i in range(0, own, step):
        here = slice(i, i + step)
        value = state_ref[here, :] + mm(inverse_halo_ref[here, :], halo_ref[...])
        iterate_ref[here, :] = value
        sub_ref[here, :] = value.astype(BF)
    sub_ref[own:, :] = jnp.zeros((sub_ref.shape[0] - own, sub_ref.shape[1]), BF)
    rows, links, size, _ = blocks_ref.shape
    for j in range(rows):
        total = None
        for k in range(links):
            start = pl.multiple_of(cols_ref[j * links + k] * size, size)
            part = mm(blocks_ref[j, k], sub_ref[pl.ds(start, size), :])
            total = part if total is None else total + part
        here = slice(j * size, (j + 1) * size)
        value = rhs_ref[here, :].astype(F32) - total
        part_ref[here, :] = value
        keep_split(high_ref, low_ref, here, value)
    base_ref[...] = mm(select_ref[...], high_ref[...]) + mm(select_ref[...], low_ref[...])


def residual_body(count, part_ref, blocks_halo_ref, iterate_ref, inverse_ref, select_ref, *rest):
    got, (state_ref, base_ref, halo_ref, resid_ref, high_ref, low_ref) = rest[:count], rest[count:]
    own = part_ref.shape[0]
    fill_halo(halo_ref, got)
    step = 256
    for i in range(0, own, step):
        here = slice(i, i + step)
        outer = mm(blocks_halo_ref[0, here, :], halo_ref[...]) + mm(blocks_halo_ref[1, here, :], halo_ref[...])
        resid_ref[here, :] = (part_ref[here, :] - outer).astype(BF)
    for i in range(0, own, step):
        here = slice(i, i + step)
        value = iterate_ref[here, :] + mm(inverse_ref[here, :own], resid_ref[...])
        state_ref[here, :] = value
        keep_split(high_ref, low_ref, here, value)
    base_ref[...] = mm(select_ref[...], high_ref[...]) + mm(select_ref[...], low_ref[...])


def last_update_body(count, state_ref, inverse_halo_ref, *rest):
    got, rest = rest[:count], rest[count:]
    halo_ref = rest[-1]
    fill_halo(halo_ref, got)
    outs = rest[:-1]
    tabled = len(outs) > 1
    round_ref = outs[2] if tabled else outs[0]
    step = 256
    own = state_ref.shape[0]
    for i in range(0, own, step):
        here = slice(i, i + step)
        value = state_ref[here, :] + mm(inverse_halo_ref[here, :], halo_ref[...])
        round_ref[here, :] = value.astype(BF)
    if tabled:
        wire_body(0, round_ref, outs[0], outs[1], outs[3])


def wire_body(part, round_ref, order_ref, place_ref, wire_ref):
    parts, _, columns = place_ref.shape
    share = order_ref.shape[1] // parts
    values = round_ref[:, part * columns:(part + 1) * columns]
    total = None
    for h in range(parts):
        turned = lax.dot_general(
            values,
            order_ref[:, h * share:(h + 1) * share],
            (((0,), (0,)), ((), ())),
            preferred_element_type=F32,
        ).astype(BF)
        placed = mm(place_ref[h], turned)
        total = placed if total is None else total + placed
    wire_ref[...] = total.astype(BF)


def one_hot(rows_of, shape):
    return (iota(shape, 0) == rows_of(iota((1, shape[1]), 1))).astype(F32).astype(BF)


def tables_body(wide, narrow, cov_plane_ref, cov_vert_ref, *rest):
    order_ref, plane_ref, spread_ref, vert_ref, place_ref, take_ref = rest
    own = order_ref.shape[0]
    parts, rows, columns = place_ref.shape
    group = rows // (wide * narrow)
    small = group // parts
    for h in range(parts):
        place_ref[h] = one_hot(lambda k: lax.div(k, small) * group + h * small + lax.rem(k, small), (rows, columns))
        lanes = iota((1, rows), 1)
        inside = lax.rem(lanes, group) - h * small
        target = lax.div(lanes, group) * small + inside
        target = jnp.where(inside == jnp.clip(inside, 0, small - 1), target, -1)
        take_ref[h] = (iota((columns, rows), 0) == target).astype(F32).astype(BF)
    tile = own // ZL
    order_ref[...] = one_hot(lambda k: lax.rem(k, ZL) * tile + lax.div(k, ZL), (own, own))
    plane = wide * tile
    turn = one_hot(lambda k: lax.rem(k, wide) * tile + lax.div(k, wide), (plane, plane))
    half = mm(cov_plane_ref[...], turn).astype(BF)
    plane_ref[...] = mm(half.T, turn).astype(BF).T
    share = LANES // ZL
    depth = narrow * ZL
    width = narrow * LANES

    def source(k):
        e, n, l = lax.div(k, depth), lax.rem(lax.div(k, ZL), narrow), lax.rem(k, ZL)
        return n * LANES + e * ZL + l

    spread = one_hot(source, (width, width))
    spread_ref[...] = spread
    turned = cov_vert_ref[...].astype(F32).T
    zero = jnp.zeros_like(turned)
    blocks = jnp.concatenate(
        [jnp.concatenate([turned if i == e else zero for i in range(share)], axis=1) for e in range(share)],
        axis=0,
    ).astype(BF)
    vert_ref[...] = mm_t(blocks, spread).astype(BF)


def mix_body(wide, narrow, parts, in_ref, plane_ref, spread_ref, vert_ref, out_ref, cells_ref, flat_ref, wire_ref):
    lanes_all = in_ref.shape[1]
    group = in_ref.shape[0] // (wide * narrow)
    small = group // parts
    tile = lanes_all // ZL
    share = LANES // ZL
    depth = narrow * ZL
    block = narrow * group
    taken = in_ref[...].astype(F32).reshape(wide, narrow, group, lanes_all)
    slabs = [taken[:, n].reshape(wide * group, lanes_all).astype(BF) for n in range(narrow)]
    for g in range(tile // share):
        lanes = slice(g * LANES, (g + 1) * LANES)
        joined = jnp.concatenate([s[:, lanes] for s in slabs], axis=1)
        spread = mm(joined, spread_ref[...])
        for e in range(share):
            cells_ref[g * share + e] = spread[:, e * depth:(e + 1) * depth]
    for h in range(parts):
        for r in range(small):
            for c in range(tile):
                top = (h * tile + c) * wide
                flat_ref[top:top + wide, r * depth:(r + 1) * depth] = cells_ref[
                    c, pl.ds(h * small + r, wide, stride=group), :
                ].astype(BF)
    planar = mm(plane_ref[...], flat_ref[...]).astype(BF)
    for g in range(tile // share):
        for h in range(parts):
            first = h * tile + g * share
            stacked = jnp.concatenate(
                [
                    jnp.concatenate(
                        [
                            planar[c * wide:(c + 1) * wide, r * depth:(r + 1) * depth]
                            for c in range(first, first + share)
                        ],
                        axis=1,
                    )
                    for r in range(small)
                ],
                axis=0,
            )
            mixed = mm(stacked, vert_ref[...])
            for r in range(small):
                for n in range(narrow):
                    wire_ref[g, pl.ds(n * group + h * small + r, wide, stride=block), :] = mixed[
                        r * wide:(r + 1) * wide, n * LANES:(n + 1) * LANES
                    ]
        out_ref[:, g * LANES:(g + 1) * LANES] = wire_ref[g].astype(BF)


def unwire_rows(in_ref, order_ref, take_ref):
    joined = jnp.concatenate([mm(take_ref[h], in_ref[...]).astype(BF) for h in range(take_ref.shape[0])], axis=1)
    return lambda here: mm_t(order_ref[here, :], joined).astype(BF)


def unwire_body(in_ref, order_ref, take_ref, out_ref):
    rows = unwire_rows(in_ref, order_ref, take_ref)
    step = 256
    for i in range(0, out_ref.shape[0], step):
        out_ref[i:i + step, :] = rows(slice(i, i + step))


def last_unwire_body(count, in_ref, order_ref, take_ref, adjoint_ref, *rest):
    done, (out_hbm, adjoint_hbm, out_ref, sems) = rest[:count], rest[count:]
    own, columns = out_ref.shape
    copies = [pltpu.make_async_copy(adjoint_ref, adjoint_hbm, sems.at[0])]
    for part, piece in enumerate(done):
        lanes = pl.ds(part * columns, columns)
        copies.append(pltpu.make_async_copy(piece, out_hbm.at[:, lanes], sems.at[1 + part]))
    for copy in copies:
        copy.start()
    rows = unwire_rows(in_ref, order_ref, take_ref)
    step = 256
    for n, i in enumerate(range(0, own, step)):
        here = pl.ds(i, step)
        out_ref[here, :] = rows(slice(i, i + step))
        lanes = pl.ds(count * columns, columns)
        copy = pltpu.make_async_copy(out_ref.at[here], out_hbm.at[here, lanes], sems.at[1 + count + n])
        copy.start()
        copies.append(copy)
    for copy in copies:
        copy.wait()


def column_tables(own, columns, cov_plane, cov_vert):
    wide, narrow = lax.axis_size("wide"), lax.axis_size("narrow")
    width = narrow * LANES
    plane = cov_plane.shape[0]
    small = columns // PARTS
    shape = jax.ShapeDtypeStruct
    return call(
        functools.partial(tables_body, wide, narrow),
        [
            shape((own, own), BF),
            shape((plane, plane), BF),
            shape((width, width), BF),
            shape((width, width), BF),
            shape((PARTS, columns, small), BF),
            shape((PARTS, small, columns), BF),
        ],
        [cov_plane, cov_vert],
    )


def smooth_by_columns(rounded, wire, tables):
    wide, narrow = lax.axis_size("wide"), lax.axis_size("narrow")
    own, columns = rounded.shape
    devices = wide * narrow
    group = columns // devices
    lanes = own // PARTS
    depth = narrow * ZL
    shape = jax.ShapeDtypeStruct
    order, plane_mix, spread, vert_mix, place, take = tables
    plane = plane_mix.shape[0]
    cells = shape((columns, lanes), BF)

    def exchange(values):
        cut = values.reshape(devices, group, lanes)
        moved = lax.all_to_all(cut, ("wide", "narrow"), split_axis=0, concat_axis=0, tiled=True)
        return moved.reshape(columns, lanes)

    wires = [wire]
    for part in range(1, PARTS):
        wires += call(functools.partial(wire_body, part), [cells], [rounded, order, place])
    there = [exchange(values) for values in wires]
    back = []
    for values in there:
        (mixed,) = call(
            functools.partial(mix_body, wide, narrow, PARTS),
            [cells],
            [values, plane_mix, spread, vert_mix],
            [
                pltpu.VMEM((lanes // ZL, wide * group, depth), F32),
                pltpu.VMEM((plane, group // PARTS * depth), BF),
                pltpu.VMEM((lanes // LANES, columns, LANES), F32),
            ],
        )
        back.append(exchange(mixed))
    small = columns // PARTS
    pieces = []
    for values in back[:-1]:
        pieces += call(unwire_body, [shape((own, small), BF)], [values, order, take])
    smoothed, adjoint = call(
        functools.partial(last_unwire_body, PARTS - 1),
        [shape((own, columns), BF)] * 2,
        [back[-1], order, take, rounded, *pieces],
        [pltpu.VMEM((own, small), BF), pltpu.SemaphoreType.DMA((PARTS + own // 256,))],
        out_specs=[ANY, ANY],
    )
    return adjoint, smoothed


def smooth_by_layers(adjoint, cov_plane, cov_vert):
    own, columns = adjoint.shape
    layered = adjoint.reshape(ZL, own // ZL, -1)
    planar = jnp.einsum(
        "pq,lqr->lpr",
        cov_plane,
        lax.all_to_all(layered, "wide", split_axis=0, concat_axis=1, tiled=True),
        preferred_element_type=F32,
    ).astype(BF)
    restored = lax.all_to_all(planar, "wide", split_axis=1, concat_axis=0, tiled=True)
    slab_weights = lax.dynamic_slice_in_dim(cov_vert, lax.axis_index("narrow") * ZL, ZL, 0)
    summed = jnp.dot(
        slab_weights,
        lax.all_gather(restored.reshape(ZL, -1), "narrow", axis=0, tiled=True),
        preferred_element_type=F32,
    )
    return summed.astype(BF).reshape(own, -1)


def shards(adjoint_rhs, inverse_rows, blocks, block_cols, send_rows, cov_plane, cov_vert):
    rhs = adjoint_rhs[0, 0]
    inverse = inverse_rows[0, 0]
    block_values = blocks[0, 0]
    cols = block_cols[0, 0].reshape(-1)
    send_index = send_rows[0, 0]
    own, columns = rhs.shape
    width = send_index.shape[1]
    halo = 4 * width
    wide, narrow = lax.axis_size("wide"), lax.axis_size("narrow")
    group = columns // (wide * narrow)
    fits = own % (PARTS * LANES) == 0 and wide % 16 == 0 and narrow * ZL == LANES
    by_columns = fits and columns % (wide * narrow) == 0 and group == 8
    found = matchings()
    count = len(found)
    sent = count * width
    index, counts = [lax.axis_index("wide"), lax.axis_index("narrow")], [wide, narrow]
    above = [index[place] % 2 == parity for place, parity, _ in found]
    paired = [
        jnp.where(up, index[place] + 1 < counts[place], index[place] > 0) for up, (place, _, _) in zip(above, found)
    ]
    flags = jnp.stack(above + paired).astype(jnp.int32)
    shape = jax.ShapeDtypeStruct
    notes = [shape((width, columns), BF)] * count
    full = shape((own, columns), F32)
    base_shape = shape((sent, columns), F32)
    halo_space = pltpu.VMEM((halo, columns), BF)
    cell_space = pltpu.VMEM((own, columns), BF)
    (select,) = call(
        functools.partial(select_body, found, own),
        [shape((sent, own), BF)],
        [flags, send_index],
        specs=[SM, VM],
        flops=SELECT_FLOPS,
    )
    messages = call(pick_body, notes, [select, rhs], flops=SELECT_FLOPS)
    got = swap(messages, found)
    inverse_halo, blocks_halo, inverse_sent, blocks_sent, state, base = call(
        functools.partial(setup_body, found, width),
        [
            shape((own, halo), BF),
            shape((2, own, halo), BF),
            shape((sent, halo), BF),
            shape((2, sent, halo), BF),
            full,
            base_shape,
        ],
        [flags, cols, inverse, block_values, rhs, select],
        [
            pltpu.VMEM((own, halo), F32),
            cell_space,
            cell_space,
        ],
        [SM, SM, VM, VM, VM, VM],
        limit=12,
    )
    tables = column_tables(own, columns, cov_plane, cov_vert) if by_columns else ()
    for sweep in range(SWEEPS - 1):
        messages = call(
            functools.partial(sent_update_body, count), notes, [base, inverse_sent, *got], [halo_space], limit=4
        )
        arrived, got = got, swap(messages, found)
        iterate, part, base = call(
            functools.partial(update_body, count),
            [full, full, base_shape],
            [cols, state, inverse_halo, block_values, rhs, select, *arrived],
            [halo_space, pltpu.VMEM((own + halo, columns), BF), cell_space, cell_space],
            [SM] + [VM] * (5 + count),
        )
        messages = call(
            functools.partial(sent_residual_body, count), notes, [base, blocks_sent, *got], [halo_space], limit=4
        )
        arrived, got = got, swap(messages, found)
        if sweep == 1:
            tables, part = lax.optimization_barrier((tables, part))
        state, base = call(
            functools.partial(residual_body, count),
            [full, base_shape],
            [part, blocks_halo, iterate, inverse, select, *arrived],
            [halo_space, cell_space, cell_space, cell_space],
        )
    cells = shape((own, columns), BF)
    last = functools.partial(last_update_body, count)
    if by_columns:
        rounded, wire = call(
            last,
            [cells, shape((columns, own // PARTS), BF)],
            [state, inverse_halo, *got, tables[0], tables[4]],
            [halo_space],
        )
        adjoint, smoothed = smooth_by_columns(rounded, wire, tables)
    else:
        (adjoint,) = call(last, [cells], [state, inverse_halo, *got], [halo_space])
        smoothed = smooth_by_layers(adjoint, cov_plane, cov_vert)
    return (adjoint[None, None], smoothed[None, None])


def solution(mesh):
    in_specs = (
        P("wide", "narrow", None, None),
        P("wide", "narrow", None, None),
        P("wide", "narrow", None, None, None, None),
        P("wide", "narrow", None, None),
        P("wide", "narrow", None, None),
        P(),
        P(),
    )
    out_specs = (P("wide", "narrow", None, None), P("wide", "narrow", None, None))
    return jax.shard_map(shards, mesh=mesh, in_specs=in_specs, out_specs=out_specs, check_vma=False)
```

```python
import functools

import jax
import jax.numpy as jnp
from jax import lax
from jax.experimental import pallas as pl
from jax.experimental.pallas import tpu as pltpu
from jax.sharding import PartitionSpec as P

ZL = 64
SWEEPS = 4
LANES = 128
SELECT_FLOPS = 2 * 10 ** 9
BF = jnp.bfloat16
F32 = jnp.float32
VM = pl.BlockSpec(memory_space=pltpu.VMEM)
SM = pl.BlockSpec(memory_space=pltpu.SMEM)
ANY = pl.BlockSpec(memory_space=pl.ANY)


def matchings():
    axes = ("wide", "narrow")
    counts = [lax.axis_size(axis) for axis in axes]
    found = []
    for place in range(2):
        count, other = counts[place], counts[1 - place]
        for parity in range(2):
            if count <= parity + 1:
                continue
            pairs = []
            for i in range(count):
                partner = i + 1 if i % 2 == parity else i - 1
                for j in range(other):
                    source, target = (i, j), (partner, j)
                    if not 0 <= partner < count:
                        target = (i, j ^ 1 if j ^ 1 < other else j)
                    if place == 1:
                        source, target = source[::-1], target[::-1]
                    pairs.append((source[0] * counts[1] + source[1], target[0] * counts[1] + target[1]))
            found.append((place, parity, tuple(pairs)))
    return sorted(found, key=lambda f: (f[0] == 0 and f[1] == 0, f[0], -f[1]))


def swap(messages, found):
    return [lax.ppermute(m, ("wide", "narrow"), list(f[-1])) for m, f in zip(messages, found)]


def mm(a, b):
    return jnp.dot(a, b, preferred_element_type=F32)


def mm_t(a, b):
    return lax.dot_general(a, b, (((1,), (1,)), ((), ())), preferred_element_type=F32)


def iota(shape, dim):
    return lax.broadcasted_iota(jnp.int32, shape, dim)


def call(body, outs, args, scratch=(), specs=None, flops=0, limit=8, out_specs=None):
    size = sum(a.size * a.dtype.itemsize for a in args)
    return pl.pallas_call(
        body,
        out_shape=outs,
        in_specs=specs or [VM] * len(args),
        out_specs=out_specs or [VM] * len(outs),
        scratch_shapes=list(scratch),
        compiler_params=pltpu.CompilerParams(vmem_limit_bytes=limit * 1024 * 1024),
        cost_estimate=pl.CostEstimate(flops=flops, bytes_accessed=size, transcendentals=0),
    )(*args)


def fill_halo(halo_ref, got):
    width = got[0].shape[0]
    for m, piece in enumerate(got):
        halo_ref[m * width:(m + 1) * width, :] = piece[...]
    filled = len(got) * width
    if filled < halo_ref.shape[0]:
        halo_ref[filled:, :] = jnp.zeros((halo_ref.shape[0] - filled, halo_ref.shape[1]), halo_ref.dtype)


def send(messages, values):
    width = messages[0].shape[0]
    for m, message in enumerate(messages):
        message[...] = values[m * width:(m + 1) * width, :].astype(BF)


def keep_split(high_ref, low_ref, rows, value):
    high = value.astype(BF)
    high_ref[rows, :] = high
    low_ref[rows, :] = (value - high.astype(F32)).astype(BF)


def select_body(found, own, flags_ref, send_ref, select_ref):
    width = send_ref.shape[1]
    diagonal = iota((width, width), 0) == iota((width, width), 1)
    for m, (place, _, _) in enumerate(found):
        rows = jnp.where(
            flags_ref[m] == 1,
            send_ref[2 * place + 1:2 * place + 2, :],
            send_ref[2 * place:2 * place + 1, :],
        ).astype(F32)
        column = jnp.sum(jnp.where(diagonal, rows, 0.0), axis=1, keepdims=True).astype(jnp.int32)
        column = jnp.where(flags_ref[len(found) + m] == 1, column, -1)
        chosen = (iota((width, own), 1) == column).astype(F32).astype(BF)
        select_ref[m * width:(m + 1) * width, :] = chosen


def pick_body(select_ref, rhs_ref, *messages):
    send(messages, mm(select_ref[...], rhs_ref[...]))


def setup_body(found, width, flags_ref, cols_ref, inverse_ref, blocks_ref, rhs_ref, select_ref, *rest):
    inverse_halo_ref, blocks_halo_ref, inverse_sent_ref, blocks_sent_ref, state_ref, base_ref = rest[:6]
    sum_ref, high_ref, low_ref = rest[6:]
    own = rhs_ref.shape[0]
    halo = 4 * width
    places = iota((1, halo), 1)
    starts = jnp.full((1, halo), -halo, jnp.int32)
    for m, (place, _, _) in enumerate(found):
        here = lax.div(places, width) == m
        starts = jnp.where(here, (2 * place + flags_ref[m]) * width + lax.rem(places, width), starts)
    arrange = (iota((halo, halo), 0) == starts).astype(F32).astype(BF)
    rows, links, size, _ = blocks_ref.shape
    sum_ref[...] = jnp.zeros(sum_ref.shape, F32)
    for j in range(rows):
        for k in range(links):
            column = cols_ref[j * links + k]

            @pl.when(column * size >= own)
            def _():
                lanes = pl.ds(pl.multiple_of(column * size - own, size), size)
                here = slice(j * size, (j + 1) * size)
                sum_ref[here, lanes] = sum_ref[here, lanes] + blocks_ref[j, k].astype(F32)

    step = 256
    for i in range(0, own, step):
        here = slice(i, i + step)
        inverse_halo_ref[here, :] = mm(inverse_ref[here, own:], arrange).astype(BF)
        total = sum_ref[here, :]
        high = total.astype(BF)
        low = (total - high.astype(F32)).astype(BF)
        blocks_halo_ref[0, here, :] = mm(high, arrange).astype(BF)
        blocks_halo_ref[1, here, :] = mm(low, arrange).astype(BF)
        value = mm(inverse_ref[here, :own], rhs_ref[...])
        state_ref[here, :] = value
        keep_split(high_ref, low_ref, here, value)
    inverse_sent_ref[...] = mm(select_ref[...], inverse_halo_ref[...]).astype(BF)
    for part in range(2):
        blocks_sent_ref[part] = mm(select_ref[...], blocks_halo_ref[part]).astype(BF)
    base_ref[...] = mm(select_ref[...], high_ref[...]) + mm(select_ref[...], low_ref[...])


def sent_update_body(count, base_ref, sent_ref, *rest):
    got, messages, halo_ref = rest[:count], rest[count:-1], rest[-1]
    fill_halo(halo_ref, got)
    send(messages, base_ref[...] + mm(sent_ref[...], halo_ref[...]))


def sent_residual_body(count, base_ref, sent_ref, *rest):
    got, messages, halo_ref = rest[:count], rest[count:-1], rest[-1]
    fill_halo(halo_ref, got)
    part = mm(sent_ref[0], halo_ref[...]) + mm(sent_ref[1], halo_ref[...])
    send(messages, base_ref[...] - part)


def update_body(count, cols_ref, state_ref, inverse_halo_ref, blocks_ref, rhs_ref, select_ref, *rest):
    got, (iterate_ref, part_ref, base_ref, halo_ref, sub_ref, high_ref, low_ref) = rest[:count], rest[count:]
    own = state_ref.shape[0]
    fill_halo(halo_ref, got)
    step = 256
    for i in range(0, own, step):
        here = slice(i, i + step)
        value = state_ref[here, :] + mm(inverse_halo_ref[here, :], halo_ref[...])
        iterate_ref[here, :] = value
        sub_ref[here, :] = value.astype(BF)
    sub_ref[own:, :] = jnp.zeros((sub_ref.shape[0] - own, sub_ref.shape[1]), BF)
    rows, links, size, _ = blocks_ref.shape
    for j in range(rows):
        starts = [pl.multiple_of(cols_ref[j * links + k] * size, size) for k in range(links)]
        values = jnp.concatenate([blocks_ref[j, k] for k in range(links)], axis=1)
        coupled = jnp.concatenate([sub_ref[pl.ds(start, size), :] for start in starts], axis=0)
        total = mm(values, coupled)
        here = slice(j * size, (j + 1) * size)
        value = rhs_ref[here, :].astype(F32) - total
        part_ref[here, :] = value
        keep_split(high_ref, low_ref, here, value)
    base_ref[...] = mm(select_ref[...], high_ref[...]) + mm(select_ref[...], low_ref[...])


def residual_body(count, part_ref, blocks_halo_ref, iterate_ref, inverse_ref, select_ref, *rest):
    got, (state_ref, base_ref, halo_ref, resid_ref, high_ref, low_ref) = rest[:count], rest[count:]
    own = part_ref.shape[0]
    fill_halo(halo_ref, got)
    step = 256
    for i in range(0, own, step):
        here = slice(i, i + step)
        outer = mm(blocks_halo_ref[0, here, :], halo_ref[...]) + mm(blocks_halo_ref[1, here, :], halo_ref[...])
        resid_ref[here, :] = (part_ref[here, :] - outer).astype(BF)
    for i in range(0, own, step):
        here = slice(i, i + step)
        value = iterate_ref[here, :] + mm(inverse_ref[here, :own], resid_ref[...])
        state_ref[here, :] = value
        keep_split(high_ref, low_ref, here, value)
    base_ref[...] = mm(select_ref[...], high_ref[...]) + mm(select_ref[...], low_ref[...])


def last_update_body(count, state_ref, inverse_halo_ref, *rest):
    got, rest = rest[:count], rest[count:]
    halo_ref = rest[-1]
    fill_halo(halo_ref, got)
    outs = rest[:-1]
    order_ref = outs[0] if len(outs) == 3 else None
    round_ref = outs[-2] if order_ref is not None else outs[0]
    step = 256
    own = state_ref.shape[0]
    for i in range(0, own, step):
        here = slice(i, i + step)
        value = state_ref[here, :] + mm(inverse_halo_ref[here, :], halo_ref[...])
        round_ref[here, :] = value.astype(BF)
    if order_ref is not None:
        wire_ref = outs[-1]
        for i in range(0, own, step):
            turned = lax.dot_general(
                round_ref[...], order_ref[:, i:i + step], (((0,), (0,)), ((), ())), preferred_element_type=F32
            )
            wire_ref[:, i:i + step] = turned.astype(BF)


def one_hot(rows_of, shape):
    return (iota(shape, 0) == rows_of(iota((1, shape[1]), 1))).astype(F32).astype(BF)


def order_body(order_ref):
    own = order_ref.shape[0]
    tile = own // ZL
    order_ref[...] = one_hot(lambda k: lax.rem(k, ZL) * tile + lax.div(k, ZL), (own, own))


def tables_body(wide, narrow, cov_plane_ref, cov_vert_ref, plane_ref, spread_ref, vert_ref):
    plane = plane_ref.shape[0]
    tile = plane // wide
    turn = one_hot(lambda k: lax.rem(k, wide) * tile + lax.div(k, wide), (plane, plane))
    half = mm(cov_plane_ref[...], turn).astype(BF)
    plane_ref[...] = mm(half.T, turn).astype(BF).T
    share = LANES // ZL
    depth = narrow * ZL
    width = narrow * LANES

    def source(k):
        e, n, l = lax.div(k, depth), lax.rem(lax.div(k, ZL), narrow), lax.rem(k, ZL)
        return n * LANES + e * ZL + l

    spread = one_hot(source, (width, width))
    spread_ref[...] = spread
    turned = cov_vert_ref[...].astype(F32).T
    zero = jnp.zeros_like(turned)
    blocks = jnp.concatenate(
        [jnp.concatenate([turned if i == e else zero for i in range(share)], axis=1) for e in range(share)],
        axis=0,
    ).astype(BF)
    vert_ref[...] = mm_t(blocks, spread).astype(BF)


def mix_body(wide, narrow, group, in_ref, plane_ref, spread_ref, vert_ref, round_ref, *rest):
    out_ref, adjoint_hbm, cells_ref, flat_ref, wire_ref, sem = rest
    keep = pltpu.make_async_copy(round_ref, adjoint_hbm, sem)
    keep.start()
    own = in_ref.shape[1]
    tile = own // ZL
    share = LANES // ZL
    depth = narrow * ZL
    block = narrow * group
    taken = in_ref[...].astype(F32).reshape(wide, narrow, group, own)
    slabs = [taken[:, n].reshape(wide * group, own).astype(BF) for n in range(narrow)]
    for g in range(tile // share):
        lanes = slice(g * LANES, (g + 1) * LANES)
        joined = jnp.concatenate([s[:, lanes] for s in slabs], axis=1)
        spread = mm(joined, spread_ref[...])
        for e in range(share):
            cells_ref[g * share + e] = spread[:, e * depth:(e + 1) * depth]
    for r in range(group):
        for c in range(tile):
            flat_ref[c * wide:(c + 1) * wide, r * depth:(r + 1) * depth] = cells_ref[
                c, pl.ds(r, wide, stride=group), :
            ].astype(BF)
    planar = mm(plane_ref[...], flat_ref[...]).astype(BF)
    for g in range(tile // share):
        stacked = jnp.concatenate(
            [
                jnp.concatenate(
                    [
                        planar[c * wide:(c + 1) * wide, r * depth:(r + 1) * depth]
                        for c in range(g * share, (g + 1) * share)
                    ],
                    axis=1,
                )
                for r in range(group)
            ],
            axis=0,
        )
        mixed = mm(stacked, vert_ref[...])
        for r in range(group):
            for n in range(narrow):
                wire_ref[g, pl.ds(n * group + r, wide, stride=block), :] = mixed[
                    r * wide:(r + 1) * wide, n * LANES:(n + 1) * LANES
                ]
        out_ref[:, g * LANES:(g + 1) * LANES] = wire_ref[g].astype(BF)
    keep.wait()


def unwire_body(in_ref, order_ref, out_hbm, out_ref, sems):
    step = 256
    copies = []
    for n, i in enumerate(range(0, out_ref.shape[0], step)):
        here = pl.ds(i, step)
        out_ref[here, :] = mm_t(order_ref[here, :], in_ref[...]).astype(BF)
        copy = pltpu.make_async_copy(out_ref.at[here], out_hbm.at[here], sems.at[n])
        copy.start()
        copies.append(copy)
    for copy in copies:
        copy.wait()


def column_tables(own, cov_plane, cov_vert):
    wide, narrow = lax.axis_size("wide"), lax.axis_size("narrow")
    width = narrow * LANES
    plane = cov_plane.shape[0]
    shape = jax.ShapeDtypeStruct
    order = call(order_body, [shape((own, own), BF)], [])
    rest = call(
        functools.partial(tables_body, wide, narrow),
        [shape((plane, plane), BF), shape((width, width), BF), shape((width, width), BF)],
        [cov_plane, cov_vert],
    )
    return [tuple(order), tuple(rest)]


def smooth_by_columns(rounded, wire, tables):
    wide, narrow = lax.axis_size("wide"), lax.axis_size("narrow")
    own, columns = rounded.shape
    devices = wide * narrow
    group = columns // devices
    depth = narrow * ZL
    tile = own // ZL
    shape = jax.ShapeDtypeStruct
    (order,), (plane_mix, spread, vert_mix) = tables
    there = lax.all_to_all(
        wire.reshape(devices, group, own), ("wide", "narrow"), split_axis=0, concat_axis=0, tiled=True
    )
    mixed, adjoint = call(
        functools.partial(mix_body, wide, narrow, group),
        [shape((columns, own), BF), shape((own, columns), BF)],
        [there.reshape(columns, own), plane_mix, spread, vert_mix, rounded],
        [
            pltpu.VMEM((tile, wide * group, depth), F32),
            pltpu.VMEM((plane_mix.shape[0], group * depth), BF),
            pltpu.VMEM((own // LANES, columns, LANES), F32),
            pltpu.SemaphoreType.DMA,
        ],
        out_specs=[VM, ANY],
    )
    back = lax.all_to_all(
        mixed.reshape(devices, group, own), ("wide", "narrow"), split_axis=0, concat_axis=0, tiled=True
    )
    (smoothed,) = call(
        unwire_body,
        [shape((own, columns), BF)],
        [back.reshape(columns, own), order],
        [pltpu.VMEM((own, columns), BF), pltpu.SemaphoreType.DMA((own // 256,))],
        out_specs=[ANY],
    )
    return adjoint, smoothed


def smooth_by_layers(adjoint, cov_plane, cov_vert):
    own, columns = adjoint.shape
    layered = adjoint.reshape(ZL, own // ZL, -1)
    planar = jnp.einsum(
        "pq,lqr->lpr",
        cov_plane,
        lax.all_to_all(layered, "wide", split_axis=0, concat_axis=1, tiled=True),
        preferred_element_type=F32,
    ).astype(BF)
    restored = lax.all_to_all(planar, "wide", split_axis=1, concat_axis=0, tiled=True)
    slab_weights = lax.dynamic_slice_in_dim(cov_vert, lax.axis_index("narrow") * ZL, ZL, 0)
    summed = jnp.dot(
        slab_weights,
        lax.all_gather(restored.reshape(ZL, -1), "narrow", axis=0, tiled=True),
        preferred_element_type=F32,
    )
    return summed.astype(BF).reshape(own, -1)


def shards(adjoint_rhs, inverse_rows, blocks, block_cols, send_rows, cov_plane, cov_vert):
    rhs = adjoint_rhs[0, 0]
    inverse = inverse_rows[0, 0]
    block_values = blocks[0, 0]
    cols = block_cols[0, 0].reshape(-1)
    send_index = send_rows[0, 0]
    own, columns = rhs.shape
    width = send_index.shape[1]
    halo = 4 * width
    wide, narrow = lax.axis_size("wide"), lax.axis_size("narrow")
    group = columns // (wide * narrow)
    by_columns = columns % (wide * narrow) == 0 and group % 8 == 0 and narrow * ZL == LANES and wide % 16 == 0
    found = matchings()
    count = len(found)
    sent = count * width
    index, counts = [lax.axis_index("wide"), lax.axis_index("narrow")], [wide, narrow]
    above = [index[place] % 2 == parity for place, parity, _ in found]
    paired = [
        jnp.where(up, index[place] + 1 < counts[place], index[place] > 0) for up, (place, _, _) in zip(above, found)
    ]
    flags = jnp.stack(above + paired).astype(jnp.int32)
    shape = jax.ShapeDtypeStruct
    notes = [shape((width, columns), BF)] * count
    full = shape((own, columns), F32)
    base_shape = shape((sent, columns), F32)
    halo_space = pltpu.VMEM((halo, columns), BF)
    cell_space = pltpu.VMEM((own, columns), BF)
    (select,) = call(
        functools.partial(select_body, found, own),
        [shape((sent, own), BF)],
        [flags, send_index],
        specs=[SM, VM],
        flops=SELECT_FLOPS,
    )
    messages = call(pick_body, notes, [select, rhs], flops=SELECT_FLOPS)
    got = swap(messages, found)
    inverse_halo, blocks_halo, inverse_sent, blocks_sent, state, base = call(
        functools.partial(setup_body, found, width),
        [
            shape((own, halo), BF),
            shape((2, own, halo), BF),
            shape((sent, halo), BF),
            shape((2, sent, halo), BF),
            full,
            base_shape,
        ],
        [flags, cols, inverse, block_values, rhs, select],
        [
            pltpu.VMEM((own, halo), F32),
            cell_space,
            cell_space,
        ],
        [SM, SM, VM, VM, VM, VM],
        limit=12,
    )
    tables = column_tables(own, cov_plane, cov_vert) if by_columns else []
    for sweep in range(SWEEPS - 1):
        messages = call(
            functools.partial(sent_update_body, count), notes, [base, inverse_sent, *got], [halo_space], limit=4
        )
        arrived, got = got, swap(messages, found)
        iterate, part, base = call(
            functools.partial(update_body, count),
            [full, full, base_shape],
            [cols, state, inverse_halo, block_values, rhs, select, *arrived],
            [halo_space, pltpu.VMEM((own + halo, columns), BF), cell_space, cell_space],
            [SM] + [VM] * (5 + count),
        )
        messages = call(
            functools.partial(sent_residual_body, count), notes, [base, blocks_sent, *got], [halo_space], limit=4
        )
        arrived, got = got, swap(messages, found)
        if sweep < len(tables):
            tables[sweep], part = lax.optimization_barrier((tables[sweep], part))
        state, base = call(
            functools.partial(residual_body, count),
            [full, base_shape],
            [part, blocks_halo, iterate, inverse, select, *arrived],
            [halo_space, cell_space, cell_space, cell_space],
        )
    cells = shape((own, columns), BF)
    last = functools.partial(last_update_body, count)
    if by_columns:
        rounded, wire = call(
            last, [cells, shape((columns, own), BF)], [state, inverse_halo, *got, tables[0][0]], [halo_space]
        )
        adjoint, smoothed = smooth_by_columns(rounded, wire, tables)
    else:
        (adjoint,) = call(last, [cells], [state, inverse_halo, *got], [halo_space])
        smoothed = smooth_by_layers(adjoint, cov_plane, cov_vert)
    return (adjoint[None, None], smoothed[None, None])


def solution(mesh):
    in_specs = (
        P("wide", "narrow", None, None),
        P("wide", "narrow", None, None),
        P("wide", "narrow", None, None, None, None),
        P("wide", "narrow", None, None),
        P("wide", "narrow", None, None),
        P(),
        P(),
    )
    out_specs = (P("wide", "narrow", None, None), P("wide", "narrow", None, None))
    return jax.shard_map(shards, mesh=mesh, in_specs=in_specs, out_specs=out_specs, check_vma=False)
```

```python
import functools

import jax
import jax.numpy as jnp
from jax import lax
from jax.experimental import pallas as pl
from jax.experimental.pallas import tpu as pltpu
from jax.sharding import PartitionSpec as P

ZL = 64
SWEEPS = 4
LANES = 128
SELECT_FLOPS = 2 * 10 ** 9
BF = jnp.bfloat16
F32 = jnp.float32
VM = pl.BlockSpec(memory_space=pltpu.VMEM)
SM = pl.BlockSpec(memory_space=pltpu.SMEM)
ANY = pl.BlockSpec(memory_space=pl.ANY)


def matchings():
    axes = ("wide", "narrow")
    counts = [lax.axis_size(axis) for axis in axes]
    found = []
    for place in range(2):
        count, other = counts[place], counts[1 - place]
        for parity in range(2):
            if count <= parity + 1:
                continue
            pairs = []
            for i in range(count):
                partner = i + 1 if i % 2 == parity else i - 1
                for j in range(other):
                    source, target = (i, j), (partner, j)
                    if not 0 <= partner < count:
                        target = (i, j ^ 1 if j ^ 1 < other else j)
                    if place == 1:
                        source, target = source[::-1], target[::-1]
                    pairs.append((source[0] * counts[1] + source[1], target[0] * counts[1] + target[1]))
            found.append((place, parity, tuple(pairs)))
    return sorted(found, key=lambda f: (f[0] == 0 and f[1] == 0, f[0], -f[1]))


def swap(messages, found):
    return [lax.ppermute(m, ("wide", "narrow"), list(f[-1])) for m, f in zip(messages, found)]


def mm(a, b):
    return jnp.dot(a, b, preferred_element_type=F32)


def mm_t(a, b):
    return lax.dot_general(a, b, (((1,), (1,)), ((), ())), preferred_element_type=F32)


def iota(shape, dim):
    return lax.broadcasted_iota(jnp.int32, shape, dim)


def call(body, outs, args, scratch=(), specs=None, flops=0, limit=8, out_specs=None):
    size = sum(a.size * a.dtype.itemsize for a in args)
    return pl.pallas_call(
        body,
        out_shape=outs,
        in_specs=specs or [VM] * len(args),
        out_specs=out_specs or [VM] * len(outs),
        scratch_shapes=list(scratch),
        compiler_params=pltpu.CompilerParams(vmem_limit_bytes=limit * 1024 * 1024),
        cost_estimate=pl.CostEstimate(flops=flops, bytes_accessed=size, transcendentals=0),
    )(*args)


def fill_halo(halo_ref, got):
    width = got[0].shape[0]
    for m, piece in enumerate(got):
        halo_ref[m * width:(m + 1) * width, :] = piece[...]
    filled = len(got) * width
    if filled < halo_ref.shape[0]:
        halo_ref[filled:, :] = jnp.zeros((halo_ref.shape[0] - filled, halo_ref.shape[1]), halo_ref.dtype)


def send(messages, values):
    width = messages[0].shape[0]
    for m, message in enumerate(messages):
        message[...] = values[m * width:(m + 1) * width, :].astype(BF)


def keep_split(high_ref, low_ref, rows, value):
    high = value.astype(BF)
    high_ref[rows, :] = high
    low_ref[rows, :] = (value - high.astype(F32)).astype(BF)


def select_body(found, own, flags_ref, send_ref, select_ref):
    width = send_ref.shape[1]
    diagonal = iota((width, width), 0) == iota((width, width), 1)
    count = len(found)
    pieces = []
    for m, (place, _, _) in enumerate(found):
        rows = jnp.where(
            flags_ref[m] == 1,
            send_ref[2 * place + 1:2 * place + 2, :],
            send_ref[2 * place:2 * place + 1, :],
        )
        rows = jnp.where(flags_ref[count + m] == 1, rows, -1).astype(F32)
        pieces.append(jnp.where(diagonal, rows, 0.0))
    column = jnp.sum(jnp.concatenate(pieces, axis=0), axis=1, keepdims=True).astype(jnp.int32)
    select_ref[...] = (iota((count * width, own), 1) == column).astype(F32).astype(BF)


def pick_body(select_ref, rhs_ref, *messages):
    send(messages, mm(select_ref[...], rhs_ref[...]))


def setup_body(found, width, flags_ref, cols_ref, inverse_ref, blocks_ref, rhs_ref, select_ref, *rest):
    inverse_halo_ref, blocks_halo_ref, inverse_sent_ref, blocks_sent_ref, state_ref, base_ref = rest[:6]
    sum_ref, high_ref, low_ref = rest[6:]
    own = rhs_ref.shape[0]
    halo = 4 * width
    places = iota((1, halo), 1)
    starts = jnp.full((1, halo), -halo, jnp.int32)
    for m, (place, _, _) in enumerate(found):
        here = lax.div(places, width) == m
        starts = jnp.where(here, (2 * place + flags_ref[m]) * width + lax.rem(places, width), starts)
    arrange = (iota((halo, halo), 0) == starts).astype(F32).astype(BF)
    rows, links, size, _ = blocks_ref.shape
    sum_ref[...] = jnp.zeros(sum_ref.shape, F32)
    for j in range(rows):
        for k in range(links):
            column = cols_ref[j * links + k]

            @pl.when(column * size >= own)
            def _():
                lanes = pl.ds(pl.multiple_of(column * size - own, size), size)
                here = slice(j * size, (j + 1) * size)
                sum_ref[here, lanes] = sum_ref[here, lanes] + blocks_ref[j, k].astype(F32)

    step = 256
    for i in range(0, own, step):
        here = slice(i, i + step)
        inverse_halo_ref[here, :] = mm(inverse_ref[here, own:], arrange).astype(BF)
        total = sum_ref[here, :]
        high = total.astype(BF)
        low = (total - high.astype(F32)).astype(BF)
        blocks_halo_ref[0, here, :] = mm(high, arrange).astype(BF)
        blocks_halo_ref[1, here, :] = mm(low, arrange).astype(BF)
        value = mm(inverse_ref[here, :own], rhs_ref[...])
        state_ref[here, :] = value
        keep_split(high_ref, low_ref, here, value)
    inverse_sent_ref[...] = mm(select_ref[...], inverse_halo_ref[...]).astype(BF)
    for part in range(2):
        blocks_sent_ref[part] = mm(select_ref[...], blocks_halo_ref[part]).astype(BF)
    base_ref[...] = mm(select_ref[...], high_ref[...]) + mm(select_ref[...], low_ref[...])


def sent_update_body(count, base_ref, sent_ref, *rest):
    got, messages, halo_ref = rest[:count], rest[count:-1], rest[-1]
    fill_halo(halo_ref, got)
    send(messages, base_ref[...] + mm(sent_ref[...], halo_ref[...]))


def sent_residual_body(count, turn, base_ref, sent_ref, *rest):
    got, messages, halo_ref = rest[:count], rest[count:-1], rest[-1]
    fill_halo(halo_ref, got[turn:] + got[:turn])
    part = mm(sent_ref[0], halo_ref[...]) + mm(sent_ref[1], halo_ref[...])
    send(messages, base_ref[...] - part)


def update_body(count, cols_ref, state_ref, inverse_halo_ref, blocks_ref, rhs_ref, select_ref, *rest):
    got, (iterate_ref, part_ref, base_ref, halo_ref, sub_ref, high_ref, low_ref) = rest[:count], rest[count:]
    own = state_ref.shape[0]
    fill_halo(halo_ref, got)
    step = 256
    for i in range(0, own, step):
        here = slice(i, i + step)
        value = state_ref[here, :] + mm(inverse_halo_ref[here, :], halo_ref[...])
        iterate_ref[here, :] = value
        sub_ref[here, :] = value.astype(BF)
    sub_ref[own:, :] = jnp.zeros((sub_ref.shape[0] - own, sub_ref.shape[1]), BF)
    rows, links, size, _ = blocks_ref.shape
    for j in range(rows):
        starts = [pl.multiple_of(cols_ref[j * links + k] * size, size) for k in range(links)]
        values = jnp.concatenate([blocks_ref[j, k] for k in range(links)], axis=1)
        coupled = jnp.concatenate([sub_ref[pl.ds(start, size), :] for start in starts], axis=0)
        total = mm(values, coupled)
        here = slice(j * size, (j + 1) * size)
        value = rhs_ref[here, :].astype(F32) - total
        part_ref[here, :] = value
        keep_split(high_ref, low_ref, here, value)
    base_ref[...] = mm(select_ref[...], high_ref[...]) + mm(select_ref[...], low_ref[...])


def residual_body(count, turn, part_ref, blocks_halo_ref, iterate_ref, inverse_ref, select_ref, *rest):
    got, (state_ref, base_ref, halo_ref, resid_ref, high_ref, low_ref) = rest[:count], rest[count:]
    own = part_ref.shape[0]
    fill_halo(halo_ref, got[turn:] + got[:turn])
    step = 256
    for i in range(0, own, step):
        here = slice(i, i + step)
        outer = mm(blocks_halo_ref[0, here, :], halo_ref[...]) + mm(blocks_halo_ref[1, here, :], halo_ref[...])
        resid_ref[here, :] = (part_ref[here, :] - outer).astype(BF)
    for i in range(0, own, step):
        here = slice(i, i + step)
        value = iterate_ref[here, :] + mm(inverse_ref[here, :own], resid_ref[...])
        state_ref[here, :] = value
        keep_split(high_ref, low_ref, here, value)
    base_ref[...] = mm(select_ref[...], high_ref[...]) + mm(select_ref[...], low_ref[...])


def last_update_body(count, state_ref, inverse_halo_ref, *rest):
    got, rest = rest[:count], rest[count:]
    halo_ref = rest[-1]
    fill_halo(halo_ref, got)
    outs = rest[:-1]
    order_ref = outs[0] if len(outs) == 3 else None
    round_ref = outs[-2] if order_ref is not None else outs[0]
    step = 256
    own = state_ref.shape[0]
    for i in range(0, own, step):
        here = slice(i, i + step)
        value = state_ref[here, :] + mm(inverse_halo_ref[here, :], halo_ref[...])
        round_ref[here, :] = value.astype(BF)
    if order_ref is not None:
        wire_ref = outs[-1]
        turned = round_ref[...].T
        for i in range(0, own, step):
            wire_ref[:, i:i + step] = mm(turned, order_ref[:, i:i + step]).astype(BF)


def one_hot(rows_of, shape):
    return (iota(shape, 0) == rows_of(iota((1, shape[1]), 1))).astype(F32).astype(BF)


def order_body(order_ref):
    own = order_ref.shape[0]
    tile = own // ZL
    order_ref[...] = one_hot(lambda k: lax.rem(k, ZL) * tile + lax.div(k, ZL), (own, own))


def tables_body(wide, narrow, cov_plane_ref, cov_vert_ref, plane_ref, spread_ref, vert_ref):
    plane = plane_ref.shape[0]
    tile = plane // wide
    turn = one_hot(lambda k: lax.rem(k, wide) * tile + lax.div(k, wide), (plane, plane))
    half = mm(cov_plane_ref[...], turn).astype(BF)
    plane_ref[...] = mm(half.T, turn).astype(BF).T
    share = LANES // ZL
    depth = narrow * ZL
    width = narrow * LANES

    def source(k):
        e, n, l = lax.div(k, depth), lax.rem(lax.div(k, ZL), narrow), lax.rem(k, ZL)
        return n * LANES + e * ZL + l

    spread = one_hot(source, (width, width))
    spread_ref[...] = spread
    turned = cov_vert_ref[...].astype(F32).T
    zero = jnp.zeros_like(turned)
    blocks = jnp.concatenate(
        [jnp.concatenate([turned if i == e else zero for i in range(share)], axis=1) for e in range(share)],
        axis=0,
    ).astype(BF)
    vert_ref[...] = mm_t(blocks, spread).astype(BF)


def mix_body(wide, narrow, group, in_ref, plane_ref, spread_ref, vert_ref, round_ref, *rest):
    out_ref, adjoint_hbm, cells_ref, flat_ref, wire_ref, sem = rest
    keep = pltpu.make_async_copy(round_ref, adjoint_hbm, sem)
    keep.start()
    own = in_ref.shape[1]
    tile = own // ZL
    share = LANES // ZL
    depth = narrow * ZL
    block = narrow * group
    taken = in_ref[...].astype(F32).reshape(wide, narrow, group, own)
    slabs = [taken[:, n].reshape(wide * group, own).astype(BF) for n in range(narrow)]
    for g in range(tile // share):
        lanes = slice(g * LANES, (g + 1) * LANES)
        joined = jnp.concatenate([s[:, lanes] for s in slabs], axis=1)
        spread = mm(joined, spread_ref[...])
        for e in range(share):
            cells_ref[g * share + e] = spread[:, e * depth:(e + 1) * depth]
    for r in range(group):
        for c in range(tile):
            flat_ref[c * wide:(c + 1) * wide, r * depth:(r + 1) * depth] = cells_ref[
                c, pl.ds(r, wide, stride=group), :
            ].astype(BF)
    planar = mm(plane_ref[...], flat_ref[...]).astype(BF)
    for g in range(tile // share):
        stacked = jnp.concatenate(
            [
                jnp.concatenate(
                    [
                        planar[c * wide:(c + 1) * wide, r * depth:(r + 1) * depth]
                        for c in range(g * share, (g + 1) * share)
                    ],
                    axis=1,
                )
                for r in range(group)
            ],
            axis=0,
        )
        mixed = mm(stacked, vert_ref[...])
        for r in range(group):
            for n in range(narrow):
                wire_ref[g, pl.ds(n * group + r, wide, stride=block), :] = mixed[
                    r * wide:(r + 1) * wide, n * LANES:(n + 1) * LANES
                ]
        out_ref[:, g * LANES:(g + 1) * LANES] = wire_ref[g].astype(BF)
    keep.wait()


def unwire_body(in_ref, order_ref, out_hbm, out_ref, sems):
    step = 256
    copies = []
    for n, i in enumerate(range(0, out_ref.shape[0], step)):
        here = pl.ds(i, step)
        out_ref[here, :] = mm_t(order_ref[here, :], in_ref[...]).astype(BF)
        copy = pltpu.make_async_copy(out_ref.at[here], out_hbm.at[here], sems.at[n])
        copy.start()
        copies.append(copy)
    for copy in copies:
        copy.wait()


def column_tables(own, cov_plane, cov_vert):
    wide, narrow = lax.axis_size("wide"), lax.axis_size("narrow")
    width = narrow * LANES
    plane = cov_plane.shape[0]
    shape = jax.ShapeDtypeStruct
    order = call(order_body, [shape((own, own), BF)], [])
    rest = call(
        functools.partial(tables_body, wide, narrow),
        [shape((plane, plane), BF), shape((width, width), BF), shape((width, width), BF)],
        [cov_plane, cov_vert],
    )
    return [tuple(order), tuple(rest)]


def smooth_by_columns(rounded, wire, tables):
    wide, narrow = lax.axis_size("wide"), lax.axis_size("narrow")
    own, columns = rounded.shape
    devices = wide * narrow
    group = columns // devices
    depth = narrow * ZL
    tile = own // ZL
    shape = jax.ShapeDtypeStruct
    (order,), (plane_mix, spread, vert_mix) = tables
    there = lax.all_to_all(
        wire.reshape(devices, group, own), ("wide", "narrow"), split_axis=0, concat_axis=0, tiled=True
    )
    mixed, adjoint = call(
        functools.partial(mix_body, wide, narrow, group),
        [shape((columns, own), BF), shape((own, columns), BF)],
        [there.reshape(columns, own), plane_mix, spread, vert_mix, rounded],
        [
            pltpu.VMEM((tile, wide * group, depth), F32),
            pltpu.VMEM((plane_mix.shape[0], group * depth), BF),
            pltpu.VMEM((own // LANES, columns, LANES), F32),
            pltpu.SemaphoreType.DMA,
        ],
        out_specs=[VM, ANY],
    )
    back = lax.all_to_all(
        mixed.reshape(devices, group, own), ("wide", "narrow"), split_axis=0, concat_axis=0, tiled=True
    )
    (smoothed,) = call(
        unwire_body,
        [shape((own, columns), BF)],
        [back.reshape(columns, own), order],
        [pltpu.VMEM((own, columns), BF), pltpu.SemaphoreType.DMA((own // 256,))],
        out_specs=[ANY],
    )
    return adjoint, smoothed


def smooth_by_layers(adjoint, cov_plane, cov_vert):
    own, columns = adjoint.shape
    layered = adjoint.reshape(ZL, own // ZL, -1)
    planar = jnp.einsum(
        "pq,lqr->lpr",
        cov_plane,
        lax.all_to_all(layered, "wide", split_axis=0, concat_axis=1, tiled=True),
        preferred_element_type=F32,
    ).astype(BF)
    restored = lax.all_to_all(planar, "wide", split_axis=1, concat_axis=0, tiled=True)
    slab_weights = lax.dynamic_slice_in_dim(cov_vert, lax.axis_index("narrow") * ZL, ZL, 0)
    summed = jnp.dot(
        slab_weights,
        lax.all_gather(restored.reshape(ZL, -1), "narrow", axis=0, tiled=True),
        preferred_element_type=F32,
    )
    return summed.astype(BF).reshape(own, -1)


def shards(adjoint_rhs, inverse_rows, blocks, block_cols, send_rows, cov_plane, cov_vert):
    rhs = adjoint_rhs[0, 0]
    inverse = inverse_rows[0, 0]
    block_values = blocks[0, 0]
    cols = block_cols[0, 0].reshape(-1)
    send_index = send_rows[0, 0]
    own, columns = rhs.shape
    width = send_index.shape[1]
    halo = 4 * width
    wide, narrow = lax.axis_size("wide"), lax.axis_size("narrow")
    group = columns // (wide * narrow)
    by_columns = columns % (wide * narrow) == 0 and group % 8 == 0 and narrow * ZL == LANES and wide % 16 == 0
    found = matchings()
    count = len(found)
    sent = count * width
    index, counts = [lax.axis_index("wide"), lax.axis_index("narrow")], [wide, narrow]
    above = [index[place] % 2 == parity for place, parity, _ in found]
    paired = [
        jnp.where(up, index[place] + 1 < counts[place], index[place] > 0) for up, (place, _, _) in zip(above, found)
    ]
    flags = jnp.stack(above + paired).astype(jnp.int32)
    shape = jax.ShapeDtypeStruct
    notes = [shape((width, columns), BF)] * count
    full = shape((own, columns), F32)
    base_shape = shape((sent, columns), F32)
    halo_space = pltpu.VMEM((halo, columns), BF)
    cell_space = pltpu.VMEM((own, columns), BF)
    (select,) = call(
        functools.partial(select_body, found, own),
        [shape((sent, own), BF)],
        [flags, send_index],
        specs=[SM, VM],
        flops=SELECT_FLOPS,
    )
    messages = call(pick_body, notes, [select, rhs], flops=SELECT_FLOPS)
    got = swap(messages, found)
    inverse_halo, blocks_halo, inverse_sent, blocks_sent, state, base = call(
        functools.partial(setup_body, found, width),
        [
            shape((own, halo), BF),
            shape((2, own, halo), BF),
            shape((sent, halo), BF),
            shape((2, sent, halo), BF),
            full,
            base_shape,
        ],
        [flags, cols, inverse, block_values, rhs, select],
        [
            pltpu.VMEM((own, halo), F32),
            cell_space,
            cell_space,
        ],
        [SM, SM, VM, VM, VM, VM],
        limit=12,
    )
    tables = column_tables(own, cov_plane, cov_vert) if by_columns else []
    for sweep in range(SWEEPS - 1):
        messages = call(
            functools.partial(sent_update_body, count), notes, [base, inverse_sent, *got], [halo_space], limit=4
        )
        arrived, got = got, swap(messages, found)
        iterate, part, base = call(
            functools.partial(update_body, count),
            [full, full, base_shape],
            [cols, state, inverse_halo, block_values, rhs, select, *arrived],
            [halo_space, pltpu.VMEM((own + halo, columns), BF), cell_space, cell_space],
            [SM] + [VM] * (5 + count),
        )
        turn = 1 if sweep == 1 and count == 3 else 0
        arrived = got[count - turn:] + got[:count - turn]
        messages = call(
            functools.partial(sent_residual_body, count, turn),
            notes,
            [base, blocks_sent, *arrived],
            [halo_space],
            limit=4,
        )
        got = swap(messages, found)
        if tables and sweep != 1:
            tables[sweep // 2], part = lax.optimization_barrier((tables[sweep // 2], part))
        state, base = call(
            functools.partial(residual_body, count, turn),
            [full, base_shape],
            [part, blocks_halo, iterate, inverse, select, *arrived],
            [halo_space, cell_space, cell_space, cell_space],
        )
    cells = shape((own, columns), BF)
    last = functools.partial(last_update_body, count)
    if by_columns:
        rounded, wire = call(
            last, [cells, shape((columns, own), BF)], [state, inverse_halo, *got, tables[0][0]], [halo_space]
        )
        adjoint, smoothed = smooth_by_columns(rounded, wire, tables)
    else:
        (adjoint,) = call(last, [cells], [state, inverse_halo, *got], [halo_space])
        smoothed = smooth_by_layers(adjoint, cov_plane, cov_vert)
    return (adjoint[None, None], smoothed[None, None])


def solution(mesh):
    in_specs = (
        P("wide", "narrow", None, None),
        P("wide", "narrow", None, None),
        P("wide", "narrow", None, None, None, None),
        P("wide", "narrow", None, None),
        P("wide", "narrow", None, None),
        P(),
        P(),
    )
    out_specs = (P("wide", "narrow", None, None), P("wide", "narrow", None, None))
    return jax.shard_map(shards, mesh=mesh, in_specs=in_specs, out_specs=out_specs, check_vma=False)
```

```python
import functools

import jax
import jax.numpy as jnp
from jax import lax
from jax.experimental import pallas as pl
from jax.experimental.pallas import tpu as pltpu
from jax.sharding import PartitionSpec as P

ZL = 64
SWEEPS = 4
LANES = 128
SELECT_FLOPS = 2 * 10 ** 9
BF = jnp.bfloat16
F32 = jnp.float32
VM = pl.BlockSpec(memory_space=pltpu.VMEM)
SM = pl.BlockSpec(memory_space=pltpu.SMEM)
ANY = pl.BlockSpec(memory_space=pl.ANY)


def wide_slot(w, n, parity):
    return (w & 1) ^ parity ^ 1


def narrow_slot(w, n, parity):
    return 2 + ((n & 1) ^ parity ^ 1)


def mixed_slot(w, n, kind):
    turn = (w ^ (w >> 1) ^ kind) & 1
    return (1 - turn) * wide_slot(w, n, 1) + turn * narrow_slot(w, n, 0)


def has_partner(w, n, slot, wide, narrow):
    inside = [w > 0, w + 1 < wide, n > 0, n + 1 < narrow]
    return sum((slot == k) * inside[k] for k in range(4))


def matchings():
    wide, narrow = lax.axis_size("wide"), lax.axis_size("narrow")
    if narrow == 2 and wide % 4 == 0:
        rules = [(mixed_slot, 0), (mixed_slot, 1), (wide_slot, 0)]
    else:
        rules = [(wide_slot, 1)] * (wide > 2) + [(narrow_slot, 1)] * (narrow > 2)
        rules += [(narrow_slot, 0)] * (narrow > 1) + [(wide_slot, 0)] * (wide > 1)
    found = []
    for rule, kind in rules:
        pairs = []
        for w in range(wide):
            for n in range(narrow):
                slot = rule(w, n, kind)
                if has_partner(w, n, slot, wide, narrow):
                    step = ((-1, 0), (1, 0), (0, -1), (0, 1))[slot]
                    target = (w + step[0], n + step[1])
                elif slot < 2:
                    target = (w, n ^ 1 if n ^ 1 < narrow else n)
                else:
                    target = (w ^ 1 if w ^ 1 < wide else w, n)
                pairs.append((w * narrow + n, target[0] * narrow + target[1]))
        found.append((rule, kind, tuple(pairs)))
    return found


def swap(messages, found):
    return [lax.ppermute(m, ("wide", "narrow"), list(f[-1])) for m, f in zip(messages, found)]


def mm(a, b):
    return jnp.dot(a, b, preferred_element_type=F32)


def mm_t(a, b):
    return lax.dot_general(a, b, (((1,), (1,)), ((), ())), preferred_element_type=F32)


def iota(shape, dim):
    return lax.broadcasted_iota(jnp.int32, shape, dim)


def call(body, outs, args, scratch=(), specs=None, flops=0, limit=8, out_specs=None):
    size = sum(a.size * a.dtype.itemsize for a in args)
    return pl.pallas_call(
        body,
        out_shape=outs,
        in_specs=specs or [VM] * len(args),
        out_specs=out_specs or [VM] * len(outs),
        scratch_shapes=list(scratch),
        compiler_params=pltpu.CompilerParams(vmem_limit_bytes=limit * 1024 * 1024),
        cost_estimate=pl.CostEstimate(flops=flops, bytes_accessed=size, transcendentals=0),
    )(*args)


def fill_halo(halo_ref, got):
    width = got[0].shape[0]
    for m, piece in enumerate(got):
        halo_ref[m * width:(m + 1) * width, :] = piece[...]
    filled = len(got) * width
    if filled < halo_ref.shape[0]:
        halo_ref[filled:, :] = jnp.zeros((halo_ref.shape[0] - filled, halo_ref.shape[1]), halo_ref.dtype)


def send(messages, values):
    width = messages[0].shape[0]
    for m, message in enumerate(messages):
        message[...] = values[m * width:(m + 1) * width, :].astype(BF)


def keep_split(high_ref, low_ref, rows, value):
    high = value.astype(BF)
    high_ref[rows, :] = high
    low_ref[rows, :] = (value - high.astype(F32)).astype(BF)


def select_body(count, own, flags_ref, send_ref, select_ref):
    width = send_ref.shape[1]
    diagonal = iota((width, width), 0) == iota((width, width), 1)
    pieces = []
    for m in range(count):
        rows = send_ref[pl.ds(flags_ref[m], 1), :]
        rows = jnp.where(flags_ref[count + m] == 1, rows, -1).astype(F32)
        pieces.append(jnp.where(diagonal, rows, 0.0))
    column = jnp.sum(jnp.concatenate(pieces, axis=0), axis=1, keepdims=True).astype(jnp.int32)
    select_ref[...] = (iota((count * width, own), 1) == column).astype(F32).astype(BF)


def pick_body(select_ref, rhs_ref, *messages):
    send(messages, mm(select_ref[...], rhs_ref[...]))


def setup_body(count, width, flags_ref, cols_ref, inverse_ref, blocks_ref, rhs_ref, select_ref, *rest):
    inverse_halo_ref, blocks_halo_ref, inverse_sent_ref, blocks_sent_ref, state_ref, base_ref = rest[:6]
    sum_ref, high_ref, low_ref = rest[6:]
    own = rhs_ref.shape[0]
    halo = 4 * width
    places = iota((1, halo), 1)
    starts = jnp.full((1, halo), -halo, jnp.int32)
    for m in range(count):
        here = lax.div(places, width) == m
        starts = jnp.where(here, flags_ref[m] * width + lax.rem(places, width), starts)
    arrange = (iota((halo, halo), 0) == starts).astype(F32).astype(BF)
    rows, links, size, _ = blocks_ref.shape
    sum_ref[...] = jnp.zeros(sum_ref.shape, F32)
    for j in range(rows):
        for k in range(links):
            column = cols_ref[j * links + k]

            @pl.when(column * size >= own)
            def _():
                lanes = pl.ds(pl.multiple_of(column * size - own, size), size)
                here = slice(j * size, (j + 1) * size)
                sum_ref[here, lanes] = sum_ref[here, lanes] + blocks_ref[j, k].astype(F32)

    step = 256
    for i in range(0, own, step):
        here = slice(i, i + step)
        inverse_halo_ref[here, :] = mm(inverse_ref[here, own:], arrange).astype(BF)
        total = sum_ref[here, :]
        high = total.astype(BF)
        low = (total - high.astype(F32)).astype(BF)
        blocks_halo_ref[0, here, :] = mm(high, arrange).astype(BF)
        blocks_halo_ref[1, here, :] = mm(low, arrange).astype(BF)
        value = mm(inverse_ref[here, :own], rhs_ref[...])
        state_ref[here, :] = value
        keep_split(high_ref, low_ref, here, value)
    inverse_sent_ref[...] = mm(select_ref[...], inverse_halo_ref[...]).astype(BF)
    for part in range(2):
        blocks_sent_ref[part] = mm(select_ref[...], blocks_halo_ref[part]).astype(BF)
    base_ref[...] = mm(select_ref[...], high_ref[...]) + mm(select_ref[...], low_ref[...])


def sent_update_body(count, base_ref, sent_ref, *rest):
    got, messages, halo_ref = rest[:count], rest[count:-1], rest[-1]
    fill_halo(halo_ref, got)
    send(messages, base_ref[...] + mm(sent_ref[...], halo_ref[...]))


def sent_residual_body(count, turn, base_ref, sent_ref, *rest):
    got, messages, halo_ref = rest[:count], rest[count:-1], rest[-1]
    fill_halo(halo_ref, got[turn:] + got[:turn])
    part = mm(sent_ref[0], halo_ref[...]) + mm(sent_ref[1], halo_ref[...])
    send(messages, base_ref[...] - part)


def update_body(count, cols_ref, state_ref, inverse_halo_ref, blocks_ref, rhs_ref, select_ref, *rest):
    got, (iterate_ref, part_ref, base_ref, halo_ref, sub_ref, high_ref, low_ref) = rest[:count], rest[count:]
    own = state_ref.shape[0]
    fill_halo(halo_ref, got)
    step = 256
    for i in range(0, own, step):
        here = slice(i, i + step)
        value = state_ref[here, :] + mm(inverse_halo_ref[here, :], halo_ref[...])
        iterate_ref[here, :] = value
        sub_ref[here, :] = value.astype(BF)
    sub_ref[own:, :] = jnp.zeros((sub_ref.shape[0] - own, sub_ref.shape[1]), BF)
    rows, links, size, _ = blocks_ref.shape
    for j in range(rows):
        starts = [pl.multiple_of(cols_ref[j * links + k] * size, size) for k in range(links)]
        values = jnp.concatenate([blocks_ref[j, k] for k in range(links)], axis=1)
        coupled = jnp.concatenate([sub_ref[pl.ds(start, size), :] for start in starts], axis=0)
        total = mm(values, coupled)
        here = slice(j * size, (j + 1) * size)
        value = rhs_ref[here, :].astype(F32) - total
        part_ref[here, :] = value
        keep_split(high_ref, low_ref, here, value)
    base_ref[...] = mm(select_ref[...], high_ref[...]) + mm(select_ref[...], low_ref[...])


def residual_body(count, turn, part_ref, blocks_halo_ref, iterate_ref, inverse_ref, select_ref, *rest):
    got, rest = rest[:count], list(rest[count:])
    state_ref = rest.pop(0)
    halo_ref, resid_ref, *split = rest[-4:] if len(rest) == 5 else rest
    own = part_ref.shape[0]
    fill_halo(halo_ref, got[turn:] + got[:turn])
    step = 256
    for i in range(0, own, step):
        here = slice(i, i + step)
        outer = mm(blocks_halo_ref[0, here, :], halo_ref[...]) + mm(blocks_halo_ref[1, here, :], halo_ref[...])
        resid_ref[here, :] = (part_ref[here, :] - outer).astype(BF)
    for i in range(0, own, step):
        here = slice(i, i + step)
        value = iterate_ref[here, :] + mm(inverse_ref[here, :own], resid_ref[...])
        state_ref[here, :] = value
        if split:
            keep_split(*split, here, value)
    if split:
        rest[0][...] = mm(select_ref[...], split[0][...]) + mm(select_ref[...], split[1][...])


def last_update_body(count, state_ref, inverse_halo_ref, *rest):
    got, rest = rest[:count], rest[count:]
    halo_ref = rest[-1]
    fill_halo(halo_ref, got)
    outs = rest[:-1]
    order_ref = outs[0] if len(outs) == 3 else None
    round_ref = outs[-2] if order_ref is not None else outs[0]
    step = 256
    own = state_ref.shape[0]
    for i in range(0, own, step):
        here = slice(i, i + step)
        value = state_ref[here, :] + mm(inverse_halo_ref[here, :], halo_ref[...])
        round_ref[here, :] = value.astype(BF)
    if order_ref is not None:
        wire_ref = outs[-1]
        turned = round_ref[...].T
        for i in range(0, own, step):
            wire_ref[:, i:i + step] = mm(turned, order_ref[:, i:i + step]).astype(BF)


def one_hot(rows_of, shape):
    return (iota(shape, 0) == rows_of(iota((1, shape[1]), 1))).astype(F32).astype(BF)


def order_body(order_ref):
    own = order_ref.shape[0]
    tile = own // ZL
    order_ref[...] = one_hot(lambda k: lax.rem(k, ZL) * tile + lax.div(k, ZL), (own, own))


def tables_body(wide, narrow, cov_plane_ref, cov_vert_ref, plane_ref, spread_ref, vert_ref):
    plane = plane_ref.shape[0]
    tile = plane // wide
    turn = one_hot(lambda k: lax.rem(k, wide) * tile + lax.div(k, wide), (plane, plane))
    half = mm(cov_plane_ref[...], turn).astype(BF)
    plane_ref[...] = mm(half.T, turn).astype(BF).T
    share = LANES // ZL
    depth = narrow * ZL
    width = narrow * LANES

    def source(k):
        e, n, l = lax.div(k, depth), lax.rem(lax.div(k, ZL), narrow), lax.rem(k, ZL)
        return n * LANES + e * ZL + l

    spread = one_hot(source, (width, width))
    spread_ref[...] = spread
    turned = cov_vert_ref[...].astype(F32).T
    zero = jnp.zeros_like(turned)
    blocks = jnp.concatenate(
        [jnp.concatenate([turned if i == e else zero for i in range(share)], axis=1) for e in range(share)],
        axis=0,
    ).astype(BF)
    vert_ref[...] = mm_t(blocks, spread).astype(BF)


def mix_body(wide, narrow, group, in_ref, plane_ref, spread_ref, vert_ref, round_ref, *rest):
    out_ref, adjoint_hbm, cells_ref, flat_ref, wire_ref, sem = rest
    keep = pltpu.make_async_copy(round_ref, adjoint_hbm, sem)
    keep.start()
    own = in_ref.shape[1]
    tile = own // ZL
    share = LANES // ZL
    depth = narrow * ZL
    block = narrow * group
    taken = in_ref[...].astype(F32).reshape(wide, narrow, group, own)
    slabs = [taken[:, n].reshape(wide * group, own).astype(BF) for n in range(narrow)]
    for g in range(tile // share):
        lanes = slice(g * LANES, (g + 1) * LANES)
        joined = jnp.concatenate([s[:, lanes] for s in slabs], axis=1)
        spread = mm(joined, spread_ref[...])
        for e in range(share):
            cells_ref[g * share + e] = spread[:, e * depth:(e + 1) * depth]
    for r in range(group):
        for c in range(tile):
            flat_ref[c * wide:(c + 1) * wide, r * depth:(r + 1) * depth] = cells_ref[
                c, pl.ds(r, wide, stride=group), :
            ].astype(BF)
    planar = mm(plane_ref[...], flat_ref[...]).astype(BF)
    for g in range(tile // share):
        stacked = jnp.concatenate(
            [
                jnp.concatenate(
                    [
                        planar[c * wide:(c + 1) * wide, r * depth:(r + 1) * depth]
                        for c in range(g * share, (g + 1) * share)
                    ],
                    axis=1,
                )
                for r in range(group)
            ],
            axis=0,
        )
        mixed = mm(stacked, vert_ref[...])
        for r in range(group):
            for n in range(narrow):
                wire_ref[g, pl.ds(n * group + r, wide, stride=block), :] = mixed[
                    r * wide:(r + 1) * wide, n * LANES:(n + 1) * LANES
                ]
        out_ref[:, g * LANES:(g + 1) * LANES] = wire_ref[g].astype(BF)
    keep.wait()


def unwire_body(in_ref, order_ref, out_hbm, out_ref, sems):
    step = 256
    copies = []
    for n, i in enumerate(range(0, out_ref.shape[0], step)):
        here = pl.ds(i, step)
        out_ref[here, :] = mm_t(order_ref[here, :], in_ref[...]).astype(BF)
        copy = pltpu.make_async_copy(out_ref.at[here], out_hbm.at[here], sems.at[n])
        copy.start()
        copies.append(copy)
    for copy in copies:
        copy.wait()


def column_tables(own, cov_plane, cov_vert):
    wide, narrow = lax.axis_size("wide"), lax.axis_size("narrow")
    width = narrow * LANES
    plane = cov_plane.shape[0]
    shape = jax.ShapeDtypeStruct
    order = call(order_body, [shape((own, own), BF)], [])
    rest = call(
        functools.partial(tables_body, wide, narrow),
        [shape((plane, plane), BF), shape((width, width), BF), shape((width, width), BF)],
        [cov_plane, cov_vert],
    )
    return [tuple(order), tuple(rest)]


def smooth_by_columns(rounded, wire, tables):
    wide, narrow = lax.axis_size("wide"), lax.axis_size("narrow")
    own, columns = rounded.shape
    devices = wide * narrow
    group = columns // devices
    depth = narrow * ZL
    tile = own // ZL
    shape = jax.ShapeDtypeStruct
    (order,), (plane_mix, spread, vert_mix) = tables
    there = lax.all_to_all(
        wire.reshape(devices, group, own), ("wide", "narrow"), split_axis=0, concat_axis=0, tiled=True
    )
    mixed, adjoint = call(
        functools.partial(mix_body, wide, narrow, group),
        [shape((columns, own), BF), shape((own, columns), BF)],
        [there.reshape(columns, own), plane_mix, spread, vert_mix, rounded],
        [
            pltpu.VMEM((tile, wide * group, depth), F32),
            pltpu.VMEM((plane_mix.shape[0], group * depth), BF),
            pltpu.VMEM((own // LANES, columns, LANES), F32),
            pltpu.SemaphoreType.DMA,
        ],
        out_specs=[VM, ANY],
    )
    back = lax.all_to_all(
        mixed.reshape(devices, group, own), ("wide", "narrow"), split_axis=0, concat_axis=0, tiled=True
    )
    (smoothed,) = call(
        unwire_body,
        [shape((own, columns), BF)],
        [back.reshape(columns, own), order],
        [pltpu.VMEM((own, columns), BF), pltpu.SemaphoreType.DMA((own // 256,))],
        out_specs=[ANY],
    )
    return adjoint, smoothed


def smooth_by_layers(adjoint, cov_plane, cov_vert):
    own, columns = adjoint.shape
    layered = adjoint.reshape(ZL, own // ZL, -1)
    planar = jnp.einsum(
        "pq,lqr->lpr",
        cov_plane,
        lax.all_to_all(layered, "wide", split_axis=0, concat_axis=1, tiled=True),
        preferred_element_type=F32,
    ).astype(BF)
    restored = lax.all_to_all(planar, "wide", split_axis=1, concat_axis=0, tiled=True)
    slab_weights = lax.dynamic_slice_in_dim(cov_vert, lax.axis_index("narrow") * ZL, ZL, 0)
    summed = jnp.dot(
        slab_weights,
        lax.all_gather(restored.reshape(ZL, -1), "narrow", axis=0, tiled=True),
        preferred_element_type=F32,
    )
    return summed.astype(BF).reshape(own, -1)


def shards(adjoint_rhs, inverse_rows, blocks, block_cols, send_rows, cov_plane, cov_vert):
    rhs = adjoint_rhs[0, 0]
    inverse = inverse_rows[0, 0]
    block_values = blocks[0, 0]
    cols = block_cols[0, 0].reshape(-1)
    send_index = send_rows[0, 0]
    own, columns = rhs.shape
    width = send_index.shape[1]
    halo = 4 * width
    wide, narrow = lax.axis_size("wide"), lax.axis_size("narrow")
    group = columns // (wide * narrow)
    by_columns = columns % (wide * narrow) == 0 and group % 8 == 0 and narrow * ZL == LANES and wide % 16 == 0
    found = matchings()
    count = len(found)
    sent = count * width
    w, n = lax.axis_index("wide"), lax.axis_index("narrow")
    slots = [rule(w, n, kind) for rule, kind, _ in found]
    flags = jnp.stack(slots + [has_partner(w, n, slot, wide, narrow) for slot in slots]).astype(jnp.int32)
    shape = jax.ShapeDtypeStruct
    notes = [shape((width, columns), BF)] * count
    full = shape((own, columns), F32)
    base_shape = shape((sent, columns), F32)
    halo_space = pltpu.VMEM((halo, columns), BF)
    cell_space = pltpu.VMEM((own, columns), BF)
    (select,) = call(
        functools.partial(select_body, count, own),
        [shape((sent, own), BF)],
        [flags, send_index],
        specs=[SM, VM],
        flops=SELECT_FLOPS,
    )
    messages = call(pick_body, notes, [select, rhs], flops=SELECT_FLOPS)
    got = swap(messages, found)
    inverse_halo, blocks_halo, inverse_sent, blocks_sent, state, base = call(
        functools.partial(setup_body, count, width),
        [
            shape((own, halo), BF),
            shape((2, own, halo), BF),
            shape((sent, halo), BF),
            shape((2, sent, halo), BF),
            full,
            base_shape,
        ],
        [flags, cols, inverse, block_values, rhs, select],
        [
            pltpu.VMEM((own, halo), F32),
            cell_space,
            cell_space,
        ],
        [SM, SM, VM, VM, VM, VM],
        limit=12,
    )
    tables = column_tables(own, cov_plane, cov_vert) if by_columns else []
    for sweep in range(SWEEPS - 1):
        messages = call(
            functools.partial(sent_update_body, count), notes, [base, inverse_sent, *got], [halo_space], limit=4
        )
        arrived, got = got, swap(messages, found)
        iterate, part, base = call(
            functools.partial(update_body, count),
            [full, full, base_shape],
            [cols, state, inverse_halo, block_values, rhs, select, *arrived],
            [halo_space, pltpu.VMEM((own + halo, columns), BF), cell_space, cell_space],
            [SM] + [VM] * (5 + count),
        )
        turn = 1 if sweep == 1 and count == 3 else 0
        arrived = got[count - turn:] + got[:count - turn]
        messages = call(
            functools.partial(sent_residual_body, count, turn),
            notes,
            [base, blocks_sent, *arrived],
            [halo_space],
            limit=4,
        )
        got = swap(messages, found)
        if sweep < len(tables):
            tables[sweep], part = lax.optimization_barrier((tables[sweep], part))
        more = sweep < SWEEPS - 2
        state, *bases = call(
            functools.partial(residual_body, count, turn),
            [full] + [base_shape] * more,
            [part, blocks_halo, iterate, inverse, select, *arrived],
            [halo_space, cell_space] + [cell_space] * (2 * more),
        )
        base = bases[0] if more else None
    cells = shape((own, columns), BF)
    last = functools.partial(last_update_body, count)
    if by_columns:
        rounded, wire = call(
            last, [cells, shape((columns, own), BF)], [state, inverse_halo, *got, tables[0][0]], [halo_space]
        )
        adjoint, smoothed = smooth_by_columns(rounded, wire, tables)
    else:
        (adjoint,) = call(last, [cells], [state, inverse_halo, *got], [halo_space])
        smoothed = smooth_by_layers(adjoint, cov_plane, cov_vert)
    return (adjoint[None, None], smoothed[None, None])


def solution(mesh):
    in_specs = (
        P("wide", "narrow", None, None),
        P("wide", "narrow", None, None),
        P("wide", "narrow", None, None, None, None),
        P("wide", "narrow", None, None),
        P("wide", "narrow", None, None),
        P(),
        P(),
    )
    out_specs = (P("wide", "narrow", None, None), P("wide", "narrow", None, None))
    return jax.shard_map(shards, mesh=mesh, in_specs=in_specs, out_specs=out_specs, check_vma=False)
```

```python
import functools

import jax
import jax.numpy as jnp
from jax import lax
from jax.experimental import pallas as pl
from jax.experimental.pallas import tpu as pltpu
from jax.sharding import PartitionSpec as P

ZL = 64
SWEEPS = 4
LANES = 128
SELECT_FLOPS = 6 * 10 ** 8
PICK_FLOPS = 2 * 10 ** 9
BF = jnp.bfloat16
F32 = jnp.float32
VM = pl.BlockSpec(memory_space=pltpu.VMEM)
ANY = pl.BlockSpec(memory_space=pl.ANY)


def wide_slot(w, n, parity):
    return (w & 1) ^ parity ^ 1


def narrow_slot(w, n, parity):
    return 2 + ((n & 1) ^ parity ^ 1)


def mixed_slot(w, n, kind):
    turn = (w ^ (w >> 1) ^ kind) & 1
    return (1 - turn) * wide_slot(w, n, 1) + turn * narrow_slot(w, n, 0)


def has_partner(w, n, slot, wide, narrow):
    inside = [w > 0, w + 1 < wide, n > 0, n + 1 < narrow]
    return sum((slot == k) * inside[k] for k in range(4))


def matchings():
    wide, narrow = lax.axis_size("wide"), lax.axis_size("narrow")
    if narrow == 2 and wide % 4 == 0:
        rules = [(mixed_slot, 0), (mixed_slot, 1), (wide_slot, 0)]
    else:
        rules = [(wide_slot, 1)] * (wide > 2) + [(narrow_slot, 1)] * (narrow > 2)
        rules += [(narrow_slot, 0)] * (narrow > 1) + [(wide_slot, 0)] * (wide > 1)
    found = []
    for rule, kind in rules:
        pairs = []
        for w in range(wide):
            for n in range(narrow):
                slot = rule(w, n, kind)
                if has_partner(w, n, slot, wide, narrow):
                    step = ((-1, 0), (1, 0), (0, -1), (0, 1))[slot]
                    target = (w + step[0], n + step[1])
                elif slot < 2:
                    target = (w, n ^ 1 if n ^ 1 < narrow else n)
                else:
                    target = (w ^ 1 if w ^ 1 < wide else w, n)
                pairs.append((w * narrow + n, target[0] * narrow + target[1]))
        found.append((rule, kind, tuple(pairs)))
    return found


def own_slots(found):
    w, n = lax.axis_index("wide"), lax.axis_index("narrow")
    wide, narrow = lax.axis_size("wide"), lax.axis_size("narrow")
    slots = [rule(w, n, kind) for rule, kind, _ in found]
    return [(slot, has_partner(w, n, slot, wide, narrow) == 1) for slot in slots]


def swap(messages, found):
    return [lax.ppermute(m, ("wide", "narrow"), list(f[-1])) for m, f in zip(messages, found)]


def mm(a, b):
    return jnp.dot(a, b, preferred_element_type=F32)


def mm_t(a, b):
    return lax.dot_general(a, b, (((1,), (1,)), ((), ())), preferred_element_type=F32)


def iota(shape, dim):
    return lax.broadcasted_iota(jnp.int32, shape, dim)


def call(body, outs, args, scratch=(), specs=None, flops=0, limit=8, out_specs=None):
    size = sum(a.size * a.dtype.itemsize for a in args)
    return pl.pallas_call(
        body,
        out_shape=outs,
        in_specs=specs or [VM] * len(args),
        out_specs=out_specs or [VM] * len(outs),
        scratch_shapes=list(scratch),
        compiler_params=pltpu.CompilerParams(vmem_limit_bytes=limit * 1024 * 1024),
        cost_estimate=pl.CostEstimate(flops=flops, bytes_accessed=size, transcendentals=0),
    )(*args)


def fill_halo(halo_ref, got):
    width = got[0].shape[0]
    for m, piece in enumerate(got):
        halo_ref[m * width:(m + 1) * width, :] = piece[...]
    filled = len(got) * width
    if filled < halo_ref.shape[0]:
        halo_ref[filled:, :] = jnp.zeros((halo_ref.shape[0] - filled, halo_ref.shape[1]), halo_ref.dtype)


def send(messages, values):
    width = messages[0].shape[0]
    for m, message in enumerate(messages):
        message[...] = values[m * width:(m + 1) * width, :].astype(BF)


def keep_split(high_ref, low_ref, rows, value):
    high = value.astype(BF)
    high_ref[rows] = high
    low_ref[rows] = (value - high.astype(F32)).astype(BF)


def select_body(found, own, send_ref, select_ref):
    width = send_ref.shape[1]
    diagonal = iota((width, width), 0) == iota((width, width), 1)
    pieces = []
    for slot, paired in own_slots(found):
        rows = jnp.where(paired, send_ref[pl.ds(slot, 1), :], -1).astype(F32)
        pieces.append(jnp.where(diagonal, rows, 0.0))
    column = jnp.sum(jnp.concatenate(pieces, axis=0), axis=1, keepdims=True).astype(jnp.int32)
    select_ref[...] = (iota((len(found) * width, own), 1) == column).astype(F32).astype(BF)


def pick_body(select_ref, rhs_ref, *messages):
    send(messages, mm(select_ref[...], rhs_ref[...]))


def setup_body(found, width, cols_ref, inverse_ref, blocks_ref, rhs_ref, select_ref, *rest):
    inverse_halo_ref, blocks_halo_ref, inverse_sent_ref, blocks_sent_ref, state_ref, base_ref = rest[:6]
    high_ref, low_ref = rest[6:]
    own = rhs_ref.shape[0]
    halo = 4 * width
    places = iota((1, halo), 1)
    starts = jnp.full((1, halo), -halo, jnp.int32)
    for m, (slot, _) in enumerate(own_slots(found)):
        here = lax.div(places, width) == m
        starts = jnp.where(here, slot * width + lax.rem(places, width), starts)
    arrange = (iota((halo, halo), 0) == starts).astype(F32).astype(BF)
    rows, links, size, _ = blocks_ref.shape
    for j in range(rows):
        here = slice(j * size, (j + 1) * size)
        columns = [cols_ref[j, k] for k in range(links)]
        for c in range(halo // size):
            total = None
            for k in range(links):
                part = jnp.where(columns[k] == own // size + c, blocks_ref[j, k].astype(F32), 0.0)
                total = part if total is None else total + part
            lanes = slice(c * size, (c + 1) * size)
            keep_split(high_ref, low_ref, (here, lanes), total)
    for part, half_ref in enumerate((high_ref, low_ref)):
        blocks_halo_ref[part] = mm(half_ref[...], arrange).astype(BF)
    step = 256
    for i in range(0, own, step):
        here = slice(i, i + step)
        inverse_halo_ref[here, :] = mm(inverse_ref[here, own:], arrange).astype(BF)
        value = mm(inverse_ref[here, :own], rhs_ref[...])
        state_ref[here, :] = value
        keep_split(high_ref, low_ref, here, value)
    inverse_sent_ref[...] = mm(select_ref[...], inverse_halo_ref[...]).astype(BF)
    for part in range(2):
        blocks_sent_ref[part] = mm(select_ref[...], blocks_halo_ref[part]).astype(BF)
    base_ref[...] = mm(select_ref[...], high_ref[...]) + mm(select_ref[...], low_ref[...])


def sent_update_body(count, base_ref, sent_ref, *rest):
    got, messages, halo_ref = rest[:count], rest[count:-1], rest[-1]
    fill_halo(halo_ref, got)
    send(messages, base_ref[...] + mm(sent_ref[...], halo_ref[...]))


def sent_residual_body(count, turn, base_ref, sent_ref, *rest):
    got, messages, halo_ref = rest[:count], rest[count:-1], rest[-1]
    fill_halo(halo_ref, got[turn:] + got[:turn])
    part = mm(sent_ref[0], halo_ref[...]) + mm(sent_ref[1], halo_ref[...])
    send(messages, base_ref[...] - part)


def update_body(count, cols_ref, state_ref, inverse_halo_ref, blocks_ref, rhs_ref, select_ref, *rest):
    got, (iterate_ref, part_ref, base_ref, halo_ref, sub_ref, high_ref, low_ref) = rest[:count], rest[count:]
    own = state_ref.shape[0]
    fill_halo(halo_ref, got)
    step = 256
    for i in range(0, own, step):
        here = slice(i, i + step)
        value = state_ref[here, :] + mm(inverse_halo_ref[here, :], halo_ref[...])
        iterate_ref[here, :] = value
        sub_ref[here, :] = value.astype(BF)
    sub_ref[own:, :] = jnp.zeros((sub_ref.shape[0] - own, sub_ref.shape[1]), BF)
    rows, links, size, _ = blocks_ref.shape
    for j in range(rows):
        starts = [pl.multiple_of(cols_ref[j, k] * size, size) for k in range(links)]
        values = jnp.concatenate([blocks_ref[j, k] for k in range(links)], axis=1)
        coupled = jnp.concatenate([sub_ref[pl.ds(start, size), :] for start in starts], axis=0)
        total = mm(values, coupled)
        here = slice(j * size, (j + 1) * size)
        value = rhs_ref[here, :].astype(F32) - total
        part_ref[here, :] = value
        keep_split(high_ref, low_ref, here, value)
    base_ref[...] = mm(select_ref[...], high_ref[...]) + mm(select_ref[...], low_ref[...])


def residual_body(count, turn, part_ref, blocks_halo_ref, iterate_ref, inverse_ref, select_ref, *rest):
    got, rest = rest[:count], list(rest[count:])
    state_ref = rest.pop(0)
    halo_ref, resid_ref, *split = rest[-4:] if len(rest) == 5 else rest
    own = part_ref.shape[0]
    fill_halo(halo_ref, got[turn:] + got[:turn])
    step = 256
    for i in range(0, own, step):
        here = slice(i, i + step)
        outer = mm(blocks_halo_ref[0, here, :], halo_ref[...]) + mm(blocks_halo_ref[1, here, :], halo_ref[...])
        resid_ref[here, :] = (part_ref[here, :] - outer).astype(BF)
    for i in range(0, own, step):
        here = slice(i, i + step)
        value = iterate_ref[here, :] + mm(inverse_ref[here, :own], resid_ref[...])
        state_ref[here, :] = value
        if split:
            keep_split(*split, here, value)
    if split:
        rest[0][...] = mm(select_ref[...], split[0][...]) + mm(select_ref[...], split[1][...])


def last_update_body(count, state_ref, inverse_halo_ref, *rest):
    got, rest = rest[:count], rest[count:]
    halo_ref = rest[-1]
    fill_halo(halo_ref, got)
    outs = rest[:-1]
    order_ref = outs[0] if len(outs) == 3 else None
    round_ref = outs[-2] if order_ref is not None else outs[0]
    step = 256
    own = state_ref.shape[0]
    for i in range(0, own, step):
        here = slice(i, i + step)
        value = state_ref[here, :] + mm(inverse_halo_ref[here, :], halo_ref[...])
        round_ref[here, :] = value.astype(BF)
    if order_ref is not None:
        wire_ref = outs[-1]
        turned = round_ref[...].T
        for i in range(0, own, step):
            wire_ref[:, i:i + step] = mm(turned, order_ref[:, i:i + step]).astype(BF)


def one_hot(rows_of, shape):
    return (iota(shape, 0) == rows_of(iota((1, shape[1]), 1))).astype(F32).astype(BF)


def order_body(order_ref):
    own = order_ref.shape[0]
    tile = own // ZL
    order_ref[...] = one_hot(lambda k: lax.rem(k, ZL) * tile + lax.div(k, ZL), (own, own))


def tables_body(wide, narrow, cov_plane_ref, cov_vert_ref, plane_ref, spread_ref, vert_ref):
    plane = plane_ref.shape[0]
    tile = plane // wide
    turn = one_hot(lambda k: lax.rem(k, wide) * tile + lax.div(k, wide), (plane, plane))
    half = mm(cov_plane_ref[...], turn).astype(BF)
    plane_ref[...] = mm(half.T, turn).astype(BF).T
    share = LANES // ZL
    depth = narrow * ZL
    width = narrow * LANES

    def source(k):
        e, n, l = lax.div(k, depth), lax.rem(lax.div(k, ZL), narrow), lax.rem(k, ZL)
        return n * LANES + e * ZL + l

    spread = one_hot(source, (width, width))
    spread_ref[...] = spread
    turned = cov_vert_ref[...].astype(F32).T
    zero = jnp.zeros_like(turned)
    blocks = jnp.concatenate(
        [jnp.concatenate([turned if i == e else zero for i in range(share)], axis=1) for e in range(share)],
        axis=0,
    ).astype(BF)
    vert_ref[...] = mm_t(blocks, spread).astype(BF)


def mix_body(wide, narrow, group, in_ref, plane_ref, spread_ref, vert_ref, round_ref, *rest):
    out_ref, adjoint_hbm, cells_ref, flat_ref, wire_ref, sem = rest
    keep = pltpu.make_async_copy(round_ref, adjoint_hbm, sem)
    keep.start()
    own = in_ref.shape[1]
    tile = own // ZL
    share = LANES // ZL
    depth = narrow * ZL
    block = narrow * group
    taken = in_ref[...].astype(F32).reshape(wide, narrow, group, own)
    slabs = [taken[:, n].reshape(wide * group, own).astype(BF) for n in range(narrow)]
    for g in range(tile // share):
        lanes = slice(g * LANES, (g + 1) * LANES)
        joined = jnp.concatenate([s[:, lanes] for s in slabs], axis=1)
        spread = mm(joined, spread_ref[...])
        for e in range(share):
            cells_ref[g * share + e] = spread[:, e * depth:(e + 1) * depth]
    for r in range(group):
        for c in range(tile):
            flat_ref[c * wide:(c + 1) * wide, r * depth:(r + 1) * depth] = cells_ref[
                c, pl.ds(r, wide, stride=group), :
            ].astype(BF)
    planar = mm(plane_ref[...], flat_ref[...]).astype(BF)
    for g in range(tile // share):
        stacked = jnp.concatenate(
            [
                jnp.concatenate(
                    [
                        planar[c * wide:(c + 1) * wide, r * depth:(r + 1) * depth]
                        for c in range(g * share, (g + 1) * share)
                    ],
                    axis=1,
                )
                for r in range(group)
            ],
            axis=0,
        )
        mixed = mm(stacked, vert_ref[...])
        for r in range(group):
            for n in range(narrow):
                wire_ref[g, pl.ds(n * group + r, wide, stride=block), :] = mixed[
                    r * wide:(r + 1) * wide, n * LANES:(n + 1) * LANES
                ]
        out_ref[:, g * LANES:(g + 1) * LANES] = wire_ref[g].astype(BF)
    keep.wait()


def unwire_body(in_ref, order_ref, out_hbm, out_ref, sems):
    step = 256
    copies = []
    for n, i in enumerate(range(0, out_ref.shape[0], step)):
        here = pl.ds(i, step)
        out_ref[here, :] = mm_t(order_ref[here, :], in_ref[...]).astype(BF)
        copy = pltpu.make_async_copy(out_ref.at[here], out_hbm.at[here], sems.at[n])
        copy.start()
        copies.append(copy)
    for copy in copies:
        copy.wait()


def column_tables(own, cov_plane, cov_vert):
    wide, narrow = lax.axis_size("wide"), lax.axis_size("narrow")
    width = narrow * LANES
    plane = cov_plane.shape[0]
    shape = jax.ShapeDtypeStruct
    order = call(order_body, [shape((own, own), BF)], [])
    rest = call(
        functools.partial(tables_body, wide, narrow),
        [shape((plane, plane), BF), shape((width, width), BF), shape((width, width), BF)],
        [cov_plane, cov_vert],
    )
    return [tuple(order), tuple(rest)]


def smooth_by_columns(rounded, wire, tables):
    wide, narrow = lax.axis_size("wide"), lax.axis_size("narrow")
    own, columns = rounded.shape
    devices = wide * narrow
    group = columns // devices
    depth = narrow * ZL
    tile = own // ZL
    shape = jax.ShapeDtypeStruct
    (order,), (plane_mix, spread, vert_mix) = tables
    there = lax.all_to_all(
        wire.reshape(devices, group, own), ("wide", "narrow"), split_axis=0, concat_axis=0, tiled=True
    )
    mixed, adjoint = call(
        functools.partial(mix_body, wide, narrow, group),
        [shape((columns, own), BF), shape((own, columns), BF)],
        [there.reshape(columns, own), plane_mix, spread, vert_mix, rounded],
        [
            pltpu.VMEM((tile, wide * group, depth), F32),
            pltpu.VMEM((plane_mix.shape[0], group * depth), BF),
            pltpu.VMEM((own // LANES, columns, LANES), F32),
            pltpu.SemaphoreType.DMA,
        ],
        out_specs=[VM, ANY],
    )
    back = lax.all_to_all(
        mixed.reshape(devices, group, own), ("wide", "narrow"), split_axis=0, concat_axis=0, tiled=True
    )
    (smoothed,) = call(
        unwire_body,
        [shape((own, columns), BF)],
        [back.reshape(columns, own), order],
        [pltpu.VMEM((own, columns), BF), pltpu.SemaphoreType.DMA((own // 256,))],
        out_specs=[ANY],
    )
    return adjoint, smoothed


def smooth_by_layers(adjoint, cov_plane, cov_vert):
    own, columns = adjoint.shape
    layered = adjoint.reshape(ZL, own // ZL, -1)
    planar = jnp.einsum(
        "pq,lqr->lpr",
        cov_plane,
        lax.all_to_all(layered, "wide", split_axis=0, concat_axis=1, tiled=True),
        preferred_element_type=F32,
    ).astype(BF)
    restored = lax.all_to_all(planar, "wide", split_axis=1, concat_axis=0, tiled=True)
    slab_weights = lax.dynamic_slice_in_dim(cov_vert, lax.axis_index("narrow") * ZL, ZL, 0)
    summed = jnp.dot(
        slab_weights,
        lax.all_gather(restored.reshape(ZL, -1), "narrow", axis=0, tiled=True),
        preferred_element_type=F32,
    )
    return summed.astype(BF).reshape(own, -1)


def shards(adjoint_rhs, inverse_rows, blocks, block_cols, send_rows, cov_plane, cov_vert):
    rhs = adjoint_rhs[0, 0]
    inverse = inverse_rows[0, 0]
    block_values = blocks[0, 0]
    cols = block_cols[0, 0]
    send_index = send_rows[0, 0]
    own, columns = rhs.shape
    width = send_index.shape[1]
    halo = 4 * width
    wide, narrow = lax.axis_size("wide"), lax.axis_size("narrow")
    group = columns // (wide * narrow)
    by_columns = columns % (wide * narrow) == 0 and group % 8 == 0 and narrow * ZL == LANES and wide % 16 == 0
    found = matchings()
    count = len(found)
    sent = count * width
    shape = jax.ShapeDtypeStruct
    notes = [shape((width, columns), BF)] * count
    full = shape((own, columns), F32)
    base_shape = shape((sent, columns), F32)
    halo_space = pltpu.VMEM((halo, columns), BF)
    cell_space = pltpu.VMEM((own, columns), BF)
    (select,) = call(
        functools.partial(select_body, found, own),
        [shape((sent, own), BF)],
        [send_index],
        flops=SELECT_FLOPS,
    )
    messages = call(pick_body, notes, [select, rhs], flops=PICK_FLOPS)
    got = swap(messages, found)
    inverse_halo, blocks_halo, inverse_sent, blocks_sent, state, base = call(
        functools.partial(setup_body, found, width),
        [
            shape((own, halo), BF),
            shape((2, own, halo), BF),
            shape((sent, halo), BF),
            shape((2, sent, halo), BF),
            full,
            base_shape,
        ],
        [cols, inverse, block_values, rhs, select],
        [cell_space, cell_space],
        limit=12,
    )
    tables = column_tables(own, cov_plane, cov_vert) if by_columns else []
    for sweep in range(SWEEPS - 1):
        messages = call(
            functools.partial(sent_update_body, count), notes, [base, inverse_sent, *got], [halo_space], limit=4
        )
        arrived, got = got, swap(messages, found)
        iterate, part, base = call(
            functools.partial(update_body, count),
            [full, full, base_shape],
            [cols, state, inverse_halo, block_values, rhs, select, *arrived],
            [halo_space, pltpu.VMEM((own + halo, columns), BF), cell_space, cell_space],
        )
        turn = 1 if sweep == 1 and count == 3 else 0
        arrived = got[count - turn:] + got[:count - turn]
        messages = call(
            functools.partial(sent_residual_body, count, turn),
            notes,
            [base, blocks_sent, *arrived],
            [halo_space],
            limit=4,
        )
        got = swap(messages, found)
        if sweep < len(tables):
            tables[sweep], part = lax.optimization_barrier((tables[sweep], part))
        more = sweep < SWEEPS - 2
        state, *bases = call(
            functools.partial(residual_body, count, turn),
            [full] + [base_shape] * more,
            [part, blocks_halo, iterate, inverse, select, *arrived],
            [halo_space, cell_space] + [cell_space] * (2 * more),
        )
        base = bases[0] if more else None
    cells = shape((own, columns), BF)
    last = functools.partial(last_update_body, count)
    if by_columns:
        rounded, wire = call(
            last, [cells, shape((columns, own), BF)], [state, inverse_halo, *got, tables[0][0]], [halo_space]
        )
        adjoint, smoothed = smooth_by_columns(rounded, wire, tables)
    else:
        (adjoint,) = call(last, [cells], [state, inverse_halo, *got], [halo_space])
        smoothed = smooth_by_layers(adjoint, cov_plane, cov_vert)
    return (adjoint[None, None], smoothed[None, None])


def solution(mesh):
    in_specs = (
        P("wide", "narrow", None, None),
        P("wide", "narrow", None, None),
        P("wide", "narrow", None, None, None, None),
        P("wide", "narrow", None, None),
        P("wide", "narrow", None, None),
        P(),
        P(),
    )
    out_specs = (P("wide", "narrow", None, None), P("wide", "narrow", None, None))
    return jax.shard_map(shards, mesh=mesh, in_specs=in_specs, out_specs=out_specs, check_vma=False)
```

```python
import functools

import jax
import jax.numpy as jnp
from jax import lax
from jax.experimental import pallas as pl
from jax.experimental.pallas import tpu as pltpu
from jax.sharding import PartitionSpec as P

ZL = 64
SWEEPS = 4
LANES = 128
SELECT_FLOPS = 6 * 10 ** 8
PICK_FLOPS = 2 * 10 ** 9
BF = jnp.bfloat16
F32 = jnp.float32
VM = pl.BlockSpec(memory_space=pltpu.VMEM)
ANY = pl.BlockSpec(memory_space=pl.ANY)


def wide_slot(w, n, parity):
    return (w & 1) ^ parity ^ 1


def narrow_slot(w, n, parity):
    return 2 + ((n & 1) ^ parity ^ 1)


def mixed_slot(w, n, kind):
    turn = (w ^ (w >> 1) ^ kind) & 1
    return (1 - turn) * wide_slot(w, n, 1) + turn * narrow_slot(w, n, 0)


def has_partner(w, n, slot, wide, narrow):
    inside = [w > 0, w + 1 < wide, n > 0, n + 1 < narrow]
    return sum((slot == k) * inside[k] for k in range(4))


def matchings():
    wide, narrow = lax.axis_size("wide"), lax.axis_size("narrow")
    if narrow == 2 and wide % 4 == 0:
        rules = [(mixed_slot, 0), (mixed_slot, 1), (wide_slot, 0)]
    else:
        rules = [(wide_slot, 1)] * (wide > 2) + [(narrow_slot, 1)] * (narrow > 2)
        rules += [(narrow_slot, 0)] * (narrow > 1) + [(wide_slot, 0)] * (wide > 1)
    found = []
    for rule, kind in rules:
        pairs = []
        for w in range(wide):
            for n in range(narrow):
                slot = rule(w, n, kind)
                if has_partner(w, n, slot, wide, narrow):
                    step = ((-1, 0), (1, 0), (0, -1), (0, 1))[slot]
                    target = (w + step[0], n + step[1])
                elif slot < 2:
                    target = (w, n ^ 1 if n ^ 1 < narrow else n)
                else:
                    target = (w ^ 1 if w ^ 1 < wide else w, n)
                pairs.append((w * narrow + n, target[0] * narrow + target[1]))
        found.append((rule, kind, tuple(pairs)))
    return found


def own_slots(found):
    w, n = lax.axis_index("wide"), lax.axis_index("narrow")
    wide, narrow = lax.axis_size("wide"), lax.axis_size("narrow")
    slots = [rule(w, n, kind) for rule, kind, _ in found]
    return [(slot, has_partner(w, n, slot, wide, narrow) == 1) for slot in slots]


def swap(messages, found):
    return [lax.ppermute(m, ("wide", "narrow"), list(f[-1])) for m, f in zip(messages, found)]


def mm(a, b):
    return jnp.dot(a, b, preferred_element_type=F32)


def mm_t(a, b):
    return lax.dot_general(a, b, (((1,), (1,)), ((), ())), preferred_element_type=F32)


def iota(shape, dim):
    return lax.broadcasted_iota(jnp.int32, shape, dim)


def call(body, outs, args, scratch=(), specs=None, flops=0, limit=8, out_specs=None):
    size = sum(a.size * a.dtype.itemsize for a in args)
    return pl.pallas_call(
        body,
        out_shape=outs,
        in_specs=specs or [VM] * len(args),
        out_specs=out_specs or [VM] * len(outs),
        scratch_shapes=list(scratch),
        compiler_params=pltpu.CompilerParams(vmem_limit_bytes=limit * 1024 * 1024),
        cost_estimate=pl.CostEstimate(flops=flops, bytes_accessed=size, transcendentals=0),
    )(*args)


def join_halo(got):
    pieces = [piece[...] for piece in got]
    return jnp.concatenate(pieces + [jnp.zeros_like(pieces[0])] * (4 - len(pieces)), axis=0)


def send(messages, values):
    width = messages[0].shape[0]
    for m, message in enumerate(messages):
        message[...] = values[m * width:(m + 1) * width, :].astype(BF)


def keep_split(high_ref, low_ref, rows, value):
    high = value.astype(BF)
    high_ref[rows] = high
    low_ref[rows] = (value - high.astype(F32)).astype(BF)


def select_body(found, own, send_ref, select_ref):
    width = send_ref.shape[1]
    diagonal = iota((width, width), 0) == iota((width, width), 1)
    pieces = []
    for slot, paired in own_slots(found):
        rows = jnp.where(paired, send_ref[pl.ds(slot, 1), :], -1).astype(F32)
        pieces.append(jnp.where(diagonal, rows, 0.0))
    column = jnp.sum(jnp.concatenate(pieces, axis=0), axis=1, keepdims=True).astype(jnp.int32)
    select_ref[...] = (iota((len(found) * width, own), 1) == column).astype(F32).astype(BF)


def pick_body(select_ref, rhs_ref, *messages):
    send(messages, mm(select_ref[...], rhs_ref[...]))


def setup_body(found, width, cols_ref, inverse_ref, blocks_ref, rhs_ref, select_ref, *rest):
    inverse_halo_ref, blocks_halo_ref, inverse_sent_ref, blocks_sent_ref, state_ref, base_ref = rest[:6]
    high_ref, low_ref = rest[6:]
    own = rhs_ref.shape[0]
    halo = 4 * width
    places = iota((1, halo), 1)
    starts = jnp.full((1, halo), -halo, jnp.int32)
    for m, (slot, _) in enumerate(own_slots(found)):
        here = lax.div(places, width) == m
        starts = jnp.where(here, slot * width + lax.rem(places, width), starts)
    arrange = (iota((halo, halo), 0) == starts).astype(F32).astype(BF)
    rows, links, size, _ = blocks_ref.shape
    for j in range(rows):
        here = slice(j * size, (j + 1) * size)
        columns = [cols_ref[j, k] for k in range(links)]
        for c in range(halo // size):
            total = None
            for k in range(links):
                part = jnp.where(columns[k] == own // size + c, blocks_ref[j, k].astype(F32), 0.0)
                total = part if total is None else total + part
            lanes = slice(c * size, (c + 1) * size)
            keep_split(high_ref, low_ref, (here, lanes), total)
    for part, half_ref in enumerate((high_ref, low_ref)):
        blocks_halo_ref[part] = mm(half_ref[...], arrange).astype(BF)
    step = 256
    for i in range(0, own, step):
        here = slice(i, i + step)
        inverse_halo_ref[here, :] = mm(inverse_ref[here, own:], arrange).astype(BF)
        value = mm(inverse_ref[here, :own], rhs_ref[...])
        state_ref[here, :] = value
        keep_split(high_ref, low_ref, here, value)
    inverse_sent_ref[...] = mm(select_ref[...], inverse_halo_ref[...]).astype(BF)
    for part in range(2):
        blocks_sent_ref[part] = mm(select_ref[...], blocks_halo_ref[part]).astype(BF)
    base_ref[...] = mm(select_ref[...], high_ref[...]) + mm(select_ref[...], low_ref[...])


def sent_update_body(count, base_ref, sent_ref, *rest):
    got, messages = rest[:count], rest[count:]
    send(messages, base_ref[...] + mm(sent_ref[...], join_halo(got)))


def sent_residual_body(count, turn, base_ref, sent_ref, *rest):
    got, messages = rest[:count], rest[count:]
    halo = join_halo(got[turn:] + got[:turn])
    part = mm(sent_ref[0], halo) + mm(sent_ref[1], halo)
    send(messages, base_ref[...] - part)


def update_body(count, cols_ref, state_ref, inverse_halo_ref, blocks_ref, rhs_ref, select_ref, *rest):
    got, (iterate_ref, part_ref, base_ref, sub_ref, high_ref, low_ref) = rest[:count], rest[count:]
    own = state_ref.shape[0]
    halo = join_halo(got)
    step = 256
    for i in range(0, own, step):
        here = slice(i, i + step)
        value = state_ref[here, :] + mm(inverse_halo_ref[here, :], halo)
        iterate_ref[here, :] = value
        sub_ref[here, :] = value.astype(BF)
    sub_ref[own:, :] = jnp.zeros((sub_ref.shape[0] - own, sub_ref.shape[1]), BF)
    rows, links, size, _ = blocks_ref.shape
    for j in range(rows):
        starts = [pl.multiple_of(cols_ref[j, k] * size, size) for k in range(links)]
        values = jnp.concatenate([blocks_ref[j, k] for k in range(links)], axis=1)
        coupled = jnp.concatenate([sub_ref[pl.ds(start, size), :] for start in starts], axis=0)
        total = mm(values, coupled)
        here = slice(j * size, (j + 1) * size)
        value = rhs_ref[here, :].astype(F32) - total
        part_ref[here, :] = value
        keep_split(high_ref, low_ref, here, value)
    base_ref[...] = mm(select_ref[...], high_ref[...]) + mm(select_ref[...], low_ref[...])


def residual_body(count, turn, part_ref, blocks_halo_ref, iterate_ref, inverse_ref, select_ref, *rest):
    got, rest = rest[:count], list(rest[count:])
    state_ref = rest.pop(0)
    resid_ref, *split = rest[-3:] if len(rest) == 4 else rest
    own = part_ref.shape[0]
    halo = join_halo(got[turn:] + got[:turn])
    step = 256
    for i in range(0, own, step):
        here = slice(i, i + step)
        outer = mm(blocks_halo_ref[0, here, :], halo) + mm(blocks_halo_ref[1, here, :], halo)
        resid_ref[here, :] = (part_ref[here, :] - outer).astype(BF)
    for i in range(0, own, step):
        here = slice(i, i + step)
        value = iterate_ref[here, :] + mm(inverse_ref[here, :own], resid_ref[...])
        state_ref[here, :] = value
        if split:
            keep_split(*split, here, value)
    if split:
        rest[0][...] = mm(select_ref[...], split[0][...]) + mm(select_ref[...], split[1][...])


def last_update_body(count, state_ref, inverse_halo_ref, *rest):
    got, (round_ref,) = rest[:count], rest[count:]
    halo = join_halo(got)
    step = 256
    for i in range(0, state_ref.shape[0], step):
        here = slice(i, i + step)
        round_ref[here, :] = (state_ref[here, :] + mm(inverse_halo_ref[here, :], halo)).astype(BF)


def turn_body(state_ref, order_ref, turned_ref):
    value = state_ref[...]
    high = value.astype(BF)
    low = (value - high.astype(F32)).astype(BF)
    turned_ref[...] = mm(high.T, order_ref[...]) + mm(low.T, order_ref[...])


def wire_body(count, turned_ref, halo_table_ref, *rest):
    got, (wire_ref,) = rest[:count], rest[count:]
    wire_ref[...] = (turned_ref[...] + mm(join_halo(got).T, halo_table_ref[...])).astype(BF)


def one_hot(rows_of, shape):
    return (iota(shape, 0) == rows_of(iota((1, shape[1]), 1))).astype(F32).astype(BF)


def order_body(inverse_halo_ref, order_ref, halo_table_ref):
    own = order_ref.shape[0]
    tile = own // ZL
    order_ref[...] = one_hot(lambda k: lax.rem(k, ZL) * tile + lax.div(k, ZL), (own, own))
    halo_table_ref[...] = mm(inverse_halo_ref[...].T, order_ref[...]).astype(BF)


def tables_body(wide, narrow, cov_plane_ref, cov_vert_ref, plane_ref, spread_ref, vert_ref):
    plane = plane_ref.shape[0]
    tile = plane // wide
    turn = one_hot(lambda k: lax.rem(k, wide) * tile + lax.div(k, wide), (plane, plane))
    half = mm(cov_plane_ref[...], turn).astype(BF)
    plane_ref[...] = mm(half.T, turn).astype(BF).T
    share = LANES // ZL
    depth = narrow * ZL
    width = narrow * LANES

    def source(k):
        e, n, l = lax.div(k, depth), lax.rem(lax.div(k, ZL), narrow), lax.rem(k, ZL)
        return n * LANES + e * ZL + l

    spread = one_hot(source, (width, width))
    spread_ref[...] = spread
    turned = cov_vert_ref[...].astype(F32).T
    zero = jnp.zeros_like(turned)
    blocks = jnp.concatenate(
        [jnp.concatenate([turned if i == e else zero for i in range(share)], axis=1) for e in range(share)],
        axis=0,
    ).astype(BF)
    vert_ref[...] = mm_t(blocks, spread).astype(BF)


def mix_body(wide, narrow, group, in_ref, plane_ref, spread_ref, vert_ref, state_ref, inverse_halo_ref, *rest):
    got, (out_ref, adjoint_hbm, cells_ref, flat_ref, wire_ref, round_ref, sem) = rest[:-7], rest[-7:]
    last_update_body(len(got), state_ref, inverse_halo_ref, *got, round_ref)
    keep = pltpu.make_async_copy(round_ref, adjoint_hbm, sem)
    keep.start()
    own = in_ref.shape[1]
    tile = own // ZL
    share = LANES // ZL
    depth = narrow * ZL
    block = narrow * group
    taken = in_ref[...].astype(F32).reshape(wide, narrow, group, own)
    slabs = [taken[:, n].reshape(wide * group, own).astype(BF) for n in range(narrow)]
    for g in range(tile // share):
        lanes = slice(g * LANES, (g + 1) * LANES)
        joined = jnp.concatenate([s[:, lanes] for s in slabs], axis=1)
        spread = mm(joined, spread_ref[...])
        for e in range(share):
            cells_ref[g * share + e] = spread[:, e * depth:(e + 1) * depth]
    for r in range(group):
        for c in range(tile):
            flat_ref[c * wide:(c + 1) * wide, r * depth:(r + 1) * depth] = cells_ref[
                c, pl.ds(r, wide, stride=group), :
            ].astype(BF)
    planar = mm(plane_ref[...], flat_ref[...]).astype(BF)
    for g in range(tile // share):
        stacked = jnp.concatenate(
            [
                jnp.concatenate(
                    [
                        planar[c * wide:(c + 1) * wide, r * depth:(r + 1) * depth]
                        for c in range(g * share, (g + 1) * share)
                    ],
                    axis=1,
                )
                for r in range(group)
            ],
            axis=0,
        )
        mixed = mm(stacked, vert_ref[...])
        for r in range(group):
            for n in range(narrow):
                wire_ref[g, pl.ds(n * group + r, wide, stride=block), :] = mixed[
                    r * wide:(r + 1) * wide, n * LANES:(n + 1) * LANES
                ]
        out_ref[:, g * LANES:(g + 1) * LANES] = wire_ref[g].astype(BF)
    keep.wait()


def unwire_body(in_ref, order_ref, out_hbm, out_ref, sems):
    step = 128
    copies = []
    for n, i in enumerate(range(0, out_ref.shape[0], step)):
        here = pl.ds(i, step)
        out_ref[here, :] = mm_t(order_ref[here, :], in_ref[...]).astype(BF)
        copy = pltpu.make_async_copy(out_ref.at[here], out_hbm.at[here], sems.at[n])
        copy.start()
        copies.append(copy)
    for copy in copies:
        copy.wait()


def column_tables(inverse_halo, cov_plane, cov_vert):
    own, halo = inverse_halo.shape
    wide, narrow = lax.axis_size("wide"), lax.axis_size("narrow")
    width = narrow * LANES
    plane = cov_plane.shape[0]
    shape = jax.ShapeDtypeStruct
    order = call(order_body, [shape((own, own), BF), shape((halo, own), BF)], [inverse_halo])
    rest = call(
        functools.partial(tables_body, wide, narrow),
        [shape((plane, plane), BF), shape((width, width), BF), shape((width, width), BF)],
        [cov_plane, cov_vert],
    )
    return [tuple(order), tuple(rest)]


def smooth_by_columns(state, inverse_halo, got, tables):
    wide, narrow = lax.axis_size("wide"), lax.axis_size("narrow")
    own, columns = state.shape
    devices = wide * narrow
    group = columns // devices
    depth = narrow * ZL
    tile = own // ZL
    shape = jax.ShapeDtypeStruct
    (order, halo_table), (plane_mix, spread, vert_mix) = tables
    (turned,) = call(turn_body, [shape((columns, own), F32)], [state, order])
    (wire,) = call(functools.partial(wire_body, len(got)), [shape((columns, own), BF)], [turned, halo_table, *got])
    there = lax.all_to_all(
        wire.reshape(devices, group, own), ("wide", "narrow"), split_axis=0, concat_axis=0, tiled=True
    )
    mixed, adjoint = call(
        functools.partial(mix_body, wide, narrow, group),
        [shape((columns, own), BF), shape((own, columns), BF)],
        [there.reshape(columns, own), plane_mix, spread, vert_mix, state, inverse_halo, *got],
        [
            pltpu.VMEM((tile, wide * group, depth), F32),
            pltpu.VMEM((plane_mix.shape[0], group * depth), BF),
            pltpu.VMEM((own // LANES, columns, LANES), F32),
            pltpu.VMEM((own, columns), BF),
            pltpu.SemaphoreType.DMA,
        ],
        out_specs=[VM, ANY],
    )
    back = lax.all_to_all(
        mixed.reshape(devices, group, own), ("wide", "narrow"), split_axis=0, concat_axis=0, tiled=True
    )
    (smoothed,) = call(
        unwire_body,
        [shape((own, columns), BF)],
        [back.reshape(columns, own), order],
        [pltpu.VMEM((own, columns), BF), pltpu.SemaphoreType.DMA((own // 128,))],
        out_specs=[ANY],
    )
    return adjoint, smoothed


def smooth_by_layers(adjoint, cov_plane, cov_vert):
    own, columns = adjoint.shape
    layered = adjoint.reshape(ZL, own // ZL, -1)
    planar = jnp.einsum(
        "pq,lqr->lpr",
        cov_plane,
        lax.all_to_all(layered, "wide", split_axis=0, concat_axis=1, tiled=True),
        preferred_element_type=F32,
    ).astype(BF)
    restored = lax.all_to_all(planar, "wide", split_axis=1, concat_axis=0, tiled=True)
    slab_weights = lax.dynamic_slice_in_dim(cov_vert, lax.axis_index("narrow") * ZL, ZL, 0)
    summed = jnp.dot(
        slab_weights,
        lax.all_gather(restored.reshape(ZL, -1), "narrow", axis=0, tiled=True),
        preferred_element_type=F32,
    )
    return summed.astype(BF).reshape(own, -1)


def shards(adjoint_rhs, inverse_rows, blocks, block_cols, send_rows, cov_plane, cov_vert):
    rhs = adjoint_rhs[0, 0]
    inverse = inverse_rows[0, 0]
    block_values = blocks[0, 0]
    cols = block_cols[0, 0]
    send_index = send_rows[0, 0]
    own, columns = rhs.shape
    width = send_index.shape[1]
    halo = 4 * width
    wide, narrow = lax.axis_size("wide"), lax.axis_size("narrow")
    group = columns // (wide * narrow)
    by_columns = columns % (wide * narrow) == 0 and group % 8 == 0 and narrow * ZL == LANES and wide % 16 == 0
    found = matchings()
    count = len(found)
    sent = count * width
    shape = jax.ShapeDtypeStruct
    notes = [shape((width, columns), BF)] * count
    full = shape((own, columns), F32)
    base_shape = shape((sent, columns), F32)
    cell_space = pltpu.VMEM((own, columns), BF)
    (select,) = call(
        functools.partial(select_body, found, own),
        [shape((sent, own), BF)],
        [send_index],
        flops=SELECT_FLOPS,
    )
    messages = call(pick_body, notes, [select, rhs], flops=PICK_FLOPS)
    got = swap(messages, found)
    inverse_halo, blocks_halo, inverse_sent, blocks_sent, state, base = call(
        functools.partial(setup_body, found, width),
        [
            shape((own, halo), BF),
            shape((2, own, halo), BF),
            shape((sent, halo), BF),
            shape((2, sent, halo), BF),
            full,
            base_shape,
        ],
        [cols, inverse, block_values, rhs, select],
        [cell_space, cell_space],
        limit=12,
    )
    tables = column_tables(inverse_halo, cov_plane, cov_vert) if by_columns else []
    for sweep in range(SWEEPS - 1):
        messages = call(
            functools.partial(sent_update_body, count), notes, [base, inverse_sent, *got], limit=4
        )
        arrived, got = got, swap(messages, found)
        iterate, part, base = call(
            functools.partial(update_body, count),
            [full, full, base_shape],
            [cols, state, inverse_halo, block_values, rhs, select, *arrived],
            [pltpu.VMEM((own + halo, columns), BF), cell_space, cell_space],
        )
        turn = 1 if sweep == 1 and count == 3 else 0
        arrived = got[count - turn:] + got[:count - turn]
        messages = call(
            functools.partial(sent_residual_body, count, turn),
            notes,
            [base, blocks_sent, *arrived],
            limit=4,
        )
        got = swap(messages, found)
        if sweep < len(tables):
            tables[sweep], part = lax.optimization_barrier((tables[sweep], part))
        more = sweep < SWEEPS - 2
        state, *bases = call(
            functools.partial(residual_body, count, turn),
            [full] + [base_shape] * more,
            [part, blocks_halo, iterate, inverse, select, *arrived],
            [cell_space] * (1 + 2 * more),
        )
        base = bases[0] if more else None
    if by_columns:
        adjoint, smoothed = smooth_by_columns(state, inverse_halo, got, tables)
    else:
        cells = shape((own, columns), BF)
        (adjoint,) = call(functools.partial(last_update_body, count), [cells], [state, inverse_halo, *got])
        smoothed = smooth_by_layers(adjoint, cov_plane, cov_vert)
    return (adjoint[None, None], smoothed[None, None])


def solution(mesh):
    in_specs = (
        P("wide", "narrow", None, None),
        P("wide", "narrow", None, None),
        P("wide", "narrow", None, None, None, None),
        P("wide", "narrow", None, None),
        P("wide", "narrow", None, None),
        P(),
        P(),
    )
    out_specs = (P("wide", "narrow", None, None), P("wide", "narrow", None, None))
    return jax.shard_map(shards, mesh=mesh, in_specs=in_specs, out_specs=out_specs, check_vma=False)
```

```python
import functools

import jax
import jax.numpy as jnp
from jax import lax
from jax.experimental import pallas as pl
from jax.experimental.pallas import tpu as pltpu
from jax.sharding import PartitionSpec as P

ZL = 64
SWEEPS = 4
LANES = 128
SELECT_FLOPS = 6 * 10 ** 8
PICK_FLOPS = 2 * 10 ** 9
BF = jnp.bfloat16
F32 = jnp.float32
VM = pl.BlockSpec(memory_space=pltpu.VMEM)
ANY = pl.BlockSpec(memory_space=pl.ANY)


def wide_slot(w, n, parity):
    return (w & 1) ^ parity ^ 1


def narrow_slot(w, n, parity):
    return 2 + ((n & 1) ^ parity ^ 1)


def mixed_slot(w, n, kind):
    turn = (w ^ (w >> 1) ^ kind) & 1
    return (1 - turn) * wide_slot(w, n, 1) + turn * narrow_slot(w, n, 0)


def has_partner(w, n, slot, wide, narrow):
    inside = [w > 0, w + 1 < wide, n > 0, n + 1 < narrow]
    return sum((slot == k) * inside[k] for k in range(4))


def matchings():
    wide, narrow = lax.axis_size("wide"), lax.axis_size("narrow")
    if narrow == 2 and wide % 4 == 0:
        rules = [(mixed_slot, 0), (mixed_slot, 1), (wide_slot, 0)]
    else:
        rules = [(wide_slot, 1)] * (wide > 2) + [(narrow_slot, 1)] * (narrow > 2)
        rules += [(narrow_slot, 0)] * (narrow > 1) + [(wide_slot, 0)] * (wide > 1)
    found = []
    for rule, kind in rules:
        pairs = []
        for w in range(wide):
            for n in range(narrow):
                slot = rule(w, n, kind)
                if has_partner(w, n, slot, wide, narrow):
                    step = ((-1, 0), (1, 0), (0, -1), (0, 1))[slot]
                    target = (w + step[0], n + step[1])
                elif slot < 2:
                    target = (w, n ^ 1 if n ^ 1 < narrow else n)
                else:
                    target = (w ^ 1 if w ^ 1 < wide else w, n)
                pairs.append((w * narrow + n, target[0] * narrow + target[1]))
        found.append((rule, kind, tuple(pairs)))
    return found


def own_slots(found):
    w, n = lax.axis_index("wide"), lax.axis_index("narrow")
    wide, narrow = lax.axis_size("wide"), lax.axis_size("narrow")
    slots = [rule(w, n, kind) for rule, kind, _ in found]
    return [(slot, has_partner(w, n, slot, wide, narrow) == 1) for slot in slots]


def swap(messages, found):
    return [lax.ppermute(m, ("wide", "narrow"), list(f[-1])) for m, f in zip(messages, found)]


def mm(a, b):
    return jnp.dot(a, b, preferred_element_type=F32)


def mm_t(a, b):
    return lax.dot_general(a, b, (((1,), (1,)), ((), ())), preferred_element_type=F32)


def iota(shape, dim):
    return lax.broadcasted_iota(jnp.int32, shape, dim)


def call(body, outs, args, scratch=(), specs=None, flops=0, limit=8, out_specs=None):
    size = sum(a.size * a.dtype.itemsize for a in args)
    return pl.pallas_call(
        body,
        out_shape=outs,
        in_specs=specs or [VM] * len(args),
        out_specs=out_specs or [VM] * len(outs),
        scratch_shapes=list(scratch),
        compiler_params=pltpu.CompilerParams(vmem_limit_bytes=limit * 1024 * 1024),
        cost_estimate=pl.CostEstimate(flops=flops, bytes_accessed=size, transcendentals=0),
    )(*args)


def join_halo(got):
    pieces = [piece[...] for piece in got]
    return jnp.concatenate(pieces + [jnp.zeros_like(pieces[0])] * (4 - len(pieces)), axis=0)


def send(messages, values):
    width = messages[0].shape[0]
    for m, message in enumerate(messages):
        message[...] = values[m * width:(m + 1) * width, :].astype(BF)


def keep_split(high_ref, low_ref, rows, value):
    high = value.astype(BF)
    high_ref[rows] = high
    low_ref[rows] = (value - high.astype(F32)).astype(BF)


def select_body(found, own, send_ref, select_ref):
    width = send_ref.shape[1]
    diagonal = iota((width, width), 0) == iota((width, width), 1)
    pieces = []
    for slot, paired in own_slots(found):
        rows = jnp.where(paired, send_ref[pl.ds(slot, 1), :], -1).astype(F32)
        pieces.append(jnp.where(diagonal, rows, 0.0))
    column = jnp.sum(jnp.concatenate(pieces, axis=0), axis=1, keepdims=True).astype(jnp.int32)
    select_ref[...] = (iota((len(found) * width, own), 1) == column).astype(F32).astype(BF)


def pick_body(select_ref, rhs_ref, *messages):
    send(messages, mm(select_ref[...], rhs_ref[...]))


def setup_body(found, width, cols_ref, inverse_ref, blocks_ref, rhs_ref, select_ref, *rest):
    inverse_halo_ref, blocks_halo_ref, inverse_sent_ref, blocks_sent_ref, state_ref, base_ref = rest[:6]
    high_ref, low_ref = rest[6:]
    own = rhs_ref.shape[0]
    halo = 4 * width
    places = iota((1, halo), 1)
    starts = jnp.full((1, halo), -halo, jnp.int32)
    for m, (slot, _) in enumerate(own_slots(found)):
        here = lax.div(places, width) == m
        starts = jnp.where(here, slot * width + lax.rem(places, width), starts)
    arrange = (iota((halo, halo), 0) == starts).astype(F32).astype(BF)
    rows, links, size, _ = blocks_ref.shape
    for j in range(rows):
        here = slice(j * size, (j + 1) * size)
        columns = [cols_ref[j, k] for k in range(links)]
        for c in range(halo // size):
            total = None
            for k in range(links):
                part = jnp.where(columns[k] == own // size + c, blocks_ref[j, k].astype(F32), 0.0)
                total = part if total is None else total + part
            lanes = slice(c * size, (c + 1) * size)
            keep_split(high_ref, low_ref, (here, lanes), total)
    for part, half_ref in enumerate((high_ref, low_ref)):
        blocks_halo_ref[part] = mm(half_ref[...], arrange).astype(BF)
    step = own // 2
    for i in range(0, own, step):
        here = slice(i, i + step)
        inverse_halo_ref[here, :] = mm(inverse_ref[here, own:], arrange).astype(BF)
        value = mm(inverse_ref[here, :own], rhs_ref[...])
        state_ref[here, :] = value
        keep_split(high_ref, low_ref, here, value)
    inverse_sent_ref[...] = mm(select_ref[...], inverse_halo_ref[...]).astype(BF)
    for part in range(2):
        blocks_sent_ref[part] = mm(select_ref[...], blocks_halo_ref[part]).astype(BF)
    base_ref[...] = mm(select_ref[...], high_ref[...]) + mm(select_ref[...], low_ref[...])


def sent_update_body(count, base_ref, sent_ref, *rest):
    got, messages = rest[:count], rest[count:]
    send(messages, base_ref[...] + mm(sent_ref[...], join_halo(got)))


def sent_residual_body(count, turn, base_ref, sent_ref, *rest):
    got, messages = rest[:count], rest[count:]
    halo = join_halo(got[turn:] + got[:turn])
    part = mm(sent_ref[0], halo) + mm(sent_ref[1], halo)
    send(messages, base_ref[...] - part)


def update_body(count, cols_ref, state_ref, inverse_halo_ref, blocks_ref, rhs_ref, select_ref, *rest):
    got, (iterate_ref, part_ref, base_ref, sub_ref, high_ref, low_ref) = rest[:count], rest[count:]
    own = state_ref.shape[0]
    halo = join_halo(got)
    step = own // 2
    for i in range(0, own, step):
        here = slice(i, i + step)
        value = state_ref[here, :] + mm(inverse_halo_ref[here, :], halo)
        iterate_ref[here, :] = value
        sub_ref[here, :] = value.astype(BF)
    sub_ref[own:, :] = jnp.zeros((sub_ref.shape[0] - own, sub_ref.shape[1]), BF)
    rows, links, size, _ = blocks_ref.shape
    for j in range(rows):
        starts = [pl.multiple_of(cols_ref[j, k] * size, size) for k in range(links)]
        values = jnp.concatenate([blocks_ref[j, k] for k in range(links)], axis=1)
        coupled = jnp.concatenate([sub_ref[pl.ds(start, size), :] for start in starts], axis=0)
        total = mm(values, coupled)
        here = slice(j * size, (j + 1) * size)
        value = rhs_ref[here, :].astype(F32) - total
        part_ref[here, :] = value
        keep_split(high_ref, low_ref, here, value)
    base_ref[...] = mm(select_ref[...], high_ref[...]) + mm(select_ref[...], low_ref[...])


def residual_body(count, turn, part_ref, blocks_halo_ref, iterate_ref, inverse_ref, select_ref, *rest):
    got, rest = rest[:count], list(rest[count:])
    state_ref = rest.pop(0)
    resid_ref, *split = rest[-3:] if len(rest) == 4 else rest
    own = part_ref.shape[0]
    halo = join_halo(got[turn:] + got[:turn])
    step = own // 2
    for i in range(0, own, step):
        here = slice(i, i + step)
        outer = mm(blocks_halo_ref[0, here, :], halo) + mm(blocks_halo_ref[1, here, :], halo)
        resid_ref[here, :] = (part_ref[here, :] - outer).astype(BF)
    for i in range(0, own, step):
        here = slice(i, i + step)
        value = iterate_ref[here, :] + mm(inverse_ref[here, :own], resid_ref[...])
        state_ref[here, :] = value
        if split:
            keep_split(*split, here, value)
    if split:
        rest[0][...] = mm(select_ref[...], split[0][...]) + mm(select_ref[...], split[1][...])


def last_update_body(count, state_ref, inverse_halo_ref, *rest):
    got, (round_ref,) = rest[:count], rest[count:]
    halo = join_halo(got)
    step = state_ref.shape[0] // 2
    for i in range(0, state_ref.shape[0], step):
        here = slice(i, i + step)
        round_ref[here, :] = (state_ref[here, :] + mm(inverse_halo_ref[here, :], halo)).astype(BF)


def turn_body(state_ref, order_ref, turned_ref):
    value = state_ref[...]
    high = value.astype(BF)
    low = (value - high.astype(F32)).astype(BF)
    columns = value.shape[1]
    both = mm(jnp.concatenate([high, low], axis=1).T, order_ref[...])
    turned_ref[...] = both[:columns] + both[columns:]


def wire_body(count, turned_ref, halo_table_ref, *rest):
    got, (wire_ref,) = rest[:count], rest[count:]
    wire_ref[...] = (turned_ref[...] + mm(join_halo(got).T, halo_table_ref[...])).astype(BF)


def one_hot(rows_of, shape):
    return (iota(shape, 0) == rows_of(iota((1, shape[1]), 1))).astype(F32).astype(BF)


def order_body(inverse_halo_ref, order_ref, halo_table_ref):
    own = order_ref.shape[0]
    tile = own // ZL
    order_ref[...] = one_hot(lambda k: lax.rem(k, ZL) * tile + lax.div(k, ZL), (own, own))
    halo_table_ref[...] = mm(inverse_halo_ref[...].T, order_ref[...]).astype(BF)


def tables_body(wide, narrow, cov_plane_ref, cov_vert_ref, plane_ref, spread_ref, vert_ref):
    plane = plane_ref.shape[0]
    tile = plane // wide
    turn = one_hot(lambda k: lax.rem(k, wide) * tile + lax.div(k, wide), (plane, plane))
    half = mm(cov_plane_ref[...], turn).astype(BF)
    plane_ref[...] = mm(half.T, turn).astype(BF).T
    share = LANES // ZL
    depth = narrow * ZL
    width = narrow * LANES

    def source(k):
        e, n, l = lax.div(k, depth), lax.rem(lax.div(k, ZL), narrow), lax.rem(k, ZL)
        return n * LANES + e * ZL + l

    spread = one_hot(source, (width, width))
    spread_ref[...] = spread
    turned = cov_vert_ref[...].astype(F32).T
    zero = jnp.zeros_like(turned)
    blocks = jnp.concatenate(
        [jnp.concatenate([turned if i == e else zero for i in range(share)], axis=1) for e in range(share)],
        axis=0,
    ).astype(BF)
    vert_ref[...] = mm_t(blocks, spread).astype(BF)


def mix_body(wide, narrow, group, in_ref, plane_ref, spread_ref, vert_ref, state_ref, inverse_halo_ref, *rest):
    got, (out_ref, adjoint_hbm, cells_ref, flat_ref, wire_ref, round_ref, sem) = rest[:-7], rest[-7:]
    last_update_body(len(got), state_ref, inverse_halo_ref, *got, round_ref)
    keep = pltpu.make_async_copy(round_ref, adjoint_hbm, sem)
    keep.start()
    own = in_ref.shape[1]
    tile = own // ZL
    share = LANES // ZL
    depth = narrow * ZL
    block = narrow * group
    taken = in_ref[...].astype(F32).reshape(wide, narrow, group, own)
    slabs = [taken[:, n].reshape(wide * group, own).astype(BF) for n in range(narrow)]
    for g in range(tile // share):
        lanes = slice(g * LANES, (g + 1) * LANES)
        joined = jnp.concatenate([s[:, lanes] for s in slabs], axis=1)
        spread = mm(joined, spread_ref[...])
        for e in range(share):
            cells_ref[g * share + e] = spread[:, e * depth:(e + 1) * depth]
    for r in range(group):
        for c in range(tile):
            flat_ref[c * wide:(c + 1) * wide, r * depth:(r + 1) * depth] = cells_ref[
                c, pl.ds(r, wide, stride=group), :
            ].astype(BF)
    planar = mm(plane_ref[...], flat_ref[...]).astype(BF)
    for g in range(tile // share):
        stacked = jnp.concatenate(
            [
                jnp.concatenate(
                    [
                        planar[c * wide:(c + 1) * wide, r * depth:(r + 1) * depth]
                        for c in range(g * share, (g + 1) * share)
                    ],
                    axis=1,
                )
                for r in range(group)
            ],
            axis=0,
        )
        mixed = mm(stacked, vert_ref[...])
        for r in range(group):
            for n in range(narrow):
                wire_ref[g, pl.ds(n * group + r, wide, stride=block), :] = mixed[
                    r * wide:(r + 1) * wide, n * LANES:(n + 1) * LANES
                ]
        out_ref[:, g * LANES:(g + 1) * LANES] = wire_ref[g].astype(BF)
    keep.wait()


def unwire_body(in_ref, order_ref, out_hbm, out_ref, sems):
    step = out_ref.shape[0] // 2
    copies = []
    for n, i in enumerate(range(0, out_ref.shape[0], step)):
        here = pl.ds(i, step)
        out_ref[here, :] = mm_t(order_ref[here, :], in_ref[...]).astype(BF)
        copy = pltpu.make_async_copy(out_ref.at[here], out_hbm.at[here], sems.at[n])
        copy.start()
        copies.append(copy)
    for copy in copies:
        copy.wait()


def column_tables(inverse_halo, cov_plane, cov_vert):
    own, halo = inverse_halo.shape
    wide, narrow = lax.axis_size("wide"), lax.axis_size("narrow")
    width = narrow * LANES
    plane = cov_plane.shape[0]
    shape = jax.ShapeDtypeStruct
    order = call(order_body, [shape((own, own), BF), shape((halo, own), BF)], [inverse_halo])
    rest = call(
        functools.partial(tables_body, wide, narrow),
        [shape((plane, plane), BF), shape((width, width), BF), shape((width, width), BF)],
        [cov_plane, cov_vert],
    )
    return [tuple(order), tuple(rest)]


def smooth_by_columns(state, inverse_halo, got, tables):
    wide, narrow = lax.axis_size("wide"), lax.axis_size("narrow")
    own, columns = state.shape
    devices = wide * narrow
    group = columns // devices
    depth = narrow * ZL
    tile = own // ZL
    shape = jax.ShapeDtypeStruct
    (order, halo_table), (plane_mix, spread, vert_mix) = tables
    (turned,) = call(turn_body, [shape((columns, own), F32)], [state, order])
    (wire,) = call(functools.partial(wire_body, len(got)), [shape((columns, own), BF)], [turned, halo_table, *got])
    there = lax.all_to_all(
        wire.reshape(devices, group, own), ("wide", "narrow"), split_axis=0, concat_axis=0, tiled=True
    )
    mixed, adjoint = call(
        functools.partial(mix_body, wide, narrow, group),
        [shape((columns, own), BF), shape((own, columns), BF)],
        [there.reshape(columns, own), plane_mix, spread, vert_mix, state, inverse_halo, *got],
        [
            pltpu.VMEM((tile, wide * group, depth), F32),
            pltpu.VMEM((plane_mix.shape[0], group * depth), BF),
            pltpu.VMEM((own // LANES, columns, LANES), F32),
            pltpu.VMEM((own, columns), BF),
            pltpu.SemaphoreType.DMA,
        ],
        out_specs=[VM, ANY],
    )
    back = lax.all_to_all(
        mixed.reshape(devices, group, own), ("wide", "narrow"), split_axis=0, concat_axis=0, tiled=True
    )
    (smoothed,) = call(
        unwire_body,
        [shape((own, columns), BF)],
        [back.reshape(columns, own), order],
        [pltpu.VMEM((own, columns), BF), pltpu.SemaphoreType.DMA((2,))],
        out_specs=[ANY],
    )
    return adjoint, smoothed


def smooth_by_layers(adjoint, cov_plane, cov_vert):
    own, columns = adjoint.shape
    layered = adjoint.reshape(ZL, own // ZL, -1)
    planar = jnp.einsum(
        "pq,lqr->lpr",
        cov_plane,
        lax.all_to_all(layered, "wide", split_axis=0, concat_axis=1, tiled=True),
        preferred_element_type=F32,
    ).astype(BF)
    restored = lax.all_to_all(planar, "wide", split_axis=1, concat_axis=0, tiled=True)
    slab_weights = lax.dynamic_slice_in_dim(cov_vert, lax.axis_index("narrow") * ZL, ZL, 0)
    summed = jnp.dot(
        slab_weights,
        lax.all_gather(restored.reshape(ZL, -1), "narrow", axis=0, tiled=True),
        preferred_element_type=F32,
    )
    return summed.astype(BF).reshape(own, -1)


def shards(adjoint_rhs, inverse_rows, blocks, block_cols, send_rows, cov_plane, cov_vert):
    rhs = adjoint_rhs[0, 0]
    inverse = inverse_rows[0, 0]
    block_values = blocks[0, 0]
    cols = block_cols[0, 0]
    send_index = send_rows[0, 0]
    own, columns = rhs.shape
    width = send_index.shape[1]
    halo = 4 * width
    wide, narrow = lax.axis_size("wide"), lax.axis_size("narrow")
    group = columns // (wide * narrow)
    by_columns = columns % (wide * narrow) == 0 and group % 8 == 0 and narrow * ZL == LANES and wide % 16 == 0
    found = matchings()
    count = len(found)
    sent = count * width
    shape = jax.ShapeDtypeStruct
    notes = [shape((width, columns), BF)] * count
    full = shape((own, columns), F32)
    base_shape = shape((sent, columns), F32)
    cell_space = pltpu.VMEM((own, columns), BF)
    (select,) = call(
        functools.partial(select_body, found, own),
        [shape((sent, own), BF)],
        [send_index],
        flops=SELECT_FLOPS,
    )
    messages = call(pick_body, notes, [select, rhs], flops=PICK_FLOPS)
    got = swap(messages, found)
    inverse_halo, blocks_halo, inverse_sent, blocks_sent, state, base = call(
        functools.partial(setup_body, found, width),
        [
            shape((own, halo), BF),
            shape((2, own, halo), BF),
            shape((sent, halo), BF),
            shape((2, sent, halo), BF),
            full,
            base_shape,
        ],
        [cols, inverse, block_values, rhs, select],
        [cell_space, cell_space],
        limit=12,
    )
    tables = column_tables(inverse_halo, cov_plane, cov_vert) if by_columns else []
    for sweep in range(SWEEPS - 1):
        messages = call(
            functools.partial(sent_update_body, count), notes, [base, inverse_sent, *got], limit=4
        )
        arrived, got = got, swap(messages, found)
        iterate, part, base = call(
            functools.partial(update_body, count),
            [full, full, base_shape],
            [cols, state, inverse_halo, block_values, rhs, select, *arrived],
            [pltpu.VMEM((own + halo, columns), BF), cell_space, cell_space],
        )
        turn = 1 if sweep == 1 and count == 3 else 0
        arrived = got[count - turn:] + got[:count - turn]
        messages = call(
            functools.partial(sent_residual_body, count, turn),
            notes,
            [base, blocks_sent, *arrived],
            limit=4,
        )
        got = swap(messages, found)
        if sweep < len(tables):
            tables[sweep], part = lax.optimization_barrier((tables[sweep], part))
        more = sweep < SWEEPS - 2
        state, *bases = call(
            functools.partial(residual_body, count, turn),
            [full] + [base_shape] * more,
            [part, blocks_halo, iterate, inverse, select, *arrived],
            [cell_space] * (1 + 2 * more),
        )
        base = bases[0] if more else None
    if by_columns:
        adjoint, smoothed = smooth_by_columns(state, inverse_halo, got, tables)
    else:
        cells = shape((own, columns), BF)
        (adjoint,) = call(functools.partial(last_update_body, count), [cells], [state, inverse_halo, *got])
        smoothed = smooth_by_layers(adjoint, cov_plane, cov_vert)
    return (adjoint[None, None], smoothed[None, None])


def solution(mesh):
    in_specs = (
        P("wide", "narrow", None, None),
        P("wide", "narrow", None, None),
        P("wide", "narrow", None, None, None, None),
        P("wide", "narrow", None, None),
        P("wide", "narrow", None, None),
        P(),
        P(),
    )
    out_specs = (P("wide", "narrow", None, None), P("wide", "narrow", None, None))
    return jax.shard_map(shards, mesh=mesh, in_specs=in_specs, out_specs=out_specs, check_vma=False)
```

```python
import functools

import jax
import jax.numpy as jnp
from jax import lax
from jax.experimental import pallas as pl
from jax.experimental.pallas import tpu as pltpu
from jax.sharding import PartitionSpec as P

ZL = 64
SWEEPS = 4
LANES = 128
SELECT_FLOPS = 6 * 10 ** 8
PICK_FLOPS = 2 * 10 ** 9
BF = jnp.bfloat16
F32 = jnp.float32
VM = pl.BlockSpec(memory_space=pltpu.VMEM)
ANY = pl.BlockSpec(memory_space=pl.ANY)


def wide_slot(w, n, parity):
    return (w & 1) ^ parity ^ 1


def narrow_slot(w, n, parity):
    return 2 + ((n & 1) ^ parity ^ 1)


def mixed_slot(w, n, kind):
    turn = (w ^ (w >> 1) ^ kind) & 1
    return (1 - turn) * wide_slot(w, n, 1) + turn * narrow_slot(w, n, 0)


def has_partner(w, n, slot, wide, narrow):
    inside = [w > 0, w + 1 < wide, n > 0, n + 1 < narrow]
    return sum((slot == k) * inside[k] for k in range(4))


def matchings():
    wide, narrow = lax.axis_size("wide"), lax.axis_size("narrow")
    if narrow == 2 and wide % 4 == 0:
        rules = [(mixed_slot, 0), (mixed_slot, 1), (wide_slot, 0)]
    else:
        rules = [(wide_slot, 1)] * (wide > 2) + [(narrow_slot, 1)] * (narrow > 2)
        rules += [(narrow_slot, 0)] * (narrow > 1) + [(wide_slot, 0)] * (wide > 1)
    found = []
    for rule, kind in rules:
        pairs = []
        for w in range(wide):
            for n in range(narrow):
                slot = rule(w, n, kind)
                if has_partner(w, n, slot, wide, narrow):
                    step = ((-1, 0), (1, 0), (0, -1), (0, 1))[slot]
                    target = (w + step[0], n + step[1])
                elif slot < 2:
                    target = (w, n ^ 1 if n ^ 1 < narrow else n)
                else:
                    target = (w ^ 1 if w ^ 1 < wide else w, n)
                pairs.append((w * narrow + n, target[0] * narrow + target[1]))
        found.append((rule, kind, tuple(pairs)))
    return found


def own_slots(found):
    w, n = lax.axis_index("wide"), lax.axis_index("narrow")
    wide, narrow = lax.axis_size("wide"), lax.axis_size("narrow")
    slots = [rule(w, n, kind) for rule, kind, _ in found]
    return [(slot, has_partner(w, n, slot, wide, narrow) == 1) for slot in slots]


def swap(messages, found):
    return [lax.ppermute(m, ("wide", "narrow"), list(f[-1])) for m, f in zip(messages, found)]


def mm(a, b):
    return jnp.dot(a, b, preferred_element_type=F32)


def mm_t(a, b):
    return lax.dot_general(a, b, (((1,), (1,)), ((), ())), preferred_element_type=F32)


def iota(shape, dim):
    return lax.broadcasted_iota(jnp.int32, shape, dim)


def call(body, outs, args, scratch=(), specs=None, flops=0, limit=8, out_specs=None):
    size = sum(a.size * a.dtype.itemsize for a in args)
    return pl.pallas_call(
        body,
        out_shape=outs,
        in_specs=specs or [VM] * len(args),
        out_specs=out_specs or [VM] * len(outs),
        scratch_shapes=list(scratch),
        compiler_params=pltpu.CompilerParams(vmem_limit_bytes=limit * 1024 * 1024),
        cost_estimate=pl.CostEstimate(flops=flops, bytes_accessed=size, transcendentals=0),
    )(*args)


def join_halo(got):
    pieces = [piece[...] for piece in got]
    return jnp.concatenate(pieces + [jnp.zeros_like(pieces[0])] * (4 - len(pieces)), axis=0)


def send(messages, values):
    width = messages[0].shape[0]
    for m, message in enumerate(messages):
        message[...] = values[m * width:(m + 1) * width, :].astype(BF)


def keep_split(high_ref, low_ref, rows, value):
    high = value.astype(BF)
    high_ref[rows] = high
    low_ref[rows] = (value - high.astype(F32)).astype(BF)


def select_body(found, own, send_ref, select_ref):
    width = send_ref.shape[1]
    diagonal = iota((width, width), 0) == iota((width, width), 1)
    pieces = []
    for slot, paired in own_slots(found):
        rows = jnp.where(paired, send_ref[pl.ds(slot, 1), :], -1).astype(F32)
        pieces.append(jnp.where(diagonal, rows, 0.0))
    column = jnp.sum(jnp.concatenate(pieces, axis=0), axis=1, keepdims=True).astype(jnp.int32)
    select_ref[...] = (iota((len(found) * width, own), 1) == column).astype(F32).astype(BF)


def pick_body(select_ref, rhs_ref, *messages):
    send(messages, mm(select_ref[...], rhs_ref[...]))


def setup_body(found, width, cols_ref, inverse_ref, blocks_ref, rhs_ref, select_ref, *rest):
    inverse_halo_ref, blocks_halo_ref, inverse_sent_ref, blocks_sent_ref, state_ref, base_ref = rest[:6]
    high_ref, low_ref = rest[6:]
    own = rhs_ref.shape[0]
    halo = 4 * width
    places = iota((1, halo), 1)
    starts = jnp.full((1, halo), -halo, jnp.int32)
    for m, (slot, _) in enumerate(own_slots(found)):
        here = lax.div(places, width) == m
        starts = jnp.where(here, slot * width + lax.rem(places, width), starts)
    arrange = (iota((halo, halo), 0) == starts).astype(F32).astype(BF)
    rows, links, size, _ = blocks_ref.shape
    for j in range(rows):
        here = slice(j * size, (j + 1) * size)
        columns = [cols_ref[j, k] for k in range(links)]
        for c in range(halo // size):
            total = None
            for k in range(links):
                part = jnp.where(columns[k] == own // size + c, blocks_ref[j, k].astype(F32), 0.0)
                total = part if total is None else total + part
            lanes = slice(c * size, (c + 1) * size)
            keep_split(high_ref, low_ref, (here, lanes), total)
    for part, half_ref in enumerate((high_ref, low_ref)):
        blocks_halo_ref[part] = mm(half_ref[...], arrange).astype(BF)
    step = own // 2
    for i in range(0, own, step):
        here = slice(i, i + step)
        inverse_halo_ref[here, :] = mm(inverse_ref[here, own:], arrange).astype(BF)
        value = mm(inverse_ref[here, :own], rhs_ref[...])
        state_ref[here, :] = value
        keep_split(high_ref, low_ref, here, value)
    sent = mm(select_ref[...], inverse_halo_ref[...]).astype(BF)
    for m in range(len(found)):
        inverse_sent_ref[m] = sent[:, m * width:(m + 1) * width]
    for part in range(2):
        sent = mm(select_ref[...], blocks_halo_ref[part]).astype(BF)
        for m in range(len(found)):
            blocks_sent_ref[part, m] = sent[:, m * width:(m + 1) * width]
    base_ref[...] = mm(select_ref[...], high_ref[...]) + mm(select_ref[...], low_ref[...])


def sent_update_body(count, base_ref, sent_ref, *rest):
    got, messages = rest[:count], rest[count:]
    send(messages, base_ref[...] + sum(mm(sent_ref[m], piece[...]) for m, piece in enumerate(got)))


def sent_residual_body(count, turn, base_ref, sent_ref, *rest):
    got, messages = rest[:count], rest[count:]
    got = [piece[...] for piece in got[turn:] + got[:turn]]
    part = sum(mm(sent_ref[half, m], piece) for half in range(2) for m, piece in enumerate(got))
    send(messages, base_ref[...] - part)


def update_body(count, cols_ref, state_ref, inverse_halo_ref, blocks_ref, rhs_ref, select_ref, *rest):
    got, (iterate_ref, part_ref, base_ref, sub_ref, high_ref, low_ref) = rest[:count], rest[count:]
    own = state_ref.shape[0]
    halo = join_halo(got)
    step = own // 2
    for i in range(0, own, step):
        here = slice(i, i + step)
        value = state_ref[here, :] + mm(inverse_halo_ref[here, :], halo)
        iterate_ref[here, :] = value
        sub_ref[here, :] = value.astype(BF)
    sub_ref[own:, :] = jnp.zeros((sub_ref.shape[0] - own, sub_ref.shape[1]), BF)
    rows, links, size, _ = blocks_ref.shape
    for j in range(rows):
        starts = [pl.multiple_of(cols_ref[j, k] * size, size) for k in range(links)]
        values = jnp.concatenate([blocks_ref[j, k] for k in range(links)], axis=1)
        coupled = jnp.concatenate([sub_ref[pl.ds(start, size), :] for start in starts], axis=0)
        total = mm(values, coupled)
        here = slice(j * size, (j + 1) * size)
        value = rhs_ref[here, :].astype(F32) - total
        part_ref[here, :] = value
        keep_split(high_ref, low_ref, here, value)
    base_ref[...] = mm(select_ref[...], high_ref[...]) + mm(select_ref[...], low_ref[...])


def residual_body(count, turn, part_ref, blocks_halo_ref, iterate_ref, inverse_ref, select_ref, *rest):
    got, rest = rest[:count], list(rest[count:])
    state_ref = rest.pop(0)
    resid_ref, *split = rest[-3:] if len(rest) == 4 else rest
    own = part_ref.shape[0]
    halo = join_halo(got[turn:] + got[:turn])
    step = own // 2
    for i in range(0, own, step):
        here = slice(i, i + step)
        outer = mm(blocks_halo_ref[0, here, :], halo) + mm(blocks_halo_ref[1, here, :], halo)
        resid_ref[here, :] = (part_ref[here, :] - outer).astype(BF)
    for i in range(0, own, step):
        here = slice(i, i + step)
        value = iterate_ref[here, :] + mm(inverse_ref[here, :own], resid_ref[...])
        state_ref[here, :] = value
        if split:
            keep_split(*split, here, value)
    if split:
        rest[0][...] = mm(select_ref[...], split[0][...]) + mm(select_ref[...], split[1][...])


def last_update_body(count, state_ref, inverse_halo_ref, *rest):
    got, (round_ref,) = rest[:count], rest[count:]
    halo = join_halo(got)
    step = state_ref.shape[0] // 2
    for i in range(0, state_ref.shape[0], step):
        here = slice(i, i + step)
        round_ref[here, :] = (state_ref[here, :] + mm(inverse_halo_ref[here, :], halo)).astype(BF)


def turn_body(state_ref, order_ref, turned_ref):
    value = state_ref[...]
    high = value.astype(BF)
    low = (value - high.astype(F32)).astype(BF)
    columns = value.shape[1]
    both = mm(jnp.concatenate([high, low], axis=1).T, order_ref[...])
    turned_ref[...] = both[:columns] + both[columns:]


def wire_body(count, turned_ref, halo_table_ref, *rest):
    got, (wire_ref,) = rest[:count], rest[count:]
    wire_ref[...] = (turned_ref[...] + mm(join_halo(got).T, halo_table_ref[...])).astype(BF)


def one_hot(rows_of, shape):
    return (iota(shape, 0) == rows_of(iota((1, shape[1]), 1))).astype(F32).astype(BF)


def order_body(inverse_halo_ref, order_ref, halo_table_ref):
    own = order_ref.shape[0]
    tile = own // ZL
    order_ref[...] = one_hot(lambda k: lax.rem(k, ZL) * tile + lax.div(k, ZL), (own, own))
    halo_table_ref[...] = mm(inverse_halo_ref[...].T, order_ref[...]).astype(BF)


def tables_body(wide, narrow, cov_plane_ref, cov_vert_ref, plane_ref, spread_ref, vert_ref):
    plane = plane_ref.shape[0]
    tile = plane // wide
    turn = one_hot(lambda k: lax.rem(k, wide) * tile + lax.div(k, wide), (plane, plane))
    half = mm(cov_plane_ref[...], turn).astype(BF)
    plane_ref[...] = mm(half.T, turn).astype(BF).T
    share = LANES // ZL
    depth = narrow * ZL
    width = narrow * LANES

    def source(k):
        e, n, l = lax.div(k, depth), lax.rem(lax.div(k, ZL), narrow), lax.rem(k, ZL)
        return n * LANES + e * ZL + l

    spread = one_hot(source, (width, width))
    spread_ref[...] = spread
    turned = cov_vert_ref[...].astype(F32).T
    zero = jnp.zeros_like(turned)
    blocks = jnp.concatenate(
        [jnp.concatenate([turned if i == e else zero for i in range(share)], axis=1) for e in range(share)],
        axis=0,
    ).astype(BF)
    vert_ref[...] = mm_t(blocks, spread).astype(BF)


def mix_body(wide, narrow, group, in_ref, plane_ref, spread_ref, vert_ref, state_ref, inverse_halo_ref, *rest):
    got, (out_ref, adjoint_hbm, cells_ref, flat_ref, wire_ref, round_ref, sem) = rest[:-7], rest[-7:]
    last_update_body(len(got), state_ref, inverse_halo_ref, *got, round_ref)
    keep = pltpu.make_async_copy(round_ref, adjoint_hbm, sem)
    keep.start()
    own = in_ref.shape[1]
    tile = own // ZL
    share = LANES // ZL
    depth = narrow * ZL
    block = narrow * group
    taken = in_ref[...].astype(F32).reshape(wide, narrow, group, own)
    slabs = [taken[:, n].reshape(wide * group, own).astype(BF) for n in range(narrow)]
    for g in range(tile // share):
        lanes = slice(g * LANES, (g + 1) * LANES)
        joined = jnp.concatenate([s[:, lanes] for s in slabs], axis=1)
        spread = mm(joined, spread_ref[...])
        for e in range(share):
            cells_ref[g * share + e] = spread[:, e * depth:(e + 1) * depth]
    for r in range(group):
        for c in range(tile):
            flat_ref[c * wide:(c + 1) * wide, r * depth:(r + 1) * depth] = cells_ref[
                c, pl.ds(r, wide, stride=group), :
            ].astype(BF)
    planar = mm(plane_ref[...], flat_ref[...]).astype(BF)
    for g in range(tile // share):
        stacked = jnp.concatenate(
            [
                jnp.concatenate(
                    [
                        planar[c * wide:(c + 1) * wide, r * depth:(r + 1) * depth]
                        for c in range(g * share, (g + 1) * share)
                    ],
                    axis=1,
                )
                for r in range(group)
            ],
            axis=0,
        )
        mixed = mm(stacked, vert_ref[...])
        for r in range(group):
            for n in range(narrow):
                wire_ref[g, pl.ds(n * group + r, wide, stride=block), :] = mixed[
                    r * wide:(r + 1) * wide, n * LANES:(n + 1) * LANES
                ]
        out_ref[:, g * LANES:(g + 1) * LANES] = wire_ref[g].astype(BF)
    keep.wait()


def unwire_body(in_ref, order_ref, out_hbm, out_ref, sems):
    step = out_ref.shape[0] // 3
    copies = []
    for n, i in enumerate(range(0, out_ref.shape[0], step)):
        here = pl.ds(i, step)
        out_ref[here, :] = mm_t(order_ref[here, :], in_ref[...]).astype(BF)
        copy = pltpu.make_async_copy(out_ref.at[here], out_hbm.at[here], sems.at[n])
        copy.start()
        copies.append(copy)
    for copy in copies:
        copy.wait()


def column_tables(inverse_halo, cov_plane, cov_vert):
    own, halo = inverse_halo.shape
    wide, narrow = lax.axis_size("wide"), lax.axis_size("narrow")
    width = narrow * LANES
    plane = cov_plane.shape[0]
    shape = jax.ShapeDtypeStruct
    order = call(order_body, [shape((own, own), BF), shape((halo, own), BF)], [inverse_halo])
    rest = call(
        functools.partial(tables_body, wide, narrow),
        [shape((plane, plane), BF), shape((width, width), BF), shape((width, width), BF)],
        [cov_plane, cov_vert],
    )
    return [tuple(order), tuple(rest)]


def smooth_by_columns(state, inverse_halo, got, tables):
    wide, narrow = lax.axis_size("wide"), lax.axis_size("narrow")
    own, columns = state.shape
    devices = wide * narrow
    group = columns // devices
    depth = narrow * ZL
    tile = own // ZL
    shape = jax.ShapeDtypeStruct
    (order, halo_table), (plane_mix, spread, vert_mix) = tables
    (turned,) = call(turn_body, [shape((columns, own), F32)], [state, order])
    (wire,) = call(functools.partial(wire_body, len(got)), [shape((columns, own), BF)], [turned, halo_table, *got])
    there = lax.all_to_all(
        wire.reshape(devices, group, own), ("wide", "narrow"), split_axis=0, concat_axis=0, tiled=True
    )
    mixed, adjoint = call(
        functools.partial(mix_body, wide, narrow, group),
        [shape((columns, own), BF), shape((own, columns), BF)],
        [there.reshape(columns, own), plane_mix, spread, vert_mix, state, inverse_halo, *got],
        [
            pltpu.VMEM((tile, wide * group, depth), F32),
            pltpu.VMEM((plane_mix.shape[0], group * depth), BF),
            pltpu.VMEM((own // LANES, columns, LANES), F32),
            pltpu.VMEM((own, columns), BF),
            pltpu.SemaphoreType.DMA,
        ],
        out_specs=[VM, ANY],
    )
    back = lax.all_to_all(
        mixed.reshape(devices, group, own), ("wide", "narrow"), split_axis=0, concat_axis=0, tiled=True
    )
    (smoothed,) = call(
        unwire_body,
        [shape((own, columns), BF)],
        [back.reshape(columns, own), order],
        [pltpu.VMEM((own, columns), BF), pltpu.SemaphoreType.DMA((3,))],
        out_specs=[ANY],
    )
    return adjoint, smoothed


def smooth_by_layers(adjoint, cov_plane, cov_vert):
    own, columns = adjoint.shape
    layered = adjoint.reshape(ZL, own // ZL, -1)
    planar = jnp.einsum(
        "pq,lqr->lpr",
        cov_plane,
        lax.all_to_all(layered, "wide", split_axis=0, concat_axis=1, tiled=True),
        preferred_element_type=F32,
    ).astype(BF)
    restored = lax.all_to_all(planar, "wide", split_axis=1, concat_axis=0, tiled=True)
    slab_weights = lax.dynamic_slice_in_dim(cov_vert, lax.axis_index("narrow") * ZL, ZL, 0)
    summed = jnp.dot(
        slab_weights,
        lax.all_gather(restored.reshape(ZL, -1), "narrow", axis=0, tiled=True),
        preferred_element_type=F32,
    )
    return summed.astype(BF).reshape(own, -1)


def shards(adjoint_rhs, inverse_rows, blocks, block_cols, send_rows, cov_plane, cov_vert):
    rhs = adjoint_rhs[0, 0]
    inverse = inverse_rows[0, 0]
    block_values = blocks[0, 0]
    cols = block_cols[0, 0]
    send_index = send_rows[0, 0]
    own, columns = rhs.shape
    width = send_index.shape[1]
    halo = 4 * width
    wide, narrow = lax.axis_size("wide"), lax.axis_size("narrow")
    group = columns // (wide * narrow)
    by_columns = columns % (wide * narrow) == 0 and group % 8 == 0 and narrow * ZL == LANES and wide % 16 == 0
    found = matchings()
    count = len(found)
    sent = count * width
    shape = jax.ShapeDtypeStruct
    notes = [shape((width, columns), BF)] * count
    full = shape((own, columns), F32)
    base_shape = shape((sent, columns), F32)
    cell_space = pltpu.VMEM((own, columns), BF)
    (select,) = call(
        functools.partial(select_body, found, own),
        [shape((sent, own), BF)],
        [send_index],
        flops=SELECT_FLOPS,
    )
    messages = call(pick_body, notes, [select, rhs], flops=PICK_FLOPS)
    got = swap(messages, found)
    inverse_halo, blocks_halo, inverse_sent, blocks_sent, state, base = call(
        functools.partial(setup_body, found, width),
        [
            shape((own, halo), BF),
            shape((2, own, halo), BF),
            shape((count, sent, width), BF),
            shape((2, count, sent, width), BF),
            full,
            base_shape,
        ],
        [cols, inverse, block_values, rhs, select],
        [cell_space, cell_space],
        limit=12,
    )
    tables = column_tables(inverse_halo, cov_plane, cov_vert) if by_columns else []
    for sweep in range(SWEEPS - 1):
        messages = call(
            functools.partial(sent_update_body, count), notes, [base, inverse_sent, *got], limit=4
        )
        arrived, got = got, swap(messages, found)
        if tables and sweep == 1:
            tables[1], state = lax.optimization_barrier((tables[1], state))
        iterate, part, base = call(
            functools.partial(update_body, count),
            [full, full, base_shape],
            [cols, state, inverse_halo, block_values, rhs, select, *arrived],
            [pltpu.VMEM((own + halo, columns), BF), cell_space, cell_space],
        )
        turn = 1 if sweep == 1 and count == 3 else 0
        arrived = got[count - turn:] + got[:count - turn]
        messages = call(
            functools.partial(sent_residual_body, count, turn),
            notes,
            [base, blocks_sent, *arrived],
            limit=4,
        )
        got = swap(messages, found)
        if tables and sweep == 0:
            tables[0], part = lax.optimization_barrier((tables[0], part))
        more = sweep < SWEEPS - 2
        state, *bases = call(
            functools.partial(residual_body, count, turn),
            [full] + [base_shape] * more,
            [part, blocks_halo, iterate, inverse, select, *arrived],
            [cell_space] * (1 + 2 * more),
        )
        base = bases[0] if more else None
    if by_columns:
        adjoint, smoothed = smooth_by_columns(state, inverse_halo, got, tables)
    else:
        cells = shape((own, columns), BF)
        (adjoint,) = call(functools.partial(last_update_body, count), [cells], [state, inverse_halo, *got])
        smoothed = smooth_by_layers(adjoint, cov_plane, cov_vert)
    return (adjoint[None, None], smoothed[None, None])


def solution(mesh):
    in_specs = (
        P("wide", "narrow", None, None),
        P("wide", "narrow", None, None),
        P("wide", "narrow", None, None, None, None),
        P("wide", "narrow", None, None),
        P("wide", "narrow", None, None),
        P(),
        P(),
    )
    out_specs = (P("wide", "narrow", None, None), P("wide", "narrow", None, None))
    return jax.shard_map(shards, mesh=mesh, in_specs=in_specs, out_specs=out_specs, check_vma=False)
```

```python
import functools

import jax
import jax.numpy as jnp
from jax import lax
from jax.experimental import pallas as pl
from jax.experimental.pallas import tpu as pltpu
from jax.sharding import PartitionSpec as P

ZL = 64
SWEEPS = 4
LANES = 128
SELECT_FLOPS = 6 * 10 ** 8
PICK_FLOPS = 2 * 10 ** 9
BF = jnp.bfloat16
F32 = jnp.float32
VM = pl.BlockSpec(memory_space=pltpu.VMEM)
ANY = pl.BlockSpec(memory_space=pl.ANY)


def wide_slot(w, n, parity):
    return (w & 1) ^ parity ^ 1


def narrow_slot(w, n, parity):
    return 2 + ((n & 1) ^ parity ^ 1)


def mixed_slot(w, n, kind):
    turn = (w ^ (w >> 1) ^ kind) & 1
    return (1 - turn) * wide_slot(w, n, 1) + turn * narrow_slot(w, n, 0)


def has_partner(w, n, slot, wide, narrow):
    inside = [w > 0, w + 1 < wide, n > 0, n + 1 < narrow]
    return sum((slot == k) * inside[k] for k in range(4))


def matchings():
    wide, narrow = lax.axis_size("wide"), lax.axis_size("narrow")
    if narrow == 2 and wide % 4 == 0:
        rules = [(mixed_slot, 0), (mixed_slot, 1), (wide_slot, 0)]
    else:
        rules = [(wide_slot, 1)] * (wide > 2) + [(narrow_slot, 1)] * (narrow > 2)
        rules += [(narrow_slot, 0)] * (narrow > 1) + [(wide_slot, 0)] * (wide > 1)
    found = []
    for rule, kind in rules:
        pairs = []
        for w in range(wide):
            for n in range(narrow):
                slot = rule(w, n, kind)
                if has_partner(w, n, slot, wide, narrow):
                    step = ((-1, 0), (1, 0), (0, -1), (0, 1))[slot]
                    target = (w + step[0], n + step[1])
                elif slot < 2:
                    target = (w, n ^ 1 if n ^ 1 < narrow else n)
                else:
                    target = (w ^ 1 if w ^ 1 < wide else w, n)
                pairs.append((w * narrow + n, target[0] * narrow + target[1]))
        found.append((rule, kind, tuple(pairs)))
    return found


def own_slots(found):
    w, n = lax.axis_index("wide"), lax.axis_index("narrow")
    wide, narrow = lax.axis_size("wide"), lax.axis_size("narrow")
    slots = [rule(w, n, kind) for rule, kind, _ in found]
    return [(slot, has_partner(w, n, slot, wide, narrow) == 1) for slot in slots]


def swap(messages, found):
    return [lax.ppermute(m, ("wide", "narrow"), list(f[-1])) for m, f in zip(messages, found)]


def mm(a, b):
    return jnp.dot(a, b, preferred_element_type=F32)


def mm_t(a, b):
    return lax.dot_general(a, b, (((1,), (1,)), ((), ())), preferred_element_type=F32)


def iota(shape, dim):
    return lax.broadcasted_iota(jnp.int32, shape, dim)


def call(body, outs, args, scratch=(), specs=None, flops=0, limit=8, out_specs=None):
    size = sum(a.size * a.dtype.itemsize for a in args)
    return pl.pallas_call(
        body,
        out_shape=outs,
        in_specs=specs or [VM] * len(args),
        out_specs=out_specs or [VM] * len(outs),
        scratch_shapes=list(scratch),
        compiler_params=pltpu.CompilerParams(vmem_limit_bytes=limit * 1024 * 1024),
        cost_estimate=pl.CostEstimate(flops=flops, bytes_accessed=size, transcendentals=0),
    )(*args)


def join_halo(got):
    pieces = [piece[...] for piece in got]
    return jnp.concatenate(pieces + [jnp.zeros_like(pieces[0])] * (4 - len(pieces)), axis=0)


def send(messages, values):
    width = messages[0].shape[0]
    for m, message in enumerate(messages):
        message[...] = values[m * width:(m + 1) * width, :].astype(BF)


def keep_split(high_ref, low_ref, rows, value):
    high = value.astype(BF)
    high_ref[rows] = high
    low_ref[rows] = (value - high.astype(F32)).astype(BF)


def select_body(found, own, send_ref, select_ref):
    width = send_ref.shape[1]
    diagonal = iota((width, width), 0) == iota((width, width), 1)
    pieces = []
    for slot, paired in own_slots(found):
        rows = jnp.where(paired, send_ref[pl.ds(slot, 1), :], -1).astype(F32)
        pieces.append(jnp.where(diagonal, rows, 0.0))
    column = jnp.sum(jnp.concatenate(pieces, axis=0), axis=1, keepdims=True).astype(jnp.int32)
    select_ref[...] = (iota((len(found) * width, own), 1) == column).astype(F32).astype(BF)


def pick_body(select_ref, rhs_ref, *messages):
    send(messages, mm(select_ref[...], rhs_ref[...]))


def setup_body(found, width, cols_ref, inverse_ref, blocks_ref, rhs_ref, select_ref, *rest):
    inverse_halo_ref, blocks_halo_ref, inverse_sent_ref, blocks_sent_ref, state_ref, base_ref = rest[:6]
    high_ref, low_ref = rest[6:]
    own = rhs_ref.shape[0]
    halo = 4 * width
    places = iota((1, halo), 1)
    starts = jnp.full((1, halo), -halo, jnp.int32)
    for m, (slot, _) in enumerate(own_slots(found)):
        here = lax.div(places, width) == m
        starts = jnp.where(here, slot * width + lax.rem(places, width), starts)
    arrange = (iota((halo, halo), 0) == starts).astype(F32).astype(BF)
    rows, links, size, _ = blocks_ref.shape
    for j in range(rows):
        here = slice(j * size, (j + 1) * size)
        columns = [cols_ref[j, k] for k in range(links)]
        for c in range(halo // size):
            total = None
            for k in range(links):
                part = jnp.where(columns[k] == own // size + c, blocks_ref[j, k].astype(F32), 0.0)
                total = part if total is None else total + part
            lanes = slice(c * size, (c + 1) * size)
            keep_split(high_ref, low_ref, (here, lanes), total)
    for part, half_ref in enumerate((high_ref, low_ref)):
        blocks_halo_ref[part] = mm(half_ref[...], arrange).astype(BF)
    step = own // 2
    for i in range(0, own, step):
        here = slice(i, i + step)
        inverse_halo_ref[here, :] = mm(inverse_ref[here, own:], arrange).astype(BF)
        value = mm(inverse_ref[here, :own], rhs_ref[...])
        state_ref[here, :] = value
        keep_split(high_ref, low_ref, here, value)
    inverse_sent_ref[...] = mm(select_ref[...], inverse_halo_ref[...]).astype(BF)
    sent = select_ref.shape[0]
    for part in range(2):
        here = slice(part * sent, (part + 1) * sent)
        blocks_sent_ref[here, :] = mm(select_ref[...], blocks_halo_ref[part]).astype(BF)
    base_ref[...] = mm(select_ref[...], high_ref[...]) + mm(select_ref[...], low_ref[...])


def sent_update_body(count, base_ref, sent_ref, *rest):
    got, messages = rest[:count], rest[count:]
    send(messages, base_ref[...] + mm(sent_ref[...], join_halo(got)))


def sent_residual_body(count, turn, base_ref, sent_ref, *rest):
    got, messages = rest[:count], rest[count:]
    halo = join_halo(got[turn:] + got[:turn])
    part = mm(sent_ref[...], halo)
    sent = base_ref.shape[0]
    send(messages, base_ref[...] - (part[:sent] + part[sent:]))


def update_body(count, cols_ref, state_ref, inverse_halo_ref, blocks_ref, rhs_ref, select_ref, *rest):
    got, (iterate_ref, part_ref, base_ref, sub_ref, high_ref, low_ref) = rest[:count], rest[count:]
    own = state_ref.shape[0]
    halo = join_halo(got)
    step = own // 2
    for i in range(0, own, step):
        here = slice(i, i + step)
        value = state_ref[here, :] + mm(inverse_halo_ref[here, :], halo)
        iterate_ref[here, :] = value
        sub_ref[here, :] = value.astype(BF)
    sub_ref[own:, :] = jnp.zeros((sub_ref.shape[0] - own, sub_ref.shape[1]), BF)
    rows, links, size, _ = blocks_ref.shape
    for j in range(rows):
        starts = [pl.multiple_of(cols_ref[j, k] * size, size) for k in range(links)]
        values = jnp.concatenate([blocks_ref[j, k] for k in range(links)], axis=1)
        coupled = jnp.concatenate([sub_ref[pl.ds(start, size), :] for start in starts], axis=0)
        total = mm(values, coupled)
        here = slice(j * size, (j + 1) * size)
        value = rhs_ref[here, :].astype(F32) - total
        part_ref[here, :] = value
        keep_split(high_ref, low_ref, here, value)
    base_ref[...] = mm(select_ref[...], high_ref[...]) + mm(select_ref[...], low_ref[...])


def residual_body(count, turn, part_ref, blocks_halo_ref, iterate_ref, inverse_ref, select_ref, *rest):
    got, rest = rest[:count], list(rest[count:])
    state_ref = rest.pop(0)
    resid_ref, *split = rest[-3:] if len(rest) == 4 else rest
    own = part_ref.shape[0]
    halo = join_halo(got[turn:] + got[:turn])
    step = own // 2
    for i in range(0, own, step):
        here = slice(i, i + step)
        outer = mm(blocks_halo_ref[0, here, :], halo) + mm(blocks_halo_ref[1, here, :], halo)
        resid_ref[here, :] = (part_ref[here, :] - outer).astype(BF)
    for i in range(0, own, step):
        here = slice(i, i + step)
        value = iterate_ref[here, :] + mm(inverse_ref[here, :own], resid_ref[...])
        state_ref[here, :] = value
        if split:
            keep_split(*split, here, value)
    if split:
        rest[0][...] = mm(select_ref[...], split[0][...]) + mm(select_ref[...], split[1][...])


def last_update_body(count, state_ref, inverse_halo_ref, *rest):
    got, (round_ref,) = rest[:count], rest[count:]
    halo = join_halo(got)
    step = state_ref.shape[0] // 2
    for i in range(0, state_ref.shape[0], step):
        here = slice(i, i + step)
        round_ref[here, :] = (state_ref[here, :] + mm(inverse_halo_ref[here, :], halo)).astype(BF)


def turn_body(state_ref, order_ref, turned_ref):
    value = state_ref[...]
    high = value.astype(BF)
    low = (value - high.astype(F32)).astype(BF)
    columns = value.shape[1]
    both = mm(jnp.concatenate([high, low], axis=1).T, order_ref[...])
    turned_ref[...] = both[:columns] + both[columns:]


def wire_body(count, turned_ref, halo_table_ref, *rest):
    got, (wire_ref,) = rest[:count], rest[count:]
    wire_ref[...] = (turned_ref[...] + mm(join_halo(got).T, halo_table_ref[...])).astype(BF)


def one_hot(rows_of, shape):
    return (iota(shape, 0) == rows_of(iota((1, shape[1]), 1))).astype(F32).astype(BF)


def order_body(inverse_halo_ref, order_ref, halo_table_ref):
    own = order_ref.shape[0]
    tile = own // ZL
    order_ref[...] = one_hot(lambda k: lax.rem(k, ZL) * tile + lax.div(k, ZL), (own, own))
    halo_table_ref[...] = mm(inverse_halo_ref[...].T, order_ref[...]).astype(BF)


def tables_body(wide, narrow, cov_plane_ref, cov_vert_ref, plane_ref, spread_ref, vert_ref):
    plane = plane_ref.shape[0]
    tile = plane // wide
    turn = one_hot(lambda k: lax.rem(k, wide) * tile + lax.div(k, wide), (plane, plane))
    half = mm(cov_plane_ref[...], turn).astype(BF)
    plane_ref[...] = mm(half.T, turn).astype(BF).T
    share = LANES // ZL
    depth = narrow * ZL
    width = narrow * LANES

    def source(k):
        e, n, l = lax.div(k, depth), lax.rem(lax.div(k, ZL), narrow), lax.rem(k, ZL)
        return n * LANES + e * ZL + l

    spread = one_hot(source, (width, width))
    spread_ref[...] = spread
    turned = cov_vert_ref[...].astype(F32).T
    zero = jnp.zeros_like(turned)
    blocks = jnp.concatenate(
        [jnp.concatenate([turned if i == e else zero for i in range(share)], axis=1) for e in range(share)],
        axis=0,
    ).astype(BF)
    vert_ref[...] = mm_t(blocks, spread).astype(BF)


def mix_body(wide, narrow, group, in_ref, plane_ref, spread_ref, vert_ref, state_ref, inverse_halo_ref, *rest):
    got, (out_ref, adjoint_hbm, cells_ref, flat_ref, wire_ref, round_ref, sem) = rest[:-7], rest[-7:]
    last_update_body(len(got), state_ref, inverse_halo_ref, *got, round_ref)
    keep = pltpu.make_async_copy(round_ref, adjoint_hbm, sem)
    keep.start()
    own = in_ref.shape[1]
    tile = own // ZL
    share = LANES // ZL
    depth = narrow * ZL
    block = wide * group
    for g in range(tile // share):
        lanes = slice(g * LANES, (g + 1) * LANES)
        joined = jnp.concatenate([in_ref[n * block:(n + 1) * block, lanes] for n in range(narrow)], axis=1)
        spread = mm(joined, spread_ref[...])
        for e in range(share):
            cells_ref[g * share + e] = spread[:, e * depth:(e + 1) * depth]
    for r in range(group):
        for c in range(tile):
            flat_ref[c * wide:(c + 1) * wide, r * depth:(r + 1) * depth] = cells_ref[
                c, pl.ds(r, wide, stride=group), :
            ].astype(BF)
    planar = mm(plane_ref[...], flat_ref[...]).astype(BF)
    for g in range(tile // share):
        stacked = jnp.concatenate(
            [
                jnp.concatenate(
                    [
                        planar[c * wide:(c + 1) * wide, r * depth:(r + 1) * depth]
                        for c in range(g * share, (g + 1) * share)
                    ],
                    axis=1,
                )
                for r in range(group)
            ],
            axis=0,
        )
        mixed = mm(stacked, vert_ref[...])
        for r in range(group):
            for n in range(narrow):
                wire_ref[g, pl.ds(n * block + r, wide, stride=group), :] = mixed[
                    r * wide:(r + 1) * wide, n * LANES:(n + 1) * LANES
                ]
        out_ref[:, g * LANES:(g + 1) * LANES] = wire_ref[g].astype(BF)
    keep.wait()


def unwire_body(in_ref, order_ref, out_hbm, out_ref, sems):
    step = out_ref.shape[0] // 3
    copies = []
    for n, i in enumerate(range(0, out_ref.shape[0], step)):
        here = pl.ds(i, step)
        out_ref[here, :] = mm_t(order_ref[here, :], in_ref[...]).astype(BF)
        copy = pltpu.make_async_copy(out_ref.at[here], out_hbm.at[here], sems.at[n])
        copy.start()
        copies.append(copy)
    for copy in copies:
        copy.wait()


def column_tables(inverse_halo, cov_plane, cov_vert):
    own, halo = inverse_halo.shape
    wide, narrow = lax.axis_size("wide"), lax.axis_size("narrow")
    width = narrow * LANES
    plane = cov_plane.shape[0]
    shape = jax.ShapeDtypeStruct
    order = call(order_body, [shape((own, own), BF), shape((halo, own), BF)], [inverse_halo])
    rest = call(
        functools.partial(tables_body, wide, narrow),
        [shape((plane, plane), BF), shape((width, width), BF), shape((width, width), BF)],
        [cov_plane, cov_vert],
    )
    return [tuple(order), tuple(rest)]


def smooth_by_columns(state, inverse_halo, got, tables):
    wide, narrow = lax.axis_size("wide"), lax.axis_size("narrow")
    own, columns = state.shape
    devices = wide * narrow
    group = columns // devices
    depth = narrow * ZL
    tile = own // ZL
    shape = jax.ShapeDtypeStruct
    (order, halo_table), (plane_mix, spread, vert_mix) = tables
    (turned,) = call(turn_body, [shape((columns, own), F32)], [state, order])
    (wire,) = call(functools.partial(wire_body, len(got)), [shape((columns, own), BF)], [turned, halo_table, *got])
    there = lax.all_to_all(
        wire.reshape(devices, group, own), ("narrow", "wide"), split_axis=0, concat_axis=0, tiled=True
    )
    mixed, adjoint = call(
        functools.partial(mix_body, wide, narrow, group),
        [shape((columns, own), BF), shape((own, columns), BF)],
        [there.reshape(columns, own), plane_mix, spread, vert_mix, state, inverse_halo, *got],
        [
            pltpu.VMEM((tile, wide * group, depth), F32),
            pltpu.VMEM((plane_mix.shape[0], group * depth), BF),
            pltpu.VMEM((own // LANES, columns, LANES), F32),
            pltpu.VMEM((own, columns), BF),
            pltpu.SemaphoreType.DMA,
        ],
        out_specs=[VM, ANY],
    )
    back = lax.all_to_all(
        mixed.reshape(devices, group, own), ("narrow", "wide"), split_axis=0, concat_axis=0, tiled=True
    )
    (smoothed,) = call(
        unwire_body,
        [shape((own, columns), BF)],
        [back.reshape(columns, own), order],
        [pltpu.VMEM((own, columns), BF), pltpu.SemaphoreType.DMA((3,))],
        out_specs=[ANY],
    )
    return adjoint, smoothed


def smooth_by_layers(adjoint, cov_plane, cov_vert):
    own, columns = adjoint.shape
    layered = adjoint.reshape(ZL, own // ZL, -1)
    planar = jnp.einsum(
        "pq,lqr->lpr",
        cov_plane,
        lax.all_to_all(layered, "wide", split_axis=0, concat_axis=1, tiled=True),
        preferred_element_type=F32,
    ).astype(BF)
    restored = lax.all_to_all(planar, "wide", split_axis=1, concat_axis=0, tiled=True)
    slab_weights = lax.dynamic_slice_in_dim(cov_vert, lax.axis_index("narrow") * ZL, ZL, 0)
    summed = jnp.dot(
        slab_weights,
        lax.all_gather(restored.reshape(ZL, -1), "narrow", axis=0, tiled=True),
        preferred_element_type=F32,
    )
    return summed.astype(BF).reshape(own, -1)


def shards(adjoint_rhs, inverse_rows, blocks, block_cols, send_rows, cov_plane, cov_vert):
    rhs = adjoint_rhs[0, 0]
    inverse = inverse_rows[0, 0]
    block_values = blocks[0, 0]
    cols = block_cols[0, 0]
    send_index = send_rows[0, 0]
    own, columns = rhs.shape
    width = send_index.shape[1]
    halo = 4 * width
    wide, narrow = lax.axis_size("wide"), lax.axis_size("narrow")
    group = columns // (wide * narrow)
    by_columns = columns % (wide * narrow) == 0 and group % 8 == 0 and narrow * ZL == LANES and wide % 16 == 0
    found = matchings()
    count = len(found)
    sent = count * width
    shape = jax.ShapeDtypeStruct
    notes = [shape((width, columns), BF)] * count
    full = shape((own, columns), F32)
    base_shape = shape((sent, columns), F32)
    cell_space = pltpu.VMEM((own, columns), BF)
    (select,) = call(
        functools.partial(select_body, found, own),
        [shape((sent, own), BF)],
        [send_index],
        flops=SELECT_FLOPS,
    )
    messages = call(pick_body, notes, [select, rhs], flops=PICK_FLOPS)
    got = swap(messages, found)
    inverse_halo, blocks_halo, inverse_sent, blocks_sent, state, base = call(
        functools.partial(setup_body, found, width),
        [
            shape((own, halo), BF),
            shape((2, own, halo), BF),
            shape((sent, halo), BF),
            shape((2 * sent, halo), BF),
            full,
            base_shape,
        ],
        [cols, inverse, block_values, rhs, select],
        [cell_space, cell_space],
        limit=12,
    )
    tables = column_tables(inverse_halo, cov_plane, cov_vert) if by_columns else []
    for sweep in range(SWEEPS - 1):
        messages = call(
            functools.partial(sent_update_body, count), notes, [base, inverse_sent, *got], limit=4
        )
        arrived, got = got, swap(messages, found)
        iterate, part, base = call(
            functools.partial(update_body, count),
            [full, full, base_shape],
            [cols, state, inverse_halo, block_values, rhs, select, *arrived],
            [pltpu.VMEM((own + halo, columns), BF), cell_space, cell_space],
        )
        turn = 1 if sweep == 1 and count == 3 else 0
        arrived = got[count - turn:] + got[:count - turn]
        messages = call(
            functools.partial(sent_residual_body, count, turn),
            notes,
            [base, blocks_sent, *arrived],
            limit=4,
        )
        got = swap(messages, found)
        if sweep < len(tables):
            tables[sweep], part = lax.optimization_barrier((tables[sweep], part))
        more = sweep < SWEEPS - 2
        state, *bases = call(
            functools.partial(residual_body, count, turn),
            [full] + [base_shape] * more,
            [part, blocks_halo, iterate, inverse, select, *arrived],
            [cell_space] * (1 + 2 * more),
        )
        base = bases[0] if more else None
    if by_columns:
        adjoint, smoothed = smooth_by_columns(state, inverse_halo, got, tables)
    else:
        cells = shape((own, columns), BF)
        (adjoint,) = call(functools.partial(last_update_body, count), [cells], [state, inverse_halo, *got])
        smoothed = smooth_by_layers(adjoint, cov_plane, cov_vert)
    return (adjoint[None, None], smoothed[None, None])


def solution(mesh):
    in_specs = (
        P("wide", "narrow", None, None),
        P("wide", "narrow", None, None),
        P("wide", "narrow", None, None, None, None),
        P("wide", "narrow", None, None),
        P("wide", "narrow", None, None),
        P(),
        P(),
    )
    out_specs = (P("wide", "narrow", None, None), P("wide", "narrow", None, None))
    return jax.shard_map(shards, mesh=mesh, in_specs=in_specs, out_specs=out_specs, check_vma=False)
```

```python
import functools

import jax
import jax.numpy as jnp
from jax import lax
from jax.experimental import pallas as pl
from jax.experimental.pallas import tpu as pltpu
from jax.sharding import PartitionSpec as P

ZL = 64
SWEEPS = 4
LANES = 128
SELECT_FLOPS = 6 * 10 ** 8
PICK_FLOPS = 2 * 10 ** 9
BF = jnp.bfloat16
F32 = jnp.float32
VM = pl.BlockSpec(memory_space=pltpu.VMEM)
ANY = pl.BlockSpec(memory_space=pl.ANY)


def wide_slot(w, n, parity):
    return (w & 1) ^ parity ^ 1


def narrow_slot(w, n, parity):
    return 2 + ((n & 1) ^ parity ^ 1)


def mixed_slot(w, n, kind):
    turn = (w ^ (w >> 1) ^ kind) & 1
    return (1 - turn) * wide_slot(w, n, 1) + turn * narrow_slot(w, n, 0)


def has_partner(w, n, slot, wide, narrow):
    inside = [w > 0, w + 1 < wide, n > 0, n + 1 < narrow]
    return sum((slot == k) * inside[k] for k in range(4))


def matchings():
    wide, narrow = lax.axis_size("wide"), lax.axis_size("narrow")
    if narrow == 2 and wide % 4 == 0:
        rules = [(mixed_slot, 0), (mixed_slot, 1), (wide_slot, 0)]
    else:
        rules = [(wide_slot, 1)] * (wide > 2) + [(narrow_slot, 1)] * (narrow > 2)
        rules += [(narrow_slot, 0)] * (narrow > 1) + [(wide_slot, 0)] * (wide > 1)
    found = []
    for rule, kind in rules:
        pairs = []
        for w in range(wide):
            for n in range(narrow):
                slot = rule(w, n, kind)
                if has_partner(w, n, slot, wide, narrow):
                    step = ((-1, 0), (1, 0), (0, -1), (0, 1))[slot]
                    target = (w + step[0], n + step[1])
                elif slot < 2:
                    target = (w, n ^ 1 if n ^ 1 < narrow else n)
                else:
                    target = (w ^ 1 if w ^ 1 < wide else w, n)
                pairs.append((w * narrow + n, target[0] * narrow + target[1]))
        found.append((rule, kind, tuple(pairs)))
    return found


def own_slots(found):
    w, n = lax.axis_index("wide"), lax.axis_index("narrow")
    wide, narrow = lax.axis_size("wide"), lax.axis_size("narrow")
    slots = [rule(w, n, kind) for rule, kind, _ in found]
    return [(slot, has_partner(w, n, slot, wide, narrow) == 1) for slot in slots]


def swap(messages, found):
    return [lax.ppermute(m, ("wide", "narrow"), list(f[-1])) for m, f in zip(messages, found)]


def mm(a, b):
    return jnp.dot(a, b, preferred_element_type=F32)


def mm_t(a, b):
    return lax.dot_general(a, b, (((1,), (1,)), ((), ())), preferred_element_type=F32)


def iota(shape, dim):
    return lax.broadcasted_iota(jnp.int32, shape, dim)


def call(body, outs, args, scratch=(), specs=None, flops=0, limit=8, out_specs=None):
    size = sum(a.size * a.dtype.itemsize for a in args)
    return pl.pallas_call(
        body,
        out_shape=outs,
        in_specs=specs or [VM] * len(args),
        out_specs=out_specs or [VM] * len(outs),
        scratch_shapes=list(scratch),
        compiler_params=pltpu.CompilerParams(vmem_limit_bytes=limit * 1024 * 1024),
        cost_estimate=pl.CostEstimate(flops=flops, bytes_accessed=size, transcendentals=0),
    )(*args)


def join_halo(got):
    pieces = [piece[...] for piece in got]
    return jnp.concatenate(pieces + [jnp.zeros_like(pieces[0])] * (4 - len(pieces)), axis=0)


def send(messages, values):
    width = messages[0].shape[0]
    for m, message in enumerate(messages):
        message[...] = values[m * width:(m + 1) * width, :].astype(BF)


def keep_split(high_ref, low_ref, rows, value):
    high = value.astype(BF)
    high_ref[rows] = high
    low_ref[rows] = (value - high.astype(F32)).astype(BF)


def select_body(found, own, send_ref, select_ref):
    width = send_ref.shape[1]
    diagonal = iota((width, width), 0) == iota((width, width), 1)
    pieces = []
    for slot, paired in own_slots(found):
        rows = jnp.where(paired, send_ref[pl.ds(slot, 1), :], -1).astype(F32)
        pieces.append(jnp.where(diagonal, rows, 0.0))
    column = jnp.sum(jnp.concatenate(pieces, axis=0), axis=1, keepdims=True).astype(jnp.int32)
    select_ref[...] = (iota((len(found) * width, own), 1) == column).astype(F32).astype(BF)


def pick_body(select_ref, rhs_ref, *messages):
    send(messages, mm(select_ref[...], rhs_ref[...]))


def setup_body(found, width, cols_ref, inverse_ref, blocks_ref, rhs_ref, select_ref, *rest):
    inverse_halo_ref, blocks_halo_ref, inverse_sent_ref, blocks_sent_ref, state_ref, base_ref = rest[:6]
    high_ref, low_ref = rest[6:]
    own = rhs_ref.shape[0]
    halo = 4 * width
    places = iota((1, halo), 1)
    starts = jnp.full((1, halo), -halo, jnp.int32)
    for m, (slot, _) in enumerate(own_slots(found)):
        here = lax.div(places, width) == m
        starts = jnp.where(here, slot * width + lax.rem(places, width), starts)
    arrange = (iota((halo, halo), 0) == starts).astype(F32).astype(BF)
    rows, links, size, _ = blocks_ref.shape
    for j in range(rows):
        here = slice(j * size, (j + 1) * size)
        columns = [cols_ref[j, k] for k in range(links)]
        for c in range(halo // size):
            total = None
            for k in range(links):
                part = jnp.where(columns[k] == own // size + c, blocks_ref[j, k].astype(F32), 0.0)
                total = part if total is None else total + part
            lanes = slice(c * size, (c + 1) * size)
            keep_split(high_ref, low_ref, (here, lanes), total)
    for part, half_ref in enumerate((high_ref, low_ref)):
        blocks_halo_ref[part] = mm(half_ref[...], arrange).astype(BF)
    step = own // 2
    for i in range(0, own, step):
        here = slice(i, i + step)
        inverse_halo_ref[here, :] = mm(inverse_ref[here, own:], arrange).astype(BF)
        value = mm(inverse_ref[here, :own], rhs_ref[...])
        state_ref[here, :] = value
        keep_split(high_ref, low_ref, here, value)
    inverse_sent_ref[...] = mm(select_ref[...], inverse_halo_ref[...]).astype(BF)
    sent = select_ref.shape[0]
    for part in range(2):
        here = slice(part * sent, (part + 1) * sent)
        blocks_sent_ref[here, :] = mm(select_ref[...], blocks_halo_ref[part]).astype(BF)
    base_ref[...] = mm(select_ref[...], high_ref[...]) + mm(select_ref[...], low_ref[...])


def sent_update_body(count, base_ref, sent_ref, *rest):
    got, messages = rest[:count], rest[count:]
    send(messages, base_ref[...] + mm(sent_ref[...], join_halo(got)))


def sent_residual_body(count, turn, base_ref, sent_ref, *rest):
    got, messages = rest[:count], rest[count:]
    halo = join_halo(got[turn:] + got[:turn])
    part = mm(sent_ref[...], halo)
    sent = base_ref.shape[0]
    send(messages, base_ref[...] - (part[:sent] + part[sent:]))


def update_body(count, cols_ref, state_ref, inverse_halo_ref, blocks_ref, rhs_ref, select_ref, *rest):
    got, (iterate_ref, part_ref, base_ref, sub_ref, high_ref, low_ref) = rest[:count], rest[count:]
    own = state_ref.shape[0]
    halo = join_halo(got)
    step = own // 2
    for i in range(0, own, step):
        here = slice(i, i + step)
        value = state_ref[here, :] + mm(inverse_halo_ref[here, :], halo)
        iterate_ref[here, :] = value
        sub_ref[here, :] = value.astype(BF)
    sub_ref[own:, :] = jnp.zeros((sub_ref.shape[0] - own, sub_ref.shape[1]), BF)
    rows, links, size, _ = blocks_ref.shape
    for j in range(rows):
        starts = [pl.multiple_of(cols_ref[j, k] * size, size) for k in range(links)]
        values = jnp.concatenate([blocks_ref[j, k] for k in range(links)], axis=1)
        coupled = jnp.concatenate([sub_ref[pl.ds(start, size), :] for start in starts], axis=0)
        total = mm(values, coupled)
        here = slice(j * size, (j + 1) * size)
        value = rhs_ref[here, :].astype(F32) - total
        part_ref[here, :] = value
        keep_split(high_ref, low_ref, here, value)
    base_ref[...] = mm(select_ref[...], high_ref[...]) + mm(select_ref[...], low_ref[...])


def residual_body(count, turn, part_ref, blocks_halo_ref, iterate_ref, inverse_ref, select_ref, *rest):
    got, rest = rest[:count], list(rest[count:])
    state_ref = rest.pop(0)
    resid_ref, *split = rest[-3:] if len(rest) == 4 else rest
    own = part_ref.shape[0]
    halo = join_halo(got[turn:] + got[:turn])
    step = own // 2
    for i in range(0, own, step):
        here = slice(i, i + step)
        outer = mm(blocks_halo_ref[0, here, :], halo) + mm(blocks_halo_ref[1, here, :], halo)
        resid_ref[here, :] = (part_ref[here, :] - outer).astype(BF)
    for i in range(0, own, step):
        here = slice(i, i + step)
        value = iterate_ref[here, :] + mm(inverse_ref[here, :own], resid_ref[...])
        state_ref[here, :] = value
        if split:
            keep_split(*split, here, value)
    if split:
        rest[0][...] = mm(select_ref[...], split[0][...]) + mm(select_ref[...], split[1][...])


def last_update_body(count, state_ref, inverse_halo_ref, *rest):
    got, (round_ref,) = rest[:count], rest[count:]
    halo = join_halo(got)
    step = state_ref.shape[0] // 2
    for i in range(0, state_ref.shape[0], step):
        here = slice(i, i + step)
        round_ref[here, :] = (state_ref[here, :] + mm(inverse_halo_ref[here, :], halo)).astype(BF)


def turn_body(state_ref, order_ref, turned_ref):
    value = state_ref[...]
    high = value.astype(BF)
    low = (value - high.astype(F32)).astype(BF)
    columns = value.shape[1]
    both = mm(jnp.concatenate([high, low], axis=1).T, order_ref[...])
    turned_ref[...] = both[:columns] + both[columns:]


def wire_body(count, turned_ref, halo_table_ref, *rest):
    got, (wire_ref,) = rest[:count], rest[count:]
    wire_ref[...] = (turned_ref[...] + mm(join_halo(got).T, halo_table_ref[...])).astype(BF)


def one_hot(rows_of, shape):
    return (iota(shape, 0) == rows_of(iota((1, shape[1]), 1))).astype(F32).astype(BF)


def order_body(inverse_halo_ref, order_ref, halo_table_ref):
    own = order_ref.shape[0]
    tile = own // ZL
    order_ref[...] = one_hot(lambda k: lax.rem(k, ZL) * tile + lax.div(k, ZL), (own, own))
    halo_table_ref[...] = mm(inverse_halo_ref[...].T, order_ref[...]).astype(BF)


def tables_body(wide, narrow, cov_plane_ref, cov_vert_ref, plane_ref, spread_ref, vert_ref):
    plane = plane_ref.shape[0]
    tile = plane // wide
    turn = one_hot(lambda k: lax.rem(k, wide) * tile + lax.div(k, wide), (plane, plane))
    half = mm(cov_plane_ref[...], turn).astype(BF)
    plane_ref[...] = mm(half.T, turn).astype(BF).T
    share = LANES // ZL
    depth = narrow * ZL
    width = narrow * LANES

    def source(k):
        e, n, l = lax.div(k, depth), lax.rem(lax.div(k, ZL), narrow), lax.rem(k, ZL)
        return n * LANES + e * ZL + l

    spread = one_hot(source, (width, width))
    spread_ref[...] = spread
    turned = cov_vert_ref[...].astype(F32).T
    zero = jnp.zeros_like(turned)
    blocks = jnp.concatenate(
        [jnp.concatenate([turned if i == e else zero for i in range(share)], axis=1) for e in range(share)],
        axis=0,
    ).astype(BF)
    vert_ref[...] = mm_t(blocks, spread).astype(BF)


def mix_body(wide, narrow, group, in_ref, plane_ref, spread_ref, vert_ref, state_ref, inverse_halo_ref, *rest):
    got, (out_ref, adjoint_hbm, cells_ref, flat_ref, wire_ref, round_ref, sem) = rest[:-7], rest[-7:]
    last_update_body(len(got), state_ref, inverse_halo_ref, *got, round_ref)
    keep = pltpu.make_async_copy(round_ref, adjoint_hbm, sem)
    keep.start()
    own = in_ref.shape[1]
    tile = own // ZL
    share = LANES // ZL
    depth = narrow * ZL
    block = wide * group
    for g in range(tile // share):
        lanes = slice(g * LANES, (g + 1) * LANES)
        joined = jnp.concatenate([in_ref[n * block:(n + 1) * block, lanes] for n in range(narrow)], axis=1)
        spread = mm(joined, spread_ref[...])
        for e in range(share):
            cells_ref[g * share + e, :block, :] = spread[:, e * depth:(e + 1) * depth]
    for r in range(group):
        for c in range(tile):
            flat_ref[c * wide:(c + 1) * wide, r * depth:(r + 1) * depth] = cells_ref[
                c, pl.ds(r, wide, stride=group), :
            ].astype(BF)
    planar = mm(plane_ref[...], flat_ref[...]).astype(BF)
    for g in range(tile // share):
        stacked = jnp.concatenate(
            [
                jnp.concatenate(
                    [
                        planar[c * wide:(c + 1) * wide, r * depth:(r + 1) * depth]
                        for c in range(g * share, (g + 1) * share)
                    ],
                    axis=1,
                )
                for r in range(group)
            ],
            axis=0,
        )
        mixed = mm(stacked, vert_ref[...])
        for r in range(group):
            for n in range(narrow):
                wire_ref[g, pl.ds(n * block + r, wide, stride=group), :] = mixed[
                    r * wide:(r + 1) * wide, n * LANES:(n + 1) * LANES
                ]
        out_ref[:, g * LANES:(g + 1) * LANES] = wire_ref[g, :narrow * block, :].astype(BF)
    keep.wait()


def unwire_body(in_ref, order_ref, out_hbm, out_ref, sems):
    step = out_ref.shape[0] // 3
    turned = in_ref[...].T
    copies = []
    for n, i in enumerate(range(0, out_ref.shape[0], step)):
        here = pl.ds(i, step)
        out_ref[here, :] = mm(order_ref[here, :], turned).astype(BF)
        copy = pltpu.make_async_copy(out_ref.at[here], out_hbm.at[here], sems.at[n])
        copy.start()
        copies.append(copy)
    for copy in copies:
        copy.wait()


def column_tables(inverse_halo, cov_plane, cov_vert):
    own, halo = inverse_halo.shape
    wide, narrow = lax.axis_size("wide"), lax.axis_size("narrow")
    width = narrow * LANES
    plane = cov_plane.shape[0]
    shape = jax.ShapeDtypeStruct
    order = call(order_body, [shape((own, own), BF), shape((halo, own), BF)], [inverse_halo])
    rest = call(
        functools.partial(tables_body, wide, narrow),
        [shape((plane, plane), BF), shape((width, width), BF), shape((width, width), BF)],
        [cov_plane, cov_vert],
    )
    return [tuple(order), tuple(rest)]


def smooth_by_columns(state, inverse_halo, got, tables):
    wide, narrow = lax.axis_size("wide"), lax.axis_size("narrow")
    own, columns = state.shape
    devices = wide * narrow
    group = columns // devices
    depth = narrow * ZL
    tile = own // ZL
    shape = jax.ShapeDtypeStruct
    (order, halo_table), (plane_mix, spread, vert_mix) = tables
    (turned,) = call(turn_body, [shape((columns, own), F32)], [state, order])
    (wire,) = call(functools.partial(wire_body, len(got)), [shape((columns, own), BF)], [turned, halo_table, *got])
    there = lax.all_to_all(
        wire.reshape(devices, group, own), ("narrow", "wide"), split_axis=0, concat_axis=0, tiled=True
    )
    mixed, adjoint = call(
        functools.partial(mix_body, wide, narrow, group),
        [shape((columns, own), BF), shape((own, columns), BF)],
        [there.reshape(columns, own), plane_mix, spread, vert_mix, state, inverse_halo, *got],
        [
            pltpu.VMEM((tile, wide * group + group, depth), F32),
            pltpu.VMEM((plane_mix.shape[0], group * depth), BF),
            pltpu.VMEM((own // LANES, columns + group, LANES), F32),
            pltpu.VMEM((own, columns), BF),
            pltpu.SemaphoreType.DMA,
        ],
        out_specs=[VM, ANY],
    )
    back = lax.all_to_all(
        mixed.reshape(devices, group, own), ("narrow", "wide"), split_axis=0, concat_axis=0, tiled=True
    )
    (smoothed,) = call(
        unwire_body,
        [shape((own, columns), BF)],
        [back.reshape(columns, own), order],
        [pltpu.VMEM((own, columns), BF), pltpu.SemaphoreType.DMA((3,))],
        out_specs=[ANY],
    )
    return adjoint, smoothed


def smooth_by_layers(adjoint, cov_plane, cov_vert):
    own, columns = adjoint.shape
    layered = adjoint.reshape(ZL, own // ZL, -1)
    planar = jnp.einsum(
        "pq,lqr->lpr",
        cov_plane,
        lax.all_to_all(layered, "wide", split_axis=0, concat_axis=1, tiled=True),
        preferred_element_type=F32,
    ).astype(BF)
    restored = lax.all_to_all(planar, "wide", split_axis=1, concat_axis=0, tiled=True)
    slab_weights = lax.dynamic_slice_in_dim(cov_vert, lax.axis_index("narrow") * ZL, ZL, 0)
    summed = jnp.dot(
        slab_weights,
        lax.all_gather(restored.reshape(ZL, -1), "narrow", axis=0, tiled=True),
        preferred_element_type=F32,
    )
    return summed.astype(BF).reshape(own, -1)


def shards(adjoint_rhs, inverse_rows, blocks, block_cols, send_rows, cov_plane, cov_vert):
    rhs = adjoint_rhs[0, 0]
    inverse = inverse_rows[0, 0]
    block_values = blocks[0, 0]
    cols = block_cols[0, 0]
    send_index = send_rows[0, 0]
    own, columns = rhs.shape
    width = send_index.shape[1]
    halo = 4 * width
    wide, narrow = lax.axis_size("wide"), lax.axis_size("narrow")
    group = columns // (wide * narrow)
    by_columns = columns % (wide * narrow) == 0 and group % 8 == 0 and narrow * ZL == LANES and wide % 16 == 0
    found = matchings()
    count = len(found)
    sent = count * width
    shape = jax.ShapeDtypeStruct
    notes = [shape((width, columns), BF)] * count
    full = shape((own, columns), F32)
    base_shape = shape((sent, columns), F32)
    cell_space = pltpu.VMEM((own, columns), BF)
    (select,) = call(
        functools.partial(select_body, found, own),
        [shape((sent, own), BF)],
        [send_index],
        flops=SELECT_FLOPS,
    )
    messages = call(pick_body, notes, [select, rhs], flops=PICK_FLOPS)
    got = swap(messages, found)
    inverse_halo, blocks_halo, inverse_sent, blocks_sent, state, base = call(
        functools.partial(setup_body, found, width),
        [
            shape((own, halo), BF),
            shape((2, own, halo), BF),
            shape((sent, halo), BF),
            shape((2 * sent, halo), BF),
            full,
            base_shape,
        ],
        [cols, inverse, block_values, rhs, select],
        [cell_space, cell_space],
        limit=12,
    )
    tables = column_tables(inverse_halo, cov_plane, cov_vert) if by_columns else []
    for sweep in range(SWEEPS - 1):
        messages = call(
            functools.partial(sent_update_body, count), notes, [base, inverse_sent, *got], limit=4
        )
        arrived, got = got, swap(messages, found)
        iterate, part, base = call(
            functools.partial(update_body, count),
            [full, full, base_shape],
            [cols, state, inverse_halo, block_values, rhs, select, *arrived],
            [pltpu.VMEM((own + halo, columns), BF), cell_space, cell_space],
        )
        turn = 1 if sweep == 1 and count == 3 else 0
        arrived = got[count - turn:] + got[:count - turn]
        messages = call(
            functools.partial(sent_residual_body, count, turn),
            notes,
            [base, blocks_sent, *arrived],
            limit=4,
        )
        got = swap(messages, found)
        if sweep < len(tables):
            tables[sweep], part = lax.optimization_barrier((tables[sweep], part))
        more = sweep < SWEEPS - 2
        state, *bases = call(
            functools.partial(residual_body, count, turn),
            [full] + [base_shape] * more,
            [part, blocks_halo, iterate, inverse, select, *arrived],
            [cell_space] * (1 + 2 * more),
        )
        base = bases[0] if more else None
    if by_columns:
        adjoint, smoothed = smooth_by_columns(state, inverse_halo, got, tables)
    else:
        cells = shape((own, columns), BF)
        (adjoint,) = call(functools.partial(last_update_body, count), [cells], [state, inverse_halo, *got])
        smoothed = smooth_by_layers(adjoint, cov_plane, cov_vert)
    return (adjoint[None, None], smoothed[None, None])


def solution(mesh):
    in_specs = (
        P("wide", "narrow", None, None),
        P("wide", "narrow", None, None),
        P("wide", "narrow", None, None, None, None),
        P("wide", "narrow", None, None),
        P("wide", "narrow", None, None),
        P(),
        P(),
    )
    out_specs = (P("wide", "narrow", None, None), P("wide", "narrow", None, None))
    return jax.shard_map(shards, mesh=mesh, in_specs=in_specs, out_specs=out_specs, check_vma=False)
```

```python
import functools

import jax
import jax.numpy as jnp
from jax import lax
from jax.experimental import pallas as pl
from jax.experimental.pallas import tpu as pltpu
from jax.sharding import PartitionSpec as P

ZL = 64
SWEEPS = 4
LANES = 128
SELECT_FLOPS = 6 * 10 ** 8
PICK_FLOPS = 2 * 10 ** 9
BF = jnp.bfloat16
F32 = jnp.float32
VM = pl.BlockSpec(memory_space=pltpu.VMEM)
ANY = pl.BlockSpec(memory_space=pl.ANY)


def wide_slot(w, n, parity):
    return (w & 1) ^ parity ^ 1


def narrow_slot(w, n, parity):
    return 2 + ((n & 1) ^ parity ^ 1)


def mixed_slot(w, n, kind):
    turn = (w ^ (w >> 1) ^ kind) & 1
    return (1 - turn) * wide_slot(w, n, 1) + turn * narrow_slot(w, n, 0)


def has_partner(w, n, slot, wide, narrow):
    inside = [w > 0, w + 1 < wide, n > 0, n + 1 < narrow]
    return sum((slot == k) * inside[k] for k in range(4))


def matchings():
    wide, narrow = lax.axis_size("wide"), lax.axis_size("narrow")
    if narrow == 2 and wide % 4 == 0:
        rules = [(mixed_slot, 0), (mixed_slot, 1), (wide_slot, 0)]
    else:
        rules = [(wide_slot, 1)] * (wide > 2) + [(narrow_slot, 1)] * (narrow > 2)
        rules += [(narrow_slot, 0)] * (narrow > 1) + [(wide_slot, 0)] * (wide > 1)
    found = []
    for rule, kind in rules:
        pairs = []
        for w in range(wide):
            for n in range(narrow):
                slot = rule(w, n, kind)
                if has_partner(w, n, slot, wide, narrow):
                    step = ((-1, 0), (1, 0), (0, -1), (0, 1))[slot]
                    target = (w + step[0], n + step[1])
                elif slot < 2:
                    target = (w, n ^ 1 if n ^ 1 < narrow else n)
                else:
                    target = (w ^ 1 if w ^ 1 < wide else w, n)
                pairs.append((w * narrow + n, target[0] * narrow + target[1]))
        found.append((rule, kind, tuple(pairs)))
    return found


def own_slots(found):
    w, n = lax.axis_index("wide"), lax.axis_index("narrow")
    wide, narrow = lax.axis_size("wide"), lax.axis_size("narrow")
    slots = [rule(w, n, kind) for rule, kind, _ in found]
    return [(slot, has_partner(w, n, slot, wide, narrow) == 1) for slot in slots]


def swap(messages, found):
    return [lax.ppermute(m, ("wide", "narrow"), list(f[-1])) for m, f in zip(messages, found)]


def mm(a, b):
    return jnp.dot(a, b, preferred_element_type=F32)


def mm_t(a, b):
    return lax.dot_general(a, b, (((1,), (1,)), ((), ())), preferred_element_type=F32)


def iota(shape, dim):
    return lax.broadcasted_iota(jnp.int32, shape, dim)


def call(body, outs, args, scratch=(), specs=None, flops=0, limit=8, out_specs=None):
    size = sum(a.size * a.dtype.itemsize for a in args)
    return pl.pallas_call(
        body,
        out_shape=outs,
        in_specs=specs or [VM] * len(args),
        out_specs=out_specs or [VM] * len(outs),
        scratch_shapes=list(scratch),
        compiler_params=pltpu.CompilerParams(vmem_limit_bytes=limit * 1024 * 1024),
        cost_estimate=pl.CostEstimate(flops=flops, bytes_accessed=size, transcendentals=0),
    )(*args)


def reverse(k, count):
    bits = count.bit_length() - 1
    return sum(((k >> b) & 1) << (bits - 1 - b) for b in range(bits))


def exchange_columns(values):
    wide, narrow = lax.axis_size("wide"), lax.axis_size("narrow")
    order = [n * wide + reverse(p, wide) for n in range(narrow) for p in range(wide)]
    rows, lanes = values.shape
    cut = values.reshape(wide * narrow, -1, lanes)
    moved = lax.all_to_all(
        cut, ("narrow", "wide"), split_axis=0, concat_axis=0, axis_index_groups=[order], tiled=True
    )
    return moved.reshape(rows, lanes)


def join_halo(got):
    pieces = [piece[...] for piece in got]
    return jnp.concatenate(pieces + [jnp.zeros_like(pieces[0])] * (4 - len(pieces)), axis=0)


def send(messages, values):
    width = messages[0].shape[0]
    for m, message in enumerate(messages):
        message[...] = values[m * width:(m + 1) * width, :].astype(BF)


def keep_split(high_ref, low_ref, rows, value):
    high = value.astype(BF)
    high_ref[rows] = high
    low_ref[rows] = (value - high.astype(F32)).astype(BF)


def select_body(found, own, send_ref, select_ref):
    width = send_ref.shape[1]
    diagonal = iota((width, width), 0) == iota((width, width), 1)
    pieces = []
    for slot, paired in own_slots(found):
        rows = jnp.where(paired, send_ref[pl.ds(slot, 1), :], -1).astype(F32)
        pieces.append(jnp.where(diagonal, rows, 0.0))
    column = jnp.sum(jnp.concatenate(pieces, axis=0), axis=1, keepdims=True).astype(jnp.int32)
    select_ref[...] = (iota((len(found) * width, own), 1) == column).astype(F32).astype(BF)


def pick_body(select_ref, rhs_ref, *messages):
    send(messages, mm(select_ref[...], rhs_ref[...]))


def setup_body(found, width, cols_ref, inverse_ref, blocks_ref, rhs_ref, select_ref, *rest):
    inverse_halo_ref, blocks_halo_ref, inverse_sent_ref, blocks_sent_ref, state_ref, base_ref = rest[:6]
    high_ref, low_ref = rest[6:]
    own = rhs_ref.shape[0]
    halo = 4 * width
    places = iota((1, halo), 1)
    starts = jnp.full((1, halo), -halo, jnp.int32)
    for m, (slot, _) in enumerate(own_slots(found)):
        here = lax.div(places, width) == m
        starts = jnp.where(here, slot * width + lax.rem(places, width), starts)
    arrange = (iota((halo, halo), 0) == starts).astype(F32).astype(BF)
    rows, links, size, _ = blocks_ref.shape
    for j in range(rows):
        here = slice(j * size, (j + 1) * size)
        columns = [cols_ref[j, k] for k in range(links)]
        for c in range(halo // size):
            total = None
            for k in range(links):
                part = jnp.where(columns[k] == own // size + c, blocks_ref[j, k].astype(F32), 0.0)
                total = part if total is None else total + part
            lanes = slice(c * size, (c + 1) * size)
            keep_split(high_ref, low_ref, (here, lanes), total)
    for part, half_ref in enumerate((high_ref, low_ref)):
        blocks_halo_ref[part] = mm(half_ref[...], arrange).astype(BF)
    step = own // 2
    for i in range(0, own, step):
        here = slice(i, i + step)
        inverse_halo_ref[here, :] = mm(inverse_ref[here, own:], arrange).astype(BF)
        value = mm(inverse_ref[here, :own], rhs_ref[...])
        state_ref[here, :] = value
        keep_split(high_ref, low_ref, here, value)
    inverse_sent_ref[...] = mm(select_ref[...], inverse_halo_ref[...]).astype(BF)
    sent = select_ref.shape[0]
    for part in range(2):
        here = slice(part * sent, (part + 1) * sent)
        blocks_sent_ref[here, :] = mm(select_ref[...], blocks_halo_ref[part]).astype(BF)
    base_ref[...] = mm(select_ref[...], high_ref[...]) + mm(select_ref[...], low_ref[...])


def sent_update_body(count, base_ref, sent_ref, *rest):
    got, messages = rest[:count], rest[count:]
    send(messages, base_ref[...] + mm(sent_ref[...], join_halo(got)))


def sent_residual_body(count, turn, base_ref, sent_ref, *rest):
    got, messages = rest[:count], rest[count:]
    halo = join_halo(got[turn:] + got[:turn])
    part = mm(sent_ref[...], halo)
    sent = base_ref.shape[0]
    send(messages, base_ref[...] - (part[:sent] + part[sent:]))


def update_body(count, cols_ref, state_ref, inverse_halo_ref, blocks_ref, rhs_ref, select_ref, *rest):
    got, (iterate_ref, part_ref, base_ref, sub_ref, high_ref, low_ref) = rest[:count], rest[count:]
    own = state_ref.shape[0]
    halo = join_halo(got)
    step = own // 2
    for i in range(0, own, step):
        here = slice(i, i + step)
        value = state_ref[here, :] + mm(inverse_halo_ref[here, :], halo)
        iterate_ref[here, :] = value
        sub_ref[here, :] = value.astype(BF)
    sub_ref[own:, :] = jnp.zeros((sub_ref.shape[0] - own, sub_ref.shape[1]), BF)
    rows, links, size, _ = blocks_ref.shape
    for j in range(rows):
        starts = [pl.multiple_of(cols_ref[j, k] * size, size) for k in range(links)]
        values = jnp.concatenate([blocks_ref[j, k] for k in range(links)], axis=1)
        coupled = jnp.concatenate([sub_ref[pl.ds(start, size), :] for start in starts], axis=0)
        total = mm(values, coupled)
        here = slice(j * size, (j + 1) * size)
        value = rhs_ref[here, :].astype(F32) - total
        part_ref[here, :] = value
        keep_split(high_ref, low_ref, here, value)
    base_ref[...] = mm(select_ref[...], high_ref[...]) + mm(select_ref[...], low_ref[...])


def residual_body(count, turn, part_ref, blocks_halo_ref, iterate_ref, inverse_ref, select_ref, *rest):
    got, rest = rest[:count], list(rest[count:])
    state_ref = rest.pop(0)
    resid_ref, *split = rest[-3:] if len(rest) == 4 else rest
    own = part_ref.shape[0]
    halo = join_halo(got[turn:] + got[:turn])
    step = own // 2
    for i in range(0, own, step):
        here = slice(i, i + step)
        outer = mm(blocks_halo_ref[0, here, :], halo) + mm(blocks_halo_ref[1, here, :], halo)
        resid_ref[here, :] = (part_ref[here, :] - outer).astype(BF)
    for i in range(0, own, step):
        here = slice(i, i + step)
        value = iterate_ref[here, :] + mm(inverse_ref[here, :own], resid_ref[...])
        state_ref[here, :] = value
        if split:
            keep_split(*split, here, value)
    if split:
        rest[0][...] = mm(select_ref[...], split[0][...]) + mm(select_ref[...], split[1][...])


def last_update_body(count, state_ref, inverse_halo_ref, *rest):
    got, (round_ref,) = rest[:count], rest[count:]
    halo = join_halo(got)
    step = state_ref.shape[0] // 2
    for i in range(0, state_ref.shape[0], step):
        here = slice(i, i + step)
        round_ref[here, :] = (state_ref[here, :] + mm(inverse_halo_ref[here, :], halo)).astype(BF)


def turn_body(state_ref, order_ref, turned_ref):
    value = state_ref[...]
    high = value.astype(BF)
    low = (value - high.astype(F32)).astype(BF)
    columns = value.shape[1]
    both = mm(jnp.concatenate([high, low], axis=1).T, order_ref[...])
    turned_ref[...] = both[:columns] + both[columns:]


def wire_body(count, turned_ref, halo_table_ref, *rest):
    got, (wire_ref,) = rest[:count], rest[count:]
    wire_ref[...] = (turned_ref[...] + mm(join_halo(got).T, halo_table_ref[...])).astype(BF)


def one_hot(rows_of, shape):
    return (iota(shape, 0) == rows_of(iota((1, shape[1]), 1))).astype(F32).astype(BF)


def order_body(inverse_halo_ref, order_ref, halo_table_ref):
    own = order_ref.shape[0]
    tile = own // ZL
    order_ref[...] = one_hot(lambda k: lax.rem(k, ZL) * tile + lax.div(k, ZL), (own, own))
    halo_table_ref[...] = mm(inverse_halo_ref[...].T, order_ref[...]).astype(BF)


def tables_body(wide, narrow, cov_plane_ref, cov_vert_ref, plane_ref, spread_ref, vert_ref):
    plane = plane_ref.shape[0]
    tile = plane // wide
    turn = one_hot(lambda k: reverse(lax.rem(k, wide), wide) * tile + lax.div(k, wide), (plane, plane))
    half = mm(cov_plane_ref[...], turn).astype(BF)
    plane_ref[...] = mm(half.T, turn).astype(BF).T
    share = LANES // ZL
    depth = narrow * ZL
    width = narrow * LANES

    def source(k):
        e, n, l = lax.div(k, depth), lax.rem(lax.div(k, ZL), narrow), lax.rem(k, ZL)
        return n * LANES + e * ZL + l

    spread = one_hot(source, (width, width))
    spread_ref[...] = spread
    turned = cov_vert_ref[...].astype(F32).T
    zero = jnp.zeros_like(turned)
    blocks = jnp.concatenate(
        [jnp.concatenate([turned if i == e else zero for i in range(share)], axis=1) for e in range(share)],
        axis=0,
    ).astype(BF)
    vert_ref[...] = mm_t(blocks, spread).astype(BF)


def mix_body(wide, narrow, group, in_ref, plane_ref, spread_ref, vert_ref, state_ref, inverse_halo_ref, *rest):
    got, (out_ref, adjoint_hbm, cells_ref, flat_ref, wire_ref, round_ref, sem) = rest[:-7], rest[-7:]
    last_update_body(len(got), state_ref, inverse_halo_ref, *got, round_ref)
    keep = pltpu.make_async_copy(round_ref, adjoint_hbm, sem)
    keep.start()
    own = in_ref.shape[1]
    tile = own // ZL
    share = LANES // ZL
    depth = narrow * ZL
    block = wide * group
    for g in range(tile // share):
        lanes = slice(g * LANES, (g + 1) * LANES)
        joined = jnp.concatenate([in_ref[n * block:(n + 1) * block, lanes] for n in range(narrow)], axis=1)
        spread = mm(joined, spread_ref[...])
        for e in range(share):
            cells_ref[g * share + e, :block, :] = spread[:, e * depth:(e + 1) * depth]
    for r in range(group):
        for c in range(tile):
            flat_ref[c * wide:(c + 1) * wide, r * depth:(r + 1) * depth] = cells_ref[
                c, pl.ds(r, wide, stride=group), :
            ].astype(BF)
    planar = mm(plane_ref[...], flat_ref[...]).astype(BF)
    for g in range(tile // share):
        stacked = jnp.concatenate(
            [
                jnp.concatenate(
                    [
                        planar[c * wide:(c + 1) * wide, r * depth:(r + 1) * depth]
                        for c in range(g * share, (g + 1) * share)
                    ],
                    axis=1,
                )
                for r in range(group)
            ],
            axis=0,
        )
        mixed = mm(stacked, vert_ref[...])
        for r in range(group):
            for n in range(narrow):
                wire_ref[g, pl.ds(n * block + r, wide, stride=group), :] = mixed[
                    r * wide:(r + 1) * wide, n * LANES:(n + 1) * LANES
                ]
        out_ref[:, g * LANES:(g + 1) * LANES] = wire_ref[g, :narrow * block, :].astype(BF)
    keep.wait()


def unwire_body(in_ref, order_ref, out_hbm, out_ref, sems):
    step = out_ref.shape[0] // 3
    turned = in_ref[...].T
    copies = []
    for n, i in enumerate(range(0, out_ref.shape[0], step)):
        here = pl.ds(i, step)
        out_ref[here, :] = mm(order_ref[here, :], turned).astype(BF)
        copy = pltpu.make_async_copy(out_ref.at[here], out_hbm.at[here], sems.at[n])
        copy.start()
        copies.append(copy)
    for copy in copies:
        copy.wait()


def column_tables(inverse_halo, cov_plane, cov_vert):
    own, halo = inverse_halo.shape
    wide, narrow = lax.axis_size("wide"), lax.axis_size("narrow")
    width = narrow * LANES
    plane = cov_plane.shape[0]
    shape = jax.ShapeDtypeStruct
    order = call(order_body, [shape((own, own), BF), shape((halo, own), BF)], [inverse_halo])
    rest = call(
        functools.partial(tables_body, wide, narrow),
        [shape((plane, plane), BF), shape((width, width), BF), shape((width, width), BF)],
        [cov_plane, cov_vert],
    )
    return [tuple(order), tuple(rest)]


def smooth_by_columns(state, inverse_halo, got, tables):
    wide, narrow = lax.axis_size("wide"), lax.axis_size("narrow")
    own, columns = state.shape
    devices = wide * narrow
    group = columns // devices
    depth = narrow * ZL
    tile = own // ZL
    shape = jax.ShapeDtypeStruct
    (order, halo_table), (plane_mix, spread, vert_mix) = tables
    (turned,) = call(turn_body, [shape((columns, own), F32)], [state, order])
    (wire,) = call(functools.partial(wire_body, len(got)), [shape((columns, own), BF)], [turned, halo_table, *got])
    there = exchange_columns(wire)
    mixed, adjoint = call(
        functools.partial(mix_body, wide, narrow, group),
        [shape((columns, own), BF), shape((own, columns), BF)],
        [there, plane_mix, spread, vert_mix, state, inverse_halo, *got],
        [
            pltpu.VMEM((tile, wide * group + group, depth), F32),
            pltpu.VMEM((plane_mix.shape[0], group * depth), BF),
            pltpu.VMEM((own // LANES, columns + group, LANES), F32),
            pltpu.VMEM((own, columns), BF),
            pltpu.SemaphoreType.DMA,
        ],
        out_specs=[VM, ANY],
    )
    back = exchange_columns(mixed)
    (smoothed,) = call(
        unwire_body,
        [shape((own, columns), BF)],
        [back, order],
        [pltpu.VMEM((own, columns), BF), pltpu.SemaphoreType.DMA((3,))],
        out_specs=[ANY],
    )
    return adjoint, smoothed


def smooth_by_layers(adjoint, cov_plane, cov_vert):
    own, columns = adjoint.shape
    layered = adjoint.reshape(ZL, own // ZL, -1)
    planar = jnp.einsum(
        "pq,lqr->lpr",
        cov_plane,
        lax.all_to_all(layered, "wide", split_axis=0, concat_axis=1, tiled=True),
        preferred_element_type=F32,
    ).astype(BF)
    restored = lax.all_to_all(planar, "wide", split_axis=1, concat_axis=0, tiled=True)
    slab_weights = lax.dynamic_slice_in_dim(cov_vert, lax.axis_index("narrow") * ZL, ZL, 0)
    summed = jnp.dot(
        slab_weights,
        lax.all_gather(restored.reshape(ZL, -1), "narrow", axis=0, tiled=True),
        preferred_element_type=F32,
    )
    return summed.astype(BF).reshape(own, -1)


def shards(adjoint_rhs, inverse_rows, blocks, block_cols, send_rows, cov_plane, cov_vert):
    rhs = adjoint_rhs[0, 0]
    inverse = inverse_rows[0, 0]
    block_values = blocks[0, 0]
    cols = block_cols[0, 0]
    send_index = send_rows[0, 0]
    own, columns = rhs.shape
    width = send_index.shape[1]
    halo = 4 * width
    wide, narrow = lax.axis_size("wide"), lax.axis_size("narrow")
    group = columns // (wide * narrow)
    by_columns = columns % (wide * narrow) == 0 and group % 8 == 0 and narrow * ZL == LANES and wide % 16 == 0
    found = matchings()
    count = len(found)
    sent = count * width
    shape = jax.ShapeDtypeStruct
    notes = [shape((width, columns), BF)] * count
    full = shape((own, columns), F32)
    base_shape = shape((sent, columns), F32)
    cell_space = pltpu.VMEM((own, columns), BF)
    (select,) = call(
        functools.partial(select_body, found, own),
        [shape((sent, own), BF)],
        [send_index],
        flops=SELECT_FLOPS,
    )
    messages = call(pick_body, notes, [select, rhs], flops=PICK_FLOPS)
    got = swap(messages, found)
    inverse_halo, blocks_halo, inverse_sent, blocks_sent, state, base = call(
        functools.partial(setup_body, found, width),
        [
            shape((own, halo), BF),
            shape((2, own, halo), BF),
            shape((sent, halo), BF),
            shape((2 * sent, halo), BF),
            full,
            base_shape,
        ],
        [cols, inverse, block_values, rhs, select],
        [cell_space, cell_space],
        limit=12,
    )
    tables = column_tables(inverse_halo, cov_plane, cov_vert) if by_columns else []
    for sweep in range(SWEEPS - 1):
        messages = call(
            functools.partial(sent_update_body, count), notes, [base, inverse_sent, *got], limit=4
        )
        arrived, got = got, swap(messages, found)
        iterate, part, base = call(
            functools.partial(update_body, count),
            [full, full, base_shape],
            [cols, state, inverse_halo, block_values, rhs, select, *arrived],
            [pltpu.VMEM((own + halo, columns), BF), cell_space, cell_space],
        )
        turn = 1 if sweep == 1 and count == 3 else 0
        arrived = got[count - turn:] + got[:count - turn]
        messages = call(
            functools.partial(sent_residual_body, count, turn),
            notes,
            [base, blocks_sent, *arrived],
            limit=4,
        )
        got = swap(messages, found)
        if sweep < len(tables):
            tables[sweep], part = lax.optimization_barrier((tables[sweep], part))
        more = sweep < SWEEPS - 2
        state, *bases = call(
            functools.partial(residual_body, count, turn),
            [full] + [base_shape] * more,
            [part, blocks_halo, iterate, inverse, select, *arrived],
            [cell_space] * (1 + 2 * more),
        )
        base = bases[0] if more else None
    if by_columns:
        adjoint, smoothed = smooth_by_columns(state, inverse_halo, got, tables)
    else:
        cells = shape((own, columns), BF)
        (adjoint,) = call(functools.partial(last_update_body, count), [cells], [state, inverse_halo, *got])
        smoothed = smooth_by_layers(adjoint, cov_plane, cov_vert)
    return (adjoint[None, None], smoothed[None, None])


def solution(mesh):
    in_specs = (
        P("wide", "narrow", None, None),
        P("wide", "narrow", None, None),
        P("wide", "narrow", None, None, None, None),
        P("wide", "narrow", None, None),
        P("wide", "narrow", None, None),
        P(),
        P(),
    )
    out_specs = (P("wide", "narrow", None, None), P("wide", "narrow", None, None))
    return jax.shard_map(shards, mesh=mesh, in_specs=in_specs, out_specs=out_specs, check_vma=False)
```

```python
import functools

import jax
import jax.numpy as jnp
from jax import lax
from jax.experimental import pallas as pl
from jax.experimental.pallas import tpu as pltpu
from jax.sharding import PartitionSpec as P

ZL = 64
SWEEPS = 4
LANES = 128
SELECT_FLOPS = 6 * 10 ** 8
PICK_FLOPS = 2 * 10 ** 9
BF = jnp.bfloat16
F32 = jnp.float32
VM = pl.BlockSpec(memory_space=pltpu.VMEM)
ANY = pl.BlockSpec(memory_space=pl.ANY)


def wide_slot(w, n, parity):
    return (w & 1) ^ parity ^ 1


def narrow_slot(w, n, parity):
    return 2 + ((n & 1) ^ parity ^ 1)


def mixed_slot(w, n, kind):
    turn = (w ^ (w >> 1) ^ kind) & 1
    return (1 - turn) * wide_slot(w, n, 1) + turn * narrow_slot(w, n, 0)


def has_partner(w, n, slot, wide, narrow):
    inside = [w > 0, w + 1 < wide, n > 0, n + 1 < narrow]
    return sum((slot == k) * inside[k] for k in range(4))


def matchings():
    wide, narrow = lax.axis_size("wide"), lax.axis_size("narrow")
    if narrow == 2 and wide % 4 == 0:
        rules = [(mixed_slot, 0), (mixed_slot, 1), (wide_slot, 0)]
    else:
        rules = [(wide_slot, 1)] * (wide > 2) + [(narrow_slot, 1)] * (narrow > 2)
        rules += [(narrow_slot, 0)] * (narrow > 1) + [(wide_slot, 0)] * (wide > 1)
    found = []
    for rule, kind in rules:
        pairs = []
        for w in range(wide):
            for n in range(narrow):
                slot = rule(w, n, kind)
                if has_partner(w, n, slot, wide, narrow):
                    step = ((-1, 0), (1, 0), (0, -1), (0, 1))[slot]
                    target = (w + step[0], n + step[1])
                elif slot < 2:
                    target = (w, n ^ 1 if n ^ 1 < narrow else n)
                else:
                    target = (w ^ 1 if w ^ 1 < wide else w, n)
                pairs.append((w * narrow + n, target[0] * narrow + target[1]))
        found.append((rule, kind, tuple(pairs)))
    return found


def own_slots(found):
    w, n = lax.axis_index("wide"), lax.axis_index("narrow")
    wide, narrow = lax.axis_size("wide"), lax.axis_size("narrow")
    slots = [rule(w, n, kind) for rule, kind, _ in found]
    return [(slot, has_partner(w, n, slot, wide, narrow) == 1) for slot in slots]


def swap(messages, found):
    return [lax.ppermute(m, ("wide", "narrow"), list(f[-1])) for m, f in zip(messages, found)]


def mm(a, b):
    return jnp.dot(a, b, preferred_element_type=F32)


def mm_t(a, b):
    return lax.dot_general(a, b, (((1,), (1,)), ((), ())), preferred_element_type=F32)


def iota(shape, dim):
    return lax.broadcasted_iota(jnp.int32, shape, dim)


def call(body, outs, args, scratch=(), specs=None, flops=0, limit=8, out_specs=None):
    size = sum(a.size * a.dtype.itemsize for a in args)
    return pl.pallas_call(
        body,
        out_shape=outs,
        in_specs=specs or [VM] * len(args),
        out_specs=out_specs or [VM] * len(outs),
        scratch_shapes=list(scratch),
        compiler_params=pltpu.CompilerParams(vmem_limit_bytes=limit * 1024 * 1024),
        cost_estimate=pl.CostEstimate(flops=flops, bytes_accessed=size, transcendentals=0),
    )(*args)


def join_halo(got):
    pieces = [piece[...] for piece in got]
    return jnp.concatenate(pieces + [jnp.zeros_like(pieces[0])] * (4 - len(pieces)), axis=0)


def send(messages, values):
    width = messages[0].shape[0]
    for m, message in enumerate(messages):
        message[...] = values[m * width:(m + 1) * width, :].astype(BF)


def keep_split(high_ref, low_ref, rows, value):
    high = value.astype(BF)
    high_ref[rows] = high
    low_ref[rows] = (value - high.astype(F32)).astype(BF)


def select_body(found, own, send_ref, select_ref):
    width = send_ref.shape[1]
    diagonal = iota((width, width), 0) == iota((width, width), 1)
    pieces = []
    for slot, paired in own_slots(found):
        rows = jnp.where(paired, send_ref[pl.ds(slot, 1), :], -1).astype(F32)
        pieces.append(jnp.where(diagonal, rows, 0.0))
    column = jnp.sum(jnp.concatenate(pieces, axis=0), axis=1, keepdims=True).astype(jnp.int32)
    select_ref[...] = (iota((len(found) * width, own), 1) == column).astype(F32).astype(BF)


def pick_body(select_ref, rhs_ref, *messages):
    send(messages, mm(select_ref[...], rhs_ref[...]))


def setup_body(found, width, cols_ref, inverse_ref, blocks_ref, rhs_ref, select_ref, *rest):
    inverse_halo_ref, blocks_halo_ref, inverse_sent_ref, blocks_sent_ref, state_ref, base_ref = rest[:6]
    high_ref, low_ref = rest[6:]
    own = rhs_ref.shape[0]
    halo = 4 * width
    places = iota((1, halo), 1)
    starts = jnp.full((1, halo), -halo, jnp.int32)
    for m, (slot, _) in enumerate(own_slots(found)):
        here = lax.div(places, width) == m
        starts = jnp.where(here, slot * width + lax.rem(places, width), starts)
    arrange = (iota((halo, halo), 0) == starts).astype(F32).astype(BF)
    rows, links, size, _ = blocks_ref.shape
    for j in range(rows):
        here = slice(j * size, (j + 1) * size)
        columns = [cols_ref[j, k] for k in range(links)]
        for c in range(halo // size):
            total = None
            for k in range(links):
                part = jnp.where(columns[k] == own // size + c, blocks_ref[j, k].astype(F32), 0.0)
                total = part if total is None else total + part
            lanes = slice(c * size, (c + 1) * size)
            keep_split(high_ref, low_ref, (here, lanes), total)
    for part, half_ref in enumerate((high_ref, low_ref)):
        blocks_halo_ref[part] = mm(half_ref[...], arrange).astype(BF)
    step = own // 2
    for i in range(0, own, step):
        here = slice(i, i + step)
        inverse_halo_ref[here, :] = mm(inverse_ref[here, own:], arrange).astype(BF)
        value = mm(inverse_ref[here, :own], rhs_ref[...])
        state_ref[here, :] = value
        keep_split(high_ref, low_ref, here, value)
    inverse_sent_ref[...] = mm(select_ref[...], inverse_halo_ref[...]).astype(BF)
    sent = select_ref.shape[0]
    for part in range(2):
        here = slice(part * sent, (part + 1) * sent)
        blocks_sent_ref[here, :] = mm(select_ref[...], blocks_halo_ref[part]).astype(BF)
    base_ref[...] = mm(select_ref[...], high_ref[...]) + mm(select_ref[...], low_ref[...])


def sent_update_body(count, base_ref, sent_ref, *rest):
    got, messages = rest[:count], rest[count:]
    send(messages, base_ref[...] + mm(sent_ref[...], join_halo(got)))


def sent_residual_body(count, turn, base_ref, sent_ref, *rest):
    got, messages = rest[:count], rest[count:]
    halo = join_halo(got[turn:] + got[:turn])
    part = mm(sent_ref[...], halo)
    sent = base_ref.shape[0]
    send(messages, base_ref[...] - (part[:sent] + part[sent:]))


def update_body(count, cols_ref, state_ref, inverse_halo_ref, blocks_ref, rhs_ref, select_ref, *rest):
    got, (iterate_ref, part_ref, base_ref, sub_ref, high_ref, low_ref) = rest[:count], rest[count:]
    own = state_ref.shape[0]
    halo = join_halo(got)
    step = own // 2
    for i in range(0, own, step):
        here = slice(i, i + step)
        value = state_ref[here, :] + mm(inverse_halo_ref[here, :], halo)
        iterate_ref[here, :] = value
        sub_ref[here, :] = value.astype(BF)
    sub_ref[own:, :] = jnp.zeros((sub_ref.shape[0] - own, sub_ref.shape[1]), BF)
    rows, links, size, _ = blocks_ref.shape
    for j in range(rows):
        starts = [pl.multiple_of(cols_ref[j, k] * size, size) for k in range(links)]
        values = jnp.concatenate([blocks_ref[j, k] for k in range(links)], axis=1)
        coupled = jnp.concatenate([sub_ref[pl.ds(start, size), :] for start in starts], axis=0)
        total = mm(values, coupled)
        here = slice(j * size, (j + 1) * size)
        value = rhs_ref[here, :].astype(F32) - total
        part_ref[here, :] = value
        keep_split(high_ref, low_ref, here, value)
    base_ref[...] = mm(select_ref[...], high_ref[...]) + mm(select_ref[...], low_ref[...])


def residual_body(count, turn, part_ref, blocks_halo_ref, iterate_ref, inverse_ref, select_ref, *rest):
    got, rest = rest[:count], list(rest[count:])
    state_ref = rest.pop(0)
    resid_ref, *split = rest[-3:] if len(rest) == 4 else rest
    own = part_ref.shape[0]
    halo = join_halo(got[turn:] + got[:turn])
    step = own // 2
    for i in range(0, own, step):
        here = slice(i, i + step)
        outer = mm(blocks_halo_ref[0, here, :], halo) + mm(blocks_halo_ref[1, here, :], halo)
        resid_ref[here, :] = (part_ref[here, :] - outer).astype(BF)
    for i in range(0, own, step):
        here = slice(i, i + step)
        value = iterate_ref[here, :] + mm(inverse_ref[here, :own], resid_ref[...])
        state_ref[here, :] = value
        if split:
            keep_split(*split, here, value)
    if split:
        rest[0][...] = mm(select_ref[...], split[0][...]) + mm(select_ref[...], split[1][...])


def last_update_body(count, state_ref, inverse_halo_ref, *rest):
    got, (round_ref,) = rest[:count], rest[count:]
    halo = join_halo(got)
    step = state_ref.shape[0] // 2
    for i in range(0, state_ref.shape[0], step):
        here = slice(i, i + step)
        round_ref[here, :] = (state_ref[here, :] + mm(inverse_halo_ref[here, :], halo)).astype(BF)


def turn_body(state_ref, order_ref, turned_ref):
    value = state_ref[...]
    high = value.astype(BF)
    low = (value - high.astype(F32)).astype(BF)
    columns = value.shape[1]
    both = mm(jnp.concatenate([high, low], axis=1).T, order_ref[...])
    turned_ref[...] = both[:columns] + both[columns:]


def wire_body(count, turned_ref, halo_table_ref, *rest):
    got, (wire_ref,) = rest[:count], rest[count:]
    wire_ref[...] = (turned_ref[...] + mm(join_halo(got).T, halo_table_ref[...])).astype(BF)


def one_hot(rows_of, shape):
    return (iota(shape, 0) == rows_of(iota((1, shape[1]), 1))).astype(F32).astype(BF)


def order_body(inverse_halo_ref, order_ref, halo_table_ref):
    own = order_ref.shape[0]
    tile = own // ZL
    order_ref[...] = one_hot(lambda k: lax.rem(k, ZL) * tile + lax.div(k, ZL), (own, own))
    halo_table_ref[...] = mm(inverse_halo_ref[...].T, order_ref[...]).astype(BF)


def tables_body(wide, narrow, cov_plane_ref, cov_vert_ref, plane_ref, spread_ref, vert_ref):
    plane = plane_ref.shape[0]
    tile = plane // wide
    turn = one_hot(lambda k: lax.rem(k, wide) * tile + lax.div(k, wide), (plane, plane))
    half = mm(cov_plane_ref[...], turn).astype(BF)
    plane_ref[...] = mm(half.T, turn).astype(BF).T
    share = LANES // ZL
    depth = narrow * ZL
    width = narrow * LANES

    def source(k):
        e, n, l = lax.div(k, depth), lax.rem(lax.div(k, ZL), narrow), lax.rem(k, ZL)
        return n * LANES + e * ZL + l

    spread = one_hot(source, (width, width))
    spread_ref[...] = spread
    turned = cov_vert_ref[...].astype(F32).T
    zero = jnp.zeros_like(turned)
    blocks = jnp.concatenate(
        [jnp.concatenate([turned if i == e else zero for i in range(share)], axis=1) for e in range(share)],
        axis=0,
    ).astype(BF)
    vert_ref[...] = mm_t(blocks, spread).astype(BF)


def mix_body(wide, narrow, group, in_ref, plane_ref, spread_ref, vert_ref, state_ref, inverse_halo_ref, *rest):
    got, (out_ref, adjoint_hbm, cells_ref, flat_ref, wire_ref, round_ref, sem) = rest[:-7], rest[-7:]
    last_update_body(len(got), state_ref, inverse_halo_ref, *got, round_ref)
    keep = pltpu.make_async_copy(round_ref, adjoint_hbm, sem)
    keep.start()
    own = in_ref.shape[1]
    tile = own // ZL
    share = LANES // ZL
    depth = narrow * ZL
    block = wide * group
    pairs = tile // share
    joined = jnp.concatenate(
        [
            jnp.concatenate(
                [in_ref[n * block:(n + 1) * block, g * LANES:(g + 1) * LANES] for n in range(narrow)], axis=1
            )
            for g in range(pairs)
        ],
        axis=0,
    )
    spread = mm(joined, spread_ref[...])
    for g in range(pairs):
        for e in range(share):
            cells_ref[g * share + e, :block, :] = spread[g * block:(g + 1) * block, e * depth:(e + 1) * depth]
    for r in range(group):
        for c in range(tile):
            flat_ref[c * wide:(c + 1) * wide, r * depth:(r + 1) * depth] = cells_ref[
                c, pl.ds(r, wide, stride=group), :
            ].astype(BF)
    planar = mm(plane_ref[...], flat_ref[...]).astype(BF)
    stacked = jnp.concatenate(
        [
            jnp.concatenate(
                [planar[c * wide:(c + 1) * wide, r * depth:(r + 1) * depth] for c in range(g * share, (g + 1) * share)],
                axis=1,
            )
            for g in range(pairs)
            for r in range(group)
        ],
        axis=0,
    )
    mixed = mm(stacked, vert_ref[...])
    for g in range(pairs):
        for r in range(group):
            rows = slice(g * block + r * wide, g * block + (r + 1) * wide)
            for n in range(narrow):
                wire_ref[g, pl.ds(n * block + r, wide, stride=group), :] = mixed[rows, n * LANES:(n + 1) * LANES]
        out_ref[:, g * LANES:(g + 1) * LANES] = wire_ref[g, :narrow * block, :].astype(BF)
    keep.wait()


def unwire_body(in_ref, out_hbm, out_ref, sems):
    own = out_ref.shape[0]
    tile = own // ZL
    runs = sems.shape[0]
    run = ZL // runs
    step = run * tile
    small = one_hot(lambda k: lax.rem(k, run) * tile + lax.div(k, run), (step, step))
    turned = in_ref[...].T
    copies = []
    for b in range(runs):
        here = pl.ds(b * step, step)
        piece = jnp.concatenate([turned[c * ZL + b * run:c * ZL + (b + 1) * run] for c in range(tile)], axis=0)
        out_ref[here, :] = mm(small, piece).astype(BF)
        copy = pltpu.make_async_copy(out_ref.at[here], out_hbm.at[here], sems.at[b])
        copy.start()
        copies.append(copy)
    for copy in copies:
        copy.wait()


def column_tables(inverse_halo, cov_plane, cov_vert):
    own, halo = inverse_halo.shape
    wide, narrow = lax.axis_size("wide"), lax.axis_size("narrow")
    width = narrow * LANES
    plane = cov_plane.shape[0]
    shape = jax.ShapeDtypeStruct
    order = call(order_body, [shape((own, own), BF), shape((halo, own), BF)], [inverse_halo])
    rest = call(
        functools.partial(tables_body, wide, narrow),
        [shape((plane, plane), BF), shape((width, width), BF), shape((width, width), BF)],
        [cov_plane, cov_vert],
    )
    return [tuple(order), tuple(rest)]


def smooth_by_columns(state, inverse_halo, got, tables):
    wide, narrow = lax.axis_size("wide"), lax.axis_size("narrow")
    own, columns = state.shape
    devices = wide * narrow
    group = columns // devices
    depth = narrow * ZL
    tile = own // ZL
    shape = jax.ShapeDtypeStruct
    (order, halo_table), (plane_mix, spread, vert_mix) = tables
    (turned,) = call(turn_body, [shape((columns, own), F32)], [state, order])
    (wire,) = call(functools.partial(wire_body, len(got)), [shape((columns, own), BF)], [turned, halo_table, *got])
    there = lax.all_to_all(
        wire.reshape(devices, group, own), ("narrow", "wide"), split_axis=0, concat_axis=0, tiled=True
    )
    mixed, adjoint = call(
        functools.partial(mix_body, wide, narrow, group),
        [shape((columns, own), BF), shape((own, columns), BF)],
        [there.reshape(columns, own), plane_mix, spread, vert_mix, state, inverse_halo, *got],
        [
            pltpu.VMEM((tile, wide * group + group, depth), F32),
            pltpu.VMEM((plane_mix.shape[0], group * depth), BF),
            pltpu.VMEM((own // LANES, columns + group, LANES), F32),
            pltpu.VMEM((own, columns), BF),
            pltpu.SemaphoreType.DMA,
        ],
        out_specs=[VM, ANY],
    )
    back = lax.all_to_all(
        mixed.reshape(devices, group, own), ("narrow", "wide"), split_axis=0, concat_axis=0, tiled=True
    )
    (smoothed,) = call(
        unwire_body,
        [shape((own, columns), BF)],
        [back.reshape(columns, own)],
        [pltpu.VMEM((own, columns), BF), pltpu.SemaphoreType.DMA((4,))],
        out_specs=[ANY],
    )
    return adjoint, smoothed


def smooth_by_layers(adjoint, cov_plane, cov_vert):
    own, columns = adjoint.shape
    layered = adjoint.reshape(ZL, own // ZL, -1)
    planar = jnp.einsum(
        "pq,lqr->lpr",
        cov_plane,
        lax.all_to_all(layered, "wide", split_axis=0, concat_axis=1, tiled=True),
        preferred_element_type=F32,
    ).astype(BF)
    restored = lax.all_to_all(planar, "wide", split_axis=1, concat_axis=0, tiled=True)
    slab_weights = lax.dynamic_slice_in_dim(cov_vert, lax.axis_index("narrow") * ZL, ZL, 0)
    summed = jnp.dot(
        slab_weights,
        lax.all_gather(restored.reshape(ZL, -1), "narrow", axis=0, tiled=True),
        preferred_element_type=F32,
    )
    return summed.astype(BF).reshape(own, -1)


def shards(adjoint_rhs, inverse_rows, blocks, block_cols, send_rows, cov_plane, cov_vert):
    rhs = adjoint_rhs[0, 0]
    inverse = inverse_rows[0, 0]
    block_values = blocks[0, 0]
    cols = block_cols[0, 0]
    send_index = send_rows[0, 0]
    own, columns = rhs.shape
    width = send_index.shape[1]
    halo = 4 * width
    wide, narrow = lax.axis_size("wide"), lax.axis_size("narrow")
    group = columns // (wide * narrow)
    by_columns = columns % (wide * narrow) == 0 and group % 8 == 0 and narrow * ZL == LANES and wide % 16 == 0
    found = matchings()
    count = len(found)
    sent = count * width
    shape = jax.ShapeDtypeStruct
    notes = [shape((width, columns), BF)] * count
    full = shape((own, columns), F32)
    base_shape = shape((sent, columns), F32)
    cell_space = pltpu.VMEM((own, columns), BF)
    (select,) = call(
        functools.partial(select_body, found, own),
        [shape((sent, own), BF)],
        [send_index],
        flops=SELECT_FLOPS,
    )
    messages = call(pick_body, notes, [select, rhs], flops=PICK_FLOPS)
    got = swap(messages, found)
    inverse_halo, blocks_halo, inverse_sent, blocks_sent, state, base = call(
        functools.partial(setup_body, found, width),
        [
            shape((own, halo), BF),
            shape((2, own, halo), BF),
            shape((sent, halo), BF),
            shape((2 * sent, halo), BF),
            full,
            base_shape,
        ],
        [cols, inverse, block_values, rhs, select],
        [cell_space, cell_space],
        limit=12,
    )
    tables = column_tables(inverse_halo, cov_plane, cov_vert) if by_columns else []
    for sweep in range(SWEEPS - 1):
        messages = call(
            functools.partial(sent_update_body, count), notes, [base, inverse_sent, *got], limit=4
        )
        arrived, got = got, swap(messages, found)
        iterate, part, base = call(
            functools.partial(update_body, count),
            [full, full, base_shape],
            [cols, state, inverse_halo, block_values, rhs, select, *arrived],
            [pltpu.VMEM((own + halo, columns), BF), cell_space, cell_space],
        )
        turn = 1 if sweep == 1 and count == 3 else 0
        arrived = got[count - turn:] + got[:count - turn]
        messages = call(
            functools.partial(sent_residual_body, count, turn),
            notes,
            [base, blocks_sent, *arrived],
            limit=4,
        )
        got = swap(messages, found)
        if sweep < len(tables):
            tables[sweep], part = lax.optimization_barrier((tables[sweep], part))
        more = sweep < SWEEPS - 2
        state, *bases = call(
            functools.partial(residual_body, count, turn),
            [full] + [base_shape] * more,
            [part, blocks_halo, iterate, inverse, select, *arrived],
            [cell_space] * (1 + 2 * more),
        )
        base = bases[0] if more else None
    if by_columns:
        adjoint, smoothed = smooth_by_columns(state, inverse_halo, got, tables)
    else:
        cells = shape((own, columns), BF)
        (adjoint,) = call(functools.partial(last_update_body, count), [cells], [state, inverse_halo, *got])
        smoothed = smooth_by_layers(adjoint, cov_plane, cov_vert)
    return (adjoint[None, None], smoothed[None, None])


def solution(mesh):
    in_specs = (
        P("wide", "narrow", None, None),
        P("wide", "narrow", None, None),
        P("wide", "narrow", None, None, None, None),
        P("wide", "narrow", None, None),
        P("wide", "narrow", None, None),
        P(),
        P(),
    )
    out_specs = (P("wide", "narrow", None, None), P("wide", "narrow", None, None))
    return jax.shard_map(shards, mesh=mesh, in_specs=in_specs, out_specs=out_specs, check_vma=False)
```

```python
import functools

import jax
import jax.numpy as jnp
from jax import lax
from jax.experimental import pallas as pl
from jax.experimental.pallas import tpu as pltpu
from jax.sharding import PartitionSpec as P

ZL = 64
SWEEPS = 4
LANES = 128
SELECT_FLOPS = 6 * 10 ** 8
PICK_FLOPS = 2 * 10 ** 9
BF = jnp.bfloat16
F32 = jnp.float32
VM = pl.BlockSpec(memory_space=pltpu.VMEM)
ANY = pl.BlockSpec(memory_space=pl.ANY)


def wide_slot(w, n, parity):
    return (w & 1) ^ parity ^ 1


def narrow_slot(w, n, parity):
    return 2 + ((n & 1) ^ parity ^ 1)


def mixed_slot(w, n, kind):
    turn = (w ^ (w >> 1) ^ kind) & 1
    return (1 - turn) * wide_slot(w, n, 1) + turn * narrow_slot(w, n, 0)


def has_partner(w, n, slot, wide, narrow):
    inside = [w > 0, w + 1 < wide, n > 0, n + 1 < narrow]
    return sum((slot == k) * inside[k] for k in range(4))


def matchings():
    wide, narrow = lax.axis_size("wide"), lax.axis_size("narrow")
    if narrow == 2 and wide % 4 == 0:
        rules = [(mixed_slot, 0), (mixed_slot, 1), (wide_slot, 0)]
    else:
        rules = [(wide_slot, 1)] * (wide > 2) + [(narrow_slot, 1)] * (narrow > 2)
        rules += [(narrow_slot, 0)] * (narrow > 1) + [(wide_slot, 0)] * (wide > 1)
    found = []
    for rule, kind in rules:
        pairs = []
        for w in range(wide):
            for n in range(narrow):
                slot = rule(w, n, kind)
                if has_partner(w, n, slot, wide, narrow):
                    step = ((-1, 0), (1, 0), (0, -1), (0, 1))[slot]
                    target = (w + step[0], n + step[1])
                elif slot < 2:
                    target = (w, n ^ 1 if n ^ 1 < narrow else n)
                else:
                    target = (w ^ 1 if w ^ 1 < wide else w, n)
                pairs.append((w * narrow + n, target[0] * narrow + target[1]))
        found.append((rule, kind, tuple(pairs)))
    return found


def own_slots(found):
    w, n = lax.axis_index("wide"), lax.axis_index("narrow")
    wide, narrow = lax.axis_size("wide"), lax.axis_size("narrow")
    slots = [rule(w, n, kind) for rule, kind, _ in found]
    return [(slot, has_partner(w, n, slot, wide, narrow) == 1) for slot in slots]


def swap(messages, found):
    return [lax.ppermute(m, ("wide", "narrow"), list(f[-1])) for m, f in zip(messages, found)]


def mm(a, b):
    return jnp.dot(a, b, preferred_element_type=F32)


def mm_t(a, b):
    return lax.dot_general(a, b, (((1,), (1,)), ((), ())), preferred_element_type=F32)


def iota(shape, dim):
    return lax.broadcasted_iota(jnp.int32, shape, dim)


def call(body, outs, args, scratch=(), specs=None, flops=0, limit=8, out_specs=None):
    size = sum(a.size * a.dtype.itemsize for a in args)
    return pl.pallas_call(
        body,
        out_shape=outs,
        in_specs=specs or [VM] * len(args),
        out_specs=out_specs or [VM] * len(outs),
        scratch_shapes=list(scratch),
        compiler_params=pltpu.CompilerParams(vmem_limit_bytes=limit * 1024 * 1024),
        cost_estimate=pl.CostEstimate(flops=flops, bytes_accessed=size, transcendentals=0),
    )(*args)


def join_halo(got):
    pieces = [piece[...] for piece in got]
    return jnp.concatenate(pieces + [jnp.zeros_like(pieces[0])] * (4 - len(pieces)), axis=0)


def send(messages, values):
    width = messages[0].shape[0]
    for m, message in enumerate(messages):
        message[...] = values[m * width:(m + 1) * width, :].astype(BF)


def keep_split(high_ref, low_ref, rows, value):
    high = value.astype(BF)
    high_ref[rows] = high
    low_ref[rows] = (value - high.astype(F32)).astype(BF)


def select_body(found, own, send_ref, select_ref):
    width = send_ref.shape[1]
    diagonal = iota((width, width), 0) == iota((width, width), 1)
    pieces = []
    for slot, paired in own_slots(found):
        rows = jnp.where(paired, send_ref[pl.ds(slot, 1), :], -1).astype(F32)
        pieces.append(jnp.where(diagonal, rows, 0.0))
    column = jnp.sum(jnp.concatenate(pieces, axis=0), axis=1, keepdims=True).astype(jnp.int32)
    select_ref[...] = (iota((len(found) * width, own), 1) == column).astype(F32).astype(BF)


def pick_body(select_ref, rhs_ref, *messages):
    send(messages, mm(select_ref[...], rhs_ref[...]))


def setup_body(found, width, cols_ref, inverse_ref, blocks_ref, rhs_ref, select_ref, *rest):
    inverse_halo_ref, blocks_halo_ref, inverse_sent_ref, blocks_sent_ref, state_ref, base_ref = rest[:6]
    high_ref, low_ref = rest[6:]
    own = rhs_ref.shape[0]
    halo = 4 * width
    places = iota((1, halo), 1)
    starts = jnp.full((1, halo), -halo, jnp.int32)
    for m, (slot, _) in enumerate(own_slots(found)):
        here = lax.div(places, width) == m
        starts = jnp.where(here, slot * width + lax.rem(places, width), starts)
    arrange = (iota((halo, halo), 0) == starts).astype(F32).astype(BF)
    rows, links, size, _ = blocks_ref.shape
    for j in range(rows):
        here = slice(j * size, (j + 1) * size)
        columns = [cols_ref[j, k] for k in range(links)]
        for c in range(halo // size):
            total = None
            for k in range(links):
                part = jnp.where(columns[k] == own // size + c, blocks_ref[j, k].astype(F32), 0.0)
                total = part if total is None else total + part
            lanes = slice(c * size, (c + 1) * size)
            keep_split(high_ref, low_ref, (here, lanes), total)
    for part, half_ref in enumerate((high_ref, low_ref)):
        blocks_halo_ref[part] = mm(half_ref[...], arrange).astype(BF)
    step = own // 2
    for i in range(0, own, step):
        here = slice(i, i + step)
        inverse_halo_ref[here, :] = mm(inverse_ref[here, own:], arrange).astype(BF)
        value = mm(inverse_ref[here, :own], rhs_ref[...])
        state_ref[here, :] = value
        keep_split(high_ref, low_ref, here, value)
    inverse_sent_ref[...] = mm(select_ref[...], inverse_halo_ref[...]).astype(BF)
    sent = select_ref.shape[0]
    for part in range(2):
        here = slice(part * sent, (part + 1) * sent)
        blocks_sent_ref[here, :] = mm(select_ref[...], blocks_halo_ref[part]).astype(BF)
    base_ref[...] = mm(select_ref[...], high_ref[...]) + mm(select_ref[...], low_ref[...])


def sent_update_body(count, base_ref, sent_ref, *rest):
    got, messages = rest[:count], rest[count:]
    halo = jnp.concatenate([piece[...] for piece in got], axis=0)
    send(messages, base_ref[...] + mm(sent_ref[:, :halo.shape[0]], halo))


def sent_residual_body(count, turn, base_ref, sent_ref, *rest):
    got, messages = rest[:count], rest[count:]
    halo = jnp.concatenate([piece[...] for piece in got[turn:] + got[:turn]], axis=0)
    part = mm(sent_ref[:, :halo.shape[0]], halo)
    sent = base_ref.shape[0]
    send(messages, base_ref[...] - (part[:sent] + part[sent:]))


def update_body(count, cols_ref, state_ref, inverse_halo_ref, blocks_ref, rhs_ref, select_ref, *rest):
    got, (iterate_ref, part_ref, base_ref, sub_ref, high_ref, low_ref) = rest[:count], rest[count:]
    own = state_ref.shape[0]
    halo = join_halo(got)
    step = own // 2
    for i in range(0, own, step):
        here = slice(i, i + step)
        value = state_ref[here, :] + mm(inverse_halo_ref[here, :], halo)
        iterate_ref[here, :] = value
        sub_ref[here, :] = value.astype(BF)
    sub_ref[own:, :] = jnp.zeros((sub_ref.shape[0] - own, sub_ref.shape[1]), BF)
    rows, links, size, _ = blocks_ref.shape
    for j in range(rows):
        starts = [pl.multiple_of(cols_ref[j, k] * size, size) for k in range(links)]
        values = jnp.concatenate([blocks_ref[j, k] for k in range(links)], axis=1)
        coupled = jnp.concatenate([sub_ref[pl.ds(start, size), :] for start in starts], axis=0)
        total = mm(values, coupled)
        here = slice(j * size, (j + 1) * size)
        value = rhs_ref[here, :].astype(F32) - total
        part_ref[here, :] = value
        keep_split(high_ref, low_ref, here, value)
    base_ref[...] = mm(select_ref[...], high_ref[...]) + mm(select_ref[...], low_ref[...])


def residual_body(count, turn, part_ref, blocks_halo_ref, iterate_ref, inverse_ref, select_ref, *rest):
    got, rest = rest[:count], list(rest[count:])
    state_ref = rest.pop(0)
    resid_ref, *split = rest[-3:] if len(rest) == 4 else rest
    own = part_ref.shape[0]
    halo = join_halo(got[turn:] + got[:turn])
    step = own // 2
    for i in range(0, own, step):
        here = slice(i, i + step)
        outer = mm(blocks_halo_ref[0, here, :], halo) + mm(blocks_halo_ref[1, here, :], halo)
        resid_ref[here, :] = (part_ref[here, :] - outer).astype(BF)
    for i in range(0, own, step):
        here = slice(i, i + step)
        value = iterate_ref[here, :] + mm(inverse_ref[here, :own], resid_ref[...])
        state_ref[here, :] = value
        if split:
            keep_split(*split, here, value)
    if split:
        rest[0][...] = mm(select_ref[...], split[0][...]) + mm(select_ref[...], split[1][...])


def last_update_body(count, state_ref, inverse_halo_ref, *rest):
    got, (round_ref,) = rest[:count], rest[count:]
    halo = join_halo(got)
    step = state_ref.shape[0] // 2
    for i in range(0, state_ref.shape[0], step):
        here = slice(i, i + step)
        round_ref[here, :] = (state_ref[here, :] + mm(inverse_halo_ref[here, :], halo)).astype(BF)


def turn_body(state_ref, order_ref, turned_ref):
    value = state_ref[...]
    high = value.astype(BF)
    low = (value - high.astype(F32)).astype(BF)
    columns = value.shape[1]
    both = mm(jnp.concatenate([high, low], axis=1).T, order_ref[...])
    turned_ref[...] = both[:columns] + both[columns:]


def wire_body(count, turned_ref, halo_table_ref, *rest):
    got, (wire_ref,) = rest[:count], rest[count:]
    wire_ref[...] = (turned_ref[...] + mm(join_halo(got).T, halo_table_ref[...])).astype(BF)


def one_hot(rows_of, shape):
    return (iota(shape, 0) == rows_of(iota((1, shape[1]), 1))).astype(F32).astype(BF)


def order_body(inverse_halo_ref, order_ref, halo_table_ref):
    own = order_ref.shape[0]
    tile = own // ZL
    order_ref[...] = one_hot(lambda k: lax.rem(k, ZL) * tile + lax.div(k, ZL), (own, own))
    halo_table_ref[...] = mm(inverse_halo_ref[...].T, order_ref[...]).astype(BF)


def tables_body(wide, narrow, cov_plane_ref, cov_vert_ref, plane_ref, spread_ref, vert_ref):
    plane = plane_ref.shape[0]
    tile = plane // wide
    turn = one_hot(lambda k: lax.rem(k, wide) * tile + lax.div(k, wide), (plane, plane))
    half = mm(cov_plane_ref[...], turn).astype(BF)
    plane_ref[...] = mm(half.T, turn).astype(BF).T
    share = LANES // ZL
    depth = narrow * ZL
    width = narrow * LANES

    def source(k):
        e, n, l = lax.div(k, depth), lax.rem(lax.div(k, ZL), narrow), lax.rem(k, ZL)
        return n * LANES + e * ZL + l

    spread = one_hot(source, (width, width))
    spread_ref[...] = spread
    turned = cov_vert_ref[...].astype(F32).T
    zero = jnp.zeros_like(turned)
    blocks = jnp.concatenate(
        [jnp.concatenate([turned if i == e else zero for i in range(share)], axis=1) for e in range(share)],
        axis=0,
    ).astype(BF)
    vert_ref[...] = mm_t(blocks, spread).astype(BF)


def mix_body(wide, narrow, group, in_ref, plane_ref, spread_ref, vert_ref, state_ref, inverse_halo_ref, *rest):
    got, (out_ref, adjoint_hbm, cells_ref, flat_ref, wire_ref, round_ref, sem) = rest[:-7], rest[-7:]
    last_update_body(len(got), state_ref, inverse_halo_ref, *got, round_ref)
    keep = pltpu.make_async_copy(round_ref, adjoint_hbm, sem)
    keep.start()
    own = in_ref.shape[1]
    tile = own // ZL
    share = LANES // ZL
    depth = narrow * ZL
    block = wide * group
    for g in range(tile // share):
        lanes = slice(g * LANES, (g + 1) * LANES)
        joined = jnp.concatenate([in_ref[n * block:(n + 1) * block, lanes] for n in range(narrow)], axis=1)
        spread = mm(joined, spread_ref[...])
        for e in range(share):
            cells_ref[g * share + e, :block, :] = spread[:, e * depth:(e + 1) * depth]
    for r in range(group):
        for c in range(tile):
            flat_ref[c * wide:(c + 1) * wide, r * depth:(r + 1) * depth] = cells_ref[
                c, pl.ds(r, wide, stride=group), :
            ].astype(BF)
    planar = mm(plane_ref[...], flat_ref[...]).astype(BF)
    for g in range(tile // share):
        stacked = jnp.concatenate(
            [
                jnp.concatenate(
                    [
                        planar[c * wide:(c + 1) * wide, r * depth:(r + 1) * depth]
                        for c in range(g * share, (g + 1) * share)
                    ],
                    axis=1,
                )
                for r in range(group)
            ],
            axis=0,
        )
        mixed = mm(stacked, vert_ref[...])
        for r in range(group):
            for n in range(narrow):
                wire_ref[g, pl.ds(n * block + r, wide, stride=group), :] = mixed[
                    r * wide:(r + 1) * wide, n * LANES:(n + 1) * LANES
                ]
        out_ref[:, g * LANES:(g + 1) * LANES] = wire_ref[g, :narrow * block, :].astype(BF)
    keep.wait()


def unwire_body(in_ref, out_hbm, out_ref, sems):
    own = out_ref.shape[0]
    tile = own // ZL
    runs = sems.shape[0]
    run = ZL // runs
    step = run * tile
    small = one_hot(lambda k: lax.rem(k, run) * tile + lax.div(k, run), (step, step))
    turned = in_ref[...].T
    copies = []
    for b in range(runs):
        here = pl.ds(b * step, step)
        piece = jnp.concatenate([turned[c * ZL + b * run:c * ZL + (b + 1) * run] for c in range(tile)], axis=0)
        out_ref[here, :] = mm(small, piece).astype(BF)
        copy = pltpu.make_async_copy(out_ref.at[here], out_hbm.at[here], sems.at[b])
        copy.start()
        copies.append(copy)
    for copy in copies:
        copy.wait()


def column_tables(inverse_halo, cov_plane, cov_vert):
    own, halo = inverse_halo.shape
    wide, narrow = lax.axis_size("wide"), lax.axis_size("narrow")
    width = narrow * LANES
    plane = cov_plane.shape[0]
    shape = jax.ShapeDtypeStruct
    order = call(order_body, [shape((own, own), BF), shape((halo, own), BF)], [inverse_halo])
    rest = call(
        functools.partial(tables_body, wide, narrow),
        [shape((plane, plane), BF), shape((width, width), BF), shape((width, width), BF)],
        [cov_plane, cov_vert],
    )
    return [tuple(order), tuple(rest)]


def smooth_by_columns(state, inverse_halo, got, tables):
    wide, narrow = lax.axis_size("wide"), lax.axis_size("narrow")
    own, columns = state.shape
    devices = wide * narrow
    group = columns // devices
    depth = narrow * ZL
    tile = own // ZL
    shape = jax.ShapeDtypeStruct
    (order, halo_table), (plane_mix, spread, vert_mix) = tables
    (turned,) = call(turn_body, [shape((columns, own), F32)], [state, order])
    (wire,) = call(functools.partial(wire_body, len(got)), [shape((columns, own), BF)], [turned, halo_table, *got])
    there = lax.all_to_all(
        wire.reshape(devices, group, own), ("narrow", "wide"), split_axis=0, concat_axis=0, tiled=True
    )
    mixed, adjoint = call(
        functools.partial(mix_body, wide, narrow, group),
        [shape((columns, own), BF), shape((own, columns), BF)],
        [there.reshape(columns, own), plane_mix, spread, vert_mix, state, inverse_halo, *got],
        [
            pltpu.VMEM((tile, wide * group + group, depth), F32),
            pltpu.VMEM((plane_mix.shape[0], group * depth), BF),
            pltpu.VMEM((own // LANES, columns + group, LANES), F32),
            pltpu.VMEM((own, columns), BF),
            pltpu.SemaphoreType.DMA,
        ],
        out_specs=[VM, ANY],
    )
    back = lax.all_to_all(
        mixed.reshape(devices, group, own), ("narrow", "wide"), split_axis=0, concat_axis=0, tiled=True
    )
    (smoothed,) = call(
        unwire_body,
        [shape((own, columns), BF)],
        [back.reshape(columns, own)],
        [pltpu.VMEM((own, columns), BF), pltpu.SemaphoreType.DMA((4,))],
        out_specs=[ANY],
    )
    return adjoint, smoothed


def smooth_by_layers(adjoint, cov_plane, cov_vert):
    own, columns = adjoint.shape
    layered = adjoint.reshape(ZL, own // ZL, -1)
    planar = jnp.einsum(
        "pq,lqr->lpr",
        cov_plane,
        lax.all_to_all(layered, "wide", split_axis=0, concat_axis=1, tiled=True),
        preferred_element_type=F32,
    ).astype(BF)
    restored = lax.all_to_all(planar, "wide", split_axis=1, concat_axis=0, tiled=True)
    slab_weights = lax.dynamic_slice_in_dim(cov_vert, lax.axis_index("narrow") * ZL, ZL, 0)
    summed = jnp.dot(
        slab_weights,
        lax.all_gather(restored.reshape(ZL, -1), "narrow", axis=0, tiled=True),
        preferred_element_type=F32,
    )
    return summed.astype(BF).reshape(own, -1)


def shards(adjoint_rhs, inverse_rows, blocks, block_cols, send_rows, cov_plane, cov_vert):
    rhs = adjoint_rhs[0, 0]
    inverse = inverse_rows[0, 0]
    block_values = blocks[0, 0]
    cols = block_cols[0, 0]
    send_index = send_rows[0, 0]
    own, columns = rhs.shape
    width = send_index.shape[1]
    halo = 4 * width
    wide, narrow = lax.axis_size("wide"), lax.axis_size("narrow")
    group = columns // (wide * narrow)
    by_columns = columns % (wide * narrow) == 0 and group % 8 == 0 and narrow * ZL == LANES and wide % 16 == 0
    found = matchings()
    count = len(found)
    sent = count * width
    shape = jax.ShapeDtypeStruct
    notes = [shape((width, columns), BF)] * count
    full = shape((own, columns), F32)
    base_shape = shape((sent, columns), F32)
    cell_space = pltpu.VMEM((own, columns), BF)
    (select,) = call(
        functools.partial(select_body, found, own),
        [shape((sent, own), BF)],
        [send_index],
        flops=SELECT_FLOPS,
    )
    messages = call(pick_body, notes, [select, rhs], flops=PICK_FLOPS)
    got = swap(messages, found)
    inverse_halo, blocks_halo, inverse_sent, blocks_sent, state, base = call(
        functools.partial(setup_body, found, width),
        [
            shape((own, halo), BF),
            shape((2, own, halo), BF),
            shape((sent, halo), BF),
            shape((2 * sent, halo), BF),
            full,
            base_shape,
        ],
        [cols, inverse, block_values, rhs, select],
        [cell_space, cell_space],
        limit=12,
    )
    tables = column_tables(inverse_halo, cov_plane, cov_vert) if by_columns else []
    for sweep in range(SWEEPS - 1):
        messages = call(
            functools.partial(sent_update_body, count), notes, [base, inverse_sent, *got], limit=4
        )
        arrived, got = got, swap(messages, found)
        iterate, part, base = call(
            functools.partial(update_body, count),
            [full, full, base_shape],
            [cols, state, inverse_halo, block_values, rhs, select, *arrived],
            [pltpu.VMEM((own + halo, columns), BF), cell_space, cell_space],
        )
        turn = 1 if sweep == 1 and count == 3 else 0
        arrived = got[count - turn:] + got[:count - turn]
        messages = call(
            functools.partial(sent_residual_body, count, turn),
            notes,
            [base, blocks_sent, *arrived],
            limit=4,
        )
        got = swap(messages, found)
        if sweep < len(tables):
            tables[sweep], part = lax.optimization_barrier((tables[sweep], part))
        more = sweep < SWEEPS - 2
        state, *bases = call(
            functools.partial(residual_body, count, turn),
            [full] + [base_shape] * more,
            [part, blocks_halo, iterate, inverse, select, *arrived],
            [cell_space] * (1 + 2 * more),
        )
        base = bases[0] if more else None
    if by_columns:
        adjoint, smoothed = smooth_by_columns(state, inverse_halo, got, tables)
    else:
        cells = shape((own, columns), BF)
        (adjoint,) = call(functools.partial(last_update_body, count), [cells], [state, inverse_halo, *got])
        smoothed = smooth_by_layers(adjoint, cov_plane, cov_vert)
    return (adjoint[None, None], smoothed[None, None])


def solution(mesh):
    in_specs = (
        P("wide", "narrow", None, None),
        P("wide", "narrow", None, None),
        P("wide", "narrow", None, None, None, None),
        P("wide", "narrow", None, None),
        P("wide", "narrow", None, None),
        P(),
        P(),
    )
    out_specs = (P("wide", "narrow", None, None), P("wide", "narrow", None, None))
    return jax.shard_map(shards, mesh=mesh, in_specs=in_specs, out_specs=out_specs, check_vma=False)
```

```python
import functools

import jax
import jax.numpy as jnp
from jax import lax
from jax.experimental import pallas as pl
from jax.experimental.pallas import tpu as pltpu
from jax.sharding import PartitionSpec as P

ZL = 64
SWEEPS = 4
LANES = 128
SELECT_FLOPS = 6 * 10 ** 8
PICK_FLOPS = 2 * 10 ** 9
BF = jnp.bfloat16
F32 = jnp.float32
VM = pl.BlockSpec(memory_space=pltpu.VMEM)
ANY = pl.BlockSpec(memory_space=pl.ANY)


def wide_slot(w, n, parity):
    return (w & 1) ^ parity ^ 1


def narrow_slot(w, n, parity):
    return 2 + ((n & 1) ^ parity ^ 1)


def mixed_slot(w, n, kind):
    turn = (w ^ (w >> 1) ^ kind) & 1
    return (1 - turn) * wide_slot(w, n, 1) + turn * narrow_slot(w, n, 0)


def has_partner(w, n, slot, wide, narrow):
    inside = [w > 0, w + 1 < wide, n > 0, n + 1 < narrow]
    return sum((slot == k) * inside[k] for k in range(4))


def matchings():
    wide, narrow = lax.axis_size("wide"), lax.axis_size("narrow")
    if narrow == 2 and wide % 4 == 0:
        rules = [(mixed_slot, 0), (mixed_slot, 1), (wide_slot, 0)]
    else:
        rules = [(wide_slot, 1)] * (wide > 2) + [(narrow_slot, 1)] * (narrow > 2)
        rules += [(narrow_slot, 0)] * (narrow > 1) + [(wide_slot, 0)] * (wide > 1)
    found = []
    for rule, kind in rules:
        pairs = []
        for w in range(wide):
            for n in range(narrow):
                slot = rule(w, n, kind)
                if has_partner(w, n, slot, wide, narrow):
                    step = ((-1, 0), (1, 0), (0, -1), (0, 1))[slot]
                    target = (w + step[0], n + step[1])
                elif slot < 2:
                    target = (w, n ^ 1 if n ^ 1 < narrow else n)
                else:
                    target = (w ^ 1 if w ^ 1 < wide else w, n)
                pairs.append((w * narrow + n, target[0] * narrow + target[1]))
        found.append((rule, kind, tuple(pairs)))
    return found


def own_slots(found):
    w, n = lax.axis_index("wide"), lax.axis_index("narrow")
    wide, narrow = lax.axis_size("wide"), lax.axis_size("narrow")
    slots = [rule(w, n, kind) for rule, kind, _ in found]
    return [(slot, has_partner(w, n, slot, wide, narrow) == 1) for slot in slots]


def swap(messages, found):
    return [lax.ppermute(m, ("wide", "narrow"), list(f[-1])) for m, f in zip(messages, found)]


def mm(a, b):
    return jnp.dot(a, b, preferred_element_type=F32)


def mm_t(a, b):
    return lax.dot_general(a, b, (((1,), (1,)), ((), ())), preferred_element_type=F32)


def iota(shape, dim):
    return lax.broadcasted_iota(jnp.int32, shape, dim)


def call(body, outs, args, scratch=(), specs=None, flops=0, limit=8, out_specs=None):
    size = sum(a.size * a.dtype.itemsize for a in args)
    return pl.pallas_call(
        body,
        out_shape=outs,
        in_specs=specs or [VM] * len(args),
        out_specs=out_specs or [VM] * len(outs),
        scratch_shapes=list(scratch),
        compiler_params=pltpu.CompilerParams(vmem_limit_bytes=limit * 1024 * 1024),
        cost_estimate=pl.CostEstimate(flops=flops, bytes_accessed=size, transcendentals=0),
    )(*args)


def exchange_columns(values):
    wide, narrow = lax.axis_size("wide"), lax.axis_size("narrow")
    rows, lanes = values.shape
    devices = wide * narrow
    group, parts = rows // devices, lanes // LANES
    cut = values.reshape(devices, group, parts, LANES).transpose(0, 2, 1, 3).reshape(devices, -1, LANES)
    moved = lax.all_to_all(cut, ("narrow", "wide"), split_axis=0, concat_axis=0, tiled=True)
    return moved.reshape(devices, parts, group, LANES).transpose(0, 2, 1, 3).reshape(rows, lanes)


def join_halo(got):
    pieces = [piece[...] for piece in got]
    return jnp.concatenate(pieces + [jnp.zeros_like(pieces[0])] * (4 - len(pieces)), axis=0)


def send(messages, values):
    width = messages[0].shape[0]
    for m, message in enumerate(messages):
        message[...] = values[m * width:(m + 1) * width, :].astype(BF)


def keep_split(high_ref, low_ref, rows, value):
    high = value.astype(BF)
    high_ref[rows] = high
    low_ref[rows] = (value - high.astype(F32)).astype(BF)


def select_body(found, own, send_ref, select_ref):
    width = send_ref.shape[1]
    diagonal = iota((width, width), 0) == iota((width, width), 1)
    pieces = []
    for slot, paired in own_slots(found):
        rows = jnp.where(paired, send_ref[pl.ds(slot, 1), :], -1).astype(F32)
        pieces.append(jnp.where(diagonal, rows, 0.0))
    column = jnp.sum(jnp.concatenate(pieces, axis=0), axis=1, keepdims=True).astype(jnp.int32)
    select_ref[...] = (iota((len(found) * width, own), 1) == column).astype(F32).astype(BF)


def pick_body(select_ref, rhs_ref, *messages):
    send(messages, mm(select_ref[...], rhs_ref[...]))


def setup_body(found, width, cols_ref, inverse_ref, blocks_ref, rhs_ref, select_ref, *rest):
    inverse_halo_ref, blocks_halo_ref, inverse_sent_ref, blocks_sent_ref, state_ref, base_ref = rest[:6]
    high_ref, low_ref = rest[6:]
    own = rhs_ref.shape[0]
    halo = 4 * width
    places = iota((1, halo), 1)
    starts = jnp.full((1, halo), -halo, jnp.int32)
    for m, (slot, _) in enumerate(own_slots(found)):
        here = lax.div(places, width) == m
        starts = jnp.where(here, slot * width + lax.rem(places, width), starts)
    arrange = (iota((halo, halo), 0) == starts).astype(F32).astype(BF)
    rows, links, size, _ = blocks_ref.shape
    for j in range(rows):
        here = slice(j * size, (j + 1) * size)
        columns = [cols_ref[j, k] for k in range(links)]
        for c in range(halo // size):
            total = None
            for k in range(links):
                part = jnp.where(columns[k] == own // size + c, blocks_ref[j, k].astype(F32), 0.0)
                total = part if total is None else total + part
            lanes = slice(c * size, (c + 1) * size)
            keep_split(high_ref, low_ref, (here, lanes), total)
    for part, half_ref in enumerate((high_ref, low_ref)):
        blocks_halo_ref[part] = mm(half_ref[...], arrange).astype(BF)
    step = own // 2
    for i in range(0, own, step):
        here = slice(i, i + step)
        inverse_halo_ref[here, :] = mm(inverse_ref[here, own:], arrange).astype(BF)
        value = mm(inverse_ref[here, :own], rhs_ref[...])
        state_ref[here, :] = value
        keep_split(high_ref, low_ref, here, value)
    inverse_sent_ref[...] = mm(select_ref[...], inverse_halo_ref[...]).astype(BF)
    sent = select_ref.shape[0]
    for part in range(2):
        here = slice(part * sent, (part + 1) * sent)
        blocks_sent_ref[here, :] = mm(select_ref[...], blocks_halo_ref[part]).astype(BF)
    base_ref[...] = mm(select_ref[...], high_ref[...]) + mm(select_ref[...], low_ref[...])


def sent_update_body(count, base_ref, sent_ref, *rest):
    got, messages = rest[:count], rest[count:]
    halo = jnp.concatenate([piece[...] for piece in got], axis=0)
    send(messages, base_ref[...] + mm(sent_ref[:, :halo.shape[0]], halo))


def sent_residual_body(count, turn, base_ref, sent_ref, *rest):
    got, messages = rest[:count], rest[count:]
    halo = jnp.concatenate([piece[...] for piece in got[turn:] + got[:turn]], axis=0)
    part = mm(sent_ref[:, :halo.shape[0]], halo)
    sent = base_ref.shape[0]
    send(messages, base_ref[...] - (part[:sent] + part[sent:]))


def update_body(count, cols_ref, state_ref, inverse_halo_ref, blocks_ref, rhs_ref, select_ref, *rest):
    got, (iterate_ref, part_ref, base_ref, sub_ref, high_ref, low_ref) = rest[:count], rest[count:]
    own = state_ref.shape[0]
    halo = join_halo(got)
    step = own // 2
    for i in range(0, own, step):
        here = slice(i, i + step)
        value = state_ref[here, :] + mm(inverse_halo_ref[here, :], halo)
        iterate_ref[here, :] = value
        sub_ref[here, :] = value.astype(BF)
    sub_ref[own:, :] = jnp.zeros((sub_ref.shape[0] - own, sub_ref.shape[1]), BF)
    rows, links, size, _ = blocks_ref.shape
    for j in range(rows):
        starts = [pl.multiple_of(cols_ref[j, k] * size, size) for k in range(links)]
        values = jnp.concatenate([blocks_ref[j, k] for k in range(links)], axis=1)
        coupled = jnp.concatenate([sub_ref[pl.ds(start, size), :] for start in starts], axis=0)
        total = mm(values, coupled)
        here = slice(j * size, (j + 1) * size)
        value = rhs_ref[here, :].astype(F32) - total
        part_ref[here, :] = value
        keep_split(high_ref, low_ref, here, value)
    base_ref[...] = mm(select_ref[...], high_ref[...]) + mm(select_ref[...], low_ref[...])


def residual_body(count, turn, part_ref, blocks_halo_ref, iterate_ref, inverse_ref, select_ref, *rest):
    got, rest = rest[:count], list(rest[count:])
    state_ref = rest.pop(0)
    resid_ref, *split = rest[-3:] if len(rest) == 4 else rest
    own = part_ref.shape[0]
    halo = join_halo(got[turn:] + got[:turn])
    step = own // 2
    for i in range(0, own, step):
        here = slice(i, i + step)
        outer = mm(blocks_halo_ref[0, here, :], halo) + mm(blocks_halo_ref[1, here, :], halo)
        resid_ref[here, :] = (part_ref[here, :] - outer).astype(BF)
    for i in range(0, own, step):
        here = slice(i, i + step)
        value = iterate_ref[here, :] + mm(inverse_ref[here, :own], resid_ref[...])
        state_ref[here, :] = value
        if split:
            keep_split(*split, here, value)
    if split:
        rest[0][...] = mm(select_ref[...], split[0][...]) + mm(select_ref[...], split[1][...])


def last_update_body(count, state_ref, inverse_halo_ref, *rest):
    got, (round_ref,) = rest[:count], rest[count:]
    halo = join_halo(got)
    step = state_ref.shape[0] // 2
    for i in range(0, state_ref.shape[0], step):
        here = slice(i, i + step)
        round_ref[here, :] = (state_ref[here, :] + mm(inverse_halo_ref[here, :], halo)).astype(BF)


def turn_body(state_ref, order_ref, turned_ref):
    value = state_ref[...]
    high = value.astype(BF)
    low = (value - high.astype(F32)).astype(BF)
    columns = value.shape[1]
    both = mm(jnp.concatenate([high, low], axis=1).T, order_ref[...])
    turned_ref[...] = both[:columns] + both[columns:]


def wire_body(count, turned_ref, halo_table_ref, *rest):
    got, (wire_ref,) = rest[:count], rest[count:]
    wire_ref[...] = (turned_ref[...] + mm(join_halo(got).T, halo_table_ref[...])).astype(BF)


def one_hot(rows_of, shape):
    return (iota(shape, 0) == rows_of(iota((1, shape[1]), 1))).astype(F32).astype(BF)


def order_body(inverse_halo_ref, order_ref, halo_table_ref):
    own = order_ref.shape[0]
    tile = own // ZL
    order_ref[...] = one_hot(lambda k: lax.rem(k, ZL) * tile + lax.div(k, ZL), (own, own))
    halo_table_ref[...] = mm(inverse_halo_ref[...].T, order_ref[...]).astype(BF)


def tables_body(wide, narrow, cov_plane_ref, cov_vert_ref, plane_ref, spread_ref, vert_ref):
    plane = plane_ref.shape[0]
    tile = plane // wide
    turn = one_hot(lambda k: lax.rem(k, wide) * tile + lax.div(k, wide), (plane, plane))
    half = mm(cov_plane_ref[...], turn).astype(BF)
    plane_ref[...] = mm(half.T, turn).astype(BF).T
    share = LANES // ZL
    depth = narrow * ZL
    width = narrow * LANES

    def source(k):
        e, n, l = lax.div(k, depth), lax.rem(lax.div(k, ZL), narrow), lax.rem(k, ZL)
        return n * LANES + e * ZL + l

    spread = one_hot(source, (width, width))
    spread_ref[...] = spread
    turned = cov_vert_ref[...].astype(F32).T
    zero = jnp.zeros_like(turned)
    blocks = jnp.concatenate(
        [jnp.concatenate([turned if i == e else zero for i in range(share)], axis=1) for e in range(share)],
        axis=0,
    ).astype(BF)
    vert_ref[...] = mm_t(blocks, spread).astype(BF)


def mix_body(wide, narrow, group, in_ref, plane_ref, spread_ref, vert_ref, state_ref, inverse_halo_ref, *rest):
    got, (out_ref, adjoint_hbm, cells_ref, flat_ref, wire_ref, round_ref, sem) = rest[:-7], rest[-7:]
    last_update_body(len(got), state_ref, inverse_halo_ref, *got, round_ref)
    keep = pltpu.make_async_copy(round_ref, adjoint_hbm, sem)
    keep.start()
    own = in_ref.shape[1]
    tile = own // ZL
    share = LANES // ZL
    depth = narrow * ZL
    block = wide * group
    for g in range(tile // share):
        lanes = slice(g * LANES, (g + 1) * LANES)
        joined = jnp.concatenate([in_ref[n * block:(n + 1) * block, lanes] for n in range(narrow)], axis=1)
        spread = mm(joined, spread_ref[...])
        for e in range(share):
            cells_ref[g * share + e, :block, :] = spread[:, e * depth:(e + 1) * depth]
    for r in range(group):
        for c in range(tile):
            flat_ref[c * wide:(c + 1) * wide, r * depth:(r + 1) * depth] = cells_ref[
                c, pl.ds(r, wide, stride=group), :
            ].astype(BF)
    planar = mm(plane_ref[...], flat_ref[...]).astype(BF)
    for g in range(tile // share):
        stacked = jnp.concatenate(
            [
                jnp.concatenate(
                    [
                        planar[c * wide:(c + 1) * wide, r * depth:(r + 1) * depth]
                        for c in range(g * share, (g + 1) * share)
                    ],
                    axis=1,
                )
                for r in range(group)
            ],
            axis=0,
        )
        mixed = mm(stacked, vert_ref[...])
        for r in range(group):
            for n in range(narrow):
                wire_ref[g, pl.ds(n * block + r, wide, stride=group), :] = mixed[
                    r * wide:(r + 1) * wide, n * LANES:(n + 1) * LANES
                ]
        out_ref[:, g * LANES:(g + 1) * LANES] = wire_ref[g, :narrow * block, :].astype(BF)
    keep.wait()


def unwire_body(in_ref, out_hbm, out_ref, sems):
    own = out_ref.shape[0]
    tile = own // ZL
    runs = sems.shape[0]
    run = ZL // runs
    step = run * tile
    small = one_hot(lambda k: lax.rem(k, run) * tile + lax.div(k, run), (step, step))
    turned = in_ref[...].T
    copies = []
    for b in range(runs):
        here = pl.ds(b * step, step)
        piece = jnp.concatenate([turned[c * ZL + b * run:c * ZL + (b + 1) * run] for c in range(tile)], axis=0)
        out_ref[here, :] = mm(small, piece).astype(BF)
        copy = pltpu.make_async_copy(out_ref.at[here], out_hbm.at[here], sems.at[b])
        copy.start()
        copies.append(copy)
    for copy in copies:
        copy.wait()


def column_tables(inverse_halo, cov_plane, cov_vert):
    own, halo = inverse_halo.shape
    wide, narrow = lax.axis_size("wide"), lax.axis_size("narrow")
    width = narrow * LANES
    plane = cov_plane.shape[0]
    shape = jax.ShapeDtypeStruct
    order = call(order_body, [shape((own, own), BF), shape((halo, own), BF)], [inverse_halo])
    rest = call(
        functools.partial(tables_body, wide, narrow),
        [shape((plane, plane), BF), shape((width, width), BF), shape((width, width), BF)],
        [cov_plane, cov_vert],
    )
    return [tuple(order), tuple(rest)]


def smooth_by_columns(state, inverse_halo, got, tables):
    wide, narrow = lax.axis_size("wide"), lax.axis_size("narrow")
    own, columns = state.shape
    devices = wide * narrow
    group = columns // devices
    depth = narrow * ZL
    tile = own // ZL
    shape = jax.ShapeDtypeStruct
    (order, halo_table), (plane_mix, spread, vert_mix) = tables
    (turned,) = call(turn_body, [shape((columns, own), F32)], [state, order])
    (wire,) = call(functools.partial(wire_body, len(got)), [shape((columns, own), BF)], [turned, halo_table, *got])
    there = exchange_columns(wire)
    mixed, adjoint = call(
        functools.partial(mix_body, wide, narrow, group),
        [shape((columns, own), BF), shape((own, columns), BF)],
        [there, plane_mix, spread, vert_mix, state, inverse_halo, *got],
        [
            pltpu.VMEM((tile, wide * group + group, depth), F32),
            pltpu.VMEM((plane_mix.shape[0], group * depth), BF),
            pltpu.VMEM((own // LANES, columns + group, LANES), F32),
            pltpu.VMEM((own, columns), BF),
            pltpu.SemaphoreType.DMA,
        ],
        out_specs=[VM, ANY],
    )
    back = exchange_columns(mixed)
    (smoothed,) = call(
        unwire_body,
        [shape((own, columns), BF)],
        [back],
        [pltpu.VMEM((own, columns), BF), pltpu.SemaphoreType.DMA((4,))],
        out_specs=[ANY],
    )
    return adjoint, smoothed


def smooth_by_layers(adjoint, cov_plane, cov_vert):
    own, columns = adjoint.shape
    layered = adjoint.reshape(ZL, own // ZL, -1)
    planar = jnp.einsum(
        "pq,lqr->lpr",
        cov_plane,
        lax.all_to_all(layered, "wide", split_axis=0, concat_axis=1, tiled=True),
        preferred_element_type=F32,
    ).astype(BF)
    restored = lax.all_to_all(planar, "wide", split_axis=1, concat_axis=0, tiled=True)
    slab_weights = lax.dynamic_slice_in_dim(cov_vert, lax.axis_index("narrow") * ZL, ZL, 0)
    summed = jnp.dot(
        slab_weights,
        lax.all_gather(restored.reshape(ZL, -1), "narrow", axis=0, tiled=True),
        preferred_element_type=F32,
    )
    return summed.astype(BF).reshape(own, -1)


def shards(adjoint_rhs, inverse_rows, blocks, block_cols, send_rows, cov_plane, cov_vert):
    rhs = adjoint_rhs[0, 0]
    inverse = inverse_rows[0, 0]
    block_values = blocks[0, 0]
    cols = block_cols[0, 0]
    send_index = send_rows[0, 0]
    own, columns = rhs.shape
    width = send_index.shape[1]
    halo = 4 * width
    wide, narrow = lax.axis_size("wide"), lax.axis_size("narrow")
    group = columns // (wide * narrow)
    by_columns = columns % (wide * narrow) == 0 and group % 8 == 0 and narrow * ZL == LANES and wide % 16 == 0
    found = matchings()
    count = len(found)
    sent = count * width
    shape = jax.ShapeDtypeStruct
    notes = [shape((width, columns), BF)] * count
    full = shape((own, columns), F32)
    base_shape = shape((sent, columns), F32)
    cell_space = pltpu.VMEM((own, columns), BF)
    (select,) = call(
        functools.partial(select_body, found, own),
        [shape((sent, own), BF)],
        [send_index],
        flops=SELECT_FLOPS,
    )
    messages = call(pick_body, notes, [select, rhs], flops=PICK_FLOPS)
    got = swap(messages, found)
    inverse_halo, blocks_halo, inverse_sent, blocks_sent, state, base = call(
        functools.partial(setup_body, found, width),
        [
            shape((own, halo), BF),
            shape((2, own, halo), BF),
            shape((sent, halo), BF),
            shape((2 * sent, halo), BF),
            full,
            base_shape,
        ],
        [cols, inverse, block_values, rhs, select],
        [cell_space, cell_space],
        limit=12,
    )
    tables = column_tables(inverse_halo, cov_plane, cov_vert) if by_columns else []
    for sweep in range(SWEEPS - 1):
        messages = call(
            functools.partial(sent_update_body, count), notes, [base, inverse_sent, *got], limit=4
        )
        arrived, got = got, swap(messages, found)
        iterate, part, base = call(
            functools.partial(update_body, count),
            [full, full, base_shape],
            [cols, state, inverse_halo, block_values, rhs, select, *arrived],
            [pltpu.VMEM((own + halo, columns), BF), cell_space, cell_space],
        )
        turn = 1 if sweep == 1 and count == 3 else 0
        arrived = got[count - turn:] + got[:count - turn]
        messages = call(
            functools.partial(sent_residual_body, count, turn),
            notes,
            [base, blocks_sent, *arrived],
            limit=4,
        )
        got = swap(messages, found)
        if sweep < len(tables):
            tables[sweep], part = lax.optimization_barrier((tables[sweep], part))
        more = sweep < SWEEPS - 2
        state, *bases = call(
            functools.partial(residual_body, count, turn),
            [full] + [base_shape] * more,
            [part, blocks_halo, iterate, inverse, select, *arrived],
            [cell_space] * (1 + 2 * more),
        )
        base = bases[0] if more else None
    if by_columns:
        adjoint, smoothed = smooth_by_columns(state, inverse_halo, got, tables)
    else:
        cells = shape((own, columns), BF)
        (adjoint,) = call(functools.partial(last_update_body, count), [cells], [state, inverse_halo, *got])
        smoothed = smooth_by_layers(adjoint, cov_plane, cov_vert)
    return (adjoint[None, None], smoothed[None, None])


def solution(mesh):
    in_specs = (
        P("wide", "narrow", None, None),
        P("wide", "narrow", None, None),
        P("wide", "narrow", None, None, None, None),
        P("wide", "narrow", None, None),
        P("wide", "narrow", None, None),
        P(),
        P(),
    )
    out_specs = (P("wide", "narrow", None, None), P("wide", "narrow", None, None))
    return jax.shard_map(shards, mesh=mesh, in_specs=in_specs, out_specs=out_specs, check_vma=False)
```

```python
import functools

import jax
import jax.numpy as jnp
from jax import lax
from jax.experimental import pallas as pl
from jax.experimental.pallas import tpu as pltpu
from jax.sharding import PartitionSpec as P

ZL = 64
SWEEPS = 4
LANES = 128
SELECT_FLOPS = 6 * 10 ** 8
PICK_FLOPS = 2 * 10 ** 9
BF = jnp.bfloat16
F32 = jnp.float32
VM = pl.BlockSpec(memory_space=pltpu.VMEM)
ANY = pl.BlockSpec(memory_space=pl.ANY)


def wide_slot(w, n, parity):
    return (w & 1) ^ parity ^ 1


def narrow_slot(w, n, parity):
    return 2 + ((n & 1) ^ parity ^ 1)


def has_partner(w, n, slot, wide, narrow):
    inside = [w > 0, w + 1 < wide, n > 0, n + 1 < narrow]
    return sum((slot == k) * inside[k] for k in range(4))


def matchings():
    wide, narrow = lax.axis_size("wide"), lax.axis_size("narrow")
    rules = [(wide_slot, 1)] * (wide > 2) + [(narrow_slot, 1)] * (narrow > 2)
    rules += [(narrow_slot, 0)] * (narrow > 1) + [(wide_slot, 0)] * (wide > 1)
    found = []
    for rule, kind in rules:
        pairs = []
        for w in range(wide):
            for n in range(narrow):
                slot = rule(w, n, kind)
                if has_partner(w, n, slot, wide, narrow):
                    step = ((-1, 0), (1, 0), (0, -1), (0, 1))[slot]
                    target = (w + step[0], n + step[1])
                elif slot < 2:
                    target = (w, n ^ 1 if n ^ 1 < narrow else n)
                else:
                    target = (w ^ 1 if w ^ 1 < wide else w, n)
                pairs.append((w * narrow + n, target[0] * narrow + target[1]))
        found.append((rule, kind, tuple(pairs)))
    return found


def own_slots(found):
    w, n = lax.axis_index("wide"), lax.axis_index("narrow")
    wide, narrow = lax.axis_size("wide"), lax.axis_size("narrow")
    slots = [rule(w, n, kind) for rule, kind, _ in found]
    return [(slot, has_partner(w, n, slot, wide, narrow) == 1) for slot in slots]


def swap(messages, found):
    return [lax.ppermute(m, ("wide", "narrow"), list(f[-1])) for m, f in zip(messages, found)]


def mm(a, b):
    return jnp.dot(a, b, preferred_element_type=F32)


def mm_t(a, b):
    return lax.dot_general(a, b, (((1,), (1,)), ((), ())), preferred_element_type=F32)


def iota(shape, dim):
    return lax.broadcasted_iota(jnp.int32, shape, dim)


def call(body, outs, args, scratch=(), specs=None, flops=0, limit=8, out_specs=None):
    size = sum(a.size * a.dtype.itemsize for a in args)
    return pl.pallas_call(
        body,
        out_shape=outs,
        in_specs=specs or [VM] * len(args),
        out_specs=out_specs or [VM] * len(outs),
        scratch_shapes=list(scratch),
        compiler_params=pltpu.CompilerParams(vmem_limit_bytes=limit * 1024 * 1024),
        cost_estimate=pl.CostEstimate(flops=flops, bytes_accessed=size, transcendentals=0),
    )(*args)


def join_halo(got):
    pieces = [piece[...] for piece in got]
    return jnp.concatenate(pieces + [jnp.zeros_like(pieces[0])] * (4 - len(pieces)), axis=0)


def send(messages, values):
    width = messages[0].shape[0]
    for m, message in enumerate(messages):
        message[...] = values[m * width:(m + 1) * width, :].astype(BF)


def keep_split(high_ref, low_ref, rows, value):
    high = value.astype(BF)
    high_ref[rows] = high
    low_ref[rows] = (value - high.astype(F32)).astype(BF)


def select_body(found, own, send_ref, select_ref):
    width = send_ref.shape[1]
    diagonal = iota((width, width), 0) == iota((width, width), 1)
    pieces = []
    for slot, paired in own_slots(found):
        rows = jnp.where(paired, send_ref[pl.ds(slot, 1), :], -1).astype(F32)
        pieces.append(jnp.where(diagonal, rows, 0.0))
    column = jnp.sum(jnp.concatenate(pieces, axis=0), axis=1, keepdims=True).astype(jnp.int32)
    select_ref[...] = (iota((len(found) * width, own), 1) == column).astype(F32).astype(BF)


def pick_body(select_ref, rhs_ref, *messages):
    send(messages, mm(select_ref[...], rhs_ref[...]))


def setup_body(found, width, cols_ref, inverse_ref, blocks_ref, rhs_ref, select_ref, *rest):
    inverse_halo_ref, blocks_halo_ref, inverse_sent_ref, blocks_sent_ref, state_ref, base_ref = rest[:6]
    high_ref, low_ref = rest[6:]
    own = rhs_ref.shape[0]
    halo = 4 * width
    places = iota((1, halo), 1)
    starts = jnp.full((1, halo), -halo, jnp.int32)
    for m, (slot, _) in enumerate(own_slots(found)):
        here = lax.div(places, width) == m
        starts = jnp.where(here, slot * width + lax.rem(places, width), starts)
    arrange = (iota((halo, halo), 0) == starts).astype(F32).astype(BF)
    rows, links, size, _ = blocks_ref.shape
    for j in range(rows):
        here = slice(j * size, (j + 1) * size)
        columns = [cols_ref[j, k] for k in range(links)]
        for c in range(halo // size):
            total = None
            for k in range(links):
                part = jnp.where(columns[k] == own // size + c, blocks_ref[j, k].astype(F32), 0.0)
                total = part if total is None else total + part
            lanes = slice(c * size, (c + 1) * size)
            keep_split(high_ref, low_ref, (here, lanes), total)
    for part, half_ref in enumerate((high_ref, low_ref)):
        blocks_halo_ref[part] = mm(half_ref[...], arrange).astype(BF)
    step = own // 2
    for i in range(0, own, step):
        here = slice(i, i + step)
        inverse_halo_ref[here, :] = mm(inverse_ref[here, own:], arrange).astype(BF)
        value = mm(inverse_ref[here, :own], rhs_ref[...])
        state_ref[here, :] = value
        keep_split(high_ref, low_ref, here, value)
    inverse_sent_ref[...] = mm(select_ref[...], inverse_halo_ref[...]).astype(BF)
    sent = select_ref.shape[0]
    for part in range(2):
        here = slice(part * sent, (part + 1) * sent)
        blocks_sent_ref[here, :] = mm(select_ref[...], blocks_halo_ref[part]).astype(BF)
    base_ref[...] = mm(select_ref[...], high_ref[...]) + mm(select_ref[...], low_ref[...])


def sent_update_body(count, base_ref, sent_ref, *rest):
    got, messages = rest[:count], rest[count:]
    send(messages, base_ref[...] + mm(sent_ref[...], join_halo(got)))


def sent_residual_body(count, turn, base_ref, sent_ref, *rest):
    got, messages = rest[:count], rest[count:]
    halo = join_halo(got[turn:] + got[:turn])
    part = mm(sent_ref[...], halo)
    sent = base_ref.shape[0]
    send(messages, base_ref[...] - (part[:sent] + part[sent:]))


def update_body(count, cols_ref, state_ref, inverse_halo_ref, blocks_ref, rhs_ref, select_ref, *rest):
    got, (iterate_ref, part_ref, base_ref, sub_ref, high_ref, low_ref) = rest[:count], rest[count:]
    own = state_ref.shape[0]
    halo = join_halo(got)
    step = own // 2
    for i in range(0, own, step):
        here = slice(i, i + step)
        value = state_ref[here, :] + mm(inverse_halo_ref[here, :], halo)
        iterate_ref[here, :] = value
        sub_ref[here, :] = value.astype(BF)
    sub_ref[own:, :] = jnp.zeros((sub_ref.shape[0] - own, sub_ref.shape[1]), BF)
    rows, links, size, _ = blocks_ref.shape
    for j in range(rows):
        starts = [pl.multiple_of(cols_ref[j, k] * size, size) for k in range(links)]
        values = jnp.concatenate([blocks_ref[j, k] for k in range(links)], axis=1)
        coupled = jnp.concatenate([sub_ref[pl.ds(start, size), :] for start in starts], axis=0)
        total = mm(values, coupled)
        here = slice(j * size, (j + 1) * size)
        value = rhs_ref[here, :].astype(F32) - total
        part_ref[here, :] = value
        keep_split(high_ref, low_ref, here, value)
    base_ref[...] = mm(select_ref[...], high_ref[...]) + mm(select_ref[...], low_ref[...])


def residual_body(count, turn, part_ref, blocks_halo_ref, iterate_ref, inverse_ref, select_ref, *rest):
    got, rest = rest[:count], list(rest[count:])
    state_ref = rest.pop(0)
    resid_ref, *split = rest[-3:] if len(rest) == 4 else rest
    own = part_ref.shape[0]
    halo = join_halo(got[turn:] + got[:turn])
    step = own // 2
    for i in range(0, own, step):
        here = slice(i, i + step)
        outer = mm(blocks_halo_ref[0, here, :], halo) + mm(blocks_halo_ref[1, here, :], halo)
        resid_ref[here, :] = (part_ref[here, :] - outer).astype(BF)
    for i in range(0, own, step):
        here = slice(i, i + step)
        value = iterate_ref[here, :] + mm(inverse_ref[here, :own], resid_ref[...])
        state_ref[here, :] = value
        if split:
            keep_split(*split, here, value)
    if split:
        rest[0][...] = mm(select_ref[...], split[0][...]) + mm(select_ref[...], split[1][...])


def last_update_body(count, state_ref, inverse_halo_ref, *rest):
    got, (round_ref,) = rest[:count], rest[count:]
    halo = join_halo(got)
    step = state_ref.shape[0] // 2
    for i in range(0, state_ref.shape[0], step):
        here = slice(i, i + step)
        round_ref[here, :] = (state_ref[here, :] + mm(inverse_halo_ref[here, :], halo)).astype(BF)


def turn_body(state_ref, order_ref, turned_ref):
    value = state_ref[...]
    high = value.astype(BF)
    low = (value - high.astype(F32)).astype(BF)
    columns = value.shape[1]
    both = mm(jnp.concatenate([high, low], axis=1).T, order_ref[...])
    turned_ref[...] = both[:columns] + both[columns:]


def wire_body(count, turned_ref, halo_table_ref, *rest):
    got, (wire_ref,) = rest[:count], rest[count:]
    wire_ref[...] = (turned_ref[...] + mm(join_halo(got).T, halo_table_ref[...])).astype(BF)


def one_hot(rows_of, shape):
    return (iota(shape, 0) == rows_of(iota((1, shape[1]), 1))).astype(F32).astype(BF)


def order_body(inverse_halo_ref, order_ref, halo_table_ref):
    own = order_ref.shape[0]
    tile = own // ZL
    order_ref[...] = one_hot(lambda k: lax.rem(k, ZL) * tile + lax.div(k, ZL), (own, own))
    halo_table_ref[...] = mm(inverse_halo_ref[...].T, order_ref[...]).astype(BF)


def tables_body(wide, narrow, cov_plane_ref, cov_vert_ref, plane_ref, spread_ref, vert_ref):
    plane = plane_ref.shape[0]
    tile = plane // wide
    turn = one_hot(lambda k: lax.rem(k, wide) * tile + lax.div(k, wide), (plane, plane))
    half = mm(cov_plane_ref[...], turn).astype(BF)
    plane_ref[...] = mm(half.T, turn).astype(BF).T
    share = LANES // ZL
    depth = narrow * ZL
    width = narrow * LANES

    def source(k):
        e, n, l = lax.div(k, depth), lax.rem(lax.div(k, ZL), narrow), lax.rem(k, ZL)
        return n * LANES + e * ZL + l

    spread = one_hot(source, (width, width))
    spread_ref[...] = spread
    turned = cov_vert_ref[...].astype(F32).T
    zero = jnp.zeros_like(turned)
    blocks = jnp.concatenate(
        [jnp.concatenate([turned if i == e else zero for i in range(share)], axis=1) for e in range(share)],
        axis=0,
    ).astype(BF)
    vert_ref[...] = mm_t(blocks, spread).astype(BF)


def mix_body(wide, narrow, group, in_ref, plane_ref, spread_ref, vert_ref, state_ref, inverse_halo_ref, *rest):
    got, (out_ref, adjoint_hbm, cells_ref, flat_ref, wire_ref, round_ref, sem) = rest[:-7], rest[-7:]
    last_update_body(len(got), state_ref, inverse_halo_ref, *got, round_ref)
    keep = pltpu.make_async_copy(round_ref, adjoint_hbm, sem)
    keep.start()
    own = in_ref.shape[1]
    tile = own // ZL
    share = LANES // ZL
    depth = narrow * ZL
    block = wide * group
    for g in range(tile // share):
        lanes = slice(g * LANES, (g + 1) * LANES)
        joined = jnp.concatenate([in_ref[n * block:(n + 1) * block, lanes] for n in range(narrow)], axis=1)
        spread = mm(joined, spread_ref[...])
        for e in range(share):
            cells_ref[g * share + e, :block, :] = spread[:, e * depth:(e + 1) * depth]
    for r in range(group):
        for c in range(tile):
            flat_ref[c * wide:(c + 1) * wide, r * depth:(r + 1) * depth] = cells_ref[
                c, pl.ds(r, wide, stride=group), :
            ].astype(BF)
    planar = mm(plane_ref[...], flat_ref[...]).astype(BF)
    for g in range(tile // share):
        stacked = jnp.concatenate(
            [
                jnp.concatenate(
                    [
                        planar[c * wide:(c + 1) * wide, r * depth:(r + 1) * depth]
                        for c in range(g * share, (g + 1) * share)
                    ],
                    axis=1,
                )
                for r in range(group)
            ],
            axis=0,
        )
        mixed = mm(stacked, vert_ref[...])
        for r in range(group):
            for n in range(narrow):
                wire_ref[g, pl.ds(n * block + r, wide, stride=group), :] = mixed[
                    r * wide:(r + 1) * wide, n * LANES:(n + 1) * LANES
                ]
        out_ref[:, g * LANES:(g + 1) * LANES] = wire_ref[g, :narrow * block, :].astype(BF)
    keep.wait()


def unwire_body(in_ref, order_ref, out_hbm, out_ref, sems):
    step = out_ref.shape[0] // 3
    turned = in_ref[...].T
    copies = []
    for n, i in enumerate(range(0, out_ref.shape[0], step)):
        here = pl.ds(i, step)
        out_ref[here, :] = mm(order_ref[here, :], turned).astype(BF)
        copy = pltpu.make_async_copy(out_ref.at[here], out_hbm.at[here], sems.at[n])
        copy.start()
        copies.append(copy)
    for copy in copies:
        copy.wait()


def column_tables(inverse_halo, cov_plane, cov_vert):
    own, halo = inverse_halo.shape
    wide, narrow = lax.axis_size("wide"), lax.axis_size("narrow")
    width = narrow * LANES
    plane = cov_plane.shape[0]
    shape = jax.ShapeDtypeStruct
    order = call(order_body, [shape((own, own), BF), shape((halo, own), BF)], [inverse_halo])
    rest = call(
        functools.partial(tables_body, wide, narrow),
        [shape((plane, plane), BF), shape((width, width), BF), shape((width, width), BF)],
        [cov_plane, cov_vert],
    )
    return [tuple(order), tuple(rest)]


def smooth_by_columns(state, inverse_halo, got, tables):
    wide, narrow = lax.axis_size("wide"), lax.axis_size("narrow")
    own, columns = state.shape
    devices = wide * narrow
    group = columns // devices
    depth = narrow * ZL
    tile = own // ZL
    shape = jax.ShapeDtypeStruct
    (order, halo_table), (plane_mix, spread, vert_mix) = tables
    (turned,) = call(turn_body, [shape((columns, own), F32)], [state, order])
    (wire,) = call(functools.partial(wire_body, len(got)), [shape((columns, own), BF)], [turned, halo_table, *got])
    there = lax.all_to_all(
        wire.reshape(devices, group, own), ("narrow", "wide"), split_axis=0, concat_axis=0, tiled=True
    )
    mixed, adjoint = call(
        functools.partial(mix_body, wide, narrow, group),
        [shape((columns, own), BF), shape((own, columns), BF)],
        [there.reshape(columns, own), plane_mix, spread, vert_mix, state, inverse_halo, *got],
        [
            pltpu.VMEM((tile, wide * group + group, depth), F32),
            pltpu.VMEM((plane_mix.shape[0], group * depth), BF),
            pltpu.VMEM((own // LANES, columns + group, LANES), F32),
            pltpu.VMEM((own, columns), BF),
            pltpu.SemaphoreType.DMA,
        ],
        out_specs=[VM, ANY],
    )
    back = lax.all_to_all(
        mixed.reshape(devices, group, own), ("narrow", "wide"), split_axis=0, concat_axis=0, tiled=True
    )
    (smoothed,) = call(
        unwire_body,
        [shape((own, columns), BF)],
        [back.reshape(columns, own), order],
        [pltpu.VMEM((own, columns), BF), pltpu.SemaphoreType.DMA((3,))],
        out_specs=[ANY],
    )
    return adjoint, smoothed


def smooth_by_layers(adjoint, cov_plane, cov_vert):
    own, columns = adjoint.shape
    layered = adjoint.reshape(ZL, own // ZL, -1)
    planar = jnp.einsum(
        "pq,lqr->lpr",
        cov_plane,
        lax.all_to_all(layered, "wide", split_axis=0, concat_axis=1, tiled=True),
        preferred_element_type=F32,
    ).astype(BF)
    restored = lax.all_to_all(planar, "wide", split_axis=1, concat_axis=0, tiled=True)
    slab_weights = lax.dynamic_slice_in_dim(cov_vert, lax.axis_index("narrow") * ZL, ZL, 0)
    summed = jnp.dot(
        slab_weights,
        lax.all_gather(restored.reshape(ZL, -1), "narrow", axis=0, tiled=True),
        preferred_element_type=F32,
    )
    return summed.astype(BF).reshape(own, -1)


def shards(adjoint_rhs, inverse_rows, blocks, block_cols, send_rows, cov_plane, cov_vert):
    rhs = adjoint_rhs[0, 0]
    inverse = inverse_rows[0, 0]
    block_values = blocks[0, 0]
    cols = block_cols[0, 0]
    send_index = send_rows[0, 0]
    own, columns = rhs.shape
    width = send_index.shape[1]
    halo = 4 * width
    wide, narrow = lax.axis_size("wide"), lax.axis_size("narrow")
    group = columns // (wide * narrow)
    by_columns = columns % (wide * narrow) == 0 and group % 8 == 0 and narrow * ZL == LANES and wide % 16 == 0
    found = matchings()
    count = len(found)
    sent = count * width
    shape = jax.ShapeDtypeStruct
    notes = [shape((width, columns), BF)] * count
    full = shape((own, columns), F32)
    base_shape = shape((sent, columns), F32)
    cell_space = pltpu.VMEM((own, columns), BF)
    (select,) = call(
        functools.partial(select_body, found, own),
        [shape((sent, own), BF)],
        [send_index],
        flops=SELECT_FLOPS,
    )
    messages = call(pick_body, notes, [select, rhs], flops=PICK_FLOPS)
    got = swap(messages, found)
    inverse_halo, blocks_halo, inverse_sent, blocks_sent, state, base = call(
        functools.partial(setup_body, found, width),
        [
            shape((own, halo), BF),
            shape((2, own, halo), BF),
            shape((sent, halo), BF),
            shape((2 * sent, halo), BF),
            full,
            base_shape,
        ],
        [cols, inverse, block_values, rhs, select],
        [cell_space, cell_space],
        limit=12,
    )
    tables = column_tables(inverse_halo, cov_plane, cov_vert) if by_columns else []
    for sweep in range(SWEEPS - 1):
        messages = call(
            functools.partial(sent_update_body, count), notes, [base, inverse_sent, *got], limit=4
        )
        arrived, got = got, swap(messages, found)
        iterate, part, base = call(
            functools.partial(update_body, count),
            [full, full, base_shape],
            [cols, state, inverse_halo, block_values, rhs, select, *arrived],
            [pltpu.VMEM((own + halo, columns), BF), cell_space, cell_space],
        )
        turn = 1 if sweep == 1 and count == 3 else 0
        arrived = got[count - turn:] + got[:count - turn]
        messages = call(
            functools.partial(sent_residual_body, count, turn),
            notes,
            [base, blocks_sent, *arrived],
            limit=4,
        )
        got = swap(messages, found)
        if sweep < len(tables):
            tables[sweep], part = lax.optimization_barrier((tables[sweep], part))
        more = sweep < SWEEPS - 2
        state, *bases = call(
            functools.partial(residual_body, count, turn),
            [full] + [base_shape] * more,
            [part, blocks_halo, iterate, inverse, select, *arrived],
            [cell_space] * (1 + 2 * more),
        )
        base = bases[0] if more else None
    if by_columns:
        adjoint, smoothed = smooth_by_columns(state, inverse_halo, got, tables)
    else:
        cells = shape((own, columns), BF)
        (adjoint,) = call(functools.partial(last_update_body, count), [cells], [state, inverse_halo, *got])
        smoothed = smooth_by_layers(adjoint, cov_plane, cov_vert)
    return (adjoint[None, None], smoothed[None, None])


def solution(mesh):
    in_specs = (
        P("wide", "narrow", None, None),
        P("wide", "narrow", None, None),
        P("wide", "narrow", None, None, None, None),
        P("wide", "narrow", None, None),
        P("wide", "narrow", None, None),
        P(),
        P(),
    )
    out_specs = (P("wide", "narrow", None, None), P("wide", "narrow", None, None))
    return jax.shard_map(shards, mesh=mesh, in_specs=in_specs, out_specs=out_specs, check_vma=False)
```

```python
import functools

import jax
import jax.numpy as jnp
from jax import lax
from jax.experimental import pallas as pl
from jax.experimental.pallas import tpu as pltpu
from jax.sharding import PartitionSpec as P

ZL = 64
SWEEPS = 4
LANES = 128
SELECT_FLOPS = 6 * 10 ** 8
PICK_FLOPS = 2 * 10 ** 9
BF = jnp.bfloat16
F32 = jnp.float32
VM = pl.BlockSpec(memory_space=pltpu.VMEM)
ANY = pl.BlockSpec(memory_space=pl.ANY)


def wide_slot(w, n, parity):
    return (w & 1) ^ parity ^ 1


def narrow_slot(w, n, parity):
    return 2 + ((n & 1) ^ parity ^ 1)


def mixed_slot(w, n, kind):
    turn = (w ^ (w >> 1) ^ kind) & 1
    return (1 - turn) * wide_slot(w, n, 1) + turn * narrow_slot(w, n, 0)


def has_partner(w, n, slot, wide, narrow):
    inside = [w > 0, w + 1 < wide, n > 0, n + 1 < narrow]
    return sum((slot == k) * inside[k] for k in range(4))


def matchings():
    wide, narrow = lax.axis_size("wide"), lax.axis_size("narrow")
    if narrow == 2 and wide % 4 == 0:
        rules = [(mixed_slot, 0), (mixed_slot, 1), (wide_slot, 0)]
    else:
        rules = [(wide_slot, 1)] * (wide > 2) + [(narrow_slot, 1)] * (narrow > 2)
        rules += [(narrow_slot, 0)] * (narrow > 1) + [(wide_slot, 0)] * (wide > 1)
    found = []
    for rule, kind in rules:
        pairs = []
        for w in range(wide):
            for n in range(narrow):
                slot = rule(w, n, kind)
                if has_partner(w, n, slot, wide, narrow):
                    step = ((-1, 0), (1, 0), (0, -1), (0, 1))[slot]
                    target = (w + step[0], n + step[1])
                elif slot < 2:
                    target = (w, n ^ 1 if n ^ 1 < narrow else n)
                else:
                    target = (w ^ 1 if w ^ 1 < wide else w, n)
                pairs.append((w * narrow + n, target[0] * narrow + target[1]))
        found.append((rule, kind, tuple(pairs)))
    return found


def own_slots(found):
    w, n = lax.axis_index("wide"), lax.axis_index("narrow")
    wide, narrow = lax.axis_size("wide"), lax.axis_size("narrow")
    slots = [rule(w, n, kind) for rule, kind, _ in found]
    return [(slot, has_partner(w, n, slot, wide, narrow) == 1) for slot in slots]


def swap(messages, found):
    return [lax.ppermute(m, ("wide", "narrow"), list(f[-1])) for m, f in zip(messages, found)]


def mm(a, b):
    return jnp.dot(a, b, preferred_element_type=F32)


def mm_t(a, b):
    return lax.dot_general(a, b, (((1,), (1,)), ((), ())), preferred_element_type=F32)


def iota(shape, dim):
    return lax.broadcasted_iota(jnp.int32, shape, dim)


def call(body, outs, args, scratch=(), specs=None, flops=0, limit=8, out_specs=None):
    size = sum(a.size * a.dtype.itemsize for a in args)
    return pl.pallas_call(
        body,
        out_shape=outs,
        in_specs=specs or [VM] * len(args),
        out_specs=out_specs or [VM] * len(outs),
        scratch_shapes=list(scratch),
        compiler_params=pltpu.CompilerParams(vmem_limit_bytes=limit * 1024 * 1024),
        cost_estimate=pl.CostEstimate(flops=flops, bytes_accessed=size, transcendentals=0),
    )(*args)


def join_halo(got):
    pieces = [piece[...] for piece in got]
    return jnp.concatenate(pieces + [jnp.zeros_like(pieces[0])] * (4 - len(pieces)), axis=0)


def send(messages, values):
    width = messages[0].shape[0]
    for m, message in enumerate(messages):
        message[...] = values[m * width:(m + 1) * width, :].astype(BF)


def keep_split(high_ref, low_ref, rows, value):
    high = value.astype(BF)
    high_ref[rows] = high
    low_ref[rows] = (value - high.astype(F32)).astype(BF)


def select_body(found, own, send_ref, select_ref):
    width = send_ref.shape[1]
    diagonal = iota((width, width), 0) == iota((width, width), 1)
    pieces = []
    for slot, paired in own_slots(found):
        rows = jnp.where(paired, send_ref[pl.ds(slot, 1), :], -1).astype(F32)
        pieces.append(jnp.where(diagonal, rows, 0.0))
    column = jnp.sum(jnp.concatenate(pieces, axis=0), axis=1, keepdims=True).astype(jnp.int32)
    select_ref[...] = (iota((len(found) * width, own), 1) == column).astype(F32).astype(BF)


def pick_body(select_ref, rhs_ref, *messages):
    send(messages, mm(select_ref[...], rhs_ref[...]))


def setup_body(found, width, cols_ref, inverse_ref, blocks_ref, rhs_ref, select_ref, *rest):
    inverse_halo_ref, blocks_halo_ref, inverse_sent_ref, blocks_sent_ref, state_ref, base_ref = rest[:6]
    high_ref, low_ref = rest[6:]
    own = rhs_ref.shape[0]
    halo = 4 * width
    places = iota((1, halo), 1)
    starts = jnp.full((1, halo), -halo, jnp.int32)
    for m, (slot, _) in enumerate(own_slots(found)):
        here = lax.div(places, width) == m
        starts = jnp.where(here, slot * width + lax.rem(places, width), starts)
    arrange = (iota((halo, halo), 0) == starts).astype(F32).astype(BF)
    rows, links, size, _ = blocks_ref.shape
    for j in range(rows):
        here = slice(j * size, (j + 1) * size)
        columns = [cols_ref[j, k] for k in range(links)]
        for c in range(halo // size):
            total = None
            for k in range(links):
                part = jnp.where(columns[k] == own // size + c, blocks_ref[j, k].astype(F32), 0.0)
                total = part if total is None else total + part
            lanes = slice(c * size, (c + 1) * size)
            keep_split(high_ref, low_ref, (here, lanes), total)
    for part, half_ref in enumerate((high_ref, low_ref)):
        blocks_halo_ref[part] = mm(half_ref[...], arrange).astype(BF)
    step = own // 2
    for i in range(0, own, step):
        here = slice(i, i + step)
        inverse_halo_ref[here, :] = mm(inverse_ref[here, own:], arrange).astype(BF)
        value = mm(inverse_ref[here, :own], rhs_ref[...])
        state_ref[here, :] = value
        keep_split(high_ref, low_ref, here, value)
    inverse_sent_ref[...] = mm(select_ref[...], inverse_halo_ref[...]).astype(BF)
    sent = select_ref.shape[0]
    for part in range(2):
        here = slice(part * sent, (part + 1) * sent)
        blocks_sent_ref[here, :] = mm(select_ref[...], blocks_halo_ref[part]).astype(BF)
    base_ref[...] = mm(select_ref[...], high_ref[...]) + mm(select_ref[...], low_ref[...])


def sent_update_body(count, base_ref, sent_ref, *rest):
    got, messages = rest[:count], rest[count:]
    send(messages, base_ref[...] + mm(sent_ref[...], join_halo(got)))


def sent_residual_body(count, turn, base_ref, sent_ref, *rest):
    got, messages = rest[:count], rest[count:]
    halo = join_halo(got[turn:] + got[:turn])
    part = mm(sent_ref[...], halo)
    sent = base_ref.shape[0]
    send(messages, base_ref[...] - (part[:sent] + part[sent:]))


def update_body(count, cols_ref, state_ref, inverse_halo_ref, blocks_ref, rhs_ref, select_ref, *rest):
    got, (iterate_ref, part_ref, base_ref, sub_ref, high_ref, low_ref) = rest[:count], rest[count:]
    own = state_ref.shape[0]
    halo = join_halo(got)
    step = own // 2
    for i in range(0, own, step):
        here = slice(i, i + step)
        value = state_ref[here, :] + mm(inverse_halo_ref[here, :], halo)
        iterate_ref[here, :] = value
        sub_ref[here, :] = value.astype(BF)
    sub_ref[own:, :] = jnp.zeros((sub_ref.shape[0] - own, sub_ref.shape[1]), BF)
    rows, links, size, _ = blocks_ref.shape
    for j in range(rows):
        starts = [pl.multiple_of(cols_ref[j, k] * size, size) for k in range(links)]
        values = jnp.concatenate([blocks_ref[j, k] for k in range(links)], axis=1)
        coupled = jnp.concatenate([sub_ref[pl.ds(start, size), :] for start in starts], axis=0)
        total = mm(values, coupled)
        here = slice(j * size, (j + 1) * size)
        value = rhs_ref[here, :].astype(F32) - total
        part_ref[here, :] = value
        keep_split(high_ref, low_ref, here, value)
    base_ref[...] = mm(select_ref[...], high_ref[...]) + mm(select_ref[...], low_ref[...])


def residual_body(count, turn, part_ref, blocks_halo_ref, iterate_ref, inverse_ref, select_ref, *rest):
    got, rest = rest[:count], list(rest[count:])
    state_ref = rest.pop(0)
    resid_ref, *split = rest[-3:] if len(rest) == 4 else rest
    own = part_ref.shape[0]
    halo = join_halo(got[turn:] + got[:turn])
    step = own // 2
    for i in range(0, own, step):
        here = slice(i, i + step)
        outer = mm(blocks_halo_ref[0, here, :], halo) + mm(blocks_halo_ref[1, here, :], halo)
        resid_ref[here, :] = (part_ref[here, :] - outer).astype(BF)
    for i in range(0, own, step):
        here = slice(i, i + step)
        value = iterate_ref[here, :] + mm(inverse_ref[here, :own], resid_ref[...])
        state_ref[here, :] = value
        if split:
            keep_split(*split, here, value)
    if split:
        rest[0][...] = mm(select_ref[...], split[0][...]) + mm(select_ref[...], split[1][...])


def last_update_body(count, state_ref, inverse_halo_ref, *rest):
    got, (round_ref,) = rest[:count], rest[count:]
    halo = join_halo(got)
    step = state_ref.shape[0] // 2
    for i in range(0, state_ref.shape[0], step):
        here = slice(i, i + step)
        round_ref[here, :] = (state_ref[here, :] + mm(inverse_halo_ref[here, :], halo)).astype(BF)


def turn_body(state_ref, order_ref, turned_ref):
    value = state_ref[...]
    high = value.astype(BF)
    low = (value - high.astype(F32)).astype(BF)
    columns = value.shape[1]
    both = mm(jnp.concatenate([high, low], axis=1).T, order_ref[...])
    turned_ref[...] = both[:columns] + both[columns:]


def wire_body(count, turned_ref, halo_table_ref, *rest):
    got, (wire_ref,) = rest[:count], rest[count:]
    wire_ref[...] = (turned_ref[...] + mm(join_halo(got).T, halo_table_ref[...])).astype(BF)


def one_hot(rows_of, shape):
    return (iota(shape, 0) == rows_of(iota((1, shape[1]), 1))).astype(F32).astype(BF)


def order_body(inverse_halo_ref, order_ref, halo_table_ref):
    own = order_ref.shape[0]
    tile = own // ZL
    order_ref[...] = one_hot(lambda k: lax.rem(k, ZL) * tile + lax.div(k, ZL), (own, own))
    halo_table_ref[...] = mm(inverse_halo_ref[...].T, order_ref[...]).astype(BF)


def tables_body(wide, narrow, cov_plane_ref, cov_vert_ref, plane_ref, vert_ref):
    plane = plane_ref.shape[0]
    tile = plane // wide
    turn = one_hot(lambda k: lax.rem(k, wide) * tile + lax.div(k, wide), (plane, plane))
    half = mm(cov_plane_ref[...], turn).astype(BF)
    plane_ref[...] = mm(half.T, turn).astype(BF).T
    share = LANES // ZL
    depth = narrow * ZL
    width = narrow * LANES

    def source(k):
        e, n, l = lax.div(k, depth), lax.rem(lax.div(k, ZL), narrow), lax.rem(k, ZL)
        return n * LANES + e * ZL + l

    spread = one_hot(source, (width, width))
    turned = cov_vert_ref[...].astype(F32).T
    zero = jnp.zeros_like(turned)
    blocks = jnp.concatenate(
        [jnp.concatenate([turned if i == e else zero for i in range(share)], axis=1) for e in range(share)],
        axis=0,
    ).astype(BF)
    vert_ref[...] = mm_t(blocks, spread).astype(BF)


def mix_body(wide, narrow, group, in_ref, plane_ref, vert_ref, state_ref, inverse_halo_ref, *rest):
    got, (out_ref, adjoint_hbm, cells_ref, flat_ref, wire_ref, round_ref, sem) = rest[:-7], rest[-7:]
    last_update_body(len(got), state_ref, inverse_halo_ref, *got, round_ref)
    keep = pltpu.make_async_copy(round_ref, adjoint_hbm, sem)
    keep.start()
    own = in_ref.shape[1]
    tile = own // ZL
    share = LANES // ZL
    depth = narrow * ZL
    block = wide * group
    low = iota((block, LANES), 1) < ZL
    for g in range(tile // share):
        first, second = [
            in_ref[n * block:(n + 1) * block, g * LANES:(g + 1) * LANES].astype(F32) for n in range(narrow)
        ]
        cells_ref[g * share, :block, :] = jnp.where(low, first, pltpu.roll(second, ZL, 1))
        cells_ref[g * share + 1, :block, :] = jnp.where(low, pltpu.roll(first, ZL, 1), second)
    for r in range(group):
        for c in range(tile):
            flat_ref[c * wide:(c + 1) * wide, r * depth:(r + 1) * depth] = cells_ref[
                c, pl.ds(r, wide, stride=group), :
            ].astype(BF)
    planar = mm(plane_ref[...], flat_ref[...]).astype(BF)
    for g in range(tile // share):
        stacked = jnp.concatenate(
            [
                jnp.concatenate(
                    [
                        planar[c * wide:(c + 1) * wide, r * depth:(r + 1) * depth]
                        for c in range(g * share, (g + 1) * share)
                    ],
                    axis=1,
                )
                for r in range(group)
            ],
            axis=0,
        )
        mixed = mm(stacked, vert_ref[...])
        for r in range(group):
            for n in range(narrow):
                wire_ref[g, pl.ds(n * block + r, wide, stride=group), :] = mixed[
                    r * wide:(r + 1) * wide, n * LANES:(n + 1) * LANES
                ]
        out_ref[:, g * LANES:(g + 1) * LANES] = wire_ref[g, :narrow * block, :].astype(BF)
    keep.wait()


def unwire_body(in_ref, out_hbm, out_ref, sems):
    own = out_ref.shape[0]
    tile = own // ZL
    runs = sems.shape[0]
    run = ZL // runs
    step = run * tile
    small = one_hot(lambda k: lax.rem(k, run) * tile + lax.div(k, run), (step, step))
    turned = in_ref[...].T
    copies = []
    for b in range(runs):
        here = pl.ds(b * step, step)
        piece = jnp.concatenate([turned[c * ZL + b * run:c * ZL + (b + 1) * run] for c in range(tile)], axis=0)
        out_ref[here, :] = mm(small, piece).astype(BF)
        copy = pltpu.make_async_copy(out_ref.at[here], out_hbm.at[here], sems.at[b])
        copy.start()
        copies.append(copy)
    for copy in copies:
        copy.wait()


def column_tables(inverse_halo, cov_plane, cov_vert):
    own, halo = inverse_halo.shape
    wide, narrow = lax.axis_size("wide"), lax.axis_size("narrow")
    width = narrow * LANES
    plane = cov_plane.shape[0]
    shape = jax.ShapeDtypeStruct
    order = call(order_body, [shape((own, own), BF), shape((halo, own), BF)], [inverse_halo])
    rest = call(
        functools.partial(tables_body, wide, narrow),
        [shape((plane, plane), BF), shape((width, width), BF)],
        [cov_plane, cov_vert],
    )
    return [tuple(order), tuple(rest)]


def smooth_by_columns(state, inverse_halo, got, tables):
    wide, narrow = lax.axis_size("wide"), lax.axis_size("narrow")
    own, columns = state.shape
    devices = wide * narrow
    group = columns // devices
    depth = narrow * ZL
    tile = own // ZL
    shape = jax.ShapeDtypeStruct
    (order, halo_table), (plane_mix, vert_mix) = tables
    (turned,) = call(turn_body, [shape((columns, own), F32)], [state, order])
    (wire,) = call(functools.partial(wire_body, len(got)), [shape((columns, own), BF)], [turned, halo_table, *got])
    there = lax.all_to_all(
        wire.reshape(devices, group, own), ("narrow", "wide"), split_axis=0, concat_axis=0, tiled=True
    )
    mixed, adjoint = call(
        functools.partial(mix_body, wide, narrow, group),
        [shape((columns, own), BF), shape((own, columns), BF)],
        [there.reshape(columns, own), plane_mix, vert_mix, state, inverse_halo, *got],
        [
            pltpu.VMEM((tile, wide * group + group, depth), F32),
            pltpu.VMEM((plane_mix.shape[0], group * depth), BF),
            pltpu.VMEM((own // LANES, columns + group, LANES), F32),
            pltpu.VMEM((own, columns), BF),
            pltpu.SemaphoreType.DMA,
        ],
        out_specs=[VM, ANY],
    )
    back = lax.all_to_all(
        mixed.reshape(devices, group, own), ("narrow", "wide"), split_axis=0, concat_axis=0, tiled=True
    )
    (smoothed,) = call(
        unwire_body,
        [shape((own, columns), BF)],
        [back.reshape(columns, own)],
        [pltpu.VMEM((own, columns), BF), pltpu.SemaphoreType.DMA((4,))],
        out_specs=[ANY],
    )
    return adjoint, smoothed


def smooth_by_layers(adjoint, cov_plane, cov_vert):
    own, columns = adjoint.shape
    layered = adjoint.reshape(ZL, own // ZL, -1)
    planar = jnp.einsum(
        "pq,lqr->lpr",
        cov_plane,
        lax.all_to_all(layered, "wide", split_axis=0, concat_axis=1, tiled=True),
        preferred_element_type=F32,
    ).astype(BF)
    restored = lax.all_to_all(planar, "wide", split_axis=1, concat_axis=0, tiled=True)
    slab_weights = lax.dynamic_slice_in_dim(cov_vert, lax.axis_index("narrow") * ZL, ZL, 0)
    summed = jnp.dot(
        slab_weights,
        lax.all_gather(restored.reshape(ZL, -1), "narrow", axis=0, tiled=True),
        preferred_element_type=F32,
    )
    return summed.astype(BF).reshape(own, -1)


def shards(adjoint_rhs, inverse_rows, blocks, block_cols, send_rows, cov_plane, cov_vert):
    rhs = adjoint_rhs[0, 0]
    inverse = inverse_rows[0, 0]
    block_values = blocks[0, 0]
    cols = block_cols[0, 0]
    send_index = send_rows[0, 0]
    own, columns = rhs.shape
    width = send_index.shape[1]
    halo = 4 * width
    wide, narrow = lax.axis_size("wide"), lax.axis_size("narrow")
    group = columns // (wide * narrow)
    by_columns = columns % (wide * narrow) == 0 and group % 8 == 0 and narrow * ZL == LANES and wide % 16 == 0
    found = matchings()
    count = len(found)
    sent = count * width
    shape = jax.ShapeDtypeStruct
    notes = [shape((width, columns), BF)] * count
    full = shape((own, columns), F32)
    base_shape = shape((sent, columns), F32)
    cell_space = pltpu.VMEM((own, columns), BF)
    (select,) = call(
        functools.partial(select_body, found, own),
        [shape((sent, own), BF)],
        [send_index],
        flops=SELECT_FLOPS,
    )
    messages = call(pick_body, notes, [select, rhs], flops=PICK_FLOPS)
    got = swap(messages, found)
    inverse_halo, blocks_halo, inverse_sent, blocks_sent, state, base = call(
        functools.partial(setup_body, found, width),
        [
            shape((own, halo), BF),
            shape((2, own, halo), BF),
            shape((sent, halo), BF),
            shape((2 * sent, halo), BF),
            full,
            base_shape,
        ],
        [cols, inverse, block_values, rhs, select],
        [cell_space, cell_space],
        limit=12,
    )
    tables = column_tables(inverse_halo, cov_plane, cov_vert) if by_columns else []
    for sweep in range(SWEEPS - 1):
        messages = call(
            functools.partial(sent_update_body, count), notes, [base, inverse_sent, *got], limit=4
        )
        arrived, got = got, swap(messages, found)
        iterate, part, base = call(
            functools.partial(update_body, count),
            [full, full, base_shape],
            [cols, state, inverse_halo, block_values, rhs, select, *arrived],
            [pltpu.VMEM((own + halo, columns), BF), cell_space, cell_space],
        )
        turn = 1 if sweep == 1 and count == 3 else 0
        arrived = got[count - turn:] + got[:count - turn]
        messages = call(
            functools.partial(sent_residual_body, count, turn),
            notes,
            [base, blocks_sent, *arrived],
            limit=4,
        )
        got = swap(messages, found)
        if sweep < len(tables):
            tables[sweep], part = lax.optimization_barrier((tables[sweep], part))
        more = sweep < SWEEPS - 2
        state, *bases = call(
            functools.partial(residual_body, count, turn),
            [full] + [base_shape] * more,
            [part, blocks_halo, iterate, inverse, select, *arrived],
            [cell_space] * (1 + 2 * more),
        )
        base = bases[0] if more else None
    if by_columns:
        adjoint, smoothed = smooth_by_columns(state, inverse_halo, got, tables)
    else:
        cells = shape((own, columns), BF)
        (adjoint,) = call(functools.partial(last_update_body, count), [cells], [state, inverse_halo, *got])
        smoothed = smooth_by_layers(adjoint, cov_plane, cov_vert)
    return (adjoint[None, None], smoothed[None, None])


def solution(mesh):
    in_specs = (
        P("wide", "narrow", None, None),
        P("wide", "narrow", None, None),
        P("wide", "narrow", None, None, None, None),
        P("wide", "narrow", None, None),
        P("wide", "narrow", None, None),
        P(),
        P(),
    )
    out_specs = (P("wide", "narrow", None, None), P("wide", "narrow", None, None))
    return jax.shard_map(shards, mesh=mesh, in_specs=in_specs, out_specs=out_specs, check_vma=False)
```

```python
import functools

import jax
import jax.numpy as jnp
from jax import lax
from jax.experimental import pallas as pl
from jax.experimental.pallas import tpu as pltpu
from jax.sharding import PartitionSpec as P

ZL = 64
SWEEPS = 4
LANES = 128
SELECT_FLOPS = 6 * 10 ** 8
PICK_FLOPS = 2 * 10 ** 9
BF = jnp.bfloat16
F32 = jnp.float32
VM = pl.BlockSpec(memory_space=pltpu.VMEM)
ANY = pl.BlockSpec(memory_space=pl.ANY)


def wide_slot(w, n, parity):
    return (w & 1) ^ parity ^ 1


def narrow_slot(w, n, parity):
    return 2 + ((n & 1) ^ parity ^ 1)


def mixed_slot(w, n, kind):
    turn = (w ^ (w >> 1) ^ kind) & 1
    return (1 - turn) * wide_slot(w, n, 1) + turn * narrow_slot(w, n, 0)


def has_partner(w, n, slot, wide, narrow):
    inside = [w > 0, w + 1 < wide, n > 0, n + 1 < narrow]
    return sum((slot == k) * inside[k] for k in range(4))


def matchings():
    wide, narrow = lax.axis_size("wide"), lax.axis_size("narrow")
    if narrow == 2 and wide % 4 == 0:
        rules = [(mixed_slot, 0), (mixed_slot, 1), (wide_slot, 0)]
    else:
        rules = [(wide_slot, 1)] * (wide > 2) + [(narrow_slot, 1)] * (narrow > 2)
        rules += [(narrow_slot, 0)] * (narrow > 1) + [(wide_slot, 0)] * (wide > 1)
    found = []
    for rule, kind in rules:
        pairs = []
        for w in range(wide):
            for n in range(narrow):
                slot = rule(w, n, kind)
                if has_partner(w, n, slot, wide, narrow):
                    step = ((-1, 0), (1, 0), (0, -1), (0, 1))[slot]
                    target = (w + step[0], n + step[1])
                elif slot < 2:
                    target = (w, n ^ 1 if n ^ 1 < narrow else n)
                else:
                    target = (w ^ 1 if w ^ 1 < wide else w, n)
                pairs.append((w * narrow + n, target[0] * narrow + target[1]))
        found.append((rule, kind, tuple(pairs)))
    return found


def own_slots(found):
    w, n = lax.axis_index("wide"), lax.axis_index("narrow")
    wide, narrow = lax.axis_size("wide"), lax.axis_size("narrow")
    slots = [rule(w, n, kind) for rule, kind, _ in found]
    return [(slot, has_partner(w, n, slot, wide, narrow) == 1) for slot in slots]


def swap(messages, found):
    return [lax.ppermute(m, ("wide", "narrow"), list(f[-1])) for m, f in zip(messages, found)]


def mm(a, b):
    return jnp.dot(a, b, preferred_element_type=F32)


def mm_t(a, b):
    return lax.dot_general(a, b, (((1,), (1,)), ((), ())), preferred_element_type=F32)


def iota(shape, dim):
    return lax.broadcasted_iota(jnp.int32, shape, dim)


def call(body, outs, args, scratch=(), specs=None, flops=0, limit=8, out_specs=None):
    size = sum(a.size * a.dtype.itemsize for a in args)
    return pl.pallas_call(
        body,
        out_shape=outs,
        in_specs=specs or [VM] * len(args),
        out_specs=out_specs or [VM] * len(outs),
        scratch_shapes=list(scratch),
        compiler_params=pltpu.CompilerParams(vmem_limit_bytes=limit * 1024 * 1024),
        cost_estimate=pl.CostEstimate(flops=flops, bytes_accessed=size, transcendentals=0),
    )(*args)


def join_halo(got):
    pieces = [piece[...] for piece in got]
    return jnp.concatenate(pieces + [jnp.zeros_like(pieces[0])] * (4 - len(pieces)), axis=0)


def send(messages, values):
    width = messages[0].shape[0]
    for m, message in enumerate(messages):
        message[...] = values[m * width:(m + 1) * width, :].astype(BF)


def keep_split(high_ref, low_ref, rows, value):
    high = value.astype(BF)
    high_ref[rows] = high
    low_ref[rows] = (value - high.astype(F32)).astype(BF)


def select_body(found, own, send_ref, select_ref):
    width = send_ref.shape[1]
    diagonal = iota((width, width), 0) == iota((width, width), 1)
    pieces = []
    for slot, paired in own_slots(found):
        rows = jnp.where(paired, send_ref[pl.ds(slot, 1), :], -1).astype(F32)
        pieces.append(jnp.where(diagonal, rows, 0.0))
    column = jnp.sum(jnp.concatenate(pieces, axis=0), axis=1, keepdims=True).astype(jnp.int32)
    select_ref[...] = (iota((len(found) * width, own), 1) == column).astype(F32).astype(BF)


def pick_body(select_ref, rhs_ref, *messages):
    send(messages, mm(select_ref[...], rhs_ref[...]))


def setup_body(found, width, cols_ref, inverse_ref, blocks_ref, rhs_ref, select_ref, *rest):
    inverse_halo_ref, blocks_halo_ref, inverse_sent_ref, blocks_sent_ref, state_ref, base_ref = rest[:6]
    high_ref, low_ref = rest[6:]
    own = rhs_ref.shape[0]
    halo = 4 * width
    places = iota((1, halo), 1)
    starts = jnp.full((1, halo), -halo, jnp.int32)
    for m, (slot, _) in enumerate(own_slots(found)):
        here = lax.div(places, width) == m
        starts = jnp.where(here, slot * width + lax.rem(places, width), starts)
    arrange = (iota((halo, halo), 0) == starts).astype(F32).astype(BF)
    rows, links, size, _ = blocks_ref.shape
    for j in range(rows):
        here = slice(j * size, (j + 1) * size)
        columns = [cols_ref[j, k] for k in range(links)]
        for c in range(halo // size):
            total = None
            for k in range(links):
                part = jnp.where(columns[k] == own // size + c, blocks_ref[j, k].astype(F32), 0.0)
                total = part if total is None else total + part
            lanes = slice(c * size, (c + 1) * size)
            keep_split(high_ref, low_ref, (here, lanes), total)
    for part, half_ref in enumerate((high_ref, low_ref)):
        blocks_halo_ref[part] = mm(half_ref[...], arrange).astype(BF)
    step = own // 2
    for i in range(0, own, step):
        here = slice(i, i + step)
        inverse_halo_ref[here, :] = mm(inverse_ref[here, own:], arrange).astype(BF)
        value = mm(inverse_ref[here, :own], rhs_ref[...])
        state_ref[here, :] = value
        keep_split(high_ref, low_ref, here, value)
    inverse_sent_ref[...] = mm(select_ref[...], inverse_halo_ref[...]).astype(BF)
    sent = select_ref.shape[0]
    for part in range(2):
        here = slice(part * sent, (part + 1) * sent)
        blocks_sent_ref[here, :] = mm(select_ref[...], blocks_halo_ref[part]).astype(BF)
    base_ref[...] = mm(select_ref[...], high_ref[...]) + mm(select_ref[...], low_ref[...])


def sent_update_body(count, base_ref, sent_ref, *rest):
    got, messages = rest[:count], rest[count:]
    send(messages, base_ref[...] + mm(sent_ref[...], join_halo(got)))


def sent_residual_body(count, turn, base_ref, sent_ref, *rest):
    got, messages = rest[:count], rest[count:]
    halo = join_halo(got[turn:] + got[:turn])
    part = mm(sent_ref[...], halo)
    sent = base_ref.shape[0]
    send(messages, base_ref[...] - (part[:sent] + part[sent:]))


def update_body(count, cols_ref, state_ref, inverse_halo_ref, blocks_ref, rhs_ref, select_ref, *rest):
    got, (iterate_ref, part_ref, base_ref, sub_ref, high_ref, low_ref) = rest[:count], rest[count:]
    own = state_ref.shape[0]
    halo = join_halo(got)
    step = own // 2
    for i in range(0, own, step):
        here = slice(i, i + step)
        value = state_ref[here, :] + mm(inverse_halo_ref[here, :], halo)
        iterate_ref[here, :] = value
        sub_ref[here, :] = value.astype(BF)
    sub_ref[own:, :] = jnp.zeros((sub_ref.shape[0] - own, sub_ref.shape[1]), BF)
    rows, links, size, _ = blocks_ref.shape
    for j in range(rows):
        starts = [pl.multiple_of(cols_ref[j, k] * size, size) for k in range(links)]
        values = jnp.concatenate([blocks_ref[j, k] for k in range(links)], axis=1)
        coupled = jnp.concatenate([sub_ref[pl.ds(start, size), :] for start in starts], axis=0)
        total = mm(values, coupled)
        here = slice(j * size, (j + 1) * size)
        value = rhs_ref[here, :].astype(F32) - total
        part_ref[here, :] = value
        keep_split(high_ref, low_ref, here, value)
    base_ref[...] = mm(select_ref[...], high_ref[...]) + mm(select_ref[...], low_ref[...])


def residual_body(count, turn, part_ref, blocks_halo_ref, iterate_ref, inverse_ref, select_ref, *rest):
    got, rest = rest[:count], list(rest[count:])
    state_ref = rest.pop(0)
    resid_ref, *split = rest[-3:] if len(rest) == 4 else rest
    own = part_ref.shape[0]
    halo = join_halo(got[turn:] + got[:turn])
    step = own // 2
    for i in range(0, own, step):
        here = slice(i, i + step)
        outer = mm(blocks_halo_ref[0, here, :], halo) + mm(blocks_halo_ref[1, here, :], halo)
        resid_ref[here, :] = (part_ref[here, :] - outer).astype(BF)
    for i in range(0, own, step):
        here = slice(i, i + step)
        value = iterate_ref[here, :] + mm(inverse_ref[here, :own], resid_ref[...])
        state_ref[here, :] = value
        if split:
            keep_split(*split, here, value)
    if split:
        rest[0][...] = mm(select_ref[...], split[0][...]) + mm(select_ref[...], split[1][...])


def last_update_body(count, state_ref, inverse_halo_ref, *rest):
    got, (round_ref,) = rest[:count], rest[count:]
    halo = join_halo(got)
    step = state_ref.shape[0] // 2
    for i in range(0, state_ref.shape[0], step):
        here = slice(i, i + step)
        round_ref[here, :] = (state_ref[here, :] + mm(inverse_halo_ref[here, :], halo)).astype(BF)


def turn_body(state_ref, order_ref, turned_ref):
    value = state_ref[...]
    high = value.astype(BF)
    low = (value - high.astype(F32)).astype(BF)
    columns = value.shape[1]
    both = mm(jnp.concatenate([high, low], axis=1).T, order_ref[...])
    turned_ref[...] = both[:columns] + both[columns:]


def wire_body(count, turned_ref, halo_table_ref, *rest):
    got, (wire_ref,) = rest[:count], rest[count:]
    wire_ref[...] = (turned_ref[...] + mm(join_halo(got).T, halo_table_ref[...])).astype(BF)


def one_hot(rows_of, shape):
    return (iota(shape, 0) == rows_of(iota((1, shape[1]), 1))).astype(F32).astype(BF)


def order_body(inverse_halo_ref, order_ref, halo_table_ref):
    own = order_ref.shape[0]
    tile = own // ZL
    order_ref[...] = one_hot(lambda k: lax.rem(k, ZL) * tile + lax.div(k, ZL), (own, own))
    halo_table_ref[...] = mm(inverse_halo_ref[...].T, order_ref[...]).astype(BF)


def tables_body(wide, narrow, cov_plane_ref, cov_vert_ref, plane_ref, spread_ref, vert_ref):
    plane = plane_ref.shape[0]
    tile = plane // wide
    turn = one_hot(lambda k: lax.rem(k, wide) * tile + lax.div(k, wide), (plane, plane))
    half = mm(cov_plane_ref[...], turn).astype(BF)
    plane_ref[...] = mm(half.T, turn).astype(BF).T
    share = LANES // ZL
    depth = narrow * ZL
    width = narrow * LANES

    def source(k):
        e, n, l = lax.div(k, depth), lax.rem(lax.div(k, ZL), narrow), lax.rem(k, ZL)
        return n * LANES + e * ZL + l

    spread = one_hot(source, (width, width))
    spread_ref[...] = spread
    turned = cov_vert_ref[...].astype(F32).T
    zero = jnp.zeros_like(turned)
    blocks = jnp.concatenate(
        [jnp.concatenate([turned if i == e else zero for i in range(share)], axis=1) for e in range(share)],
        axis=0,
    ).astype(BF)
    vert_ref[...] = mm_t(blocks, spread).astype(BF)


def mix_body(wide, narrow, group, in_ref, plane_ref, spread_ref, vert_ref, state_ref, inverse_halo_ref, *rest):
    got, (out_ref, adjoint_hbm, cells_ref, flat_ref, wire_ref, round_ref, sem) = rest[:-7], rest[-7:]
    last_update_body(len(got), state_ref, inverse_halo_ref, *got, round_ref)
    keep = pltpu.make_async_copy(round_ref, adjoint_hbm, sem)
    keep.start()
    own = in_ref.shape[1]
    tile = own // ZL
    share = LANES // ZL
    depth = narrow * ZL
    block = wide * group
    pairs = tile // share
    halves = [range(0, pairs // 2), range(pairs // 2, pairs)]
    for half in halves:
        joined = jnp.concatenate(
            [
                jnp.concatenate(
                    [in_ref[n * block:(n + 1) * block, g * LANES:(g + 1) * LANES] for n in range(narrow)], axis=1
                )
                for g in half
            ],
            axis=0,
        )
        spread = mm(joined, spread_ref[...])
        for i, g in enumerate(half):
            for e in range(share):
                cells_ref[g * share + e, :block, :] = spread[i * block:(i + 1) * block, e * depth:(e + 1) * depth]
    for r in range(group):
        for c in range(tile):
            flat_ref[c * wide:(c + 1) * wide, r * depth:(r + 1) * depth] = cells_ref[
                c, pl.ds(r, wide, stride=group), :
            ].astype(BF)
    planar = mm(plane_ref[...], flat_ref[...]).astype(BF)
    for half in halves:
        stacked = jnp.concatenate(
            [
                jnp.concatenate(
                    [
                        planar[c * wide:(c + 1) * wide, r * depth:(r + 1) * depth]
                        for c in range(g * share, (g + 1) * share)
                    ],
                    axis=1,
                )
                for g in half
                for r in range(group)
            ],
            axis=0,
        )
        mixed = mm(stacked, vert_ref[...])
        for i, g in enumerate(half):
            for r in range(group):
                rows = slice(i * block + r * wide, i * block + (r + 1) * wide)
                for n in range(narrow):
                    wire_ref[g, pl.ds(n * block + r, wide, stride=group), :] = mixed[
                        rows, n * LANES:(n + 1) * LANES
                    ]
            out_ref[:, g * LANES:(g + 1) * LANES] = wire_ref[g, :narrow * block, :].astype(BF)
    keep.wait()


def unwire_body(in_ref, out_hbm, out_ref, sems):
    own = out_ref.shape[0]
    tile = own // ZL
    runs = sems.shape[0]
    run = ZL // runs
    step = run * tile
    small = one_hot(lambda k: lax.rem(k, run) * tile + lax.div(k, run), (step, step))
    turned = in_ref[...].T
    copies = []
    for b in range(runs):
        here = pl.ds(b * step, step)
        piece = jnp.concatenate([turned[c * ZL + b * run:c * ZL + (b + 1) * run] for c in range(tile)], axis=0)
        out_ref[here, :] = mm(small, piece).astype(BF)
        copy = pltpu.make_async_copy(out_ref.at[here], out_hbm.at[here], sems.at[b])
        copy.start()
        copies.append(copy)
    for copy in copies:
        copy.wait()


def column_tables(inverse_halo, cov_plane, cov_vert):
    own, halo = inverse_halo.shape
    wide, narrow = lax.axis_size("wide"), lax.axis_size("narrow")
    width = narrow * LANES
    plane = cov_plane.shape[0]
    shape = jax.ShapeDtypeStruct
    order = call(order_body, [shape((own, own), BF), shape((halo, own), BF)], [inverse_halo])
    rest = call(
        functools.partial(tables_body, wide, narrow),
        [shape((plane, plane), BF), shape((width, width), BF), shape((width, width), BF)],
        [cov_plane, cov_vert],
    )
    return [tuple(order), tuple(rest)]


def smooth_by_columns(state, inverse_halo, got, tables):
    wide, narrow = lax.axis_size("wide"), lax.axis_size("narrow")
    own, columns = state.shape
    devices = wide * narrow
    group = columns // devices
    depth = narrow * ZL
    tile = own // ZL
    shape = jax.ShapeDtypeStruct
    (order, halo_table), (plane_mix, spread, vert_mix) = tables
    (turned,) = call(turn_body, [shape((columns, own), F32)], [state, order])
    (wire,) = call(functools.partial(wire_body, len(got)), [shape((columns, own), BF)], [turned, halo_table, *got])
    there = lax.all_to_all(
        wire.reshape(devices, group, own), ("narrow", "wide"), split_axis=0, concat_axis=0, tiled=True
    )
    mixed, adjoint = call(
        functools.partial(mix_body, wide, narrow, group),
        [shape((columns, own), BF), shape((own, columns), BF)],
        [there.reshape(columns, own), plane_mix, spread, vert_mix, state, inverse_halo, *got],
        [
            pltpu.VMEM((tile, wide * group + group, depth), F32),
            pltpu.VMEM((plane_mix.shape[0], group * depth), BF),
            pltpu.VMEM((own // LANES, columns + group, LANES), F32),
            pltpu.VMEM((own, columns), BF),
            pltpu.SemaphoreType.DMA,
        ],
        out_specs=[VM, ANY],
    )
    back = lax.all_to_all(
        mixed.reshape(devices, group, own), ("narrow", "wide"), split_axis=0, concat_axis=0, tiled=True
    )
    (smoothed,) = call(
        unwire_body,
        [shape((own, columns), BF)],
        [back.reshape(columns, own)],
        [pltpu.VMEM((own, columns), BF), pltpu.SemaphoreType.DMA((4,))],
        out_specs=[ANY],
    )
    return adjoint, smoothed


def smooth_by_layers(adjoint, cov_plane, cov_vert):
    own, columns = adjoint.shape
    layered = adjoint.reshape(ZL, own // ZL, -1)
    planar = jnp.einsum(
        "pq,lqr->lpr",
        cov_plane,
        lax.all_to_all(layered, "wide", split_axis=0, concat_axis=1, tiled=True),
        preferred_element_type=F32,
    ).astype(BF)
    restored = lax.all_to_all(planar, "wide", split_axis=1, concat_axis=0, tiled=True)
    slab_weights = lax.dynamic_slice_in_dim(cov_vert, lax.axis_index("narrow") * ZL, ZL, 0)
    summed = jnp.dot(
        slab_weights,
        lax.all_gather(restored.reshape(ZL, -1), "narrow", axis=0, tiled=True),
        preferred_element_type=F32,
    )
    return summed.astype(BF).reshape(own, -1)


def shards(adjoint_rhs, inverse_rows, blocks, block_cols, send_rows, cov_plane, cov_vert):
    rhs = adjoint_rhs[0, 0]
    inverse = inverse_rows[0, 0]
    block_values = blocks[0, 0]
    cols = block_cols[0, 0]
    send_index = send_rows[0, 0]
    own, columns = rhs.shape
    width = send_index.shape[1]
    halo = 4 * width
    wide, narrow = lax.axis_size("wide"), lax.axis_size("narrow")
    group = columns // (wide * narrow)
    by_columns = columns % (wide * narrow) == 0 and group % 8 == 0 and narrow * ZL == LANES and wide % 16 == 0
    found = matchings()
    count = len(found)
    sent = count * width
    shape = jax.ShapeDtypeStruct
    notes = [shape((width, columns), BF)] * count
    full = shape((own, columns), F32)
    base_shape = shape((sent, columns), F32)
    cell_space = pltpu.VMEM((own, columns), BF)
    (select,) = call(
        functools.partial(select_body, found, own),
        [shape((sent, own), BF)],
        [send_index],
        flops=SELECT_FLOPS,
    )
    messages = call(pick_body, notes, [select, rhs], flops=PICK_FLOPS)
    got = swap(messages, found)
    inverse_halo, blocks_halo, inverse_sent, blocks_sent, state, base = call(
        functools.partial(setup_body, found, width),
        [
            shape((own, halo), BF),
            shape((2, own, halo), BF),
            shape((sent, halo), BF),
            shape((2 * sent, halo), BF),
            full,
            base_shape,
        ],
        [cols, inverse, block_values, rhs, select],
        [cell_space, cell_space],
        limit=12,
    )
    tables = column_tables(inverse_halo, cov_plane, cov_vert) if by_columns else []
    for sweep in range(SWEEPS - 1):
        messages = call(
            functools.partial(sent_update_body, count), notes, [base, inverse_sent, *got], limit=4
        )
        arrived, got = got, swap(messages, found)
        iterate, part, base = call(
            functools.partial(update_body, count),
            [full, full, base_shape],
            [cols, state, inverse_halo, block_values, rhs, select, *arrived],
            [pltpu.VMEM((own + halo, columns), BF), cell_space, cell_space],
        )
        turn = 1 if sweep == 1 and count == 3 else 0
        arrived = got[count - turn:] + got[:count - turn]
        messages = call(
            functools.partial(sent_residual_body, count, turn),
            notes,
            [base, blocks_sent, *arrived],
            limit=4,
        )
        got = swap(messages, found)
        if sweep < len(tables):
            tables[sweep], part = lax.optimization_barrier((tables[sweep], part))
        more = sweep < SWEEPS - 2
        state, *bases = call(
            functools.partial(residual_body, count, turn),
            [full] + [base_shape] * more,
            [part, blocks_halo, iterate, inverse, select, *arrived],
            [cell_space] * (1 + 2 * more),
        )
        base = bases[0] if more else None
    if by_columns:
        adjoint, smoothed = smooth_by_columns(state, inverse_halo, got, tables)
    else:
        cells = shape((own, columns), BF)
        (adjoint,) = call(functools.partial(last_update_body, count), [cells], [state, inverse_halo, *got])
        smoothed = smooth_by_layers(adjoint, cov_plane, cov_vert)
    return (adjoint[None, None], smoothed[None, None])


def solution(mesh):
    in_specs = (
        P("wide", "narrow", None, None),
        P("wide", "narrow", None, None),
        P("wide", "narrow", None, None, None, None),
        P("wide", "narrow", None, None),
        P("wide", "narrow", None, None),
        P(),
        P(),
    )
    out_specs = (P("wide", "narrow", None, None), P("wide", "narrow", None, None))
    return jax.shard_map(shards, mesh=mesh, in_specs=in_specs, out_specs=out_specs, check_vma=False)
```

```python
import functools

import jax
import jax.numpy as jnp
from jax import lax
from jax.experimental import pallas as pl
from jax.experimental.pallas import tpu as pltpu
from jax.sharding import PartitionSpec as P

ZL = 64
SWEEPS = 4
LANES = 128
SELECT_FLOPS = 6 * 10 ** 8
PICK_FLOPS = 2 * 10 ** 9
BF = jnp.bfloat16
F32 = jnp.float32
VM = pl.BlockSpec(memory_space=pltpu.VMEM)
ANY = pl.BlockSpec(memory_space=pl.ANY)


def wide_slot(w, n, parity):
    return (w & 1) ^ parity ^ 1


def narrow_slot(w, n, parity):
    return 2 + ((n & 1) ^ parity ^ 1)


def mixed_slot(w, n, kind):
    turn = (w ^ (w >> 1) ^ kind) & 1
    return (1 - turn) * wide_slot(w, n, 1) + turn * narrow_slot(w, n, 0)


def has_partner(w, n, slot, wide, narrow):
    inside = [w > 0, w + 1 < wide, n > 0, n + 1 < narrow]
    return sum((slot == k) * inside[k] for k in range(4))


def matchings():
    wide, narrow = lax.axis_size("wide"), lax.axis_size("narrow")
    if narrow == 2 and wide % 4 == 0:
        rules = [(mixed_slot, 0), (mixed_slot, 1), (wide_slot, 0)]
    else:
        rules = [(wide_slot, 1)] * (wide > 2) + [(narrow_slot, 1)] * (narrow > 2)
        rules += [(narrow_slot, 0)] * (narrow > 1) + [(wide_slot, 0)] * (wide > 1)
    found = []
    for rule, kind in rules:
        pairs = []
        for w in range(wide):
            for n in range(narrow):
                slot = rule(w, n, kind)
                if has_partner(w, n, slot, wide, narrow):
                    step = ((-1, 0), (1, 0), (0, -1), (0, 1))[slot]
                    target = (w + step[0], n + step[1])
                elif slot < 2:
                    target = (w, n ^ 1 if n ^ 1 < narrow else n)
                else:
                    target = (w ^ 1 if w ^ 1 < wide else w, n)
                pairs.append((w * narrow + n, target[0] * narrow + target[1]))
        found.append((rule, kind, tuple(pairs)))
    return found


def own_slots(found):
    w, n = lax.axis_index("wide"), lax.axis_index("narrow")
    wide, narrow = lax.axis_size("wide"), lax.axis_size("narrow")
    slots = [rule(w, n, kind) for rule, kind, _ in found]
    return [(slot, has_partner(w, n, slot, wide, narrow) == 1) for slot in slots]


def swap(messages, found):
    return [lax.ppermute(m, ("wide", "narrow"), list(f[-1])) for m, f in zip(messages, found)]


def mm(a, b):
    return jnp.dot(a, b, preferred_element_type=F32)


def mm_t(a, b):
    return lax.dot_general(a, b, (((1,), (1,)), ((), ())), preferred_element_type=F32)


def iota(shape, dim):
    return lax.broadcasted_iota(jnp.int32, shape, dim)


def call(body, outs, args, scratch=(), specs=None, flops=0, limit=8, out_specs=None):
    size = sum(a.size * a.dtype.itemsize for a in args)
    return pl.pallas_call(
        body,
        out_shape=outs,
        in_specs=specs or [VM] * len(args),
        out_specs=out_specs or [VM] * len(outs),
        scratch_shapes=list(scratch),
        compiler_params=pltpu.CompilerParams(vmem_limit_bytes=limit * 1024 * 1024),
        cost_estimate=pl.CostEstimate(flops=flops, bytes_accessed=size, transcendentals=0),
    )(*args)


def join_halo(got):
    pieces = [piece[...] for piece in got]
    return jnp.concatenate(pieces + [jnp.zeros_like(pieces[0])] * (4 - len(pieces)), axis=0)


def send(messages, values):
    width = messages[0].shape[0]
    for m, message in enumerate(messages):
        message[...] = values[m * width:(m + 1) * width, :].astype(BF)


def keep_split(high_ref, low_ref, rows, value):
    high = value.astype(BF)
    high_ref[rows] = high
    low_ref[rows] = (value - high.astype(F32)).astype(BF)


def select_body(found, own, send_ref, select_ref):
    width = send_ref.shape[1]
    diagonal = iota((width, width), 0) == iota((width, width), 1)
    pieces = []
    for slot, paired in own_slots(found):
        rows = jnp.where(paired, send_ref[pl.ds(slot, 1), :], -1).astype(F32)
        pieces.append(jnp.where(diagonal, rows, 0.0))
    column = jnp.sum(jnp.concatenate(pieces, axis=0), axis=1, keepdims=True).astype(jnp.int32)
    select_ref[...] = (iota((len(found) * width, own), 1) == column).astype(F32).astype(BF)


def pick_body(select_ref, rhs_ref, *messages):
    send(messages, mm(select_ref[...], rhs_ref[...]))


def setup_body(found, width, cols_ref, inverse_ref, blocks_ref, rhs_ref, select_ref, *rest):
    inverse_halo_ref, blocks_halo_ref, inverse_sent_ref, blocks_sent_ref, state_ref, base_ref = rest[:6]
    high_ref, low_ref = rest[6:]
    own = rhs_ref.shape[0]
    halo = 4 * width
    places = iota((1, halo), 1)
    starts = jnp.full((1, halo), -halo, jnp.int32)
    for m, (slot, _) in enumerate(own_slots(found)):
        here = lax.div(places, width) == m
        starts = jnp.where(here, slot * width + lax.rem(places, width), starts)
    arrange = (iota((halo, halo), 0) == starts).astype(F32).astype(BF)
    rows, links, size, _ = blocks_ref.shape
    for j in range(rows):
        here = slice(j * size, (j + 1) * size)
        columns = [cols_ref[j, k] for k in range(links)]
        for c in range(halo // size):
            total = None
            for k in range(links):
                part = jnp.where(columns[k] == own // size + c, blocks_ref[j, k].astype(F32), 0.0)
                total = part if total is None else total + part
            lanes = slice(c * size, (c + 1) * size)
            keep_split(high_ref, low_ref, (here, lanes), total)
    for part, half_ref in enumerate((high_ref, low_ref)):
        blocks_halo_ref[part] = mm(half_ref[...], arrange).astype(BF)
    step = own // 2
    for i in range(0, own, step):
        here = slice(i, i + step)
        inverse_halo_ref[here, :] = mm(inverse_ref[here, own:], arrange).astype(BF)
        value = mm(inverse_ref[here, :own], rhs_ref[...])
        state_ref[here, :] = value
        keep_split(high_ref, low_ref, here, value)
    inverse_sent_ref[...] = mm(select_ref[...], inverse_halo_ref[...]).astype(BF)
    sent = select_ref.shape[0]
    for part in range(2):
        here = slice(part * sent, (part + 1) * sent)
        blocks_sent_ref[here, :] = mm(select_ref[...], blocks_halo_ref[part]).astype(BF)
    base_ref[...] = mm(select_ref[...], high_ref[...]) + mm(select_ref[...], low_ref[...])


def sent_update_body(count, base_ref, sent_ref, *rest):
    got, messages = rest[:count], rest[count:]
    send(messages, base_ref[...] + mm(sent_ref[...], join_halo(got)))


def sent_residual_body(count, turn, base_ref, sent_ref, *rest):
    got, messages = rest[:count], rest[count:]
    halo = join_halo(got[turn:] + got[:turn])
    part = mm(sent_ref[...], halo)
    sent = base_ref.shape[0]
    send(messages, base_ref[...] - (part[:sent] + part[sent:]))


def update_body(count, cols_ref, state_ref, inverse_halo_ref, blocks_ref, rhs_ref, select_ref, *rest):
    got, (iterate_ref, part_ref, base_ref, sub_ref, high_ref, low_ref) = rest[:count], rest[count:]
    own = state_ref.shape[0]
    halo = join_halo(got)
    step = own // 2
    for i in range(0, own, step):
        here = slice(i, i + step)
        value = state_ref[here, :] + mm(inverse_halo_ref[here, :], halo)
        iterate_ref[here, :] = value
        sub_ref[here, :] = value.astype(BF)
    sub_ref[own:, :] = jnp.zeros((sub_ref.shape[0] - own, sub_ref.shape[1]), BF)
    rows, links, size, _ = blocks_ref.shape
    for j in range(rows):
        starts = [pl.multiple_of(cols_ref[j, k] * size, size) for k in range(links)]
        values = jnp.concatenate([blocks_ref[j, k] for k in range(links)], axis=1)
        coupled = jnp.concatenate([sub_ref[pl.ds(start, size), :] for start in starts], axis=0)
        total = mm(values, coupled)
        here = slice(j * size, (j + 1) * size)
        value = rhs_ref[here, :].astype(F32) - total
        part_ref[here, :] = value
        keep_split(high_ref, low_ref, here, value)
    base_ref[...] = mm(select_ref[...], high_ref[...]) + mm(select_ref[...], low_ref[...])


def residual_body(count, turn, part_ref, blocks_halo_ref, iterate_ref, inverse_ref, select_ref, *rest):
    got, rest = rest[:count], list(rest[count:])
    state_ref = rest.pop(0)
    resid_ref, *split = rest[-3:] if len(rest) == 4 else rest
    own = part_ref.shape[0]
    halo = join_halo(got[turn:] + got[:turn])
    step = own // 2
    for i in range(0, own, step):
        here = slice(i, i + step)
        outer = mm(blocks_halo_ref[0, here, :], halo) + mm(blocks_halo_ref[1, here, :], halo)
        resid_ref[here, :] = (part_ref[here, :] - outer).astype(BF)
    for i in range(0, own, step):
        here = slice(i, i + step)
        value = iterate_ref[here, :] + mm(inverse_ref[here, :own], resid_ref[...])
        state_ref[here, :] = value
        if split:
            keep_split(*split, here, value)
    if split:
        rest[0][...] = mm(select_ref[...], split[0][...]) + mm(select_ref[...], split[1][...])


def last_update_body(count, state_ref, inverse_halo_ref, *rest):
    got, (round_ref,) = rest[:count], rest[count:]
    halo = join_halo(got)
    step = state_ref.shape[0] // 2
    for i in range(0, state_ref.shape[0], step):
        here = slice(i, i + step)
        round_ref[here, :] = (state_ref[here, :] + mm(inverse_halo_ref[here, :], halo)).astype(BF)


def turn_body(state_ref, order_ref, turned_ref):
    value = state_ref[...]
    high = value.astype(BF)
    low = (value - high.astype(F32)).astype(BF)
    columns = value.shape[1]
    both = mm(jnp.concatenate([high, low], axis=1).T, order_ref[...])
    turned_ref[...] = both[:columns] + both[columns:]


def wire_body(count, turned_ref, halo_table_ref, *rest):
    got, (wire_ref,) = rest[:count], rest[count:]
    halo = jnp.concatenate([piece[...] for piece in got], axis=0)
    part = lax.dot_general(
        halo, halo_table_ref[:halo.shape[0], :], (((0,), (0,)), ((), ())), preferred_element_type=F32
    )
    wire_ref[...] = (turned_ref[...] + part).astype(BF)


def one_hot(rows_of, shape):
    return (iota(shape, 0) == rows_of(iota((1, shape[1]), 1))).astype(F32).astype(BF)


def order_body(inverse_halo_ref, order_ref, halo_table_ref):
    own = order_ref.shape[0]
    tile = own // ZL
    order_ref[...] = one_hot(lambda k: lax.rem(k, ZL) * tile + lax.div(k, ZL), (own, own))
    halo_table_ref[...] = mm(inverse_halo_ref[...].T, order_ref[...]).astype(BF)


def tables_body(wide, narrow, cov_plane_ref, cov_vert_ref, plane_ref, spread_ref, vert_ref):
    plane = plane_ref.shape[0]
    tile = plane // wide
    turn = one_hot(lambda k: lax.rem(k, wide) * tile + lax.div(k, wide), (plane, plane))
    half = mm(cov_plane_ref[...], turn).astype(BF)
    plane_ref[...] = mm(half.T, turn).astype(BF).T
    share = LANES // ZL
    depth = narrow * ZL
    width = narrow * LANES

    def source(k):
        e, n, l = lax.div(k, depth), lax.rem(lax.div(k, ZL), narrow), lax.rem(k, ZL)
        return n * LANES + e * ZL + l

    spread = one_hot(source, (width, width))
    spread_ref[...] = spread
    turned = cov_vert_ref[...].astype(F32).T
    zero = jnp.zeros_like(turned)
    blocks = jnp.concatenate(
        [jnp.concatenate([turned if i == e else zero for i in range(share)], axis=1) for e in range(share)],
        axis=0,
    ).astype(BF)
    vert_ref[...] = mm_t(blocks, spread).astype(BF)


def mix_body(wide, narrow, group, in_ref, plane_ref, spread_ref, vert_ref, state_ref, inverse_halo_ref, *rest):
    got, (out_ref, adjoint_hbm, cells_ref, flat_ref, wire_ref, round_ref, sem) = rest[:-7], rest[-7:]
    last_update_body(len(got), state_ref, inverse_halo_ref, *got, round_ref)
    keep = pltpu.make_async_copy(round_ref, adjoint_hbm, sem)
    keep.start()
    own = in_ref.shape[1]
    tile = own // ZL
    share = LANES // ZL
    depth = narrow * ZL
    block = wide * group
    pairs = tile // share
    halves = [range(0, pairs // 2), range(pairs // 2, pairs)]
    for half in halves:
        joined = jnp.concatenate(
            [
                jnp.concatenate(
                    [in_ref[n * block:(n + 1) * block, g * LANES:(g + 1) * LANES] for n in range(narrow)], axis=1
                )
                for g in half
            ],
            axis=0,
        )
        spread = mm(joined, spread_ref[...])
        for i, g in enumerate(half):
            for e in range(share):
                cells_ref[g * share + e, :block, :] = spread[i * block:(i + 1) * block, e * depth:(e + 1) * depth]
    for r in range(group):
        for c in range(tile):
            flat_ref[c * wide:(c + 1) * wide, r * depth:(r + 1) * depth] = cells_ref[
                c, pl.ds(r, wide, stride=group), :
            ].astype(BF)
    planar = mm(plane_ref[...], flat_ref[...]).astype(BF)
    for half in halves:
        stacked = jnp.concatenate(
            [
                jnp.concatenate(
                    [
                        planar[c * wide:(c + 1) * wide, r * depth:(r + 1) * depth]
                        for c in range(g * share, (g + 1) * share)
                    ],
                    axis=1,
                )
                for g in half
                for r in range(group)
            ],
            axis=0,
        )
        mixed = mm(stacked, vert_ref[...])
        for i, g in enumerate(half):
            for r in range(group):
                rows = slice(i * block + r * wide, i * block + (r + 1) * wide)
                for n in range(narrow):
                    wire_ref[g, pl.ds(n * block + r, wide, stride=group), :] = mixed[
                        rows, n * LANES:(n + 1) * LANES
                    ]
            out_ref[:, g * LANES:(g + 1) * LANES] = wire_ref[g, :narrow * block, :].astype(BF)
    keep.wait()


def unwire_body(in_ref, out_hbm, out_ref, sems):
    own = out_ref.shape[0]
    tile = own // ZL
    runs = sems.shape[0]
    run = ZL // runs
    step = run * tile
    small = one_hot(lambda k: lax.rem(k, run) * tile + lax.div(k, run), (step, step))
    turned = in_ref[...].T
    copies = []
    for b in range(runs):
        here = pl.ds(b * step, step)
        piece = jnp.concatenate([turned[c * ZL + b * run:c * ZL + (b + 1) * run] for c in range(tile)], axis=0)
        out_ref[here, :] = mm(small, piece).astype(BF)
        copy = pltpu.make_async_copy(out_ref.at[here], out_hbm.at[here], sems.at[b])
        copy.start()
        copies.append(copy)
    for copy in copies:
        copy.wait()


def column_tables(inverse_halo, cov_plane, cov_vert):
    own, halo = inverse_halo.shape
    wide, narrow = lax.axis_size("wide"), lax.axis_size("narrow")
    width = narrow * LANES
    plane = cov_plane.shape[0]
    shape = jax.ShapeDtypeStruct
    order = call(order_body, [shape((own, own), BF), shape((halo, own), BF)], [inverse_halo])
    rest = call(
        functools.partial(tables_body, wide, narrow),
        [shape((plane, plane), BF), shape((width, width), BF), shape((width, width), BF)],
        [cov_plane, cov_vert],
    )
    return [tuple(order), tuple(rest)]


def smooth_by_columns(state, inverse_halo, got, tables):
    wide, narrow = lax.axis_size("wide"), lax.axis_size("narrow")
    own, columns = state.shape
    devices = wide * narrow
    group = columns // devices
    depth = narrow * ZL
    tile = own // ZL
    shape = jax.ShapeDtypeStruct
    (order, halo_table), (plane_mix, spread, vert_mix) = tables
    (turned,) = call(turn_body, [shape((columns, own), F32)], [state, order])
    (wire,) = call(functools.partial(wire_body, len(got)), [shape((columns, own), BF)], [turned, halo_table, *got])
    there = lax.all_to_all(
        wire.reshape(devices, group, own), ("narrow", "wide"), split_axis=0, concat_axis=0, tiled=True
    )
    mixed, adjoint = call(
        functools.partial(mix_body, wide, narrow, group),
        [shape((columns, own), BF), shape((own, columns), BF)],
        [there.reshape(columns, own), plane_mix, spread, vert_mix, state, inverse_halo, *got],
        [
            pltpu.VMEM((tile, wide * group + group, depth), F32),
            pltpu.VMEM((plane_mix.shape[0], group * depth), BF),
            pltpu.VMEM((own // LANES, columns + group, LANES), F32),
            pltpu.VMEM((own, columns), BF),
            pltpu.SemaphoreType.DMA,
        ],
        out_specs=[VM, ANY],
    )
    back = lax.all_to_all(
        mixed.reshape(devices, group, own), ("narrow", "wide"), split_axis=0, concat_axis=0, tiled=True
    )
    (smoothed,) = call(
        unwire_body,
        [shape((own, columns), BF)],
        [back.reshape(columns, own)],
        [pltpu.VMEM((own, columns), BF), pltpu.SemaphoreType.DMA((4,))],
        out_specs=[ANY],
    )
    return adjoint, smoothed


def smooth_by_layers(adjoint, cov_plane, cov_vert):
    own, columns = adjoint.shape
    layered = adjoint.reshape(ZL, own // ZL, -1)
    planar = jnp.einsum(
        "pq,lqr->lpr",
        cov_plane,
        lax.all_to_all(layered, "wide", split_axis=0, concat_axis=1, tiled=True),
        preferred_element_type=F32,
    ).astype(BF)
    restored = lax.all_to_all(planar, "wide", split_axis=1, concat_axis=0, tiled=True)
    slab_weights = lax.dynamic_slice_in_dim(cov_vert, lax.axis_index("narrow") * ZL, ZL, 0)
    summed = jnp.dot(
        slab_weights,
        lax.all_gather(restored.reshape(ZL, -1), "narrow", axis=0, tiled=True),
        preferred_element_type=F32,
    )
    return summed.astype(BF).reshape(own, -1)


def shards(adjoint_rhs, inverse_rows, blocks, block_cols, send_rows, cov_plane, cov_vert):
    rhs = adjoint_rhs[0, 0]
    inverse = inverse_rows[0, 0]
    block_values = blocks[0, 0]
    cols = block_cols[0, 0]
    send_index = send_rows[0, 0]
    own, columns = rhs.shape
    width = send_index.shape[1]
    halo = 4 * width
    wide, narrow = lax.axis_size("wide"), lax.axis_size("narrow")
    group = columns // (wide * narrow)
    by_columns = columns % (wide * narrow) == 0 and group % 8 == 0 and narrow * ZL == LANES and wide % 16 == 0
    found = matchings()
    count = len(found)
    sent = count * width
    shape = jax.ShapeDtypeStruct
    notes = [shape((width, columns), BF)] * count
    full = shape((own, columns), F32)
    base_shape = shape((sent, columns), F32)
    cell_space = pltpu.VMEM((own, columns), BF)
    (select,) = call(
        functools.partial(select_body, found, own),
        [shape((sent, own), BF)],
        [send_index],
        flops=SELECT_FLOPS,
    )
    messages = call(pick_body, notes, [select, rhs], flops=PICK_FLOPS)
    got = swap(messages, found)
    inverse_halo, blocks_halo, inverse_sent, blocks_sent, state, base = call(
        functools.partial(setup_body, found, width),
        [
            shape((own, halo), BF),
            shape((2, own, halo), BF),
            shape((sent, halo), BF),
            shape((2 * sent, halo), BF),
            full,
            base_shape,
        ],
        [cols, inverse, block_values, rhs, select],
        [cell_space, cell_space],
        limit=12,
    )
    tables = column_tables(inverse_halo, cov_plane, cov_vert) if by_columns else []
    for sweep in range(SWEEPS - 1):
        messages = call(
            functools.partial(sent_update_body, count), notes, [base, inverse_sent, *got], limit=4
        )
        arrived, got = got, swap(messages, found)
        iterate, part, base = call(
            functools.partial(update_body, count),
            [full, full, base_shape],
            [cols, state, inverse_halo, block_values, rhs, select, *arrived],
            [pltpu.VMEM((own + halo, columns), BF), cell_space, cell_space],
        )
        turn = 1 if sweep == 1 and count == 3 else 0
        arrived = got[count - turn:] + got[:count - turn]
        messages = call(
            functools.partial(sent_residual_body, count, turn),
            notes,
            [base, blocks_sent, *arrived],
            limit=4,
        )
        got = swap(messages, found)
        if sweep < len(tables):
            tables[sweep], part = lax.optimization_barrier((tables[sweep], part))
        more = sweep < SWEEPS - 2
        state, *bases = call(
            functools.partial(residual_body, count, turn),
            [full] + [base_shape] * more,
            [part, blocks_halo, iterate, inverse, select, *arrived],
            [cell_space] * (1 + 2 * more),
        )
        base = bases[0] if more else None
    if by_columns:
        adjoint, smoothed = smooth_by_columns(state, inverse_halo, got, tables)
    else:
        cells = shape((own, columns), BF)
        (adjoint,) = call(functools.partial(last_update_body, count), [cells], [state, inverse_halo, *got])
        smoothed = smooth_by_layers(adjoint, cov_plane, cov_vert)
    return (adjoint[None, None], smoothed[None, None])


def solution(mesh):
    in_specs = (
        P("wide", "narrow", None, None),
        P("wide", "narrow", None, None),
        P("wide", "narrow", None, None, None, None),
        P("wide", "narrow", None, None),
        P("wide", "narrow", None, None),
        P(),
        P(),
    )
    out_specs = (P("wide", "narrow", None, None), P("wide", "narrow", None, None))
    return jax.shard_map(shards, mesh=mesh, in_specs=in_specs, out_specs=out_specs, check_vma=False)
```
